32 devices in a mesh: pole: 4 (over y, x), tile: 8 (over z, core).
Axes of the slice: x: 2, y: 2, z: 4, core: 2. Of those that a mesh axis runs over, the one named last changes fastest.
Arguments:
- state: float32 [3, 128, 2048], P(None, 'tile', 'pole'), may hold values from -6 to 6
- depth: float32 [128, 2048], P('tile', 'pole'), may hold values from 0.5 to 2
- pole_real: float32 [16], P('pole'), may hold values from -1.5 to -0.5
- pole_imag: float32 [16], P('pole'), may hold values from -2 to 2
- pole_weight: float32 [2, 16], P(None, 'pole'), may hold values from -3 to 3
Outputs:
- advanced: float32 [3, 128, 2048], P(None, 'tile', 'pole')
The draws below stay inside these ranges and needn't reach their ends.
All inputs are finite; a program needn't handle non-finite values.
Results may differ from the reference program's by a relative error of at most 0.00002.
Values sent between devices are 32-bit elements; how exact they have to be, the bound alone decides.
No kernel may reach another device: no remote copies, remote signals or barrier semaphores. Data moves between devices by JAX's collectives and lax.ppermute only.
A program may use at most 64 MiB of HBM per device.

```python
import jax
import jax.numpy as jnp

ITERS = 8
NX = 128
NY = 2048
POLES = 16


def levels(key, dims, pieces, low, largest):
    level = 1.0
    for dim, shards_of in pieces:
        heights = jax.random.uniform(jax.random.fold_in(jax.random.fold_in(key, 6), dim), (shards_of,), jnp.float32, low / len(pieces), largest / len(pieces))
        level = level * jnp.repeat(jnp.exp(heights), dims[dim] // shards_of).reshape((-1,) + (1,) * (len(dims) - 1 - dim))
    return level


def noise(rng, dims, scale, reach, shards=(), kind=jnp.bfloat16):
    gain = levels(rng, dims, shards, -0.22, 0.18) if shards else 1.0
    values = jax.random.normal(rng, dims, jnp.float32) * scale * gain
    return jnp.minimum(jnp.maximum(values, -reach), reach).astype(kind)


def setup_inputs(seed: int = 0) -> dict:
    key_of = jax.random.split(jax.random.key(seed), 6)
    state = noise(key_of[0], (3, NX, NY), 1.0, 6.0, ((1, 8), (2, 4)), jnp.float32)
    depth = jnp.clip(0.5 + 1.5 * jax.random.uniform(key_of[1], (NX, NY), jnp.float32) ** levels(key_of[1], (NX, NY), ((0, 8), (1, 4)), -0.2, 0.2), 0.5, 2.0)
    pole_real = jnp.clip(-1.5 + 1.0 * jax.random.uniform(key_of[2], (POLES,), jnp.float32) ** levels(key_of[2], (POLES,), ((0, 4),), -0.2, 0.2), -1.5, -0.5)
    pole_imag = jnp.clip(jax.random.uniform(key_of[3], (POLES,), jnp.float32, -2.0, 2.0) * levels(key_of[3], (POLES,), ((0, 4),), -0.4, 0.0), -2.0, 2.0)
    pole_weight = noise(key_of[4], (2, POLES), 0.5, 3.0, ((1, 4),), jnp.float32)
    return dict(state=state, depth=depth, pole_real=pole_real, pole_imag=pole_imag, pole_weight=pole_weight)


coriolis = 0.7
centre = 8.0
half_width = 8.0


def complex_product(left_real, left_imaginary, right_real, right_imaginary):
    return (left_real * right_real - left_imaginary * right_imaginary,
            left_real * right_imaginary + left_imaginary * right_real)


def complex_quotient(top_real, top_imaginary, under_real, under_imaginary):
    norm = under_real * under_real + under_imaginary * under_imaginary
    return ((top_real * under_real + top_imaginary * under_imaginary) / norm,
            (top_imaginary * under_real - top_real * under_imaginary) / norm)


def chebyshev_table(alpha_real, alpha_imaginary):
    shift_real = alpha_real * alpha_real - alpha_imaginary * alpha_imaginary + coriolis * coriolis
    shift_imaginary = 2.0 * alpha_real * alpha_imaginary
    sigma_real = (shift_real + centre) / half_width
    sigma_imaginary = shift_imaginary / half_width
    unity = jnp.ones_like(sigma_real)
    nought = jnp.zeros_like(sigma_real)
    rho_real, rho_imaginary = complex_quotient(unity, nought, sigma_real, sigma_imaginary)
    table = []
    for index in range(ITERS - 1):
        next_real, next_imaginary = complex_quotient(unity, nought, 2.0 * sigma_real - rho_real, 2.0 * sigma_imaginary - rho_imaginary)
        keep_real, keep_imaginary = complex_product(next_real, next_imaginary, rho_real, rho_imaginary)
        table.append((keep_real, keep_imaginary, 2.0 * next_real / half_width, 2.0 * next_imaginary / half_width))
        rho_real, rho_imaginary = next_real, next_imaginary
    return shift_real, shift_imaginary, table


def advance(entry, search_real, search_imaginary, resid_real, resid_imaginary):
    first_real, first_imaginary = complex_product(entry[0], entry[1], search_real, search_imaginary)
    second_real, second_imaginary = complex_product(entry[2], entry[3], resid_real, resid_imaginary)
    return first_real + second_real, first_imaginary + second_imaginary


def row_slope(field):
    return 0.5 * (jnp.roll(field, -1, 0) - jnp.roll(field, 1, 0))


def column_slope(field):
    return 0.5 * (jnp.roll(field, -1, 1) - jnp.roll(field, 1, 1))


def periodic_stiffness(field, depth):
    east = 0.5 * (depth + jnp.roll(depth, -1, 0)) * (jnp.roll(field, -1, 0) - field)
    north = 0.5 * (depth + jnp.roll(depth, -1, 1)) * (jnp.roll(field, -1, 1) - field)
    return -(east - jnp.roll(east, 1, 0) + north - jnp.roll(north, 1, 1))


def reference(state, depth, pole_real, pole_imag, pole_weight):
    height = state[0]
    east_speed = state[1]
    north_speed = state[2]
    flux_div = row_slope(depth * east_speed) + column_slope(depth * north_speed)
    flux_curl = row_slope(depth * north_speed) - column_slope(depth * east_speed)
    shift_all_real, shift_all_imaginary, table_all = chebyshev_table(pole_real, pole_imag)
    out_height = jnp.zeros_like(height)
    out_east = jnp.zeros_like(height)
    out_north = jnp.zeros_like(height)
    for pole in range(POLES):
        alpha_real = pole_real[pole]
        alpha_imaginary = pole_imag[pole]
        shift_real = shift_all_real[pole]
        shift_imaginary = shift_all_imaginary[pole]
        top_real = shift_real * height - alpha_real * flux_div - coriolis * flux_curl
        top_imaginary = shift_imaginary * height - alpha_imaginary * flux_div
        rhs_real, rhs_imaginary = complex_quotient(top_real, top_imaginary, alpha_real, alpha_imaginary)
        resid_real, resid_imaginary = rhs_real, rhs_imaginary
        search_real, search_imaginary = complex_quotient(rhs_real, rhs_imaginary, shift_real + centre, shift_imaginary)
        iterate_real = jnp.zeros_like(rhs_real)
        iterate_imaginary = jnp.zeros_like(rhs_real)
        for index in range(ITERS):
            image_real = shift_real * search_real - shift_imaginary * search_imaginary + periodic_stiffness(search_real, depth)
            image_imaginary = shift_real * search_imaginary + shift_imaginary * search_real + periodic_stiffness(search_imaginary, depth)
            iterate_real = iterate_real + search_real
            iterate_imaginary = iterate_imaginary + search_imaginary
            resid_real = resid_real - image_real
            resid_imaginary = resid_imaginary - image_imaginary
            if index < ITERS - 1:
                entry = tuple(part[pole] for part in table_all[index])
                search_real, search_imaginary = advance(entry, search_real, search_imaginary, resid_real, resid_imaginary)
        weight_real = pole_weight[0, pole]
        weight_imaginary = pole_weight[1, pole]
        scale_real, scale_imaginary = complex_quotient(weight_real, weight_imaginary, shift_real, shift_imaginary)
        push_real = east_speed - row_slope(iterate_real)
        push_imaginary = -row_slope(iterate_imaginary)
        lift_real = north_speed - column_slope(iterate_real)
        lift_imaginary = -column_slope(iterate_imaginary)
        east_real, east_imaginary = complex_product(alpha_real, alpha_imaginary, push_real, push_imaginary)
        east_real = east_real + coriolis * lift_real
        east_imaginary = east_imaginary + coriolis * lift_imaginary
        north_real, north_imaginary = complex_product(alpha_real, alpha_imaginary, lift_real, lift_imaginary)
        north_real = north_real - coriolis * push_real
        north_imaginary = north_imaginary - coriolis * push_imaginary
        out_height = out_height + (weight_real * iterate_real - weight_imaginary * iterate_imaginary)
        out_east = out_east + (scale_real * east_real - scale_imaginary * east_imaginary)
        out_north = out_north + (scale_real * north_real - scale_imaginary * north_imaginary)
    return jnp.stack([out_height, out_east, out_north])
```

```python
import functools

import jax
import jax.numpy as jnp
from jax import lax
from jax.experimental import pallas as pl
from jax.experimental.pallas import tpu as pltpu
from jax.sharding import PartitionSpec as P

ITERS = 8
REACH = ITERS + 1
SUB = 8
LANES = 128
SIDE = 32

coriolis = 0.7
centre = 8.0
half_width = 8.0


def pairs(count, phase):
    swap = []
    for i in range(phase, count + phase, 2):
        a, b = i % count, (i + 1) % count
        swap += [(a, b), (b, a)]
    return swap


def swap(block, axis, phase):
    return lax.ppermute(block, axis, pairs(lax.axis_size(axis), phase))


def shift(block, axis, step):
    count = lax.axis_size(axis)
    return lax.ppermute(block, axis, [(i, (i + step) % count) for i in range(count)])


def cmul(a, b):
    return (a[0] * b[0] - a[1] * b[1], a[0] * b[1] + a[1] * b[0])


def cinv(a):
    norm = 1.0 / (a[0] * a[0] + a[1] * a[1])
    return (a[0] * norm, -a[1] * norm)


def cscale(a, factor):
    return (a[0] * factor, a[1] * factor)


def pack_rows_kernel(state, depth, real, imag, weight, near, far, scalars):
    odd = lax.rem(lax.axis_index("tile"), 2) == 1
    rows = depth.shape[0]
    fields = [state.at[0], state.at[1], state.at[2], depth]
    for target, low in ((near, odd), (far, jnp.logical_not(odd))):
        @pl.when(low)
        def _():
            for f, field in enumerate(fields):
                target[f * SUB : (f + 1) * SUB] = field[0:SUB]
                target[4 * SUB + f : 4 * SUB + f + 1] = field[SUB : SUB + 1]

        @pl.when(jnp.logical_not(low))
        def _():
            for f, field in enumerate(fields):
                target[f * SUB : (f + 1) * SUB] = field[rows - SUB : rows]
                target[4 * SUB + f : 4 * SUB + f + 1] = field[rows - SUB - 1 : rows - SUB]

    poles = real.shape[0]
    values = [real[i] for i in range(poles)] + [imag[i] for i in range(poles)]
    values += [weight[0, i] for i in range(poles)] + [weight[1, i] for i in range(poles)]
    for i, value in enumerate(values):
        scalars[i : i + 1] = jnp.full((1, LANES), value, jnp.float32)


def column_block(fields, start):
    lane = lax.broadcasted_iota(jnp.int32, fields[0].shape, 1)
    total = None
    for f, field in enumerate(fields):
        turn = (SIDE * f - start) % LANES
        turned = pltpu.roll(field, turn, 1) if turn else field
        total = turned if total is None else jnp.where(lane < SIDE * f, total, turned)
    return total


def pack_columns_kernel(state, depth, near, far, scalars, first, second):
    odd = lax.rem(lax.axis_index("pole"), 2) == 1
    rows, columns = depth.shape
    own = [state.at[0], state.at[1], state.at[2], depth]

    def edge(side):
        lanes = pl.ds(0, LANES) if side == 0 else pl.ds(columns - LANES, LANES)
        start = 0 if side == 0 else LANES - SIDE
        out = []
        for g in range(rows // SUB):
            out.append(column_block([field[pl.ds(g * SUB, SUB), lanes] for field in own], start))
        for halo in (near, far):
            out.append(
                column_block([halo[pl.ds(f * SUB, SUB), lanes] for f in range(4)], start)
            )
        ext = jnp.concatenate(
            [near[pl.ds(4 * SUB, 4), lanes], far[pl.ds(4 * SUB, 4), lanes]], axis=0
        )
        out.append(pltpu.roll(ext, SIDE, 1) if start else ext)
        return out

    left = edge(0)
    right = edge(1)
    for i, (a, b) in enumerate(zip(left, right)):
        first[pl.ds(i * SUB, SUB)] = jnp.where(odd, a, b)
        second[pl.ds(i * SUB, SUB)] = jnp.where(odd, b, a)
    base = len(left) * SUB
    first[pl.ds(base, scalars.shape[0])] = scalars[...]
    second[pl.ds(base, scalars.shape[0])] = scalars[...]


def strips_of(tiles, west, east):
    lane = lax.broadcasted_iota(jnp.int32, (SUB, LANES), 1)
    up = [pltpu.roll(tile, SIDE, 1) for tile in tiles]
    down = [pltpu.roll(tile, LANES - SIDE, 1) for tile in tiles]
    out = []
    for q in range(len(tiles)):
        out.append(jnp.where(lane < SIDE, up[q - 1] if q else west, up[q]))
        after = down[q + 1] if q + 1 < len(tiles) else east
        out.append(jnp.where(lane < LANES - SIDE, down[q], after))
    return out


def step_kernel(state, depth, near, far, first, second, scalars, others, out, grid, poly, coef, result):
    rows, columns = depth.shape
    groups = rows // SUB
    tiles = columns // LANES
    odd_pole = lax.rem(lax.axis_index("pole"), 2) == 1
    odd_tile = lax.rem(lax.axis_index("tile"), 2) == 1
    own = [state.at[0], state.at[1], state.at[2], depth]

    def sides(index):
        one = first[pl.ds(index * SUB, SUB)]
        two = second[pl.ds(index * SUB, SUB)]
        return jnp.where(odd_pole, one, two), jnp.where(odd_pole, two, one)

    def turned(block, turn):
        return pltpu.roll(block, turn % LANES, 1) if turn % LANES else block

    def lay(block, west, east, f, at, size, stride):
        cut = [block[:, t * LANES : (t + 1) * LANES] for t in range(tiles)]
        strips = strips_of(cut, turned(west, -SIDE * f), turned(east, LANES - SIDE - SIDE * f))
        for s, strip in enumerate(strips):
            grid[pl.Slice(at * SUB + s, size, stride * SUB), :] = strip[0:size]

    for g in range(groups):
        west, east = sides(g)
        for f in range(4):
            block = own[f][pl.ds(g * SUB, SUB), :]
            lay(block, west, east, f, (REACH + g * SUB) * 4 + f, SUB, 4)
    below = REACH + rows
    near_main = jnp.where(odd_tile, 1, below)
    far_main = jnp.where(odd_tile, below, 1)
    near_ext = jnp.where(odd_tile, 0, below + SUB)
    far_ext = jnp.where(odd_tile, below + SUB, 0)
    for i, (halo, main) in enumerate(((near, near_main), (far, far_main))):
        west, east = sides(groups + i)
        for f in range(4):
            lay(halo[pl.ds(f * SUB, SUB), :], west, east, f, main * 4 + f, SUB, 4)
    west, east = sides(groups + 2)
    lay(near[pl.ds(4 * SUB, SUB), :], west, east, 0, near_ext * 4, 4, 1)
    west = pltpu.roll(west, 4, 0)
    east = pltpu.roll(east, 4, 0)
    lay(far[pl.ds(4 * SUB, SUB), :], west, east, 0, far_ext * 4, 4, 1)

    def cell(f, r):
        return grid[pl.ds((r * 4 + f) * SUB, SUB), :]

    def left(x):
        return pltpu.roll(x, 1, 1)

    def right(x):
        return pltpu.roll(x, LANES - 1, 1)

    height = rows + 2 * REACH

    across = {}
    flux_east = {}
    flux_north = {}
    for r in range(height):
        h = cell(3, r)
        flux_east[r] = h * cell(1, r)
        flux_north[r] = h * cell(2, r)
        if r < height - 1:
            across[r] = 0.125 * (h + cell(3, r + 1))
            coef[0, r] = across[r]
        if 1 <= r < height - 1:
            north = 0.125 * (h + right(h))
            south = left(north)
            coef[1, r] = north
            coef[2, r] = south
            coef[3, r] = 2.0 - ((across[r] + across[r - 1]) + (north + south))
        if r >= 2:
            c = r - 1
            east_slope = flux_east[r] - flux_east[r - 2]
            north_slope = right(flux_north[c]) - left(flux_north[c])
            poly[1, 0, c] = 0.5 * (east_slope + north_slope)
            east_slope = flux_north[r] - flux_north[r - 2]
            north_slope = right(flux_east[c]) - left(flux_east[c])
            poly[2, 0, c] = 0.5 * (east_slope - north_slope)
            poly[0, 0, c] = cell(0, c)

    blocks = [scalars[...], first[pl.ds((groups + 3) * SUB, scalars.shape[0])]]
    blocks += [second[pl.ds((groups + 3) * SUB, scalars.shape[0])]]
    blocks += [others[i] for i in range(others.shape[0])]
    poles = scalars.shape[0] // 4
    quantity = []
    for q in range(4):
        cut = [b[q * poles : (q + 1) * poles] for b in blocks]
        quantity.append(jnp.concatenate(cut, axis=0))
    alpha = (quantity[0], quantity[1])
    beta = (quantity[2], quantity[3])
    square = cmul(alpha, alpha)
    shifted = (square[0] + coriolis * coriolis, square[1])
    sigma = ((shifted[0] + centre) / half_width, shifted[1] / half_width)
    rho = [cinv(sigma)]
    for j in range(1, ITERS):
        rho.append(cinv((2.0 * sigma[0] - rho[-1][0], 2.0 * sigma[1] - rho[-1][1])))
    gain = None
    start = []
    for m in range(ITERS):
        if m == 0:
            start.append(cscale(rho[0], 1.0 / half_width))
        else:
            gain = rho[0] if gain is None else cmul(gain, rho[m - 1])
            start.append(cscale(cmul(rho[m], gain), 2.0 / half_width))
    tail = None
    weight = [None] * ITERS
    for m in reversed(range(ITERS)):
        if tail is None:
            weight[m] = start[m]
            tail = (jnp.ones_like(sigma[0]), jnp.zeros_like(sigma[0]))
        else:
            tail = cmul(cmul(rho[m + 1], rho[m]), tail)
            tail = (tail[0] + 1.0, tail[1])
            weight[m] = cmul(start[m], tail)
    inverse_alpha = cinv(alpha)
    inverse_shift = cinv(shifted)
    by_alpha = cmul(beta, inverse_alpha)
    by_shift = cmul(beta, inverse_shift)
    products = {
        "b": beta,
        "b/a": by_alpha,
        "b/s": by_shift,
        "bs/a": cmul(by_alpha, shifted),
        "ba/s": cmul(by_shift, alpha),
        "b/as": cmul(by_alpha, inverse_shift),
    }

    def total(x):
        s = x[0:SUB]
        for i in range(1, x.shape[0] // SUB):
            s = s + x[i * SUB : (i + 1) * SUB]
        for turn in (4, 2, 1):
            s = s + pltpu.roll(s, turn, 0)
        return s

    names = [("bs/a", "b", "b/a"), ("b", "ba/s", "b/s"), ("b/a", "b/s", "b/as")]
    factor = (1.0, -1.0, -coriolis)
    sums = {}
    for name in products:
        for m in range(ITERS):
            w = products[name]
            sums[name, m] = total(w[0] * weight[m][0] - w[1] * weight[m][1])
    push = total(products["ba/s"][0])
    lift = coriolis * total(products["b/s"][0])

    for m in range(ITERS - 1):
        for r in range(m + 2, height - m - 2):
            above, below_, north, south, diag = (
                coef[0, r],
                coef[0, r - 1],
                coef[1, r],
                coef[2, r],
                coef[3, r],
            )
            for f in range(3):
                w = poly[f, m, r]
                value = diag * w + (above * poly[f, m, r + 1] + below_ * poly[f, m, r - 1])
                value = value + (north * right(w) + south * left(w))
                if m == 0:
                    value = 0.5 * value
                else:
                    value = value - poly[f, m - 1, r]
                poly[f, m + 1, r] = value

    sol = {}
    for r in range(REACH - 1, REACH + rows + 1):
        for g in range(3):
            if g == 0 and not REACH <= r < REACH + rows:
                continue
            acc = None
            for f in range(3):
                part = None
                for m in range(ITERS):
                    term = sums[names[g][f], m] * poly[f, m, r]
                    part = term if part is None else part + term
                part = part if f == 0 else factor[f] * part
                acc = part if acc is None else acc + part
            sol[g, r] = acc
    for i in range(rows):
        r = REACH + i
        u, v = cell(1, r), cell(2, r)
        result[0, pl.ds(i * SUB, SUB)] = sol[0, r]
        east = 0.5 * (sol[1, r + 1] - sol[1, r - 1])
        north = 0.5 * (right(sol[2, r]) - left(sol[2, r]))
        result[1, pl.ds(i * SUB, SUB)] = (push * u + lift * v) - (east + coriolis * north)
        east = 0.5 * (sol[2, r + 1] - sol[2, r - 1])
        north = 0.5 * (right(sol[1, r]) - left(sol[1, r]))
        result[2, pl.ds(i * SUB, SUB)] = (push * v - lift * u) + (coriolis * east - north)

    lane = lax.broadcasted_iota(jnp.int32, (SUB, LANES), 1)
    for k in range(3):
        for g in range(groups):
            for t in range(tiles):
                one = result[k, pl.Slice(g * SUB * SUB + 2 * t, SUB, SUB), :]
                two = result[k, pl.Slice(g * SUB * SUB + 2 * t + 1, SUB, SUB), :]
                joined = jnp.where(
                    lane < LANES // 2, pltpu.roll(one, LANES - SIDE, 1), pltpu.roll(two, SIDE, 1)
                )
                out[k, pl.ds(g * SUB, SUB), pl.ds(t * LANES, LANES)] = joined


def shards(state, depth, pole_real, pole_imag, pole_weight):
    rows, columns = depth.shape
    poles = pole_real.shape[0]
    vmem = pl.BlockSpec(memory_space=pltpu.VMEM)
    smem = pl.BlockSpec(memory_space=pltpu.SMEM)
    f32 = jnp.float32
    halo = jax.ShapeDtypeStruct((5 * SUB, columns), f32)
    near, far, scalars = pl.pallas_call(
        pack_rows_kernel,
        out_shape=(halo, halo, jax.ShapeDtypeStruct((4 * poles, LANES), f32)),
        in_specs=[vmem, vmem, smem, smem, smem],
        out_specs=(vmem, vmem, vmem),
        name="pack_rows",
    )(state, depth, pole_real, pole_imag, pole_weight)
    far = swap(far, "tile", 1)
    near = swap(near, "tile", 0)
    count = lax.axis_size("pole")
    others = jnp.stack([shift(scalars, "pole", step) for step in range(2, count - 1)])
    block_rows = (rows // SUB + 3) * SUB + 4 * poles
    block = jax.ShapeDtypeStruct((block_rows, LANES), f32)
    first, second = pl.pallas_call(
        pack_columns_kernel,
        out_shape=(block, block),
        in_specs=[vmem] * 5,
        out_specs=(vmem, vmem),
        name="pack_columns",
    )(state, depth, near, far, scalars)
    first = swap(first, "pole", 0)
    second = swap(second, "pole", 1)
    height = rows + 2 * REACH
    return pl.pallas_call(
        step_kernel,
        out_shape=jax.ShapeDtypeStruct(state.shape, f32),
        in_specs=[vmem] * 8,
        out_specs=vmem,
        scratch_shapes=[
            pltpu.VMEM((height * 4 * SUB, LANES), f32),
            pltpu.VMEM((3, ITERS, height, SUB, LANES), f32),
            pltpu.VMEM((4, height, SUB, LANES), f32),
            pltpu.VMEM((3, rows * SUB, LANES), f32),
        ],
        compiler_params=pltpu.CompilerParams(vmem_limit_bytes=32 * 1024 * 1024),
        name="step",
    )(state, depth, near, far, first, second, scalars, others)


def solution(mesh):
    return jax.shard_map(
        shards,
        mesh=mesh,
        in_specs=(
            P(None, "tile", "pole"),
            P("tile", "pole"),
            P("pole"),
            P("pole"),
            P(None, "pole"),
        ),
        out_specs=P(None, "tile", "pole"),
        check_vma=False,
    )
```

```python
import functools

import jax
import jax.numpy as jnp
from jax import lax
from jax.experimental import pallas as pl
from jax.experimental.pallas import tpu as pltpu
from jax.sharding import PartitionSpec as P

ITERS = 8
REACH = ITERS + 1
SUB = 8
LANES = 128
GRANT = 16 * 1024 * 1024
SIDE = 32

coriolis = 0.7
centre = 8.0
half_width = 8.0


def pairs(count, phase):
    swap = []
    for i in range(phase, count + phase, 2):
        a, b = i % count, (i + 1) % count
        swap += [(a, b), (b, a)]
    return swap


def swap(block, axis, phase):
    return lax.ppermute(block, axis, pairs(lax.axis_size(axis), phase))


def shift(block, axis, step):
    count = lax.axis_size(axis)
    return lax.ppermute(block, axis, [(i, (i + step) % count) for i in range(count)])


def cmul(a, b):
    return (a[0] * b[0] - a[1] * b[1], a[0] * b[1] + a[1] * b[0])


def cinv(a):
    norm = 1.0 / (a[0] * a[0] + a[1] * a[1])
    return (a[0] * norm, -a[1] * norm)


def cscale(a, factor):
    return (a[0] * factor, a[1] * factor)


def pack_rows_kernel(state, depth, real, imag, weight, far, near, scalars):
    odd = lax.rem(lax.axis_index("tile"), 2) == 1
    rows = depth.shape[0]
    fields = [state.at[0], state.at[1], state.at[2], depth]
    for target, low in ((near, odd), (far, jnp.logical_not(odd))):
        @pl.when(low)
        def _():
            for f, field in enumerate(fields):
                target[f * SUB : (f + 1) * SUB] = field[0:SUB]
                target[4 * SUB + f : 4 * SUB + f + 1] = field[SUB : SUB + 1]

        @pl.when(jnp.logical_not(low))
        def _():
            for f, field in enumerate(fields):
                target[f * SUB : (f + 1) * SUB] = field[rows - SUB : rows]
                target[4 * SUB + f : 4 * SUB + f + 1] = field[rows - SUB - 1 : rows - SUB]

    poles = real.shape[0]
    values = [real[i] for i in range(poles)] + [imag[i] for i in range(poles)]
    values += [weight[0, i] for i in range(poles)] + [weight[1, i] for i in range(poles)]
    for i, value in enumerate(values):
        scalars[i : i + 1] = jnp.full((1, LANES), value, jnp.float32)


def column_block(fields, start):
    lane = lax.broadcasted_iota(jnp.int32, fields[0].shape, 1)
    total = None
    for f, field in enumerate(fields):
        turn = (SIDE * f - start) % LANES
        turned = pltpu.roll(field, turn, 1) if turn else field
        total = turned if total is None else jnp.where(lane < SIDE * f, total, turned)
    return total


def pack_columns_kernel(state, depth, near, far, scalars, first, second):
    odd = lax.rem(lax.axis_index("pole"), 2) == 1
    rows, columns = depth.shape
    own = [state.at[0], state.at[1], state.at[2], depth]

    def edge(side):
        lanes = pl.ds(0, LANES) if side == 0 else pl.ds(columns - LANES, LANES)
        start = 0 if side == 0 else LANES - SIDE
        out = []
        for g in range(rows // SUB):
            out.append(column_block([field[pl.ds(g * SUB, SUB), lanes] for field in own], start))
        for halo in (near, far):
            out.append(
                column_block([halo[pl.ds(f * SUB, SUB), lanes] for f in range(4)], start)
            )
        ext = jnp.concatenate(
            [near[pl.ds(4 * SUB, 4), lanes], far[pl.ds(4 * SUB, 4), lanes]], axis=0
        )
        out.append(pltpu.roll(ext, SIDE, 1) if start else ext)
        return out

    left = edge(0)
    right = edge(1)
    for i, (a, b) in enumerate(zip(left, right)):
        first[pl.ds(i * SUB, SUB)] = jnp.where(odd, a, b)
        second[pl.ds(i * SUB, SUB)] = jnp.where(odd, b, a)
    base = len(left) * SUB
    first[pl.ds(base, scalars.shape[0])] = scalars[...]
    second[pl.ds(base, scalars.shape[0])] = scalars[...]


def strips_of(tiles, west, east):
    lane = lax.broadcasted_iota(jnp.int32, (SUB, LANES), 1)
    up = [pltpu.roll(tile, SIDE, 1) for tile in tiles]
    down = [pltpu.roll(tile, LANES - SIDE, 1) for tile in tiles]
    out = []
    for q in range(len(tiles)):
        out.append(jnp.where(lane < SIDE, up[q - 1] if q else west, up[q]))
        after = down[q + 1] if q + 1 < len(tiles) else east
        out.append(jnp.where(lane < LANES - SIDE, down[q], after))
    return out


def step_kernel(state, depth, near, far, first, second, scalars, others, out, grid, poly, coef, result):
    rows, columns = depth.shape
    groups = rows // SUB
    tiles = columns // LANES
    odd_pole = lax.rem(lax.axis_index("pole"), 2) == 1
    odd_tile = lax.rem(lax.axis_index("tile"), 2) == 1
    own = [state.at[0], state.at[1], state.at[2], depth]

    def sides(index):
        one = first[pl.ds(index * SUB, SUB)]
        two = second[pl.ds(index * SUB, SUB)]
        return jnp.where(odd_pole, one, two), jnp.where(odd_pole, two, one)

    def turned(block, turn):
        return pltpu.roll(block, turn % LANES, 1) if turn % LANES else block

    def lay(block, west, east, f, at, size, stride):
        cut = [block[:, t * LANES : (t + 1) * LANES] for t in range(tiles)]
        strips = strips_of(cut, turned(west, -SIDE * f), turned(east, LANES - SIDE - SIDE * f))
        for s, strip in enumerate(strips):
            grid[pl.Slice(at * SUB + s, size, stride * SUB), :] = strip[0:size]

    for g in range(groups):
        west, east = sides(g)
        for f in range(4):
            block = own[f][pl.ds(g * SUB, SUB), :]
            lay(block, west, east, f, (REACH + g * SUB) * 4 + f, SUB, 4)
    below = REACH + rows
    near_main = jnp.where(odd_tile, 1, below)
    far_main = jnp.where(odd_tile, below, 1)
    near_ext = jnp.where(odd_tile, 0, below + SUB)
    far_ext = jnp.where(odd_tile, below + SUB, 0)
    for i, (halo, main) in enumerate(((near, near_main), (far, far_main))):
        west, east = sides(groups + i)
        for f in range(4):
            lay(halo[pl.ds(f * SUB, SUB), :], west, east, f, main * 4 + f, SUB, 4)
    west, east = sides(groups + 2)
    lay(near[pl.ds(4 * SUB, SUB), :], west, east, 0, near_ext * 4, 4, 1)
    west = pltpu.roll(west, 4, 0)
    east = pltpu.roll(east, 4, 0)
    lay(far[pl.ds(4 * SUB, SUB), :], west, east, 0, far_ext * 4, 4, 1)

    def cell(f, r):
        return grid[pl.ds((r * 4 + f) * SUB, SUB), :]

    def left(x):
        return pltpu.roll(x, 1, 1)

    def right(x):
        return pltpu.roll(x, LANES - 1, 1)

    height = rows + 2 * REACH

    across = {}
    flux_east = {}
    flux_north = {}
    for r in range(height):
        h = cell(3, r)
        flux_east[r] = h * cell(1, r)
        flux_north[r] = h * cell(2, r)
        if r < height - 1:
            across[r] = 0.125 * (h + cell(3, r + 1))
            coef[0, r] = across[r]
        if 1 <= r < height - 1:
            north = 0.125 * (h + right(h))
            south = left(north)
            coef[1, r] = north
            coef[2, r] = south
            coef[3, r] = 2.0 - ((across[r] + across[r - 1]) + (north + south))
        if r >= 2:
            c = r - 1
            east_slope = flux_east[r] - flux_east[r - 2]
            north_slope = right(flux_north[c]) - left(flux_north[c])
            poly[1, 0, c] = 0.5 * (east_slope + north_slope)
            east_slope = flux_north[r] - flux_north[r - 2]
            north_slope = right(flux_east[c]) - left(flux_east[c])
            poly[2, 0, c] = 0.5 * (east_slope - north_slope)
            poly[0, 0, c] = cell(0, c)

    blocks = [scalars[...], first[pl.ds((groups + 3) * SUB, scalars.shape[0])]]
    blocks += [second[pl.ds((groups + 3) * SUB, scalars.shape[0])]]
    blocks += [others[i] for i in range(others.shape[0])]
    poles = scalars.shape[0] // 4
    quantity = []
    for q in range(4):
        cut = [b[q * poles : (q + 1) * poles] for b in blocks]
        quantity.append(jnp.concatenate(cut, axis=0))
    alpha = (quantity[0], quantity[1])
    beta = (quantity[2], quantity[3])
    square = cmul(alpha, alpha)
    shifted = (square[0] + coriolis * coriolis, square[1])
    sigma = ((shifted[0] + centre) / half_width, shifted[1] / half_width)
    rho = [cinv(sigma)]
    for j in range(1, ITERS):
        rho.append(cinv((2.0 * sigma[0] - rho[-1][0], 2.0 * sigma[1] - rho[-1][1])))
    gain = None
    start = []
    for m in range(ITERS):
        if m == 0:
            start.append(cscale(rho[0], 1.0 / half_width))
        else:
            gain = rho[0] if gain is None else cmul(gain, rho[m - 1])
            start.append(cscale(cmul(rho[m], gain), 2.0 / half_width))
    tail = None
    weight = [None] * ITERS
    for m in reversed(range(ITERS)):
        if tail is None:
            weight[m] = start[m]
            tail = (jnp.ones_like(sigma[0]), jnp.zeros_like(sigma[0]))
        else:
            tail = cmul(cmul(rho[m + 1], rho[m]), tail)
            tail = (tail[0] + 1.0, tail[1])
            weight[m] = cmul(start[m], tail)
    inverse_alpha = cinv(alpha)
    inverse_shift = cinv(shifted)
    by_alpha = cmul(beta, inverse_alpha)
    by_shift = cmul(beta, inverse_shift)
    products = {
        "b": beta,
        "b/a": by_alpha,
        "b/s": by_shift,
        "bs/a": cmul(by_alpha, shifted),
        "ba/s": cmul(by_shift, alpha),
        "b/as": cmul(by_alpha, inverse_shift),
    }

    def total(x):
        s = x[0:SUB]
        for i in range(1, x.shape[0] // SUB):
            s = s + x[i * SUB : (i + 1) * SUB]
        for turn in (4, 2, 1):
            s = s + pltpu.roll(s, turn, 0)
        return s

    names = [("bs/a", "b", "b/a"), ("b", "ba/s", "b/s"), ("b/a", "b/s", "b/as")]
    factor = (1.0, -1.0, -coriolis)
    sums = {}
    for name in products:
        for m in range(ITERS):
            w = products[name]
            sums[name, m] = total(w[0] * weight[m][0] - w[1] * weight[m][1])
    push = total(products["ba/s"][0])
    lift = coriolis * total(products["b/s"][0])

    for m in range(ITERS - 1):
        for r in range(m + 2, height - m - 2):
            above, below_, north, south, diag = (
                coef[0, r],
                coef[0, r - 1],
                coef[1, r],
                coef[2, r],
                coef[3, r],
            )
            for f in range(3):
                w = poly[f, m, r]
                value = diag * w + (above * poly[f, m, r + 1] + below_ * poly[f, m, r - 1])
                value = value + (north * right(w) + south * left(w))
                if m == 0:
                    value = 0.5 * value
                else:
                    value = value - poly[f, m - 1, r]
                poly[f, m + 1, r] = value

    sol = {}
    for r in range(REACH - 1, REACH + rows + 1):
        for g in range(3):
            if g == 0 and not REACH <= r < REACH + rows:
                continue
            acc = None
            for f in range(3):
                part = None
                for m in range(ITERS):
                    term = sums[names[g][f], m] * poly[f, m, r]
                    part = term if part is None else part + term
                part = part if f == 0 else factor[f] * part
                acc = part if acc is None else acc + part
            sol[g, r] = acc
    for i in range(rows):
        r = REACH + i
        u, v = cell(1, r), cell(2, r)
        result[0, pl.ds(i * SUB, SUB)] = sol[0, r]
        east = 0.5 * (sol[1, r + 1] - sol[1, r - 1])
        north = 0.5 * (right(sol[2, r]) - left(sol[2, r]))
        result[1, pl.ds(i * SUB, SUB)] = (push * u + lift * v) - (east + coriolis * north)
        east = 0.5 * (sol[2, r + 1] - sol[2, r - 1])
        north = 0.5 * (right(sol[1, r]) - left(sol[1, r]))
        result[2, pl.ds(i * SUB, SUB)] = (push * v - lift * u) + (coriolis * east - north)

    lane = lax.broadcasted_iota(jnp.int32, (SUB, LANES), 1)
    for k in range(3):
        for g in range(groups):
            for t in range(tiles):
                one = result[k, pl.Slice(g * SUB * SUB + 2 * t, SUB, SUB), :]
                two = result[k, pl.Slice(g * SUB * SUB + 2 * t + 1, SUB, SUB), :]
                joined = jnp.where(
                    lane < LANES // 2, pltpu.roll(one, LANES - SIDE, 1), pltpu.roll(two, SIDE, 1)
                )
                out[k, pl.ds(g * SUB, SUB), pl.ds(t * LANES, LANES)] = joined


def shards(state, depth, pole_real, pole_imag, pole_weight):
    rows, columns = depth.shape
    poles = pole_real.shape[0]
    vmem = pl.BlockSpec(memory_space=pltpu.VMEM)
    smem = pl.BlockSpec(memory_space=pltpu.SMEM)
    f32 = jnp.float32
    halo = jax.ShapeDtypeStruct((5 * SUB, columns), f32)
    far, near, scalars = pl.pallas_call(
        pack_rows_kernel,
        out_shape=(halo, halo, jax.ShapeDtypeStruct((4 * poles, LANES), f32)),
        in_specs=[vmem, vmem, smem, smem, smem],
        out_specs=(vmem, vmem, vmem),
        compiler_params=pltpu.CompilerParams(vmem_limit_bytes=GRANT),
        name="pack_rows",
    )(state, depth, pole_real, pole_imag, pole_weight)
    far = swap(far, "tile", 1)
    near = swap(near, "tile", 0)
    count = lax.axis_size("pole")
    others = jnp.stack([shift(scalars, "pole", step) for step in range(2, count - 1)])
    block_rows = (rows // SUB + 3) * SUB + 4 * poles
    block = jax.ShapeDtypeStruct((block_rows, LANES), f32)
    first, second = pl.pallas_call(
        pack_columns_kernel,
        out_shape=(block, block),
        in_specs=[vmem] * 5,
        out_specs=(vmem, vmem),
        compiler_params=pltpu.CompilerParams(vmem_limit_bytes=GRANT),
        name="pack_columns",
    )(state, depth, near, far, scalars)
    first = swap(first, "pole", 0)
    second = swap(second, "pole", 1)
    height = rows + 2 * REACH
    return pl.pallas_call(
        step_kernel,
        out_shape=jax.ShapeDtypeStruct(state.shape, f32),
        in_specs=[vmem] * 8,
        out_specs=vmem,
        scratch_shapes=[
            pltpu.VMEM((height * 4 * SUB, LANES), f32),
            pltpu.VMEM((3, ITERS, height, SUB, LANES), f32),
            pltpu.VMEM((4, height, SUB, LANES), f32),
            pltpu.VMEM((3, rows * SUB, LANES), f32),
        ],
        compiler_params=pltpu.CompilerParams(vmem_limit_bytes=GRANT),
        name="step",
    )(state, depth, near, far, first, second, scalars, others)


def solution(mesh):
    return jax.shard_map(
        shards,
        mesh=mesh,
        in_specs=(
            P(None, "tile", "pole"),
            P("tile", "pole"),
            P("pole"),
            P("pole"),
            P(None, "pole"),
        ),
        out_specs=P(None, "tile", "pole"),
        check_vma=False,
    )
```

```python
import jax
import jax.numpy as jnp
from jax import lax
from jax.experimental import pallas as pl
from jax.experimental.pallas import tpu as pltpu
from jax.sharding import PartitionSpec as P

ITERS = 8
REACH = ITERS + 1
SUB = 8
LANES = 128
GRANT = 16 * 1024 * 1024
SIDE = 32

coriolis = 0.7
centre = 8.0
half_width = 8.0


def pairs(count, phase):
    swap = []
    for i in range(phase, count + phase, 2):
        a, b = i % count, (i + 1) % count
        swap += [(a, b), (b, a)]
    return swap


def swap(block, axis, phase):
    return lax.ppermute(block, axis, pairs(lax.axis_size(axis), phase))


def cmul(a, b):
    return (a[0] * b[0] - a[1] * b[1], a[0] * b[1] + a[1] * b[0])


def cinv(a):
    norm = 1.0 / (a[0] * a[0] + a[1] * a[1])
    return (a[0] * norm, -a[1] * norm)


def cscale(a, factor):
    return (a[0] * factor, a[1] * factor)


def pack_rows_kernel(fields, far, near):
    odd = lax.rem(lax.axis_index("tile"), 2) == 1
    rows = fields.shape[1]
    for target, low in ((far, jnp.logical_not(odd)), (near, odd)):
        @pl.when(low)
        def _():
            for f in range(4):
                target[f * SUB : (f + 1) * SUB] = fields[f, 0:SUB]
                target[4 * SUB + f : 4 * SUB + f + 1] = fields[f, SUB : SUB + 1]

        @pl.when(jnp.logical_not(low))
        def _():
            for f in range(4):
                target[f * SUB : (f + 1) * SUB] = fields[f, rows - SUB : rows]
                target[4 * SUB + f : 4 * SUB + f + 1] = fields[f, rows - SUB - 1 : rows - SUB]

        target[4 * SUB + 4 : 5 * SUB] = jnp.zeros((4, target.shape[1]), jnp.float32)


def column_block(fields, start):
    lane = lax.broadcasted_iota(jnp.int32, fields[0].shape, 1)
    total = None
    for f, field in enumerate(fields):
        turn = (SIDE * f - start) % LANES
        turned = pltpu.roll(field, turn, 1) if turn else field
        total = turned if total is None else jnp.where(lane < SIDE * f, total, turned)
    return total


def pack_columns_kernel(fields, near, far, scalars, blocks):
    me = lax.axis_index("pole")
    count = blocks.shape[0]
    rows, columns = fields.shape[1:]
    own = [fields.at[f] for f in range(4)]

    def edge(side):
        lanes = pl.ds(0, LANES) if side == 0 else pl.ds(columns - LANES, LANES)
        start = 0 if side == 0 else LANES - SIDE
        out = []
        for g in range(rows // SUB):
            out.append(column_block([field[pl.ds(g * SUB, SUB), lanes] for field in own], start))
        for halo in (near, far):
            out.append(
                column_block([halo[pl.ds(f * SUB, SUB), lanes] for f in range(4)], start)
            )
        ext = jnp.concatenate(
            [near[pl.ds(4 * SUB, 4), lanes], far[pl.ds(4 * SUB, 4), lanes]], axis=0
        )
        out.append(pltpu.roll(ext, SIDE, 1) if start else ext)
        return out

    left = edge(0)
    right = edge(1)
    base = len(left) * SUB
    for step in range(1, count):
        there = lax.rem(me + step, count)
        if step in (1, count - 1):
            for i, part in enumerate(right if step == 1 else left):
                blocks[there, pl.ds(i * SUB, SUB)] = part
        else:
            blocks[there, pl.ds(0, base)] = jnp.zeros((base, LANES), jnp.float32)
        blocks[there, pl.ds(base, scalars.shape[0])] = scalars[...]
    blocks[me] = jnp.zeros(blocks.shape[1:], jnp.float32)


def strips_of(tiles, west, east):
    lane = lax.broadcasted_iota(jnp.int32, (SUB, LANES), 1)
    up = [pltpu.roll(tile, SIDE, 1) for tile in tiles]
    down = [pltpu.roll(tile, LANES - SIDE, 1) for tile in tiles]
    out = []
    for q in range(len(tiles)):
        out.append(jnp.where(lane < SIDE, up[q - 1] if q else west, up[q]))
        after = down[q + 1] if q + 1 < len(tiles) else east
        out.append(jnp.where(lane < LANES - SIDE, down[q], after))
    return out


def step_kernel(fields, near, far, scalars, blocks, out, grid, poly, coef, result):
    rows, columns = fields.shape[1:]
    me = lax.axis_index("pole")
    count = blocks.shape[0]
    groups = rows // SUB
    tiles = columns // LANES
    after = lax.rem(me + 1, count)
    before = lax.rem(me + count - 1, count)
    odd_tile = lax.rem(lax.axis_index("tile"), 2) == 1
    own = [fields.at[f] for f in range(4)]

    def sides(index):
        return blocks[before, pl.ds(index * SUB, SUB)], blocks[after, pl.ds(index * SUB, SUB)]

    def turned(block, turn):
        return pltpu.roll(block, turn % LANES, 1) if turn % LANES else block

    def lay(block, west, east, f, at, size, stride):
        cut = [block[:, t * LANES : (t + 1) * LANES] for t in range(tiles)]
        strips = strips_of(cut, turned(west, -SIDE * f), turned(east, LANES - SIDE - SIDE * f))
        for s, strip in enumerate(strips):
            grid[pl.Slice(at * SUB + s, size, stride * SUB), :] = strip[0:size]

    for g in range(groups):
        west, east = sides(g)
        for f in range(4):
            block = own[f][pl.ds(g * SUB, SUB), :]
            lay(block, west, east, f, (REACH + g * SUB) * 4 + f, SUB, 4)
    below = REACH + rows
    near_main = jnp.where(odd_tile, 1, below)
    far_main = jnp.where(odd_tile, below, 1)
    near_ext = jnp.where(odd_tile, 0, below + SUB)
    far_ext = jnp.where(odd_tile, below + SUB, 0)
    for i, (halo, main) in enumerate(((near, near_main), (far, far_main))):
        west, east = sides(groups + i)
        for f in range(4):
            lay(halo[pl.ds(f * SUB, SUB), :], west, east, f, main * 4 + f, SUB, 4)
    west, east = sides(groups + 2)
    lay(near[pl.ds(4 * SUB, SUB), :], west, east, 0, near_ext * 4, 4, 1)
    west = pltpu.roll(west, 4, 0)
    east = pltpu.roll(east, 4, 0)
    lay(far[pl.ds(4 * SUB, SUB), :], west, east, 0, far_ext * 4, 4, 1)

    def cell(f, r):
        return grid[pl.ds((r * 4 + f) * SUB, SUB), :]

    def left(x):
        return pltpu.roll(x, 1, 1)

    def right(x):
        return pltpu.roll(x, LANES - 1, 1)

    height = rows + 2 * REACH

    across = {}
    flux_east = {}
    flux_north = {}
    for r in range(height):
        h = cell(3, r)
        flux_east[r] = h * cell(1, r)
        flux_north[r] = h * cell(2, r)
        if r < height - 1:
            across[r] = 0.125 * (h + cell(3, r + 1))
            coef[0, r] = across[r]
        if 1 <= r < height - 1:
            north = 0.125 * (h + right(h))
            south = left(north)
            coef[1, r] = north
            coef[2, r] = south
            coef[3, r] = 2.0 - ((across[r] + across[r - 1]) + (north + south))
        if r >= 2:
            c = r - 1
            east_slope = flux_east[r] - flux_east[r - 2]
            north_slope = right(flux_north[c]) - left(flux_north[c])
            poly[1, 0, c] = 0.5 * (east_slope + north_slope)
            east_slope = flux_north[r] - flux_north[r - 2]
            north_slope = right(flux_east[c]) - left(flux_east[c])
            poly[2, 0, c] = 0.5 * (east_slope - north_slope)
            poly[0, 0, c] = cell(0, c)

    given = [scalars[...]]
    for step in range(1, count):
        there = lax.rem(me + step, count)
        given.append(blocks[there, pl.ds((groups + 3) * SUB, scalars.shape[0])])
    poles = scalars.shape[0] // 4
    quantity = []
    for q in range(4):
        cut = [b[q * poles : (q + 1) * poles] for b in given]
        quantity.append(jnp.concatenate(cut, axis=0))
    alpha = (quantity[0], quantity[1])
    beta = (quantity[2], quantity[3])
    square = cmul(alpha, alpha)
    shifted = (square[0] + coriolis * coriolis, square[1])
    sigma = ((shifted[0] + centre) / half_width, shifted[1] / half_width)
    rho = [cinv(sigma)]
    for j in range(1, ITERS):
        rho.append(cinv((2.0 * sigma[0] - rho[-1][0], 2.0 * sigma[1] - rho[-1][1])))
    gain = None
    start = []
    for m in range(ITERS):
        if m == 0:
            start.append(cscale(rho[0], 1.0 / half_width))
        else:
            gain = rho[0] if gain is None else cmul(gain, rho[m - 1])
            start.append(cscale(cmul(rho[m], gain), 2.0 / half_width))
    tail = None
    weight = [None] * ITERS
    for m in reversed(range(ITERS)):
        if tail is None:
            weight[m] = start[m]
            tail = (jnp.ones_like(sigma[0]), jnp.zeros_like(sigma[0]))
        else:
            tail = cmul(cmul(rho[m + 1], rho[m]), tail)
            tail = (tail[0] + 1.0, tail[1])
            weight[m] = cmul(start[m], tail)
    inverse_alpha = cinv(alpha)
    inverse_shift = cinv(shifted)
    by_alpha = cmul(beta, inverse_alpha)
    by_shift = cmul(beta, inverse_shift)
    products = {
        "b": beta,
        "b/a": by_alpha,
        "b/s": by_shift,
        "bs/a": cmul(by_alpha, shifted),
        "ba/s": cmul(by_shift, alpha),
        "b/as": cmul(by_alpha, inverse_shift),
    }

    def total(x):
        s = x[0:SUB]
        for i in range(1, x.shape[0] // SUB):
            s = s + x[i * SUB : (i + 1) * SUB]
        for turn in (4, 2, 1):
            s = s + pltpu.roll(s, turn, 0)
        return s

    names = [("bs/a", "b", "b/a"), ("b", "ba/s", "b/s"), ("b/a", "b/s", "b/as")]
    factor = (1.0, -1.0, -coriolis)
    sums = {}
    for name in products:
        for m in range(ITERS):
            w = products[name]
            sums[name, m] = total(w[0] * weight[m][0] - w[1] * weight[m][1])
    push = total(products["ba/s"][0])
    lift = coriolis * total(products["b/s"][0])

    for m in range(ITERS - 1):
        for r in range(m + 2, height - m - 2):
            above, below_, north, south, diag = (
                coef[0, r],
                coef[0, r - 1],
                coef[1, r],
                coef[2, r],
                coef[3, r],
            )
            for f in range(3):
                w = poly[f, m, r]
                value = diag * w + (above * poly[f, m, r + 1] + below_ * poly[f, m, r - 1])
                value = value + (north * right(w) + south * left(w))
                if m == 0:
                    value = 0.5 * value
                else:
                    value = value - poly[f, m - 1, r]
                poly[f, m + 1, r] = value

    sol = {}
    for r in range(REACH - 1, REACH + rows + 1):
        for g in range(3):
            if g == 0 and not REACH <= r < REACH + rows:
                continue
            acc = None
            for f in range(3):
                part = None
                for m in range(ITERS):
                    term = sums[names[g][f], m] * poly[f, m, r]
                    part = term if part is None else part + term
                part = part if f == 0 else factor[f] * part
                acc = part if acc is None else acc + part
            sol[g, r] = acc
    for i in range(rows):
        r = REACH + i
        u, v = cell(1, r), cell(2, r)
        result[0, pl.ds(i * SUB, SUB)] = sol[0, r]
        east = 0.5 * (sol[1, r + 1] - sol[1, r - 1])
        north = 0.5 * (right(sol[2, r]) - left(sol[2, r]))
        result[1, pl.ds(i * SUB, SUB)] = (push * u + lift * v) - (east + coriolis * north)
        east = 0.5 * (sol[2, r + 1] - sol[2, r - 1])
        north = 0.5 * (right(sol[1, r]) - left(sol[1, r]))
        result[2, pl.ds(i * SUB, SUB)] = (push * v - lift * u) + (coriolis * east - north)

    lane = lax.broadcasted_iota(jnp.int32, (SUB, LANES), 1)
    for k in range(3):
        for g in range(groups):
            for t in range(tiles):
                one = result[k, pl.Slice(g * SUB * SUB + 2 * t, SUB, SUB), :]
                two = result[k, pl.Slice(g * SUB * SUB + 2 * t + 1, SUB, SUB), :]
                joined = jnp.where(
                    lane < LANES // 2, pltpu.roll(one, LANES - SIDE, 1), pltpu.roll(two, SIDE, 1)
                )
                out[k, pl.ds(g * SUB, SUB), pl.ds(t * LANES, LANES)] = joined


def shards(state, depth, pole_real, pole_imag, pole_weight):
    rows, columns = depth.shape
    poles = pole_real.shape[0]
    vmem = pl.BlockSpec(memory_space=pltpu.VMEM)
    f32 = jnp.float32
    halo = jax.ShapeDtypeStruct((5 * SUB, columns), f32)
    fields = jnp.concatenate([state, depth[None]])
    far, near = pl.pallas_call(
        pack_rows_kernel,
        out_shape=(halo, halo),
        in_specs=[vmem],
        out_specs=(vmem, vmem),
        compiler_params=pltpu.CompilerParams(vmem_limit_bytes=GRANT),
        name="pack_rows",
    )(fields)
    scalars = jnp.concatenate([pole_real, pole_imag, pole_weight[0], pole_weight[1]])
    scalars = jnp.broadcast_to(scalars[:, None], (4 * poles, LANES))
    far = swap(far, "tile", 1)
    near = swap(near, "tile", 0)
    count = lax.axis_size("pole")
    block_rows = (rows // SUB + 3) * SUB + 4 * poles
    blocks = pl.pallas_call(
        pack_columns_kernel,
        out_shape=jax.ShapeDtypeStruct((count, block_rows, LANES), f32),
        in_specs=[vmem] * 4,
        out_specs=vmem,
        compiler_params=pltpu.CompilerParams(vmem_limit_bytes=GRANT),
        name="pack_columns",
    )(fields, near, far, scalars)
    blocks = lax.all_to_all(blocks, "pole", 0, 0, tiled=True)
    height = rows + 2 * REACH
    return pl.pallas_call(
        step_kernel,
        out_shape=jax.ShapeDtypeStruct(state.shape, f32),
        in_specs=[vmem] * 5,
        out_specs=vmem,
        scratch_shapes=[
            pltpu.VMEM((height * 4 * SUB, LANES), f32),
            pltpu.VMEM((3, ITERS, height, SUB, LANES), f32),
            pltpu.VMEM((4, height, SUB, LANES), f32),
            pltpu.VMEM((3, rows * SUB, LANES), f32),
        ],
        compiler_params=pltpu.CompilerParams(vmem_limit_bytes=GRANT),
        name="step",
    )(fields, near, far, scalars, blocks)


def solution(mesh):
    return jax.shard_map(
        shards,
        mesh=mesh,
        in_specs=(
            P(None, "tile", "pole"),
            P("tile", "pole"),
            P("pole"),
            P("pole"),
            P(None, "pole"),
        ),
        out_specs=P(None, "tile", "pole"),
        check_vma=False,
    )
```

```python
import jax
import jax.numpy as jnp
from jax import lax
from jax.experimental import pallas as pl
from jax.experimental.pallas import tpu as pltpu
from jax.sharding import PartitionSpec as P

ITERS = 8
REACH = ITERS + 1
SUB = 8
LANES = 128
HALF = LANES // 2
SIDE = 32
EDGE = 12
EAST = HALF + EDGE
GRANT = 16 * 1024 * 1024

coriolis = 0.7
centre = 8.0
half_width = 8.0


def pairs(count, phase):
    swap = []
    for i in range(phase, count + phase, 2):
        a, b = i % count, (i + 1) % count
        swap += [(a, b), (b, a)]
    return swap


def swap(block, axis, phase):
    return lax.ppermute(block, axis, pairs(lax.axis_size(axis), phase))


def shift(block, axis, step):
    count = lax.axis_size(axis)
    return lax.ppermute(block, axis, [(i, (i + step) % count) for i in range(count)])


def turn(x, lanes):
    return pltpu.roll(x, lanes % LANES, 1) if lanes % LANES else x


def cmul(a, b):
    return (a[0] * b[0] - a[1] * b[1], a[0] * b[1] + a[1] * b[0])


def cinv(a):
    norm = 1.0 / (a[0] * a[0] + a[1] * a[1])
    return (a[0] * norm, -a[1] * norm)


def cscale(a, factor):
    return (a[0] * factor, a[1] * factor)


def pack_columns_kernel(
    state_west, state_east, depth_west, depth_east, real, imag, weight, first, second, scalars
):
    odd = lax.rem(lax.axis_index("pole"), 2) == 1
    rows = depth_west.shape[0]
    lane = lax.broadcasted_iota(jnp.int32, (SUB, LANES), 1)
    sub = lax.broadcasted_iota(jnp.int32, (SUB, LANES), 0)
    poles = real.shape[0]
    values = [real[i] for i in range(poles)] + [imag[i] for i in range(poles)]
    values += [weight[0, i] for i in range(poles)] + [weight[1, i] for i in range(poles)]
    spread = []
    for g in range(len(values) // SUB):
        block = jnp.full((SUB, LANES), values[g * SUB], jnp.float32)
        for i in range(1, SUB):
            block = jnp.where(sub == i, values[g * SUB + i], block)
        scalars[pl.ds(g * SUB, SUB)] = block
        spread.append(block)
    for g in range(rows // SUB):
        cut = pl.ds(g * SUB, SUB)
        rest = spread[g] if g < len(spread) else jnp.zeros((SUB, LANES), jnp.float32)
        eastward = rest
        westward = rest
        for f in range(4):
            west = depth_west[cut, :] if f == 3 else state_west[f, cut, :]
            east = depth_east[cut, :] if f == 3 else state_east[f, cut, :]
            low, high = EDGE * f, EDGE * (f + 1)
            take = jnp.logical_and(lane >= low, lane < high)
            eastward = jnp.where(take, turn(east, low + EDGE), eastward)
            take = jnp.logical_and(lane >= EAST + low, lane < EAST + high)
            westward = jnp.where(take, turn(west, EAST + low), westward)
        first[cut, :] = jnp.where(odd, westward, eastward)
        second[cut, :] = jnp.where(odd, eastward, westward)


def sides_of(first, second, cut):
    odd = lax.rem(lax.axis_index("pole"), 2) == 1
    lane = lax.broadcasted_iota(jnp.int32, (SUB, LANES), 1)
    from_first = jnp.logical_xor(lane >= HALF, odd)
    return jnp.where(from_first, first[cut, :], second[cut, :])


def pack_rows_kernel(state, depth, first, second, far, near):
    odd = lax.rem(lax.axis_index("tile"), 2) == 1
    rows = depth.shape[0]
    fields = [state.at[0], state.at[1], state.at[2], depth]
    for target, low in ((far, jnp.logical_not(odd)), (near, odd)):
        def fill(main, ext):
            for f in range(4):
                target[f * SUB : (f + 1) * SUB] = fields[f][main : main + SUB]
                target[4 * SUB + f : 4 * SUB + f + 1] = fields[f][ext : ext + 1]
            side = sides_of(first, second, pl.ds(main, SUB))
            base = 4 * SUB + 4
            target[base : base + 4, 0:LANES] = side[0:4]
            target[base : base + 4, LANES : 2 * LANES] = side[4:8]
            group = ext // SUB * SUB
            side = sides_of(first, second, pl.ds(group, SUB))
            target[base : base + 1, 2 * LANES : 3 * LANES] = side[ext - group : ext - group + 1]

        pl.when(low)(lambda: fill(0, SUB))
        pl.when(jnp.logical_not(low))(lambda: fill(rows - SUB, rows - SUB - 1))


def pole_sums_kernel(scalars, first, second, others, sums):
    odd = lax.rem(lax.axis_index("pole"), 2) == 1
    count = scalars.shape[0]
    lane = lax.broadcasted_iota(jnp.int32, (SUB, LANES), 1)
    blocks = [[scalars[pl.ds(g, SUB)] for g in range(0, count, SUB)]]
    for i, message in enumerate((first, second)):
        low = jnp.logical_xor(lane < HALF, odd if i == 0 else jnp.logical_not(odd))
        part = []
        for g in range(0, count, SUB):
            x = message[pl.ds(g, SUB), :]
            part.append(jnp.where(low, x, turn(x, HALF)))
        blocks.append(part)
    for i in range(others.shape[0]):
        blocks.append([others[i, pl.ds(g, SUB)] for g in range(0, count, SUB)])
    poles = count // 4
    quantity = []
    for q in range(4):
        cut = []
        for block in blocks:
            whole = jnp.concatenate(block, axis=0)
            cut.append(whole[q * poles : (q + 1) * poles])
        quantity.append(jnp.concatenate(cut, axis=0))
    alpha = (quantity[0], quantity[1])
    beta = (quantity[2], quantity[3])
    square = cmul(alpha, alpha)
    shifted = (square[0] + coriolis * coriolis, square[1])
    sigma = ((shifted[0] + centre) / half_width, shifted[1] / half_width)
    rho = [cinv(sigma)]
    for j in range(1, ITERS):
        rho.append(cinv((2.0 * sigma[0] - rho[-1][0], 2.0 * sigma[1] - rho[-1][1])))
    gain = None
    start = []
    for m in range(ITERS):
        if m == 0:
            start.append(cscale(rho[0], 1.0 / half_width))
        else:
            gain = rho[0] if gain is None else cmul(gain, rho[m - 1])
            start.append(cscale(cmul(rho[m], gain), 2.0 / half_width))
    tail = None
    weight = [None] * ITERS
    for m in reversed(range(ITERS)):
        if tail is None:
            weight[m] = start[m]
            tail = (jnp.ones_like(sigma[0]), jnp.zeros_like(sigma[0]))
        else:
            tail = cmul(cmul(rho[m + 1], rho[m]), tail)
            tail = (tail[0] + 1.0, tail[1])
            weight[m] = cmul(start[m], tail)
    inverse_alpha = cinv(alpha)
    inverse_shift = cinv(shifted)
    by_alpha = cmul(beta, inverse_alpha)
    by_shift = cmul(beta, inverse_shift)
    products = {
        "b": beta,
        "b/a": by_alpha,
        "b/s": by_shift,
        "bs/a": cmul(by_alpha, shifted),
        "ba/s": cmul(by_shift, alpha),
        "b/as": cmul(by_alpha, inverse_shift),
    }

    def total(x):
        s = x[0:SUB]
        for i in range(1, x.shape[0] // SUB):
            s = s + x[i * SUB : (i + 1) * SUB]
        for step in (4, 2, 1):
            s = s + pltpu.roll(s, step, 0)
        return s

    names = [("bs/a", "b", "b/a"), ("b", "ba/s", "b/s"), ("b/a", "b/s", "b/as")]
    factor = (1.0, -1.0, -coriolis)
    found = {}
    for m in range(ITERS):
        for name, w in products.items():
            found[name, m] = total(w[0] * weight[m][0] - w[1] * weight[m][1])
        for g in range(3):
            for f in range(3):
                value = found[names[g][f], m]
                sums[(g * 3 + f) * ITERS + m] = value if f == 0 else factor[f] * value
    sums[9 * ITERS] = total(products["ba/s"][0])
    sums[9 * ITERS + 1] = coriolis * total(products["b/s"][0])


def strips_of(tiles, side):
    lane = lax.broadcasted_iota(jnp.int32, (SUB, LANES), 1)
    up = [turn(tile, SIDE) for tile in tiles]
    down = [turn(tile, -SIDE) for tile in tiles]
    out = []
    for q in range(len(tiles)):
        out.append(jnp.where(lane < SIDE, up[q - 1] if q else side, up[q]))
        after = down[q + 1] if q + 1 < len(tiles) else side
        out.append(jnp.where(lane < LANES - SIDE, down[q], after))
    return out


def step_kernel(state, depth, far, near, first, second, sums, out, grid, poly, coef, result):
    rows, columns = depth.shape
    groups = rows // SUB
    tiles = columns // LANES
    odd_tile = lax.rem(lax.axis_index("tile"), 2) == 1
    own = [state.at[0], state.at[1], state.at[2], depth]
    lane = lax.broadcasted_iota(jnp.int32, (SUB, LANES), 1)
    sub = lax.broadcasted_iota(jnp.int32, (SUB, LANES), 0)

    def lay(block, side, at, size, stride):
        cut = [block[:, t * LANES : (t + 1) * LANES] for t in range(tiles)]
        for s, strip in enumerate(strips_of(cut, side)):
            grid[pl.Slice(at * SUB + s, size, stride * SUB), :] = strip[0:size]

    def place(side, f):
        return turn(side, SIDE - EDGE - EDGE * f)

    for g in range(groups):
        side = sides_of(first, second, pl.ds(g * SUB, SUB))
        for f in range(4):
            block = own[f][pl.ds(g * SUB, SUB), :]
            lay(block, place(side, f), (REACH + g * SUB) * 4 + f, SUB, 4)
    below = REACH + rows
    near_main = jnp.where(odd_tile, 1, below)
    far_main = jnp.where(odd_tile, below, 1)
    near_ext = jnp.where(odd_tile, 0, below + SUB)
    far_ext = jnp.where(odd_tile, below + SUB, 0)
    base = 4 * SUB + 4
    for halo, main, ext in ((near, near_main, near_ext), (far, far_main, far_ext)):
        side = jnp.concatenate(
            [halo[base : base + 4, 0:LANES], halo[base : base + 4, LANES : 2 * LANES]], axis=0
        )
        for f in range(4):
            lay(halo[pl.ds(f * SUB, SUB), :], place(side, f), main * 4 + f, SUB, 4)
        line = halo[base : base + 1, 2 * LANES : 3 * LANES]
        line = jnp.broadcast_to(line, (SUB, LANES))
        side = place(line, 0)
        for f in range(1, 4):
            side = jnp.where(sub == f, place(line, f), side)
        lay(halo[pl.ds(4 * SUB, SUB), :], side, ext * 4, 4, 1)

    def cell(f, r):
        return grid[pl.ds((r * 4 + f) * SUB, SUB), :]

    def left(x):
        return pltpu.roll(x, 1, 1)

    def right(x):
        return pltpu.roll(x, LANES - 1, 1)

    height = rows + 2 * REACH

    flux_east = [None] * 3
    flux_north = [None] * 3
    depths = [None] * 2
    across = None
    for r in range(height):
        h = cell(3, r)
        flux_east = flux_east[1:] + [h * cell(1, r)]
        flux_north = flux_north[1:] + [h * cell(2, r)]
        depths = depths[1:] + [h]
        if r >= 1:
            before, across = across, 0.125 * (depths[0] + depths[1])
            coef[0, r - 1] = across
        if r >= 2:
            c = r - 1
            north = 0.125 * (depths[0] + right(depths[0]))
            south = left(north)
            coef[1, c] = north
            coef[2, c] = south
            coef[3, c] = 2.0 - ((across + before) + (north + south))
            east_slope = flux_east[2] - flux_east[0]
            north_slope = right(flux_north[1]) - left(flux_north[1])
            poly[1, 0, c] = 0.5 * (east_slope + north_slope)
            east_slope = flux_north[2] - flux_north[0]
            north_slope = right(flux_east[1]) - left(flux_east[1])
            poly[2, 0, c] = 0.5 * (east_slope - north_slope)
            poly[0, 0, c] = cell(0, c)

    for m in range(ITERS - 1):
        low, high = m + 2, height - m - 2
        back = [poly[f, m, low - 1] for f in range(3)]
        here = [poly[f, m, low] for f in range(3)]
        below_ = coef[0, low - 1]
        for r in range(low, high):
            above, north, south, diag = coef[0, r], coef[1, r], coef[2, r], coef[3, r]
            ahead = [poly[f, m, r + 1] for f in range(3)]
            for f in range(3):
                value = diag * here[f] + (above * ahead[f] + below_ * back[f])
                value = value + (north * right(here[f]) + south * left(here[f]))
                value = 0.5 * value if m == 0 else value - poly[f, m - 1, r]
                poly[f, m + 1, r] = value
            back, here, below_ = here, ahead, above

    sol = {}
    block = 6
    for r0 in range(REACH - 1, REACH + rows + 1, block):
        span = range(r0, min(r0 + block, REACH + rows + 1))
        acc = {}
        for f in range(3):
            for m in range(ITERS):
                value = [poly[f, m, r] for r in span]
                for g in range(3):
                    c = sums[(g * 3 + f) * ITERS + m]
                    for r, v in zip(span, value):
                        if g == 0 and not REACH <= r < REACH + rows:
                            continue
                        acc[g, r] = acc[g, r] + c * v if (g, r) in acc else c * v
        sol.update(acc)
    push = sums[9 * ITERS]
    lift = sums[9 * ITERS + 1]
    for i in range(rows):
        r = REACH + i
        u, v = cell(1, r), cell(2, r)
        result[0, pl.ds(i * SUB, SUB)] = sol[0, r]
        east = 0.5 * (sol[1, r + 1] - sol[1, r - 1])
        north = 0.5 * (right(sol[2, r]) - left(sol[2, r]))
        result[1, pl.ds(i * SUB, SUB)] = (push * u + lift * v) - (east + coriolis * north)
        east = 0.5 * (sol[2, r + 1] - sol[2, r - 1])
        north = 0.5 * (right(sol[1, r]) - left(sol[1, r]))
        result[2, pl.ds(i * SUB, SUB)] = (push * v - lift * u) + (coriolis * east - north)

    for k in range(3):
        for g in range(groups):
            for t in range(tiles):
                one = result[k, pl.Slice(g * SUB * SUB + 2 * t, SUB, SUB), :]
                two = result[k, pl.Slice(g * SUB * SUB + 2 * t + 1, SUB, SUB), :]
                joined = jnp.where(lane < HALF, turn(one, -SIDE), turn(two, SIDE))
                out[k, pl.ds(g * SUB, SUB), pl.ds(t * LANES, LANES)] = joined


def shards(state, depth, pole_real, pole_imag, pole_weight):
    rows, columns = depth.shape
    poles = pole_real.shape[0]
    vmem = pl.BlockSpec(memory_space=pltpu.VMEM)
    smem = pl.BlockSpec(memory_space=pltpu.SMEM)
    small = pltpu.CompilerParams(vmem_limit_bytes=GRANT)

    def f32(*shape):
        return jax.ShapeDtypeStruct(shape, jnp.float32)

    last = columns // LANES - 1
    first, second, scalars = pl.pallas_call(
        pack_columns_kernel,
        grid=(1,),
        out_shape=(f32(rows, LANES), f32(rows, LANES), f32(4 * poles, LANES)),
        in_specs=[
            pl.BlockSpec((3, rows, LANES), lambda i: (0, 0, 0)),
            pl.BlockSpec((3, rows, LANES), lambda i: (0, 0, last)),
            pl.BlockSpec((rows, LANES), lambda i: (0, 0)),
            pl.BlockSpec((rows, LANES), lambda i: (0, last)),
            smem,
            smem,
            smem,
        ],
        out_specs=(vmem, vmem, vmem),
        name="pack_columns",
    )(state, state, depth, depth, pole_real, pole_imag, pole_weight)
    first = swap(first, "pole", 0)
    second = swap(second, "pole", 1)
    halo = f32(5 * SUB, columns)
    far, near = pl.pallas_call(
        pack_rows_kernel,
        out_shape=(halo, halo),
        in_specs=[vmem] * 4,
        out_specs=(vmem, vmem),
        compiler_params=small,
        name="pack_rows",
    )(state, depth, first, second)
    far = swap(far, "tile", 1)
    near = swap(near, "tile", 0)
    count = lax.axis_size("pole")
    others = jnp.stack([shift(scalars, "pole", step) for step in range(2, count - 1)])
    sums = pl.pallas_call(
        pole_sums_kernel,
        out_shape=f32(9 * ITERS + 2, SUB, LANES),
        in_specs=[vmem] * 4,
        out_specs=vmem,
        compiler_params=small,
        name="pole_sums",
    )(scalars, first, second, others)
    height = rows + 2 * REACH
    return pl.pallas_call(
        step_kernel,
        out_shape=f32(*state.shape),
        in_specs=[vmem] * 7,
        out_specs=vmem,
        scratch_shapes=[
            pltpu.VMEM((height * 4 * SUB, LANES), jnp.float32),
            pltpu.VMEM((3, ITERS, height, SUB, LANES), jnp.float32),
            pltpu.VMEM((4, height, SUB, LANES), jnp.float32),
            pltpu.VMEM((3, rows * SUB, LANES), jnp.float32),
        ],
        compiler_params=small,
        name="step",
    )(state, depth, far, near, first, second, sums)


def solution(mesh):
    return jax.shard_map(
        shards,
        mesh=mesh,
        in_specs=(
            P(None, "tile", "pole"),
            P("tile", "pole"),
            P("pole"),
            P("pole"),
            P(None, "pole"),
        ),
        out_specs=P(None, "tile", "pole"),
        check_vma=False,
    )
```

```python
import jax
import jax.numpy as jnp
from jax import lax
from jax.experimental import pallas as pl
from jax.experimental.pallas import tpu as pltpu
from jax.sharding import PartitionSpec as P

ITERS = 8
REACH = ITERS + 1
SUB = 8
LANES = 128
HALF = LANES // 2
SIDE = 32
EDGE = 12
EAST = HALF + EDGE
GRANT = 16 * 1024 * 1024

coriolis = 0.7
centre = 8.0
half_width = 8.0


def pairs(count, phase):
    swap = []
    for i in range(phase, count + phase, 2):
        a, b = i % count, (i + 1) % count
        swap += [(a, b), (b, a)]
    return swap


def swap(block, axis, phase):
    return lax.ppermute(block, axis, pairs(lax.axis_size(axis), phase))


def shift(block, axis, step):
    count = lax.axis_size(axis)
    return lax.ppermute(block, axis, [(i, (i + step) % count) for i in range(count)])


def turn(x, lanes):
    return pltpu.roll(x, lanes % LANES, 1) if lanes % LANES else x


def cmul(a, b):
    return (a[0] * b[0] - a[1] * b[1], a[0] * b[1] + a[1] * b[0])


def cinv(a):
    norm = 1.0 / (a[0] * a[0] + a[1] * a[1])
    return (a[0] * norm, -a[1] * norm)


def cscale(a, factor):
    return (a[0] * factor, a[1] * factor)


def pack_columns_kernel(
    state_west, state_east, depth_west, depth_east, real, imag, weight, first, second, scalars
):
    odd = lax.rem(lax.axis_index("pole"), 2) == 1
    rows = depth_west.shape[0]
    lane = lax.broadcasted_iota(jnp.int32, (SUB, LANES), 1)
    sub = lax.broadcasted_iota(jnp.int32, (SUB, LANES), 0)
    poles = real.shape[0]
    values = [real[i] for i in range(poles)] + [imag[i] for i in range(poles)]
    values += [weight[0, i] for i in range(poles)] + [weight[1, i] for i in range(poles)]
    spread = []
    for g in range(len(values) // SUB):
        block = jnp.full((SUB, LANES), values[g * SUB], jnp.float32)
        for i in range(1, SUB):
            block = jnp.where(sub == i, values[g * SUB + i], block)
        scalars[pl.ds(g * SUB, SUB)] = block
        spread.append(block)
    for g in range(rows // SUB):
        cut = pl.ds(g * SUB, SUB)
        rest = spread[g] if g < len(spread) else jnp.zeros((SUB, LANES), jnp.float32)
        eastward = rest
        westward = rest
        for f in range(4):
            west = depth_west[cut, :] if f == 3 else state_west[f, cut, :]
            east = depth_east[cut, :] if f == 3 else state_east[f, cut, :]
            low, high = EDGE * f, EDGE * (f + 1)
            take = jnp.logical_and(lane >= low, lane < high)
            eastward = jnp.where(take, turn(east, low + EDGE), eastward)
            take = jnp.logical_and(lane >= EAST + low, lane < EAST + high)
            westward = jnp.where(take, turn(west, EAST + low), westward)
        first[cut, :] = jnp.where(odd, westward, eastward)
        second[cut, :] = jnp.where(odd, eastward, westward)


def sides_of(first, second, cut):
    odd = lax.rem(lax.axis_index("pole"), 2) == 1
    lane = lax.broadcasted_iota(jnp.int32, (SUB, LANES), 1)
    from_first = jnp.logical_xor(lane >= HALF, odd)
    return jnp.where(from_first, first[cut, :], second[cut, :])


def pack_rows_kernel(state, depth, first, second, far, near):
    odd = lax.rem(lax.axis_index("tile"), 2) == 1
    rows = depth.shape[0]
    fields = [state.at[0], state.at[1], state.at[2], depth]
    for target, low in ((far, jnp.logical_not(odd)), (near, odd)):
        def fill(main, ext):
            for f in range(4):
                target[f * SUB : (f + 1) * SUB] = fields[f][main : main + SUB]
                target[4 * SUB + f : 4 * SUB + f + 1] = fields[f][ext : ext + 1]
            side = sides_of(first, second, pl.ds(main, SUB))
            base = 4 * SUB + 4
            target[base : base + 4, 0:LANES] = side[0:4]
            target[base : base + 4, LANES : 2 * LANES] = side[4:8]
            group = ext // SUB * SUB
            side = sides_of(first, second, pl.ds(group, SUB))
            target[base : base + 1, 2 * LANES : 3 * LANES] = side[ext - group : ext - group + 1]

        pl.when(low)(lambda: fill(0, SUB))
        pl.when(jnp.logical_not(low))(lambda: fill(rows - SUB, rows - SUB - 1))


def pole_sums_kernel(scalars, first, second, others, poly, sums, sol):
    odd = lax.rem(lax.axis_index("pole"), 2) == 1
    count = scalars.shape[0]
    lane = lax.broadcasted_iota(jnp.int32, (SUB, LANES), 1)
    blocks = [[scalars[pl.ds(g, SUB)] for g in range(0, count, SUB)]]
    for i, message in enumerate((first, second)):
        low = jnp.logical_xor(lane < HALF, odd if i == 0 else jnp.logical_not(odd))
        part = []
        for g in range(0, count, SUB):
            x = message[pl.ds(g, SUB), :]
            part.append(jnp.where(low, x, turn(x, HALF)))
        blocks.append(part)
    for i in range(others.shape[0]):
        blocks.append([others[i, pl.ds(g, SUB)] for g in range(0, count, SUB)])
    poles = count // 4
    quantity = []
    for q in range(4):
        cut = []
        for block in blocks:
            whole = jnp.concatenate(block, axis=0)
            cut.append(whole[q * poles : (q + 1) * poles])
        quantity.append(jnp.concatenate(cut, axis=0))
    alpha = (quantity[0], quantity[1])
    beta = (quantity[2], quantity[3])
    square = cmul(alpha, alpha)
    shifted = (square[0] + coriolis * coriolis, square[1])
    sigma = ((shifted[0] + centre) / half_width, shifted[1] / half_width)
    rho = [cinv(sigma)]
    for j in range(1, ITERS):
        rho.append(cinv((2.0 * sigma[0] - rho[-1][0], 2.0 * sigma[1] - rho[-1][1])))
    gain = None
    start = []
    for m in range(ITERS):
        if m == 0:
            start.append(cscale(rho[0], 1.0 / half_width))
        else:
            gain = rho[0] if gain is None else cmul(gain, rho[m - 1])
            start.append(cscale(cmul(rho[m], gain), 2.0 / half_width))
    tail = None
    weight = [None] * ITERS
    for m in reversed(range(ITERS)):
        if tail is None:
            weight[m] = start[m]
            tail = (jnp.ones_like(sigma[0]), jnp.zeros_like(sigma[0]))
        else:
            tail = cmul(cmul(rho[m + 1], rho[m]), tail)
            tail = (tail[0] + 1.0, tail[1])
            weight[m] = cmul(start[m], tail)
    inverse_alpha = cinv(alpha)
    inverse_shift = cinv(shifted)
    by_alpha = cmul(beta, inverse_alpha)
    by_shift = cmul(beta, inverse_shift)
    products = {
        "b": beta,
        "b/a": by_alpha,
        "b/s": by_shift,
        "bs/a": cmul(by_alpha, shifted),
        "ba/s": cmul(by_shift, alpha),
        "b/as": cmul(by_alpha, inverse_shift),
    }

    def total(x):
        s = x[0:SUB]
        for i in range(1, x.shape[0] // SUB):
            s = s + x[i * SUB : (i + 1) * SUB]
        for step in (4, 2, 1):
            s = s + pltpu.roll(s, step, 0)
        return s

    names = [("bs/a", "b", "b/a"), ("b", "ba/s", "b/s"), ("b/a", "b/s", "b/as")]
    factor = (1.0, -1.0, -coriolis)
    found = {}
    for m in range(ITERS):
        for name, w in products.items():
            found[name, m] = total(w[0] * weight[m][0] - w[1] * weight[m][1])
        for g in range(3):
            for f in range(3):
                value = found[names[g][f], m]
                sums[(g * 3 + f) * ITERS + m] = value if f == 0 else factor[f] * value
    sums[9 * ITERS] = total(products["ba/s"][0])
    sums[9 * ITERS + 1] = coriolis * total(products["b/s"][0])

    odd_tile = lax.rem(lax.axis_index("tile"), 2) == 1
    rows = sol.shape[1] - 2
    start = jnp.where(odd_tile, REACH - 1, 2 * REACH - 1)
    weighted_sums(poly, sums, sol, start, rows + 2 - REACH)


def weighted_sums(poly, sums, sol, start, count, block=6):
    for r0 in range(0, count, block):
        span = range(r0, min(r0 + block, count))
        acc = {}
        for f in range(3):
            for m in range(ITERS):
                value = [poly[f, m, start + r] for r in span]
                for g in range(3):
                    c = sums[(g * 3 + f) * ITERS + m]
                    for r, v in zip(span, value):
                        acc[g, r] = acc[g, r] + c * v if (g, r) in acc else c * v
        for (g, r), v in acc.items():
            sol[g, start + r - (REACH - 1)] = v


def strips_of(tiles, side):
    lane = lax.broadcasted_iota(jnp.int32, (SUB, LANES), 1)
    up = [turn(tile, SIDE) for tile in tiles]
    down = [turn(tile, -SIDE) for tile in tiles]
    out = []
    for q in range(len(tiles)):
        out.append(jnp.where(lane < SIDE, up[q - 1] if q else side, up[q]))
        after = down[q + 1] if q + 1 < len(tiles) else side
        out.append(jnp.where(lane < LANES - SIDE, down[q], after))
    return out


def lay(grid, block, side, at, size, stride):
    cut = [block[:, t * LANES : (t + 1) * LANES] for t in range(block.shape[1] // LANES)]
    for s, strip in enumerate(strips_of(cut, side)):
        grid[pl.Slice(at * SUB + s, size, stride * SUB), :] = strip[0:size]


def place(side, f):
    return turn(side, SIDE - EDGE - EDGE * f)


def lay_halo(grid, halo, main, ext):
    sub = lax.broadcasted_iota(jnp.int32, (SUB, LANES), 0)
    base = 4 * SUB + 4
    side = jnp.concatenate(
        [halo[base : base + 4, 0:LANES], halo[base : base + 4, LANES : 2 * LANES]], axis=0
    )
    for f in range(4):
        lay(grid, halo[pl.ds(f * SUB, SUB), :], place(side, f), main * 4 + f, SUB, 4)
    line = halo[base : base + 1, 2 * LANES : 3 * LANES]
    line = jnp.broadcast_to(line, (SUB, LANES))
    side = place(line, 0)
    for f in range(1, 4):
        side = jnp.where(sub == f, place(line, f), side)
    lay(grid, halo[pl.ds(4 * SUB, SUB), :], side, ext * 4, 4, 1)


def cell(grid, f, r):
    return grid[pl.ds(pl.multiple_of((r * 4 + f) * SUB, SUB), SUB), :]


def left(x):
    return pltpu.roll(x, 1, 1)


def right(x):
    return pltpu.roll(x, LANES - 1, 1)


def prepare(grid, poly, coef, start, count):
    flux_east = [None] * 3
    flux_north = [None] * 3
    depths = [None] * 2
    across = None
    for k in range(count + 2):
        r = start + k
        h = cell(grid, 3, r)
        flux_east = flux_east[1:] + [h * cell(grid, 1, r)]
        flux_north = flux_north[1:] + [h * cell(grid, 2, r)]
        depths = depths[1:] + [h]
        if k >= 1:
            before, across = across, 0.125 * (depths[0] + depths[1])
            coef[0, r - 1] = across
        if k >= 2:
            c = r - 1
            north = 0.125 * (depths[0] + right(depths[0]))
            south = left(north)
            coef[1, c] = north
            coef[2, c] = south
            coef[3, c] = 2.0 - ((across + before) + (north + south))
            east_slope = flux_east[2] - flux_east[0]
            north_slope = right(flux_north[1]) - left(flux_north[1])
            poly[1, 0, c] = 0.5 * (east_slope + north_slope)
            east_slope = flux_north[2] - flux_north[0]
            north_slope = right(flux_east[1]) - left(flux_east[1])
            poly[2, 0, c] = 0.5 * (east_slope - north_slope)
            poly[0, 0, c] = cell(grid, 0, c)


def sweep(poly, coef, m, start, count):
    back = [poly[f, m, start - 1] for f in range(3)]
    here = [poly[f, m, start] for f in range(3)]
    below = coef[0, start - 1]
    for k in range(count):
        r = start + k
        above, north, south, diag = coef[0, r], coef[1, r], coef[2, r], coef[3, r]
        ahead = [poly[f, m, r + 1] for f in range(3)]
        for f in range(3):
            value = diag * here[f] + (above * ahead[f] + below * back[f])
            value = value + (north * right(here[f]) + south * left(here[f]))
            value = 0.5 * value if m == 0 else value - poly[f, m - 1, r]
            poly[f, m + 1, r] = value
        back, here, below = here, ahead, above


def inner_kernel(state, depth, near, first, second, grid, poly, coef):
    rows = depth.shape[0]
    odd_tile = lax.rem(lax.axis_index("tile"), 2) == 1
    own = [state.at[0], state.at[1], state.at[2], depth]
    for g in range(rows // SUB):
        side = sides_of(first, second, pl.ds(g * SUB, SUB))
        for f in range(4):
            block = own[f][pl.ds(g * SUB, SUB), :]
            lay(grid, block, place(side, f), (REACH + g * SUB) * 4 + f, SUB, 4)
    below = REACH + rows
    main = jnp.where(odd_tile, 1, below)
    ext = jnp.where(odd_tile, 0, below + SUB)
    lay_halo(grid, near, main, ext)
    start = jnp.where(odd_tile, 0, REACH)
    prepare(grid, poly, coef, start, rows + REACH - 2)
    for m in range(ITERS - 1):
        sweep(poly, coef, m, start + m + 2, rows + REACH - 4 - 2 * m)


def outer_kernel(far, sums, grid_in, poly_in, coef_in, sol_in, out, grid, poly, coef, sol, result):
    rows, columns = out.shape[1:]
    odd_tile = lax.rem(lax.axis_index("tile"), 2) == 1
    lane = lax.broadcasted_iota(jnp.int32, (SUB, LANES), 1)
    below = REACH + rows
    main = jnp.where(odd_tile, below, 1)
    ext = jnp.where(odd_tile, below + SUB, 0)
    lay_halo(grid, far, main, ext)
    start = jnp.where(odd_tile, below - 2, 0)
    prepare(grid, poly, coef, start, REACH)
    step = jnp.where(odd_tile, -1, 1)
    for m in range(ITERS - 1):
        sweep(poly, coef, m, start + 1 + step * (m + 1), REACH)
    first = jnp.where(odd_tile, rows + 1, REACH - 1)
    weighted_sums(poly, sums, sol, first, REACH)
    push = sums[9 * ITERS]
    lift = sums[9 * ITERS + 1]
    for i in range(rows):
        u, v = cell(grid, 1, REACH + i), cell(grid, 2, REACH + i)
        result[0, pl.ds(i * SUB, SUB)] = sol[0, i + 1]
        east = 0.5 * (sol[1, i + 2] - sol[1, i])
        north = 0.5 * (right(sol[2, i + 1]) - left(sol[2, i + 1]))
        result[1, pl.ds(i * SUB, SUB)] = (push * u + lift * v) - (east + coriolis * north)
        east = 0.5 * (sol[2, i + 2] - sol[2, i])
        north = 0.5 * (right(sol[1, i + 1]) - left(sol[1, i + 1]))
        result[2, pl.ds(i * SUB, SUB)] = (push * v - lift * u) + (coriolis * east - north)

    for k in range(3):
        for g in range(rows // SUB):
            for t in range(columns // LANES):
                one = result[k, pl.Slice(g * SUB * SUB + 2 * t, SUB, SUB), :]
                two = result[k, pl.Slice(g * SUB * SUB + 2 * t + 1, SUB, SUB), :]
                joined = jnp.where(lane < HALF, turn(one, -SIDE), turn(two, SIDE))
                out[k, pl.ds(g * SUB, SUB), pl.ds(t * LANES, LANES)] = joined


def shards(state, depth, pole_real, pole_imag, pole_weight):
    rows, columns = depth.shape
    poles = pole_real.shape[0]
    vmem = pl.BlockSpec(memory_space=pltpu.VMEM)
    smem = pl.BlockSpec(memory_space=pltpu.SMEM)
    small = pltpu.CompilerParams(vmem_limit_bytes=GRANT)

    def f32(*shape):
        return jax.ShapeDtypeStruct(shape, jnp.float32)

    last = columns // LANES - 1
    first, second, scalars = pl.pallas_call(
        pack_columns_kernel,
        grid=(1,),
        out_shape=(f32(rows, LANES), f32(rows, LANES), f32(4 * poles, LANES)),
        in_specs=[
            pl.BlockSpec((3, rows, LANES), lambda i: (0, 0, 0)),
            pl.BlockSpec((3, rows, LANES), lambda i: (0, 0, last)),
            pl.BlockSpec((rows, LANES), lambda i: (0, 0)),
            pl.BlockSpec((rows, LANES), lambda i: (0, last)),
            smem,
            smem,
            smem,
        ],
        out_specs=(vmem, vmem, vmem),
        name="pack_columns",
    )(state, state, depth, depth, pole_real, pole_imag, pole_weight)
    first = swap(first, "pole", 0)
    second = swap(second, "pole", 1)
    halo = f32(5 * SUB, columns)
    far, near = pl.pallas_call(
        pack_rows_kernel,
        out_shape=(halo, halo),
        in_specs=[vmem] * 4,
        out_specs=(vmem, vmem),
        compiler_params=small,
        name="pack_rows",
    )(state, depth, first, second)
    far = swap(far, "tile", 1)
    near = swap(near, "tile", 0)
    count = lax.axis_size("pole")
    others = jnp.stack([shift(scalars, "pole", step) for step in range(2, count - 1)])
    height = rows + 2 * REACH
    grid = f32(height * 4 * SUB, LANES)
    poly = f32(3, ITERS, height, SUB, LANES)
    coef = f32(4, height, SUB, LANES)
    sol = f32(3, rows + 2, SUB, LANES)
    held = 4 * SUB * LANES * height * (4 + 3 * ITERS + 4)
    inner = pl.pallas_call(
        inner_kernel,
        out_shape=(grid, poly, coef),
        in_specs=[vmem] * 5,
        out_specs=(vmem, vmem, vmem),
        compiler_params=small,
        cost_estimate=pl.CostEstimate(
            flops=40 * 3 * ITERS * height * SUB * LANES, bytes_accessed=held, transcendentals=0
        ),
        name="inner",
    )(state, depth, near, first, second)
    sums, part = pl.pallas_call(
        pole_sums_kernel,
        out_shape=(f32(9 * ITERS + 2, SUB, LANES), sol),
        in_specs=[vmem] * 5,
        out_specs=(vmem, vmem),
        compiler_params=small,
        name="pole_sums",
    )(scalars, first, second, others, inner[1])
    return pl.pallas_call(
        outer_kernel,
        out_shape=(f32(*state.shape), grid, poly, coef, sol),
        in_specs=[vmem] * 6,
        out_specs=(vmem,) * 5,
        input_output_aliases={2: 1, 3: 2, 4: 3, 5: 4},
        scratch_shapes=[pltpu.VMEM((3, rows * SUB, LANES), jnp.float32)],
        compiler_params=small,
        name="outer",
    )(far, sums, *inner, part)[0]


def solution(mesh):
    return jax.shard_map(
        shards,
        mesh=mesh,
        in_specs=(
            P(None, "tile", "pole"),
            P("tile", "pole"),
            P("pole"),
            P("pole"),
            P(None, "pole"),
        ),
        out_specs=P(None, "tile", "pole"),
        check_vma=False,
    )
```

```python
import jax
import jax.numpy as jnp
from jax import lax
from jax.experimental import pallas as pl
from jax.experimental.pallas import tpu as pltpu
from jax.sharding import PartitionSpec as P

ITERS = 8
REACH = ITERS + 1
SUB = 8
LANES = 128
HALF = LANES // 2
SIDE = 32
EDGE = 12
EAST = HALF + EDGE
GRANT = 16 * 1024 * 1024

coriolis = 0.7
centre = 8.0
half_width = 8.0


def pairs(count, phase):
    swap = []
    for i in range(phase, count + phase, 2):
        a, b = i % count, (i + 1) % count
        swap += [(a, b), (b, a)]
    return swap


def swap(block, axis, phase):
    return lax.ppermute(block, axis, pairs(lax.axis_size(axis), phase))


def shift(block, axis, step):
    count = lax.axis_size(axis)
    return lax.ppermute(block, axis, [(i, (i + step) % count) for i in range(count)])


def turn(x, lanes):
    return pltpu.roll(x, lanes % LANES, 1) if lanes % LANES else x


def cmul(a, b):
    return (a[0] * b[0] - a[1] * b[1], a[0] * b[1] + a[1] * b[0])


def cinv(a):
    norm = 1.0 / (a[0] * a[0] + a[1] * a[1])
    return (a[0] * norm, -a[1] * norm)


def cscale(a, factor):
    return (a[0] * factor, a[1] * factor)


def pack_columns_kernel(
    state, depth, real, imag, weight, fields, first, second, scalars, real_in, imag_in, weight_in, done
):
    moves = [
        pltpu.make_async_copy(state, fields.at[pl.ds(0, 3)], done.at[0]),
        pltpu.make_async_copy(depth, fields.at[3], done.at[1]),
        pltpu.make_async_copy(real, real_in, done.at[2]),
        pltpu.make_async_copy(imag, imag_in, done.at[3]),
        pltpu.make_async_copy(weight, weight_in, done.at[4]),
    ]
    for move in moves:
        move.start()
    for move in moves:
        move.wait()
    odd = lax.rem(lax.axis_index("pole"), 2) == 1
    rows, columns = fields.shape[1:]
    lane = lax.broadcasted_iota(jnp.int32, (SUB, LANES), 1)
    sub = lax.broadcasted_iota(jnp.int32, (SUB, LANES), 0)
    poles = real.shape[0]
    values = [real_in[i] for i in range(poles)] + [imag_in[i] for i in range(poles)]
    values += [weight_in[0, i] for i in range(poles)] + [weight_in[1, i] for i in range(poles)]
    spread = []
    for g in range(len(values) // SUB):
        block = jnp.full((SUB, LANES), values[g * SUB], jnp.float32)
        for i in range(1, SUB):
            block = jnp.where(sub == i, values[g * SUB + i], block)
        scalars[pl.ds(g * SUB, SUB)] = block
        spread.append(block)
    for g in range(rows // SUB):
        cut = pl.ds(g * SUB, SUB)
        rest = spread[g] if g < len(spread) else jnp.zeros((SUB, LANES), jnp.float32)
        eastward = rest
        westward = rest
        for f in range(4):
            west = fields[f, cut, 0:LANES]
            east = fields[f, cut, columns - LANES : columns]
            low, high = EDGE * f, EDGE * (f + 1)
            take = jnp.logical_and(lane >= low, lane < high)
            eastward = jnp.where(take, turn(east, low + EDGE), eastward)
            take = jnp.logical_and(lane >= EAST + low, lane < EAST + high)
            westward = jnp.where(take, turn(west, EAST + low), westward)
        first[cut, :] = jnp.where(odd, westward, eastward)
        second[cut, :] = jnp.where(odd, eastward, westward)


def sides_of(first, second, cut):
    odd = lax.rem(lax.axis_index("pole"), 2) == 1
    lane = lax.broadcasted_iota(jnp.int32, (SUB, LANES), 1)
    from_first = jnp.logical_xor(lane >= HALF, odd)
    return jnp.where(from_first, first[cut, :], second[cut, :])


def pack_rows_kernel(fields, second, first, far, near):
    odd = lax.rem(lax.axis_index("tile"), 2) == 1
    rows = fields.shape[1]
    for target, low in ((far, jnp.logical_not(odd)), (near, odd)):
        def fill(main, ext):
            for f in range(4):
                target[f * SUB : (f + 1) * SUB] = fields[f, main : main + SUB]
                target[4 * SUB + f : 4 * SUB + f + 1] = fields[f, ext : ext + 1]
            side = sides_of(first, second, pl.ds(main, SUB))
            base = 4 * SUB + 4
            target[base : base + 4, 0:LANES] = side[0:4]
            target[base : base + 4, LANES : 2 * LANES] = side[4:8]
            group = ext // SUB * SUB
            side = sides_of(first, second, pl.ds(group, SUB))
            target[base : base + 1, 2 * LANES : 3 * LANES] = side[ext - group : ext - group + 1]

        pl.when(low)(lambda: fill(0, SUB))
        pl.when(jnp.logical_not(low))(lambda: fill(rows - SUB, rows - SUB - 1))


def pole_sums_kernel(scalars, first, second, others, poly, sums, sol):
    odd = lax.rem(lax.axis_index("pole"), 2) == 1
    count = scalars.shape[0]
    lane = lax.broadcasted_iota(jnp.int32, (SUB, LANES), 1)
    blocks = [[scalars[pl.ds(g, SUB)] for g in range(0, count, SUB)]]
    for i, message in enumerate((first, second)):
        low = jnp.logical_xor(lane < HALF, odd if i == 0 else jnp.logical_not(odd))
        part = []
        for g in range(0, count, SUB):
            x = message[pl.ds(g, SUB), :]
            part.append(jnp.where(low, x, turn(x, HALF)))
        blocks.append(part)
    for i in range(others.shape[0]):
        blocks.append([others[i, pl.ds(g, SUB)] for g in range(0, count, SUB)])
    poles = count // 4
    quantity = []
    for q in range(4):
        cut = []
        for block in blocks:
            whole = jnp.concatenate(block, axis=0)
            cut.append(whole[q * poles : (q + 1) * poles])
        quantity.append(jnp.concatenate(cut, axis=0))
    alpha = (quantity[0], quantity[1])
    beta = (quantity[2], quantity[3])
    square = cmul(alpha, alpha)
    shifted = (square[0] + coriolis * coriolis, square[1])
    sigma = ((shifted[0] + centre) / half_width, shifted[1] / half_width)
    rho = [cinv(sigma)]
    for j in range(1, ITERS):
        rho.append(cinv((2.0 * sigma[0] - rho[-1][0], 2.0 * sigma[1] - rho[-1][1])))
    gain = None
    start = []
    for m in range(ITERS):
        if m == 0:
            start.append(cscale(rho[0], 1.0 / half_width))
        else:
            gain = rho[0] if gain is None else cmul(gain, rho[m - 1])
            start.append(cscale(cmul(rho[m], gain), 2.0 / half_width))
    tail = None
    weight = [None] * ITERS
    for m in reversed(range(ITERS)):
        if tail is None:
            weight[m] = start[m]
            tail = (jnp.ones_like(sigma[0]), jnp.zeros_like(sigma[0]))
        else:
            tail = cmul(cmul(rho[m + 1], rho[m]), tail)
            tail = (tail[0] + 1.0, tail[1])
            weight[m] = cmul(start[m], tail)
    inverse_alpha = cinv(alpha)
    inverse_shift = cinv(shifted)
    by_alpha = cmul(beta, inverse_alpha)
    by_shift = cmul(beta, inverse_shift)
    products = {
        "b": beta,
        "b/a": by_alpha,
        "b/s": by_shift,
        "bs/a": cmul(by_alpha, shifted),
        "ba/s": cmul(by_shift, alpha),
        "b/as": cmul(by_alpha, inverse_shift),
    }

    def total(x):
        s = x[0:SUB]
        for i in range(1, x.shape[0] // SUB):
            s = s + x[i * SUB : (i + 1) * SUB]
        for step in (4, 2, 1):
            s = s + pltpu.roll(s, step, 0)
        return s

    names = [("bs/a", "b", "b/a"), ("b", "ba/s", "b/s"), ("b/a", "b/s", "b/as")]
    factor = (1.0, -1.0, -coriolis)
    found = {}
    for m in range(ITERS):
        for name, w in products.items():
            found[name, m] = total(w[0] * weight[m][0] - w[1] * weight[m][1])
        for g in range(3):
            for f in range(3):
                value = found[names[g][f], m]
                sums[(g * 3 + f) * ITERS + m] = value if f == 0 else factor[f] * value
    sums[9 * ITERS] = total(products["ba/s"][0])
    sums[9 * ITERS + 1] = coriolis * total(products["b/s"][0])

    rows = sol.shape[1] - 2
    span = range(REACH + 1, REACH + rows - 1)
    weighted_sums(poly, sums, sol, {r: range(known(rows, r) + 1) for r in span}, False)


def known(rows, r):
    return min(ITERS - 2, r - (REACH + 1), REACH + rows - 2 - r)


def weighted_sums(poly, sums, sol, terms, more, block=6):
    low = REACH - 1
    order = sorted(terms)
    for i in range(0, len(order), block):
        span = order[i : i + block]
        acc = {}
        if more:
            for r in span:
                if len(terms[r]) < ITERS:
                    for g in range(3):
                        acc[g, r] = sol[g, r - low]
        for f in range(3):
            for m in range(ITERS):
                part = [r for r in span if m in terms[r]]
                if not part:
                    continue
                value = [poly[f, m, r] for r in part]
                for g in range(3):
                    c = sums[(g * 3 + f) * ITERS + m]
                    for r, v in zip(part, value):
                        acc[g, r] = acc[g, r] + c * v if (g, r) in acc else c * v
        for (g, r), v in acc.items():
            sol[g, r - low] = v


def strips_of(tiles, side):
    lane = lax.broadcasted_iota(jnp.int32, (SUB, LANES), 1)
    up = [turn(tile, SIDE) for tile in tiles]
    down = [turn(tile, -SIDE) for tile in tiles]
    out = []
    for q in range(len(tiles)):
        out.append(jnp.where(lane < SIDE, up[q - 1] if q else side, up[q]))
        after = down[q + 1] if q + 1 < len(tiles) else side
        out.append(jnp.where(lane < LANES - SIDE, down[q], after))
    return out


def lay(grid, block, side, at, size, stride):
    cut = [block[:, t * LANES : (t + 1) * LANES] for t in range(block.shape[1] // LANES)]
    for s, strip in enumerate(strips_of(cut, side)):
        grid[pl.Slice(at * SUB + s, size, stride * SUB), :] = strip[0:size]


def place(side, f):
    return turn(side, SIDE - EDGE - EDGE * f)


def lay_halo(grid, halo, main, ext):
    sub = lax.broadcasted_iota(jnp.int32, (SUB, LANES), 0)
    base = 4 * SUB + 4
    side = jnp.concatenate(
        [halo[base : base + 4, 0:LANES], halo[base : base + 4, LANES : 2 * LANES]], axis=0
    )
    for f in range(4):
        lay(grid, halo[pl.ds(f * SUB, SUB), :], place(side, f), main * 4 + f, SUB, 4)
    line = halo[base : base + 1, 2 * LANES : 3 * LANES]
    line = jnp.broadcast_to(line, (SUB, LANES))
    side = place(line, 0)
    for f in range(1, 4):
        side = jnp.where(sub == f, place(line, f), side)
    lay(grid, halo[pl.ds(4 * SUB, SUB), :], side, ext * 4, 4, 1)


def cell(grid, f, r):
    return grid[pl.ds(pl.multiple_of((r * 4 + f) * SUB, SUB), SUB), :]


def left(x):
    return pltpu.roll(x, 1, 1)


def right(x):
    return pltpu.roll(x, LANES - 1, 1)


def prepare(grid, poly, coef, start, count):
    flux_east = [None] * 3
    flux_north = [None] * 3
    depths = [None] * 2
    across = None
    for k in range(count + 2):
        r = start + k
        h = cell(grid, 3, r)
        flux_east = flux_east[1:] + [h * cell(grid, 1, r)]
        flux_north = flux_north[1:] + [h * cell(grid, 2, r)]
        depths = depths[1:] + [h]
        if k >= 1:
            before, across = across, 0.125 * (depths[0] + depths[1])
            coef[0, r - 1] = across
        if k >= 2:
            c = r - 1
            north = 0.125 * (depths[0] + right(depths[0]))
            south = left(north)
            coef[1, c] = north
            coef[2, c] = south
            coef[3, c] = 2.0 - ((across + before) + (north + south))
            east_slope = flux_east[2] - flux_east[0]
            north_slope = right(flux_north[1]) - left(flux_north[1])
            poly[1, 0, c] = 0.5 * (east_slope + north_slope)
            east_slope = flux_north[2] - flux_north[0]
            north_slope = right(flux_east[1]) - left(flux_east[1])
            poly[2, 0, c] = 0.5 * (east_slope - north_slope)
            poly[0, 0, c] = cell(grid, 0, c)


def sweep(poly, coef, m, start, count):
    back = [poly[f, m, start - 1] for f in range(3)]
    here = [poly[f, m, start] for f in range(3)]
    below = coef[0, start - 1]
    for k in range(count):
        r = start + k
        above, north, south, diag = coef[0, r], coef[1, r], coef[2, r], coef[3, r]
        ahead = [poly[f, m, r + 1] for f in range(3)]
        for f in range(3):
            value = diag * here[f] + (above * ahead[f] + below * back[f])
            value = value + (north * right(here[f]) + south * left(here[f]))
            value = 0.5 * value if m == 0 else value - poly[f, m - 1, r]
            poly[f, m + 1, r] = value
        back, here, below = here, ahead, above


def inner_kernel(fields, first, second, grid, poly, coef):
    rows = fields.shape[1]
    for g in range(rows // SUB):
        side = sides_of(first, second, pl.ds(g * SUB, SUB))
        for f in range(4):
            block = fields[f, pl.ds(g * SUB, SUB), :]
            lay(grid, block, place(side, f), (REACH + g * SUB) * 4 + f, SUB, 4)
    prepare(grid, poly, coef, REACH, rows - 2)
    for m in range(ITERS - 1):
        if rows - 4 - 2 * m > 0:
            sweep(poly, coef, m, REACH + 2 + m, rows - 4 - 2 * m)


def outer_kernel(far, near, sums, grid_in, poly_in, coef_in, sol_in, out, grid, poly, coef, sol, result):
    rows, columns = out.shape[1:]
    odd_tile = lax.rem(lax.axis_index("tile"), 2) == 1
    lane = lax.broadcasted_iota(jnp.int32, (SUB, LANES), 1)
    below = REACH + rows
    for halo, above in ((near, odd_tile), (far, jnp.logical_not(odd_tile))):
        main = jnp.where(above, 1, below)
        ext = jnp.where(above, 0, below + SUB)
        lay_halo(grid, halo, main, ext)
    prepare(grid, poly, coef, 0, REACH)
    prepare(grid, poly, coef, below - 2, REACH)
    for m in range(ITERS - 1):
        sweep(poly, coef, m, 2 + m, REACH)
        sweep(poly, coef, m, below - 2 - m, REACH)
    span = range(REACH - 1, REACH + rows + 1)
    terms = {r: range(max(known(rows, r), -1) + 1, ITERS) for r in span}
    weighted_sums(poly, sums, sol, terms, True)
    push = sums[9 * ITERS]
    lift = sums[9 * ITERS + 1]
    for i in range(rows):
        u, v = cell(grid, 1, REACH + i), cell(grid, 2, REACH + i)
        result[0, pl.ds(i * SUB, SUB)] = sol[0, i + 1]
        east = 0.5 * (sol[1, i + 2] - sol[1, i])
        north = 0.5 * (right(sol[2, i + 1]) - left(sol[2, i + 1]))
        result[1, pl.ds(i * SUB, SUB)] = (push * u + lift * v) - (east + coriolis * north)
        east = 0.5 * (sol[2, i + 2] - sol[2, i])
        north = 0.5 * (right(sol[1, i + 1]) - left(sol[1, i + 1]))
        result[2, pl.ds(i * SUB, SUB)] = (push * v - lift * u) + (coriolis * east - north)

    for k in range(3):
        for g in range(rows // SUB):
            for t in range(columns // LANES):
                one = result[k, pl.Slice(g * SUB * SUB + 2 * t, SUB, SUB), :]
                two = result[k, pl.Slice(g * SUB * SUB + 2 * t + 1, SUB, SUB), :]
                joined = jnp.where(lane < HALF, turn(one, -SIDE), turn(two, SIDE))
                out[k, pl.ds(g * SUB, SUB), pl.ds(t * LANES, LANES)] = joined


def shards(state, depth, pole_real, pole_imag, pole_weight):
    rows, columns = depth.shape
    poles = pole_real.shape[0]
    vmem = pl.BlockSpec(memory_space=pltpu.VMEM)
    small = pltpu.CompilerParams(vmem_limit_bytes=GRANT)

    def f32(*shape):
        return jax.ShapeDtypeStruct(shape, jnp.float32)

    given = [
        pltpu.with_memory_space_constraint(x, pltpu.HBM)
        for x in (state, depth, pole_real, pole_imag, pole_weight)
    ]
    hbm = pl.BlockSpec(memory_space=pltpu.HBM)
    message = pltpu.VMEM((rows, LANES), jnp.float32)
    fields, first, second, scalars = pl.pallas_call(
        pack_columns_kernel,
        out_shape=(
            pltpu.VMEM((4, rows, columns), jnp.float32),
            message,
            message,
            pltpu.VMEM((4 * poles, LANES), jnp.float32),
        ),
        in_specs=[hbm] * 5,
        out_specs=(vmem,) * 4,
        scratch_shapes=[
            pltpu.SMEM(pole_real.shape, jnp.float32),
            pltpu.SMEM(pole_imag.shape, jnp.float32),
            pltpu.SMEM(pole_weight.shape, jnp.float32),
            pltpu.SemaphoreType.DMA((5,)),
        ],
        compiler_params=small,
        name="pack_columns",
    )(*given)
    second = swap(second, "pole", 1)
    first = swap(first, "pole", 0)
    halo = f32(5 * SUB, columns)
    far, near = pl.pallas_call(
        pack_rows_kernel,
        out_shape=(halo, halo),
        in_specs=[vmem] * 3,
        out_specs=(vmem, vmem),
        compiler_params=small,
        name="pack_rows",
    )(fields, second, first)
    far = swap(far, "tile", 1)
    near = swap(near, "tile", 0)
    count = lax.axis_size("pole")
    others = jnp.stack([shift(scalars, "pole", step) for step in range(2, count - 1)])
    height = rows + 2 * REACH
    grid = f32(height * 4 * SUB, LANES)
    poly = f32(3, ITERS, height, SUB, LANES)
    coef = f32(4, height, SUB, LANES)
    sol = f32(3, rows + 2, SUB, LANES)
    held = 4 * SUB * LANES * height * (4 + 3 * ITERS + 4)
    inner = pl.pallas_call(
        inner_kernel,
        out_shape=(grid, poly, coef),
        in_specs=[vmem] * 3,
        out_specs=(vmem, vmem, vmem),
        compiler_params=small,
        cost_estimate=pl.CostEstimate(
            flops=40 * 3 * ITERS * height * SUB * LANES, bytes_accessed=held, transcendentals=0
        ),
        name="inner",
    )(fields, first, second)
    sums, part = pl.pallas_call(
        pole_sums_kernel,
        out_shape=(f32(9 * ITERS + 2, SUB, LANES), sol),
        in_specs=[vmem] * 5,
        out_specs=(vmem, vmem),
        compiler_params=small,
        name="pole_sums",
    )(scalars, first, second, others, inner[1])
    return pl.pallas_call(
        outer_kernel,
        out_shape=(f32(*state.shape), grid, poly, coef, sol),
        in_specs=[vmem] * 7,
        out_specs=(vmem,) * 5,
        input_output_aliases={3: 1, 4: 2, 5: 3, 6: 4},
        scratch_shapes=[pltpu.VMEM((3, rows * SUB, LANES), jnp.float32)],
        compiler_params=small,
        name="outer",
    )(far, near, sums, *inner, part)[0]


def solution(mesh):
    return jax.shard_map(
        shards,
        mesh=mesh,
        in_specs=(
            P(None, "tile", "pole"),
            P("tile", "pole"),
            P("pole"),
            P("pole"),
            P(None, "pole"),
        ),
        out_specs=P(None, "tile", "pole"),
        check_vma=False,
    )
```

```python
import jax
import jax.numpy as jnp
from jax import lax
from jax.experimental import pallas as pl
from jax.experimental.pallas import tpu as pltpu
from jax.sharding import PartitionSpec as P

ITERS = 8
REACH = ITERS + 1
SUB = 8
LANES = 128
HALF = LANES // 2
SIDE = 32
EDGE = 12
EAST = HALF + EDGE
GRANT = 16 * 1024 * 1024

coriolis = 0.7
centre = 8.0
half_width = 8.0


def pairs(count, phase):
    swap = []
    for i in range(phase, count + phase, 2):
        a, b = i % count, (i + 1) % count
        swap += [(a, b), (b, a)]
    return swap


def swap(block, axis, phase):
    return lax.ppermute(block, axis, pairs(lax.axis_size(axis), phase))


def shift(block, axis, step):
    count = lax.axis_size(axis)
    return lax.ppermute(block, axis, [(i, (i + step) % count) for i in range(count)])


def turn(x, lanes):
    return pltpu.roll(x, lanes % LANES, 1) if lanes % LANES else x


def cmul(a, b):
    return (a[0] * b[0] - a[1] * b[1], a[0] * b[1] + a[1] * b[0])


def cinv(a):
    norm = 1.0 / (a[0] * a[0] + a[1] * a[1])
    return (a[0] * norm, -a[1] * norm)


def cscale(a, factor):
    return (a[0] * factor, a[1] * factor)


def pack_columns_kernel(
    state,
    depth,
    real,
    imag,
    weight,
    fields,
    first,
    second,
    scalars,
    far,
    near,
    real_in,
    imag_in,
    weight_in,
    done,
):
    moves = [
        pltpu.make_async_copy(state, fields.at[pl.ds(0, 3)], done.at[0]),
        pltpu.make_async_copy(depth, fields.at[3], done.at[1]),
        pltpu.make_async_copy(real, real_in, done.at[2]),
        pltpu.make_async_copy(imag, imag_in, done.at[3]),
        pltpu.make_async_copy(weight, weight_in, done.at[4]),
    ]
    for move in moves:
        move.start()
    for move in moves:
        move.wait()
    odd = lax.rem(lax.axis_index("pole"), 2) == 1
    rows, columns = fields.shape[1:]
    lane = lax.broadcasted_iota(jnp.int32, (SUB, LANES), 1)
    sub = lax.broadcasted_iota(jnp.int32, (SUB, LANES), 0)
    poles = real.shape[0]
    values = [real_in[i] for i in range(poles)] + [imag_in[i] for i in range(poles)]
    values += [weight_in[0, i] for i in range(poles)] + [weight_in[1, i] for i in range(poles)]
    spread = []
    for g in range(len(values) // SUB):
        block = jnp.full((SUB, LANES), values[g * SUB], jnp.float32)
        for i in range(1, SUB):
            block = jnp.where(sub == i, values[g * SUB + i], block)
        scalars[pl.ds(g * SUB, SUB)] = block
        spread.append(block)
    for g in range(rows // SUB):
        cut = pl.ds(g * SUB, SUB)
        rest = spread[g] if g < len(spread) else jnp.zeros((SUB, LANES), jnp.float32)
        eastward = rest
        westward = rest
        for f in range(4):
            west = fields[f, cut, 0:LANES]
            east = fields[f, cut, columns - LANES : columns]
            low, high = EDGE * f, EDGE * (f + 1)
            take = jnp.logical_and(lane >= low, lane < high)
            eastward = jnp.where(take, turn(east, low + EDGE), eastward)
            take = jnp.logical_and(lane >= EAST + low, lane < EAST + high)
            westward = jnp.where(take, turn(west, EAST + low), westward)
        first[cut, :] = jnp.where(odd, westward, eastward)
        second[cut, :] = jnp.where(odd, eastward, westward)
    odd = lax.rem(lax.axis_index("tile"), 2) == 1
    for target, low in ((far, jnp.logical_not(odd)), (near, odd)):
        pl.when(low)(lambda: pack_rows(target, fields, 0, SUB))
        pl.when(jnp.logical_not(low))(
            lambda: pack_rows(target, fields, rows - SUB, rows - SUB - 1)
        )


def pack_rows(target, fields, main, ext):
    tiles = fields.shape[2] // LANES
    for f in range(4):
        for t in range(tiles):
            block = fields[f, main : main + SUB, t * LANES : (t + 1) * LANES]
            target[pl.ds((f * tiles + t) * SUB, SUB)] = block
    for f in (1, 2):
        flux = fields[3, ext : ext + 1, :] * fields[f, ext : ext + 1, :]
        for t in range(tiles):
            at = (4 * SUB + f - 1) * tiles + t
            target[at : at + 1] = flux[:, t * LANES : (t + 1) * LANES]


def sides_of(first, second, cut):
    odd = lax.rem(lax.axis_index("pole"), 2) == 1
    lane = lax.broadcasted_iota(jnp.int32, (SUB, LANES), 1)
    from_first = jnp.logical_xor(lane >= HALF, odd)
    return jnp.where(from_first, first[cut, :], second[cut, :])


def pack_corners_kernel(second, first, far, near):
    odd = lax.rem(lax.axis_index("tile"), 2) == 1
    rows = first.shape[0]
    for target, low in ((far, jnp.logical_not(odd)), (near, odd)):

        def fill(main, ext):
            target[0:SUB] = sides_of(first, second, pl.ds(main, SUB))
            group = ext // SUB * SUB
            side = sides_of(first, second, pl.ds(group, SUB))
            line = side[ext - group : ext - group + 1]
            target[SUB : 2 * SUB] = jnp.broadcast_to(line, (SUB, LANES))

        pl.when(low)(lambda: fill(0, SUB))
        pl.when(jnp.logical_not(low))(lambda: fill(rows - SUB, rows - SUB - 1))


def pole_sums_kernel(scalars, first, second, others, poly, sums, sol):
    odd = lax.rem(lax.axis_index("pole"), 2) == 1
    count = scalars.shape[0]
    lane = lax.broadcasted_iota(jnp.int32, (SUB, LANES), 1)
    blocks = [[scalars[pl.ds(g, SUB)] for g in range(0, count, SUB)]]
    for i, message in enumerate((first, second)):
        low = jnp.logical_xor(lane < HALF, odd if i == 0 else jnp.logical_not(odd))
        part = []
        for g in range(0, count, SUB):
            x = message[pl.ds(g, SUB), :]
            part.append(jnp.where(low, x, turn(x, HALF)))
        blocks.append(part)
    for i in range(others.shape[0]):
        blocks.append([others[i, pl.ds(g, SUB)] for g in range(0, count, SUB)])
    poles = count // 4
    quantity = []
    for q in range(4):
        cut = []
        for block in blocks:
            whole = jnp.concatenate(block, axis=0)
            cut.append(whole[q * poles : (q + 1) * poles])
        quantity.append(jnp.concatenate(cut, axis=0))
    alpha = (quantity[0], quantity[1])
    beta = (quantity[2], quantity[3])
    square = cmul(alpha, alpha)
    shifted = (square[0] + coriolis * coriolis, square[1])
    sigma = ((shifted[0] + centre) / half_width, shifted[1] / half_width)
    rho = [cinv(sigma)]
    for j in range(1, ITERS):
        rho.append(cinv((2.0 * sigma[0] - rho[-1][0], 2.0 * sigma[1] - rho[-1][1])))
    gain = None
    start = []
    for m in range(ITERS):
        if m == 0:
            start.append(cscale(rho[0], 1.0 / half_width))
        else:
            gain = rho[0] if gain is None else cmul(gain, rho[m - 1])
            start.append(cscale(cmul(rho[m], gain), 2.0 / half_width))
    tail = None
    weight = [None] * ITERS
    for m in reversed(range(ITERS)):
        if tail is None:
            weight[m] = start[m]
            tail = (jnp.ones_like(sigma[0]), jnp.zeros_like(sigma[0]))
        else:
            tail = cmul(cmul(rho[m + 1], rho[m]), tail)
            tail = (tail[0] + 1.0, tail[1])
            weight[m] = cmul(start[m], tail)
    inverse_alpha = cinv(alpha)
    inverse_shift = cinv(shifted)
    by_alpha = cmul(beta, inverse_alpha)
    by_shift = cmul(beta, inverse_shift)
    products = {
        "b": beta,
        "b/a": by_alpha,
        "b/s": by_shift,
        "bs/a": cmul(by_alpha, shifted),
        "ba/s": cmul(by_shift, alpha),
        "b/as": cmul(by_alpha, inverse_shift),
    }

    def total(x):
        s = x[0:SUB]
        for i in range(1, x.shape[0] // SUB):
            s = s + x[i * SUB : (i + 1) * SUB]
        for step in (4, 2, 1):
            s = s + pltpu.roll(s, step, 0)
        return s

    names = [("bs/a", "b", "b/a"), ("b", "ba/s", "b/s"), ("b/a", "b/s", "b/as")]
    factor = (1.0, -1.0, -coriolis)
    found = {}
    for m in range(ITERS):
        for name, w in products.items():
            found[name, m] = total(w[0] * weight[m][0] - w[1] * weight[m][1])
        for g in range(3):
            for f in range(3):
                value = found[names[g][f], m]
                sums[(g * 3 + f) * ITERS + m] = value if f == 0 else factor[f] * value
    sums[9 * ITERS] = total(products["ba/s"][0])
    sums[9 * ITERS + 1] = coriolis * total(products["b/s"][0])

    rows = sol.shape[1] - 2
    span = range(REACH + 1, REACH + rows - 1)
    weighted_sums(poly, sums, sol, {r: range(known(rows, r) + 1) for r in span}, False)


def known(rows, r):
    return min(ITERS - 2, r - (REACH + 1), REACH + rows - 2 - r)


def weighted_sums(poly, sums, sol, terms, more, block=6):
    low = REACH - 1
    order = sorted(terms)
    for i in range(0, len(order), block):
        span = order[i : i + block]
        acc = {}
        if more:
            for r in span:
                if len(terms[r]) < ITERS:
                    for g in range(3):
                        acc[g, r] = sol[g, r - low]
        for f in range(3):
            for m in range(ITERS):
                part = [r for r in span if m in terms[r]]
                if not part:
                    continue
                value = [poly[f, m, r] for r in part]
                for g in range(3):
                    c = sums[(g * 3 + f) * ITERS + m]
                    for r, v in zip(part, value):
                        acc[g, r] = acc[g, r] + c * v if (g, r) in acc else c * v
        for (g, r), v in acc.items():
            sol[g, r - low] = v


def strips_of(tiles, side):
    lane = lax.broadcasted_iota(jnp.int32, (SUB, LANES), 1)
    up = [turn(tile, SIDE) for tile in tiles]
    down = [turn(tile, -SIDE) for tile in tiles]
    out = []
    for q in range(len(tiles)):
        out.append(jnp.where(lane < SIDE, up[q - 1] if q else side, up[q]))
        after = down[q + 1] if q + 1 < len(tiles) else side
        out.append(jnp.where(lane < LANES - SIDE, down[q], after))
    return out


def lay(grid, cut, side, at, stride):
    for s, strip in enumerate(strips_of(cut, side)):
        grid[pl.Slice(at * SUB + s, SUB, stride * SUB), :] = strip


def place(side, f):
    return turn(side, SIDE - EDGE - EDGE * f)


def lay_halo(grid, halo, corner, main, ext):
    lane = lax.broadcasted_iota(jnp.int32, (SUB, LANES), 1)
    sub = lax.broadcasted_iota(jnp.int32, (SUB, LANES), 0)
    tiles = SUB // 2
    side = corner[0:SUB]
    for f in range(4):
        cut = [halo[pl.ds((f * tiles + t) * SUB, SUB)] for t in range(tiles)]
        lay(grid, cut, place(side, f), main * 4 + f, 4)
    line = corner[SUB : 2 * SUB]
    east_flux = place(line * turn(line, -2 * EDGE), 1)
    north_flux = place(line * turn(line, -EDGE), 2)
    side = jnp.where(sub < tiles, east_flux, north_flux)
    block = halo[pl.ds(4 * tiles * SUB, SUB)]
    up, down = turn(block, SIDE), turn(block, -SIDE)
    before = jnp.where(sub % tiles == 0, side, pltpu.roll(up, 1, 0))
    after = jnp.where(sub % tiles == tiles - 1, side, pltpu.roll(down, SUB - 1, 0))
    even = jnp.where(lane < SIDE, before, up)
    odd = jnp.where(lane < LANES - SIDE, down, after)
    for f in (1, 2):
        at = (ext * 4 + f) * SUB
        cut = slice((f - 1) * tiles, f * tiles)
        grid[pl.Slice(at, tiles, 2), :] = even[cut]
        grid[pl.Slice(at + 1, tiles, 2), :] = odd[cut]


def cell(grid, f, r):
    return grid[pl.ds(pl.multiple_of((r * 4 + f) * SUB, SUB), SUB), :]


def left(x):
    return pltpu.roll(x, 1, 1)


def right(x):
    return pltpu.roll(x, LANES - 1, 1)


def prepare(grid, poly, coef, start, count):
    flux_east = [None] * 3
    flux_north = [None] * 3
    depths = [None] * 2
    for k in range(count + 2):
        r = start + k
        h = cell(grid, 3, r)
        flux_east = flux_east[1:] + [h * cell(grid, 1, r)]
        flux_north = flux_north[1:] + [h * cell(grid, 2, r)]
        depths = depths[1:] + [h]
        if k >= 1:
            coef[0, r - 1] = 0.125 * (depths[0] + depths[1])
        if k >= 2:
            c = r - 1
            coef[1, c] = 0.125 * (depths[0] + right(depths[0]))
            east_slope = flux_east[2] - flux_east[0]
            north_slope = right(flux_north[1]) - left(flux_north[1])
            poly[1, 0, c] = 0.5 * (east_slope + north_slope)
            east_slope = flux_north[2] - flux_north[0]
            north_slope = right(flux_east[1]) - left(flux_east[1])
            poly[2, 0, c] = 0.5 * (east_slope - north_slope)
            poly[0, 0, c] = cell(grid, 0, c)


def sweep(poly, coef, m, start, count):
    here = [poly[f, m, start] for f in range(3)]
    across = coef[0, start - 1]
    back = [across * (here[f] - poly[f, m, start - 1]) for f in range(3)]
    for k in range(count):
        r = start + k
        across, along = coef[0, r], coef[1, r]
        for f in range(3):
            w = here[f]
            ahead = poly[f, m, r + 1]
            east = across * (ahead - w)
            north = along * (right(w) - w)
            change = (east - back[f]) + (north - left(north))
            if m == 0:
                value = w + 0.5 * change
            else:
                value = (w - poly[f, m - 1, r]) + (w + change)
            poly[f, m + 1, r] = value
            here[f], back[f] = ahead, east


def inner_kernel(fields, first, second, grid, poly, coef):
    rows = fields.shape[1]
    for g in range(rows // SUB):
        side = sides_of(first, second, pl.ds(g * SUB, SUB))
        for f in range(4):
            cut = [
                fields[f, pl.ds(g * SUB, SUB), pl.ds(t * LANES, LANES)]
                for t in range(fields.shape[2] // LANES)
            ]
            lay(grid, cut, place(side, f), (REACH + g * SUB) * 4 + f, 4)
    prepare(grid, poly, coef, REACH, rows - 2)
    for m in range(ITERS - 1):
        if rows - 4 - 2 * m > 0:
            sweep(poly, coef, m, REACH + 2 + m, rows - 4 - 2 * m)


def outer_kernel(
    far,
    near,
    far_corner,
    near_corner,
    sums,
    grid_in,
    poly_in,
    coef_in,
    sol_in,
    out,
    grid,
    poly,
    coef,
    sol,
    result,
):
    rows, columns = out.shape[1:]
    odd_tile = lax.rem(lax.axis_index("tile"), 2) == 1
    lane = lax.broadcasted_iota(jnp.int32, (SUB, LANES), 1)
    below = REACH + rows
    for r in (0, below + SUB):
        grid[pl.ds((r * 4 + 3) * SUB, SUB), :] = jnp.ones((SUB, LANES), jnp.float32)
    halos = ((near, near_corner, odd_tile), (far, far_corner, jnp.logical_not(odd_tile)))
    for halo, corner, above in halos:
        main = jnp.where(above, 1, below)
        ext = jnp.where(above, 0, below + SUB)
        lay_halo(grid, halo, corner, main, ext)
    prepare(grid, poly, coef, 0, REACH)
    prepare(grid, poly, coef, below - 2, REACH)
    for m in range(ITERS - 1):
        sweep(poly, coef, m, 2 + m, REACH)
        sweep(poly, coef, m, below - 2 - m, REACH)
    span = range(REACH - 1, REACH + rows + 1)
    terms = {r: range(max(known(rows, r), -1) + 1, ITERS) for r in span}
    weighted_sums(poly, sums, sol, terms, True)
    push = sums[9 * ITERS]
    lift = sums[9 * ITERS + 1]
    for i in range(rows):
        u, v = cell(grid, 1, REACH + i), cell(grid, 2, REACH + i)
        result[0, pl.ds(i * SUB, SUB)] = sol[0, i + 1]
        east = 0.5 * (sol[1, i + 2] - sol[1, i])
        north = 0.5 * (right(sol[2, i + 1]) - left(sol[2, i + 1]))
        result[1, pl.ds(i * SUB, SUB)] = (push * u + lift * v) - (east + coriolis * north)
        east = 0.5 * (sol[2, i + 2] - sol[2, i])
        north = 0.5 * (right(sol[1, i + 1]) - left(sol[1, i + 1]))
        result[2, pl.ds(i * SUB, SUB)] = (push * v - lift * u) + (coriolis * east - north)

    for k in range(3):
        for g in range(rows // SUB):
            for t in range(columns // LANES):
                one = result[k, pl.Slice(g * SUB * SUB + 2 * t, SUB, SUB), :]
                two = result[k, pl.Slice(g * SUB * SUB + 2 * t + 1, SUB, SUB), :]
                joined = jnp.where(lane < HALF, turn(one, -SIDE), turn(two, SIDE))
                out[k, pl.ds(g * SUB, SUB), pl.ds(t * LANES, LANES)] = joined


def shards(state, depth, pole_real, pole_imag, pole_weight):
    rows, columns = depth.shape
    poles = pole_real.shape[0]
    vmem = pl.BlockSpec(memory_space=pltpu.VMEM)
    small = pltpu.CompilerParams(vmem_limit_bytes=GRANT)

    def f32(*shape):
        return jax.ShapeDtypeStruct(shape, jnp.float32)

    given = [
        pltpu.with_memory_space_constraint(x, pltpu.HBM)
        for x in (state, depth, pole_real, pole_imag, pole_weight)
    ]
    hbm = pl.BlockSpec(memory_space=pltpu.HBM)
    message = pltpu.VMEM((rows, LANES), jnp.float32)
    halo = pltpu.VMEM(((4 * SUB + 2) * columns // LANES, LANES), jnp.float32)
    fields, first, second, scalars, far, near = pl.pallas_call(
        pack_columns_kernel,
        out_shape=(
            pltpu.VMEM((4, rows, columns), jnp.float32),
            message,
            message,
            pltpu.VMEM((4 * poles, LANES), jnp.float32),
            halo,
            halo,
        ),
        in_specs=[hbm] * 5,
        out_specs=(vmem,) * 6,
        scratch_shapes=[
            pltpu.SMEM(pole_real.shape, jnp.float32),
            pltpu.SMEM(pole_imag.shape, jnp.float32),
            pltpu.SMEM(pole_weight.shape, jnp.float32),
            pltpu.SemaphoreType.DMA((5,)),
        ],
        compiler_params=small,
        name="pack_columns",
    )(*given)
    second = swap(second, "pole", 1)
    first = swap(first, "pole", 0)
    far = swap(far, "tile", 1)
    near = swap(near, "tile", 0)
    corner = f32(2 * SUB, LANES)
    far_corner, near_corner = pl.pallas_call(
        pack_corners_kernel,
        out_shape=(corner, corner),
        in_specs=[vmem] * 2,
        out_specs=(vmem, vmem),
        compiler_params=small,
        name="pack_corners",
    )(second, first)
    far_corner = swap(far_corner, "tile", 1)
    near_corner = swap(near_corner, "tile", 0)
    count = lax.axis_size("pole")
    others = jnp.stack([shift(scalars, "pole", step) for step in range(2, count - 1)])
    height = rows + 2 * REACH
    grid = f32(height * 4 * SUB, LANES)
    poly = f32(3, ITERS, height, SUB, LANES)
    coef = f32(2, height, SUB, LANES)
    sol = f32(3, rows + 2, SUB, LANES)
    held = 4 * SUB * LANES * rows * (4 + 2 * ITERS + 2)
    inner = pl.pallas_call(
        inner_kernel,
        out_shape=(grid, poly, coef),
        in_specs=[vmem] * 3,
        out_specs=(vmem, vmem, vmem),
        compiler_params=small,
        cost_estimate=pl.CostEstimate(
            flops=10 * ITERS * rows * SUB * LANES, bytes_accessed=held, transcendentals=0
        ),
        name="inner",
    )(fields, first, second)
    sums, part = pl.pallas_call(
        pole_sums_kernel,
        out_shape=(f32(9 * ITERS + 2, SUB, LANES), sol),
        in_specs=[vmem] * 5,
        out_specs=(vmem, vmem),
        compiler_params=small,
        name="pole_sums",
    )(scalars, first, second, others, inner[1])
    return pl.pallas_call(
        outer_kernel,
        out_shape=(f32(*state.shape), grid, poly, coef, sol),
        in_specs=[vmem] * 9,
        out_specs=(vmem,) * 5,
        input_output_aliases={5: 1, 6: 2, 7: 3, 8: 4},
        scratch_shapes=[pltpu.VMEM((3, rows * SUB, LANES), jnp.float32)],
        compiler_params=small,
        name="outer",
    )(far, near, far_corner, near_corner, sums, *inner, part)[0]


def solution(mesh):
    return jax.shard_map(
        shards,
        mesh=mesh,
        in_specs=(
            P(None, "tile", "pole"),
            P("tile", "pole"),
            P("pole"),
            P("pole"),
            P(None, "pole"),
        ),
        out_specs=P(None, "tile", "pole"),
        check_vma=False,
    )
```

```python
import jax
import jax.numpy as jnp
from jax import lax
from jax.experimental import pallas as pl
from jax.experimental.pallas import tpu as pltpu
from jax.sharding import PartitionSpec as P

ITERS = 8
REACH = ITERS + 1
SUB = 8
LANES = 128
HALF = LANES // 2
SIDE = 32
EDGE = 12
EAST = HALF + EDGE
GRANT = 16 * 1024 * 1024

coriolis = 0.7
centre = 8.0
half_width = 8.0


def pairs(count, phase):
    swap = []
    for i in range(phase, count + phase, 2):
        a, b = i % count, (i + 1) % count
        swap += [(a, b), (b, a)]
    return swap


def swap(block, axis, phase):
    return lax.ppermute(block, axis, pairs(lax.axis_size(axis), phase))


def shift(block, axis, step):
    count = lax.axis_size(axis)
    return lax.ppermute(block, axis, [(i, (i + step) % count) for i in range(count)])


def turn(x, lanes):
    return pltpu.roll(x, lanes % LANES, 1) if lanes % LANES else x


def cmul(a, b):
    return (a[0] * b[0] - a[1] * b[1], a[0] * b[1] + a[1] * b[0])


def cinv(a):
    norm = 1.0 / (a[0] * a[0] + a[1] * a[1])
    return (a[0] * norm, -a[1] * norm)


def cscale(a, factor):
    return (a[0] * factor, a[1] * factor)


def pack_columns_kernel(
    state,
    depth,
    real,
    imag,
    weight,
    fields,
    first,
    second,
    scalars,
    real_in,
    imag_in,
    weight_in,
    done,
):
    moves = [
        pltpu.make_async_copy(state, fields.at[pl.ds(0, 3)], done.at[0]),
        pltpu.make_async_copy(depth, fields.at[3], done.at[1]),
        pltpu.make_async_copy(real, real_in, done.at[2]),
        pltpu.make_async_copy(imag, imag_in, done.at[3]),
        pltpu.make_async_copy(weight, weight_in, done.at[4]),
    ]
    for move in moves:
        move.start()
    for move in moves:
        move.wait()
    odd = lax.rem(lax.axis_index("pole"), 2) == 1
    rows, columns = fields.shape[1:]
    lane = lax.broadcasted_iota(jnp.int32, (SUB, LANES), 1)
    sub = lax.broadcasted_iota(jnp.int32, (SUB, LANES), 0)
    poles = real.shape[0]
    values = [real_in[i] for i in range(poles)] + [imag_in[i] for i in range(poles)]
    values += [weight_in[0, i] for i in range(poles)] + [weight_in[1, i] for i in range(poles)]
    spread = []
    for g in range(len(values) // SUB):
        block = jnp.full((SUB, LANES), values[g * SUB], jnp.float32)
        for i in range(1, SUB):
            block = jnp.where(sub == i, values[g * SUB + i], block)
        scalars[pl.ds(g * SUB, SUB)] = block
        spread.append(block)
    for g in range(rows // SUB):
        cut = pl.ds(g * SUB, SUB)
        rest = spread[g] if g < len(spread) else jnp.zeros((SUB, LANES), jnp.float32)
        eastward = rest
        westward = rest
        for f in range(4):
            west = fields[f, cut, 0:LANES]
            east = fields[f, cut, columns - LANES : columns]
            low, high = EDGE * f, EDGE * (f + 1)
            take = jnp.logical_and(lane >= low, lane < high)
            eastward = jnp.where(take, turn(east, low + EDGE), eastward)
            take = jnp.logical_and(lane >= EAST + low, lane < EAST + high)
            westward = jnp.where(take, turn(west, EAST + low), westward)
        first[cut, :] = jnp.where(odd, westward, eastward)
        second[cut, :] = jnp.where(odd, eastward, westward)


def sides_of(first, second, cut):
    odd = lax.rem(lax.axis_index("pole"), 2) == 1
    lane = lax.broadcasted_iota(jnp.int32, (SUB, LANES), 1)
    from_first = jnp.logical_xor(lane >= HALF, odd)
    return jnp.where(from_first, first[cut, :], second[cut, :])


def pack_rows_kernel(fields, second, first, far, near):
    odd = lax.rem(lax.axis_index("tile"), 2) == 1
    rows = fields.shape[1]
    for target, low in ((far, jnp.logical_not(odd)), (near, odd)):
        fill = lambda main, ext: pack_rows(target, fields, second, first, main, ext)
        pl.when(low)(lambda: fill(0, SUB))
        pl.when(jnp.logical_not(low))(lambda: fill(rows - SUB, rows - SUB - 1))


def pack_rows(target, fields, second, first, main, ext):
    sub = lax.broadcasted_iota(jnp.int32, (SUB, LANES), 0)
    lane = lax.broadcasted_iota(jnp.int32, (SUB, LANES), 1)
    tiles = fields.shape[2] // LANES
    for f in range(4):
        for t in range(tiles):
            block = fields[f, main : main + SUB, t * LANES : (t + 1) * LANES]
            target[pl.ds((f * tiles + t) * SUB, SUB)] = block
    for f in (1, 2):
        flux = fields[3, ext : ext + 1, :] * fields[f, ext : ext + 1, :]
        for t in range(tiles):
            at = (4 * SUB + f - 1) * tiles + t
            target[at : at + 1] = flux[:, t * LANES : (t + 1) * LANES]
    side = sides_of(first, second, pl.ds(main, SUB))
    group = ext // SUB * SUB
    line = sides_of(first, second, pl.ds(group, SUB))[ext - group : ext - group + 1]
    line = jnp.broadcast_to(line, (SUB, LANES))
    for f in (1, 2):
        flux = line * turn(line, -(3 - f) * EDGE)
        west = turn(flux, (4 - f) * EDGE)
        east = turn(flux, 5 * EDGE - (EAST + f * EDGE))
        spare = jnp.where(lane < 5 * EDGE, west, east)
        take = jnp.logical_and(lane >= 4 * EDGE, lane < 6 * EDGE)
        side = jnp.where(jnp.logical_and(take, sub == f - 1), spare, side)
    target[pl.ds((4 * SUB + 2) * tiles, SUB)] = side


def pole_sums_kernel(scalars, first, second, others, poly, sums, sol):
    odd = lax.rem(lax.axis_index("pole"), 2) == 1
    count = scalars.shape[0]
    lane = lax.broadcasted_iota(jnp.int32, (SUB, LANES), 1)
    blocks = [[scalars[pl.ds(g, SUB)] for g in range(0, count, SUB)]]
    for i, message in enumerate((first, second)):
        low = jnp.logical_xor(lane < HALF, odd if i == 0 else jnp.logical_not(odd))
        part = []
        for g in range(0, count, SUB):
            x = message[pl.ds(g, SUB), :]
            part.append(jnp.where(low, x, turn(x, HALF)))
        blocks.append(part)
    for i in range(others.shape[0]):
        blocks.append([others[i, pl.ds(g, SUB)] for g in range(0, count, SUB)])
    poles = count // 4
    quantity = []
    for q in range(4):
        cut = []
        for block in blocks:
            whole = jnp.concatenate(block, axis=0)
            cut.append(whole[q * poles : (q + 1) * poles])
        quantity.append(jnp.concatenate(cut, axis=0))
    alpha = (quantity[0], quantity[1])
    beta = (quantity[2], quantity[3])
    square = cmul(alpha, alpha)
    shifted = (square[0] + coriolis * coriolis, square[1])
    sigma = ((shifted[0] + centre) / half_width, shifted[1] / half_width)
    rho = [cinv(sigma)]
    for j in range(1, ITERS):
        rho.append(cinv((2.0 * sigma[0] - rho[-1][0], 2.0 * sigma[1] - rho[-1][1])))
    gain = None
    start = []
    for m in range(ITERS):
        if m == 0:
            start.append(cscale(rho[0], 1.0 / half_width))
        else:
            gain = rho[0] if gain is None else cmul(gain, rho[m - 1])
            start.append(cscale(cmul(rho[m], gain), 2.0 / half_width))
    tail = None
    weight = [None] * ITERS
    for m in reversed(range(ITERS)):
        if tail is None:
            weight[m] = start[m]
            tail = (jnp.ones_like(sigma[0]), jnp.zeros_like(sigma[0]))
        else:
            tail = cmul(cmul(rho[m + 1], rho[m]), tail)
            tail = (tail[0] + 1.0, tail[1])
            weight[m] = cmul(start[m], tail)
    inverse_alpha = cinv(alpha)
    inverse_shift = cinv(shifted)
    by_alpha = cmul(beta, inverse_alpha)
    by_shift = cmul(beta, inverse_shift)
    products = {
        "b": beta,
        "b/a": by_alpha,
        "b/s": by_shift,
        "bs/a": cmul(by_alpha, shifted),
        "ba/s": cmul(by_shift, alpha),
        "b/as": cmul(by_alpha, inverse_shift),
    }

    def total(x):
        s = x[0:SUB]
        for i in range(1, x.shape[0] // SUB):
            s = s + x[i * SUB : (i + 1) * SUB]
        for step in (4, 2, 1):
            s = s + pltpu.roll(s, step, 0)
        return s

    names = [("bs/a", "b", "b/a"), ("b", "ba/s", "b/s"), ("b/a", "b/s", "b/as")]
    factor = (1.0, -1.0, -coriolis)
    found = {}
    for m in range(ITERS):
        for name, w in products.items():
            found[name, m] = total(w[0] * weight[m][0] - w[1] * weight[m][1])
        for g in range(3):
            for f in range(3):
                value = found[names[g][f], m]
                sums[(g * 3 + f) * ITERS + m] = value if f == 0 else factor[f] * value
    sums[9 * ITERS] = total(products["ba/s"][0])
    sums[9 * ITERS + 1] = coriolis * total(products["b/s"][0])

    rows = sol.shape[1] - 2
    span = range(REACH + 1, REACH + rows - 1)
    weighted_sums(poly, sums, sol, {r: range(known(rows, r) + 1) for r in span}, False)


def known(rows, r):
    return min(ITERS - 2, r - (REACH + 1), REACH + rows - 2 - r)


def weighted_sums(poly, sums, sol, terms, more, block=6):
    low = REACH - 1
    order = sorted(terms)
    for i in range(0, len(order), block):
        span = order[i : i + block]
        acc = {}
        if more:
            for r in span:
                if len(terms[r]) < ITERS:
                    for g in range(3):
                        acc[g, r] = sol[g, r - low]
        for f in range(3):
            for m in range(ITERS):
                part = [r for r in span if m in terms[r]]
                if not part:
                    continue
                value = [poly[f, m, r] for r in part]
                for g in range(3):
                    c = sums[(g * 3 + f) * ITERS + m]
                    for r, v in zip(part, value):
                        acc[g, r] = acc[g, r] + c * v if (g, r) in acc else c * v
        for (g, r), v in acc.items():
            sol[g, r - low] = v


def strips_of(tiles, side):
    lane = lax.broadcasted_iota(jnp.int32, (SUB, LANES), 1)
    up = [turn(tile, SIDE) for tile in tiles]
    down = [turn(tile, -SIDE) for tile in tiles]
    out = []
    for q in range(len(tiles)):
        out.append(jnp.where(lane < SIDE, up[q - 1] if q else side, up[q]))
        after = down[q + 1] if q + 1 < len(tiles) else side
        out.append(jnp.where(lane < LANES - SIDE, down[q], after))
    return out


def lay(grid, cut, side, at, stride):
    for s, strip in enumerate(strips_of(cut, side)):
        grid[pl.Slice(at * SUB + s, SUB, stride * SUB), :] = strip


def place(side, f):
    return turn(side, SIDE - EDGE - EDGE * f)


def lay_halo(grid, halo, main, ext):
    lane = lax.broadcasted_iota(jnp.int32, (SUB, LANES), 1)
    sub = lax.broadcasted_iota(jnp.int32, (SUB, LANES), 0)
    tiles = SUB // 2
    side = halo[pl.ds((4 * SUB + 2) * tiles, SUB)]
    for f in range(4):
        cut = [halo[pl.ds((f * tiles + t) * SUB, SUB)] for t in range(tiles)]
        lay(grid, cut, place(side, f), main * 4 + f, 4)
    line = jnp.where(sub < tiles, side[0:1], side[1:2])
    line = jnp.where(lane < HALF, turn(line, SIDE - 5 * EDGE), turn(line, -SIDE - 5 * EDGE))
    side = line
    block = halo[pl.ds(4 * tiles * SUB, SUB)]
    up, down = turn(block, SIDE), turn(block, -SIDE)
    before = jnp.where(sub % tiles == 0, side, pltpu.roll(up, 1, 0))
    after = jnp.where(sub % tiles == tiles - 1, side, pltpu.roll(down, SUB - 1, 0))
    even = jnp.where(lane < SIDE, before, up)
    odd = jnp.where(lane < LANES - SIDE, down, after)
    for f in (1, 2):
        at = (ext * 4 + f) * SUB
        cut = slice((f - 1) * tiles, f * tiles)
        grid[pl.Slice(at, tiles, 2), :] = even[cut]
        grid[pl.Slice(at + 1, tiles, 2), :] = odd[cut]


def cell(grid, f, r):
    return grid[pl.ds(pl.multiple_of((r * 4 + f) * SUB, SUB), SUB), :]


def left(x):
    return pltpu.roll(x, 1, 1)


def right(x):
    return pltpu.roll(x, LANES - 1, 1)


def prepare(grid, poly, coef, start, count):
    flux_east = [None] * 3
    flux_north = [None] * 3
    depths = [None] * 2
    across = None
    for k in range(count + 2):
        r = start + k
        h = cell(grid, 3, r)
        flux_east = flux_east[1:] + [h * cell(grid, 1, r)]
        flux_north = flux_north[1:] + [h * cell(grid, 2, r)]
        depths = depths[1:] + [h]
        if k >= 1:
            before, across = across, 0.125 * (depths[0] + depths[1])
            coef[0, r - 1] = across
        if k >= 2:
            c = r - 1
            north = 0.125 * (depths[0] + right(depths[0]))
            south = 0.125 * (depths[0] + left(depths[0]))
            coef[1, c] = north
            coef[2, c] = south
            coef[3, c] = 2.0 - ((across + before) + (north + south))
            east_slope = flux_east[2] - flux_east[0]
            north_slope = right(flux_north[1]) - left(flux_north[1])
            poly[1, 0, c] = 0.5 * (east_slope + north_slope)
            east_slope = flux_north[2] - flux_north[0]
            north_slope = right(flux_east[1]) - left(flux_east[1])
            poly[2, 0, c] = 0.5 * (east_slope - north_slope)
            poly[0, 0, c] = cell(grid, 0, c)


def sweep(poly, coef, m, start, count):
    back = [poly[f, m, start - 1] for f in range(3)]
    here = [poly[f, m, start] for f in range(3)]
    below = coef[0, start - 1]
    for k in range(count):
        r = start + k
        above, north, south, diag = coef[0, r], coef[1, r], coef[2, r], coef[3, r]
        ahead = [poly[f, m, r + 1] for f in range(3)]
        for f in range(3):
            value = diag * here[f]
            if m > 0:
                value = value - poly[f, m - 1, r]
            value = value + above * ahead[f]
            value = value + below * back[f]
            value = value + north * right(here[f])
            value = value + south * left(here[f])
            poly[f, m + 1, r] = 0.5 * value if m == 0 else value
        back, here, below = here, ahead, above


def inner_kernel(fields, first, second, grid, poly, coef):
    rows = fields.shape[1]
    for g in range(rows // SUB):
        side = sides_of(first, second, pl.ds(g * SUB, SUB))
        for f in range(4):
            cut = [
                fields[f, pl.ds(g * SUB, SUB), pl.ds(t * LANES, LANES)]
                for t in range(fields.shape[2] // LANES)
            ]
            lay(grid, cut, place(side, f), (REACH + g * SUB) * 4 + f, 4)
    prepare(grid, poly, coef, REACH, rows - 2)
    for m in range(ITERS - 1):
        if rows - 4 - 2 * m > 0:
            sweep(poly, coef, m, REACH + 2 + m, rows - 4 - 2 * m)


def outer_kernel(
    far,
    near,
    sums,
    grid_in,
    poly_in,
    coef_in,
    sol_in,
    out,
    grid,
    poly,
    coef,
    sol,
    result,
):
    rows, columns = out.shape[1:]
    odd_tile = lax.rem(lax.axis_index("tile"), 2) == 1
    lane = lax.broadcasted_iota(jnp.int32, (SUB, LANES), 1)
    below = REACH + rows
    for r in (0, below + SUB):
        grid[pl.ds((r * 4 + 3) * SUB, SUB), :] = jnp.ones((SUB, LANES), jnp.float32)
    for halo, above in ((near, odd_tile), (far, jnp.logical_not(odd_tile))):
        main = jnp.where(above, 1, below)
        ext = jnp.where(above, 0, below + SUB)
        lay_halo(grid, halo, main, ext)
    prepare(grid, poly, coef, 0, REACH)
    prepare(grid, poly, coef, below - 2, REACH)
    for m in range(ITERS - 1):
        sweep(poly, coef, m, 2 + m, REACH)
        sweep(poly, coef, m, below - 2 - m, REACH)
    span = range(REACH - 1, REACH + rows + 1)
    terms = {r: range(max(known(rows, r), -1) + 1, ITERS) for r in span}
    weighted_sums(poly, sums, sol, terms, True)
    push = sums[9 * ITERS]
    lift = sums[9 * ITERS + 1]
    for i in range(rows):
        u, v = cell(grid, 1, REACH + i), cell(grid, 2, REACH + i)
        result[0, pl.ds(i * SUB, SUB)] = sol[0, i + 1]
        east = 0.5 * (sol[1, i + 2] - sol[1, i])
        north = 0.5 * (right(sol[2, i + 1]) - left(sol[2, i + 1]))
        result[1, pl.ds(i * SUB, SUB)] = (push * u + lift * v) - (east + coriolis * north)
        east = 0.5 * (sol[2, i + 2] - sol[2, i])
        north = 0.5 * (right(sol[1, i + 1]) - left(sol[1, i + 1]))
        result[2, pl.ds(i * SUB, SUB)] = (push * v - lift * u) + (coriolis * east - north)

    for k in range(3):
        for g in range(rows // SUB):
            for t in range(columns // LANES):
                one = result[k, pl.Slice(g * SUB * SUB + 2 * t, SUB, SUB), :]
                two = result[k, pl.Slice(g * SUB * SUB + 2 * t + 1, SUB, SUB), :]
                joined = jnp.where(lane < HALF, turn(one, -SIDE), turn(two, SIDE))
                out[k, pl.ds(g * SUB, SUB), pl.ds(t * LANES, LANES)] = joined


def shards(state, depth, pole_real, pole_imag, pole_weight):
    rows, columns = depth.shape
    poles = pole_real.shape[0]
    vmem = pl.BlockSpec(memory_space=pltpu.VMEM)
    small = pltpu.CompilerParams(vmem_limit_bytes=GRANT)

    def f32(*shape):
        return jax.ShapeDtypeStruct(shape, jnp.float32)

    given = [
        pltpu.with_memory_space_constraint(x, pltpu.HBM)
        for x in (state, depth, pole_real, pole_imag, pole_weight)
    ]
    hbm = pl.BlockSpec(memory_space=pltpu.HBM)
    message = pltpu.VMEM((rows, LANES), jnp.float32)
    fields, first, second, scalars = pl.pallas_call(
        pack_columns_kernel,
        out_shape=(
            pltpu.VMEM((4, rows, columns), jnp.float32),
            message,
            message,
            pltpu.VMEM((4 * poles, LANES), jnp.float32),
        ),
        in_specs=[hbm] * 5,
        out_specs=(vmem,) * 4,
        scratch_shapes=[
            pltpu.SMEM(pole_real.shape, jnp.float32),
            pltpu.SMEM(pole_imag.shape, jnp.float32),
            pltpu.SMEM(pole_weight.shape, jnp.float32),
            pltpu.SemaphoreType.DMA((5,)),
        ],
        compiler_params=small,
        name="pack_columns",
    )(*given)
    second = swap(second, "pole", 1)
    first = swap(first, "pole", 0)
    halo = f32((4 * SUB + 2) * columns // LANES + SUB, LANES)
    far, near = pl.pallas_call(
        pack_rows_kernel,
        out_shape=(halo, halo),
        in_specs=[vmem] * 3,
        out_specs=(vmem, vmem),
        compiler_params=small,
        name="pack_rows",
    )(fields, second, first)
    far = swap(far, "tile", 1)
    near = swap(near, "tile", 0)
    count = lax.axis_size("pole")
    others = jnp.stack([shift(scalars, "pole", step) for step in range(2, count - 1)])
    height = rows + 2 * REACH
    grid = f32(height * 4 * SUB, LANES)
    poly = f32(3, ITERS, height, SUB, LANES)
    coef = f32(4, height, SUB, LANES)
    sol = f32(3, rows + 2, SUB, LANES)
    held = 4 * SUB * LANES * rows * (4 + 2 * ITERS + 2)
    inner = pl.pallas_call(
        inner_kernel,
        out_shape=(grid, poly, coef),
        in_specs=[vmem] * 3,
        out_specs=(vmem, vmem, vmem),
        compiler_params=small,
        cost_estimate=pl.CostEstimate(
            flops=10 * ITERS * rows * SUB * LANES, bytes_accessed=held, transcendentals=0
        ),
        name="inner",
    )(fields, first, second)
    sums, part = pl.pallas_call(
        pole_sums_kernel,
        out_shape=(f32(9 * ITERS + 2, SUB, LANES), sol),
        in_specs=[vmem] * 5,
        out_specs=(vmem, vmem),
        compiler_params=small,
        name="pole_sums",
    )(scalars, first, second, others, inner[1])
    return pl.pallas_call(
        outer_kernel,
        out_shape=(f32(*state.shape), grid, poly, coef, sol),
        in_specs=[vmem] * 7,
        out_specs=(vmem,) * 5,
        input_output_aliases={3: 1, 4: 2, 5: 3, 6: 4},
        scratch_shapes=[pltpu.VMEM((3, rows * SUB, LANES), jnp.float32)],
        compiler_params=small,
        name="outer",
    )(far, near, sums, *inner, part)[0]


def solution(mesh):
    return jax.shard_map(
        shards,
        mesh=mesh,
        in_specs=(
            P(None, "tile", "pole"),
            P("tile", "pole"),
            P("pole"),
            P("pole"),
            P(None, "pole"),
        ),
        out_specs=P(None, "tile", "pole"),
        check_vma=False,
    )
```

```python
import jax
import jax.numpy as jnp
from jax import lax
from jax.experimental import pallas as pl
from jax.experimental.pallas import tpu as pltpu
from jax.sharding import PartitionSpec as P

ITERS = 8
REACH = ITERS + 1
SUB = 8
LANES = 128
HALF = LANES // 2
SIDE = 32
EDGE = 12
EAST = HALF + EDGE
GRANT = 16 * 1024 * 1024

coriolis = 0.7
centre = 8.0
half_width = 8.0


def pairs(count, phase):
    swap = []
    for i in range(phase, count + phase, 2):
        a, b = i % count, (i + 1) % count
        swap += [(a, b), (b, a)]
    return swap


def swap(block, axis, phase):
    return lax.ppermute(block, axis, pairs(lax.axis_size(axis), phase))


def shift(block, axis, step):
    count = lax.axis_size(axis)
    return lax.ppermute(block, axis, [(i, (i + step) % count) for i in range(count)])


def turn(x, lanes):
    return pltpu.roll(x, lanes % LANES, 1) if lanes % LANES else x


def cmul(a, b):
    return (a[0] * b[0] - a[1] * b[1], a[0] * b[1] + a[1] * b[0])


def cinv(a):
    norm = 1.0 / (a[0] * a[0] + a[1] * a[1])
    return (a[0] * norm, -a[1] * norm)


def cscale(a, factor):
    return (a[0] * factor, a[1] * factor)


def pack_columns_kernel(
    state,
    depth,
    real,
    imag,
    weight,
    fields,
    first,
    second,
    scalars,
    far,
    near,
    real_in,
    imag_in,
    weight_in,
    done,
):
    moves = [
        pltpu.make_async_copy(state, fields.at[pl.ds(0, 3)], done.at[0]),
        pltpu.make_async_copy(depth, fields.at[3], done.at[1]),
        pltpu.make_async_copy(real, real_in, done.at[2]),
        pltpu.make_async_copy(imag, imag_in, done.at[3]),
        pltpu.make_async_copy(weight, weight_in, done.at[4]),
    ]
    for move in moves:
        move.start()
    for move in moves:
        move.wait()
    odd = lax.rem(lax.axis_index("pole"), 2) == 1
    rows, columns = fields.shape[1:]
    lane = lax.broadcasted_iota(jnp.int32, (SUB, LANES), 1)
    sub = lax.broadcasted_iota(jnp.int32, (SUB, LANES), 0)
    poles = real.shape[0]
    values = [real_in[i] for i in range(poles)] + [imag_in[i] for i in range(poles)]
    values += [weight_in[0, i] for i in range(poles)] + [weight_in[1, i] for i in range(poles)]
    spread = []
    for g in range(len(values) // SUB):
        block = jnp.full((SUB, LANES), values[g * SUB], jnp.float32)
        for i in range(1, SUB):
            block = jnp.where(sub == i, values[g * SUB + i], block)
        scalars[pl.ds(g * SUB, SUB)] = block
        spread.append(block)
    for g in range(rows // SUB):
        cut = pl.ds(g * SUB, SUB)
        rest = spread[g] if g < len(spread) else jnp.zeros((SUB, LANES), jnp.float32)
        eastward = rest
        westward = rest
        for f in range(4):
            west = fields[f, cut, 0:LANES]
            east = fields[f, cut, columns - LANES : columns]
            low, high = EDGE * f, EDGE * (f + 1)
            take = jnp.logical_and(lane >= low, lane < high)
            eastward = jnp.where(take, turn(east, low + EDGE), eastward)
            take = jnp.logical_and(lane >= EAST + low, lane < EAST + high)
            westward = jnp.where(take, turn(west, EAST + low), westward)
        first[cut, :] = jnp.where(odd, westward, eastward)
        second[cut, :] = jnp.where(odd, eastward, westward)
    for target, low in towards(far, near):
        pl.when(low)(lambda: pack_rows(target, fields, 0, SUB))
        pl.when(jnp.logical_not(low))(
            lambda: pack_rows(target, fields, rows - SUB, rows - SUB - 1)
        )


def towards(far, near):
    odd = lax.rem(lax.axis_index("tile"), 2) == 1
    return ((far, jnp.logical_not(odd)), (near, odd))


def pack_rows(target, fields, main, ext):
    tiles = fields.shape[2] // LANES
    for f in range(4):
        for t in range(tiles):
            block = fields[f, main : main + SUB, t * LANES : (t + 1) * LANES]
            target[pl.ds((f * tiles + t) * SUB, SUB)] = block
    for f in (1, 2):
        flux = fields[3, ext : ext + 1, :] * fields[f, ext : ext + 1, :]
        for t in range(tiles):
            at = (4 * SUB + f - 1) * tiles + t
            target[at : at + 1] = flux[:, t * LANES : (t + 1) * LANES]


def sides_of(first, second, cut):
    odd = lax.rem(lax.axis_index("pole"), 2) == 1
    lane = lax.broadcasted_iota(jnp.int32, (SUB, LANES), 1)
    from_first = jnp.logical_xor(lane >= HALF, odd)
    return jnp.where(from_first, first[cut, :], second[cut, :])


def pack_sides_kernel(second, first, far_in, far, near_side):
    (_, far_low), (_, near_low) = towards(None, None)
    far[pl.ds(far.shape[0] - SUB, SUB)] = pack_sides(second, first, far_low)
    near_side[...] = pack_sides(second, first, near_low)


def pack_sides(second, first, low):
    rows = first.shape[0]
    sub = lax.broadcasted_iota(jnp.int32, (SUB, LANES), 0)
    lane = lax.broadcasted_iota(jnp.int32, (SUB, LANES), 1)
    side = jnp.where(
        low,
        sides_of(first, second, pl.ds(0, SUB)),
        sides_of(first, second, pl.ds(rows - SUB, SUB)),
    )
    line = jnp.where(
        low,
        sides_of(first, second, pl.ds(SUB, SUB))[0:1],
        sides_of(first, second, pl.ds(rows - 2 * SUB, SUB))[SUB - 1 : SUB],
    )
    line = jnp.broadcast_to(line, (SUB, LANES))
    for f in (1, 2):
        flux = line * turn(line, -(3 - f) * EDGE)
        west = turn(flux, (4 - f) * EDGE)
        east = turn(flux, 5 * EDGE - (EAST + f * EDGE))
        spare = jnp.where(lane < 5 * EDGE, west, east)
        take = jnp.logical_and(lane >= 4 * EDGE, lane < 6 * EDGE)
        side = jnp.where(jnp.logical_and(take, sub == f - 1), spare, side)
    return side


def pole_sums_kernel(scalars, first, second, others, poly, sums, sol):
    odd = lax.rem(lax.axis_index("pole"), 2) == 1
    count = scalars.shape[0]
    lane = lax.broadcasted_iota(jnp.int32, (SUB, LANES), 1)
    blocks = [[scalars[pl.ds(g, SUB)] for g in range(0, count, SUB)]]
    for i, message in enumerate((first, second)):
        low = jnp.logical_xor(lane < HALF, odd if i == 0 else jnp.logical_not(odd))
        part = []
        for g in range(0, count, SUB):
            x = message[pl.ds(g, SUB), :]
            part.append(jnp.where(low, x, turn(x, HALF)))
        blocks.append(part)
    for i in range(others.shape[0]):
        blocks.append([others[i, pl.ds(g, SUB)] for g in range(0, count, SUB)])
    poles = count // 4
    quantity = []
    for q in range(4):
        cut = []
        for block in blocks:
            whole = jnp.concatenate(block, axis=0)
            cut.append(whole[q * poles : (q + 1) * poles])
        quantity.append(jnp.concatenate(cut, axis=0))
    alpha = (quantity[0], quantity[1])
    beta = (quantity[2], quantity[3])
    square = cmul(alpha, alpha)
    shifted = (square[0] + coriolis * coriolis, square[1])
    sigma = ((shifted[0] + centre) / half_width, shifted[1] / half_width)
    rho = [cinv(sigma)]
    for j in range(1, ITERS):
        rho.append(cinv((2.0 * sigma[0] - rho[-1][0], 2.0 * sigma[1] - rho[-1][1])))
    gain = None
    start = []
    for m in range(ITERS):
        if m == 0:
            start.append(cscale(rho[0], 1.0 / half_width))
        else:
            gain = rho[0] if gain is None else cmul(gain, rho[m - 1])
            start.append(cscale(cmul(rho[m], gain), 2.0 / half_width))
    tail = None
    weight = [None] * ITERS
    for m in reversed(range(ITERS)):
        if tail is None:
            weight[m] = start[m]
            tail = (jnp.ones_like(sigma[0]), jnp.zeros_like(sigma[0]))
        else:
            tail = cmul(cmul(rho[m + 1], rho[m]), tail)
            tail = (tail[0] + 1.0, tail[1])
            weight[m] = cmul(start[m], tail)
    inverse_alpha = cinv(alpha)
    inverse_shift = cinv(shifted)
    by_alpha = cmul(beta, inverse_alpha)
    by_shift = cmul(beta, inverse_shift)
    products = {
        "b": beta,
        "b/a": by_alpha,
        "b/s": by_shift,
        "bs/a": cmul(by_alpha, shifted),
        "ba/s": cmul(by_shift, alpha),
        "b/as": cmul(by_alpha, inverse_shift),
    }

    def total(x):
        s = x[0:SUB]
        for i in range(1, x.shape[0] // SUB):
            s = s + x[i * SUB : (i + 1) * SUB]
        for step in (4, 2, 1):
            s = s + pltpu.roll(s, step, 0)
        return s

    names = [("bs/a", "b", "b/a"), ("b", "ba/s", "b/s"), ("b/a", "b/s", "b/as")]
    factor = (1.0, -1.0, -coriolis)
    found = {}
    for m in range(ITERS):
        for name, w in products.items():
            found[name, m] = total(w[0] * weight[m][0] - w[1] * weight[m][1])
        for g in range(3):
            for f in range(3):
                value = found[names[g][f], m]
                sums[(g * 3 + f) * ITERS + m] = value if f == 0 else factor[f] * value
    sums[9 * ITERS] = total(products["ba/s"][0])
    sums[9 * ITERS + 1] = coriolis * total(products["b/s"][0])

    rows = sol.shape[1] - 2
    span = range(REACH + 1, REACH + rows - 1)
    weighted_sums(poly, sums, sol, {r: range(known(rows, r) + 1) for r in span}, False)


def known(rows, r):
    return min(ITERS - 2, r - (REACH + 1), REACH + rows - 2 - r)


def weighted_sums(poly, sums, sol, terms, more, block=6):
    low = REACH - 1
    order = sorted(terms)
    for i in range(0, len(order), block):
        span = order[i : i + block]
        acc = {}
        if more:
            for r in span:
                if len(terms[r]) < ITERS:
                    for g in range(3):
                        acc[g, r] = sol[g, r - low]
        for f in range(3):
            for m in range(ITERS):
                part = [r for r in span if m in terms[r]]
                if not part:
                    continue
                value = [poly[f, m, r] for r in part]
                for g in range(3):
                    c = sums[(g * 3 + f) * ITERS + m]
                    for r, v in zip(part, value):
                        acc[g, r] = acc[g, r] + c * v if (g, r) in acc else c * v
        for (g, r), v in acc.items():
            sol[g, r - low] = v


def strips_of(tiles, side):
    lane = lax.broadcasted_iota(jnp.int32, (SUB, LANES), 1)
    up = [turn(tile, SIDE) for tile in tiles]
    down = [turn(tile, -SIDE) for tile in tiles]
    out = []
    for q in range(len(tiles)):
        out.append(jnp.where(lane < SIDE, up[q - 1] if q else side, up[q]))
        after = down[q + 1] if q + 1 < len(tiles) else side
        out.append(jnp.where(lane < LANES - SIDE, down[q], after))
    return out


def lay(grid, cut, side, at, stride):
    for s, strip in enumerate(strips_of(cut, side)):
        grid[pl.Slice(at * SUB + s, SUB, stride * SUB), :] = strip


def place(side, f):
    return turn(side, SIDE - EDGE - EDGE * f)


def lay_halo(grid, halo, side, main, ext):
    lane = lax.broadcasted_iota(jnp.int32, (SUB, LANES), 1)
    sub = lax.broadcasted_iota(jnp.int32, (SUB, LANES), 0)
    tiles = SUB // 2
    for f in range(4):
        cut = [halo[pl.ds((f * tiles + t) * SUB, SUB)] for t in range(tiles)]
        lay(grid, cut, place(side, f), main * 4 + f, 4)
    line = jnp.where(sub < tiles, side[0:1], side[1:2])
    line = jnp.where(lane < HALF, turn(line, SIDE - 5 * EDGE), turn(line, -SIDE - 5 * EDGE))
    side = line
    block = halo[pl.ds(4 * tiles * SUB, SUB)]
    up, down = turn(block, SIDE), turn(block, -SIDE)
    before = jnp.where(sub % tiles == 0, side, pltpu.roll(up, 1, 0))
    after = jnp.where(sub % tiles == tiles - 1, side, pltpu.roll(down, SUB - 1, 0))
    even = jnp.where(lane < SIDE, before, up)
    odd = jnp.where(lane < LANES - SIDE, down, after)
    for f in (1, 2):
        at = (ext * 4 + f) * SUB
        cut = slice((f - 1) * tiles, f * tiles)
        grid[pl.Slice(at, tiles, 2), :] = even[cut]
        grid[pl.Slice(at + 1, tiles, 2), :] = odd[cut]


def cell(grid, f, r):
    return grid[pl.ds(pl.multiple_of((r * 4 + f) * SUB, SUB), SUB), :]


def left(x):
    return pltpu.roll(x, 1, 1)


def right(x):
    return pltpu.roll(x, LANES - 1, 1)


def prepare(grid, poly, coef, start, count):
    flux_east = [None] * 3
    flux_north = [None] * 3
    depths = [None] * 2
    across = None
    for k in range(count + 2):
        r = start + k
        h = cell(grid, 3, r)
        flux_east = flux_east[1:] + [h * cell(grid, 1, r)]
        flux_north = flux_north[1:] + [h * cell(grid, 2, r)]
        depths = depths[1:] + [h]
        if k >= 1:
            before, across = across, 0.125 * (depths[0] + depths[1])
            coef[0, r - 1] = across
        if k >= 2:
            c = r - 1
            north = 0.125 * (depths[0] + right(depths[0]))
            south = 0.125 * (depths[0] + left(depths[0]))
            coef[1, c] = north
            coef[2, c] = south
            coef[3, c] = 2.0 - ((across + before) + (north + south))
            east_slope = flux_east[2] - flux_east[0]
            north_slope = right(flux_north[1]) - left(flux_north[1])
            poly[1, 0, c] = 0.5 * (east_slope + north_slope)
            east_slope = flux_north[2] - flux_north[0]
            north_slope = right(flux_east[1]) - left(flux_east[1])
            poly[2, 0, c] = 0.5 * (east_slope - north_slope)
            poly[0, 0, c] = cell(grid, 0, c)


def sweep(poly, coef, m, start, count):
    back = [poly[f, m, start - 1] for f in range(3)]
    here = [poly[f, m, start] for f in range(3)]
    below = coef[0, start - 1]
    for k in range(count):
        r = start + k
        above, north, south, diag = coef[0, r], coef[1, r], coef[2, r], coef[3, r]
        ahead = [poly[f, m, r + 1] for f in range(3)]
        for f in range(3):
            value = diag * here[f]
            if m > 0:
                value = value - poly[f, m - 1, r]
            value = value + above * ahead[f]
            value = value + below * back[f]
            value = value + north * right(here[f])
            value = value + south * left(here[f])
            poly[f, m + 1, r] = 0.5 * value if m == 0 else value
        back, here, below = here, ahead, above


def inner_kernel(fields, first, second, grid, poly, coef):
    rows = fields.shape[1]
    for g in range(rows // SUB):
        side = sides_of(first, second, pl.ds(g * SUB, SUB))
        for f in range(4):
            cut = [
                fields[f, pl.ds(g * SUB, SUB), pl.ds(t * LANES, LANES)]
                for t in range(fields.shape[2] // LANES)
            ]
            lay(grid, cut, place(side, f), (REACH + g * SUB) * 4 + f, 4)
    prepare(grid, poly, coef, REACH, rows - 2)
    for m in range(ITERS - 1):
        if rows - 4 - 2 * m > 0:
            sweep(poly, coef, m, REACH + 2 + m, rows - 4 - 2 * m)


def one_side(halo, side, above, sums, grid, poly, coef, sol):
    rows = sol.shape[1] - 2
    below = REACH + rows
    main, ext, start = (1, 0, 0) if above else (below, below + SUB, below - 2)
    grid[pl.ds((ext * 4 + 3) * SUB, SUB), :] = jnp.ones((SUB, LANES), jnp.float32)
    lay_halo(grid, halo, side, main, ext)
    prepare(grid, poly, coef, start, REACH)
    for m in range(ITERS - 1):
        sweep(poly, coef, m, 2 + m if above else below - 2 - m, REACH)
    low = REACH - 1 if above else below - ITERS
    terms = {r: range(max(known(rows, r), -1) + 1, ITERS) for r in range(low, low + REACH)}
    weighted_sums(poly, sums, sol, terms, True)


def both_ways(above, *rest):
    pl.when(above)(lambda: one_side(*rest[:2], True, *rest[2:]))
    pl.when(jnp.logical_not(above))(lambda: one_side(*rest[:2], False, *rest[2:]))


def mid_kernel(near, side, sums, grid_in, poly_in, coef_in, sol_in, grid, poly, coef, sol):
    _, (_, above) = towards(None, None)
    both_ways(above, near, side[...], sums, grid, poly, coef, sol)


def outer_kernel(
    far, sums, grid_in, poly_in, coef_in, sol_in, out, grid, poly, coef, sol, result
):
    rows, columns = out.shape[1:]
    lane = lax.broadcasted_iota(jnp.int32, (SUB, LANES), 1)
    (_, above), _ = towards(None, None)
    side = far[pl.ds(far.shape[0] - SUB, SUB)]
    both_ways(above, far, side, sums, grid, poly, coef, sol)
    push = sums[9 * ITERS]
    lift = sums[9 * ITERS + 1]
    for i in range(rows):
        u, v = cell(grid, 1, REACH + i), cell(grid, 2, REACH + i)
        result[0, pl.ds(i * SUB, SUB)] = sol[0, i + 1]
        east = 0.5 * (sol[1, i + 2] - sol[1, i])
        north = 0.5 * (right(sol[2, i + 1]) - left(sol[2, i + 1]))
        result[1, pl.ds(i * SUB, SUB)] = (push * u + lift * v) - (east + coriolis * north)
        east = 0.5 * (sol[2, i + 2] - sol[2, i])
        north = 0.5 * (right(sol[1, i + 1]) - left(sol[1, i + 1]))
        result[2, pl.ds(i * SUB, SUB)] = (push * v - lift * u) + (coriolis * east - north)

    for k in range(3):
        for g in range(rows // SUB):
            for t in range(columns // LANES):
                one = result[k, pl.Slice(g * SUB * SUB + 2 * t, SUB, SUB), :]
                two = result[k, pl.Slice(g * SUB * SUB + 2 * t + 1, SUB, SUB), :]
                joined = jnp.where(lane < HALF, turn(one, -SIDE), turn(two, SIDE))
                out[k, pl.ds(g * SUB, SUB), pl.ds(t * LANES, LANES)] = joined


def shards(state, depth, pole_real, pole_imag, pole_weight):
    rows, columns = depth.shape
    poles = pole_real.shape[0]
    vmem = pl.BlockSpec(memory_space=pltpu.VMEM)
    small = pltpu.CompilerParams(vmem_limit_bytes=GRANT)

    def f32(*shape):
        return jax.ShapeDtypeStruct(shape, jnp.float32)

    given = [
        pltpu.with_memory_space_constraint(x, pltpu.HBM)
        for x in (state, depth, pole_real, pole_imag, pole_weight)
    ]
    hbm = pl.BlockSpec(memory_space=pltpu.HBM)
    message = pltpu.VMEM((rows, LANES), jnp.float32)
    count = (4 * SUB + 2) * columns // LANES
    fields, first, second, scalars, far, near = pl.pallas_call(
        pack_columns_kernel,
        out_shape=(
            pltpu.VMEM((4, rows, columns), jnp.float32),
            message,
            message,
            pltpu.VMEM((4 * poles, LANES), jnp.float32),
            pltpu.VMEM((count + SUB, LANES), jnp.float32),
            pltpu.VMEM((count, LANES), jnp.float32),
        ),
        in_specs=[hbm] * 5,
        out_specs=(vmem,) * 6,
        scratch_shapes=[
            pltpu.SMEM(pole_real.shape, jnp.float32),
            pltpu.SMEM(pole_imag.shape, jnp.float32),
            pltpu.SMEM(pole_weight.shape, jnp.float32),
            pltpu.SemaphoreType.DMA((5,)),
        ],
        compiler_params=small,
        name="pack_columns",
    )(*given)
    second = swap(second, "pole", 1)
    first = swap(first, "pole", 0)
    far, near_side = pl.pallas_call(
        pack_sides_kernel,
        out_shape=(f32(*far.shape), f32(SUB, LANES)),
        in_specs=[vmem] * 3,
        out_specs=(vmem, vmem),
        input_output_aliases={2: 0},
        compiler_params=small,
        name="pack_sides",
    )(second, first, far)
    far = swap(far, "tile", 1)
    near = swap(near, "tile", 0)
    near_side = swap(near_side, "tile", 0)
    count = lax.axis_size("pole")
    others = jnp.stack([shift(scalars, "pole", step) for step in range(2, count - 1)])
    height = rows + 2 * REACH
    grid = f32(height * 4 * SUB, LANES)
    poly = f32(3, ITERS, height, SUB, LANES)
    coef = f32(4, height, SUB, LANES)
    sol = f32(3, rows + 2, SUB, LANES)
    cost = pl.CostEstimate(
        flops=10 * ITERS * rows * SUB * LANES,
        bytes_accessed=4 * SUB * LANES * rows * (4 + 2 * ITERS + 2),
        transcendentals=0,
    )
    inner = pl.pallas_call(
        inner_kernel,
        out_shape=(grid, poly, coef),
        in_specs=[vmem] * 3,
        out_specs=(vmem, vmem, vmem),
        compiler_params=small,
        cost_estimate=cost,
        name="inner",
    )(fields, first, second)
    sums, part = pl.pallas_call(
        pole_sums_kernel,
        out_shape=(f32(9 * ITERS + 2, SUB, LANES), sol),
        in_specs=[vmem] * 5,
        out_specs=(vmem, vmem),
        compiler_params=small,
        name="pole_sums",
    )(scalars, first, second, others, inner[1])
    held = (*inner, part)
    held = pl.pallas_call(
        mid_kernel,
        out_shape=(grid, poly, coef, sol),
        in_specs=[vmem] * 7,
        out_specs=(vmem,) * 4,
        input_output_aliases={3: 0, 4: 1, 5: 2, 6: 3},
        compiler_params=small,
        cost_estimate=cost,
        name="mid",
    )(near, near_side, sums, *held)
    return pl.pallas_call(
        outer_kernel,
        out_shape=(f32(*state.shape), grid, poly, coef, sol),
        in_specs=[vmem] * 6,
        out_specs=(vmem,) * 5,
        input_output_aliases={2: 1, 3: 2, 4: 3, 5: 4},
        scratch_shapes=[pltpu.VMEM((3, rows * SUB, LANES), jnp.float32)],
        compiler_params=small,
        name="outer",
    )(far, sums, *held)[0]


def solution(mesh):
    return jax.shard_map(
        shards,
        mesh=mesh,
        in_specs=(
            P(None, "tile", "pole"),
            P("tile", "pole"),
            P("pole"),
            P("pole"),
            P(None, "pole"),
        ),
        out_specs=P(None, "tile", "pole"),
        check_vma=False,
    )
```

```python
import jax
import jax.numpy as jnp
from jax import lax
from jax.experimental import pallas as pl
from jax.experimental.pallas import tpu as pltpu
from jax.sharding import PartitionSpec as P

ITERS = 8
REACH = ITERS + 1
SUB = 8
LANES = 128
HALF = LANES // 2
SIDE = 32
EDGE = 12
EAST = HALF + EDGE
GRANT = 16 * 1024 * 1024

coriolis = 0.7
centre = 8.0
half_width = 8.0


def pairs(count, phase):
    swap = []
    for i in range(phase, count + phase, 2):
        a, b = i % count, (i + 1) % count
        swap += [(a, b), (b, a)]
    return swap


def swap(block, axis, phase):
    return lax.ppermute(block, axis, pairs(lax.axis_size(axis), phase))


def shift(block, axis, step):
    count = lax.axis_size(axis)
    return lax.ppermute(block, axis, [(i, (i + step) % count) for i in range(count)])


def turn(x, lanes):
    return pltpu.roll(x, lanes % LANES, 1) if lanes % LANES else x


def cmul(a, b):
    return (a[0] * b[0] - a[1] * b[1], a[0] * b[1] + a[1] * b[0])


def cinv(a):
    norm = 1.0 / (a[0] * a[0] + a[1] * a[1])
    return (a[0] * norm, -a[1] * norm)


def cscale(a, factor):
    return (a[0] * factor, a[1] * factor)


def pack_columns_kernel(
    state,
    depth,
    real,
    imag,
    weight,
    fields,
    first,
    second,
    scalars,
    far,
    near,
    real_in,
    imag_in,
    weight_in,
    done,
):
    moves = [
        pltpu.make_async_copy(state, fields.at[pl.ds(0, 3)], done.at[0]),
        pltpu.make_async_copy(depth, fields.at[3], done.at[1]),
        pltpu.make_async_copy(real, real_in, done.at[2]),
        pltpu.make_async_copy(imag, imag_in, done.at[3]),
        pltpu.make_async_copy(weight, weight_in, done.at[4]),
    ]
    for move in moves:
        move.start()
    for move in moves:
        move.wait()
    odd = lax.rem(lax.axis_index("pole"), 2) == 1
    rows, columns = fields.shape[1:]
    lane = lax.broadcasted_iota(jnp.int32, (SUB, LANES), 1)
    sub = lax.broadcasted_iota(jnp.int32, (SUB, LANES), 0)
    poles = real.shape[0]
    values = [real_in[i] for i in range(poles)] + [imag_in[i] for i in range(poles)]
    values += [weight_in[0, i] for i in range(poles)] + [weight_in[1, i] for i in range(poles)]
    spread = []
    for g in range(len(values) // SUB):
        block = jnp.full((SUB, LANES), values[g * SUB], jnp.float32)
        for i in range(1, SUB):
            block = jnp.where(sub == i, values[g * SUB + i], block)
        scalars[pl.ds(g * SUB, SUB)] = block
        spread.append(block)
    for g in range(rows // SUB):
        cut = pl.ds(g * SUB, SUB)
        rest = spread[g] if g < len(spread) else jnp.zeros((SUB, LANES), jnp.float32)
        eastward = rest
        westward = rest
        for f in range(4):
            west = fields[f, cut, 0:LANES]
            east = fields[f, cut, columns - LANES : columns]
            low, high = EDGE * f, EDGE * (f + 1)
            take = jnp.logical_and(lane >= low, lane < high)
            eastward = jnp.where(take, turn(east, low + EDGE), eastward)
            take = jnp.logical_and(lane >= EAST + low, lane < EAST + high)
            westward = jnp.where(take, turn(west, EAST + low), westward)
        first[cut, :] = jnp.where(odd, westward, eastward)
        second[cut, :] = jnp.where(odd, eastward, westward)
    for target, low in towards(far, near):
        pl.when(low)(lambda: pack_rows(target, fields, 0, SUB))
        pl.when(jnp.logical_not(low))(
            lambda: pack_rows(target, fields, rows - SUB, rows - SUB - 1)
        )


def towards(far, near):
    odd = lax.rem(lax.axis_index("tile"), 2) == 1
    return ((far, jnp.logical_not(odd)), (near, odd))


def pack_rows(target, fields, main, ext):
    tiles = fields.shape[2] // LANES
    for f in range(4):
        for t in range(tiles):
            block = fields[f, main : main + SUB, t * LANES : (t + 1) * LANES]
            target[pl.ds((f * tiles + t) * SUB, SUB)] = block
    for f in (1, 2):
        flux = fields[3, ext : ext + 1, :] * fields[f, ext : ext + 1, :]
        for t in range(tiles):
            at = (4 * SUB + f - 1) * tiles + t
            target[at : at + 1] = flux[:, t * LANES : (t + 1) * LANES]


def sides_of(first, second, cut):
    odd = lax.rem(lax.axis_index("pole"), 2) == 1
    lane = lax.broadcasted_iota(jnp.int32, (SUB, LANES), 1)
    from_first = jnp.logical_xor(lane >= HALF, odd)
    return jnp.where(from_first, first[cut, :], second[cut, :])


def pack_sides_kernel(second, first, far_in, far, near_side):
    (_, far_low), (_, near_low) = towards(None, None)
    far[pl.ds(far.shape[0] - SUB, SUB)] = pack_sides(second, first, far_low)
    near_side[...] = pack_sides(second, first, near_low)


def pack_sides(second, first, low):
    rows = first.shape[0]
    sub = lax.broadcasted_iota(jnp.int32, (SUB, LANES), 0)
    lane = lax.broadcasted_iota(jnp.int32, (SUB, LANES), 1)
    side = jnp.where(
        low,
        sides_of(first, second, pl.ds(0, SUB)),
        sides_of(first, second, pl.ds(rows - SUB, SUB)),
    )
    line = jnp.where(
        low,
        sides_of(first, second, pl.ds(SUB, SUB))[0:1],
        sides_of(first, second, pl.ds(rows - 2 * SUB, SUB))[SUB - 1 : SUB],
    )
    line = jnp.broadcast_to(line, (SUB, LANES))
    for f in (1, 2):
        flux = line * turn(line, -(3 - f) * EDGE)
        west = turn(flux, (4 - f) * EDGE)
        east = turn(flux, 5 * EDGE - (EAST + f * EDGE))
        spare = jnp.where(lane < 5 * EDGE, west, east)
        take = jnp.logical_and(lane >= 4 * EDGE, lane < 6 * EDGE)
        side = jnp.where(jnp.logical_and(take, sub == f - 1), spare, side)
    return side


def pole_sums_kernel(scalars, first, second, others, grid, poly, sums, sol, result):
    odd = lax.rem(lax.axis_index("pole"), 2) == 1
    count = scalars.shape[0]
    lane = lax.broadcasted_iota(jnp.int32, (SUB, LANES), 1)
    blocks = [[scalars[pl.ds(g, SUB)] for g in range(0, count, SUB)]]
    for i, message in enumerate((first, second)):
        low = jnp.logical_xor(lane < HALF, odd if i == 0 else jnp.logical_not(odd))
        part = []
        for g in range(0, count, SUB):
            x = message[pl.ds(g, SUB), :]
            part.append(jnp.where(low, x, turn(x, HALF)))
        blocks.append(part)
    for i in range(others.shape[0]):
        blocks.append([others[i, pl.ds(g, SUB)] for g in range(0, count, SUB)])
    poles = count // 4
    quantity = []
    for q in range(4):
        cut = []
        for block in blocks:
            whole = jnp.concatenate(block, axis=0)
            cut.append(whole[q * poles : (q + 1) * poles])
        quantity.append(jnp.concatenate(cut, axis=0))
    alpha = (quantity[0], quantity[1])
    beta = (quantity[2], quantity[3])
    square = cmul(alpha, alpha)
    shifted = (square[0] + coriolis * coriolis, square[1])
    sigma = ((shifted[0] + centre) / half_width, shifted[1] / half_width)
    rho = [cinv(sigma)]
    for j in range(1, ITERS):
        rho.append(cinv((2.0 * sigma[0] - rho[-1][0], 2.0 * sigma[1] - rho[-1][1])))
    gain = None
    start = []
    for m in range(ITERS):
        if m == 0:
            start.append(cscale(rho[0], 1.0 / half_width))
        else:
            gain = rho[0] if gain is None else cmul(gain, rho[m - 1])
            start.append(cscale(cmul(rho[m], gain), 2.0 / half_width))
    tail = None
    weight = [None] * ITERS
    for m in reversed(range(ITERS)):
        if tail is None:
            weight[m] = start[m]
            tail = (jnp.ones_like(sigma[0]), jnp.zeros_like(sigma[0]))
        else:
            tail = cmul(cmul(rho[m + 1], rho[m]), tail)
            tail = (tail[0] + 1.0, tail[1])
            weight[m] = cmul(start[m], tail)
    inverse_alpha = cinv(alpha)
    inverse_shift = cinv(shifted)
    by_alpha = cmul(beta, inverse_alpha)
    by_shift = cmul(beta, inverse_shift)
    products = {
        "b": beta,
        "b/a": by_alpha,
        "b/s": by_shift,
        "bs/a": cmul(by_alpha, shifted),
        "ba/s": cmul(by_shift, alpha),
        "b/as": cmul(by_alpha, inverse_shift),
    }

    def total(x):
        s = x[0:SUB]
        for i in range(1, x.shape[0] // SUB):
            s = s + x[i * SUB : (i + 1) * SUB]
        for step in (4, 2, 1):
            s = s + pltpu.roll(s, step, 0)
        return s

    names = [("bs/a", "b", "b/a"), ("b", "ba/s", "b/s"), ("b/a", "b/s", "b/as")]
    factor = (1.0, -1.0, -coriolis)
    found = {}
    for m in range(ITERS):
        for name, w in products.items():
            found[name, m] = total(w[0] * weight[m][0] - w[1] * weight[m][1])
        for g in range(3):
            for f in range(3):
                value = found[names[g][f], m]
                sums[(g * 3 + f) * ITERS + m] = value if f == 0 else factor[f] * value
    sums[9 * ITERS] = total(products["ba/s"][0])
    sums[9 * ITERS + 1] = coriolis * total(products["b/s"][0])

    _, (_, above) = towards(None, None)

    def near_rows(above):
        rows = sol.shape[1] - 2
        whole = side_rows(rows, above)
        terms = {r: range(ITERS) for r in whole}
        for r in side_rows(rows, not above):
            if known(rows, r) >= 0:
                terms[r] = range(known(rows, r) + 1)
        weighted_sums(poly, sums, sol, terms, False)
        inside = [r for r in whole if r - 1 in whole and r + 1 in whole]
        finish(grid, sums, sol, result, [r for r in inside if REACH <= r < REACH + rows])

    pl.when(above)(lambda: near_rows(True))
    pl.when(jnp.logical_not(above))(lambda: near_rows(False))


def side_rows(rows, above):
    middle = REACH + rows // 2
    return range(REACH - 1, middle) if above else range(middle, REACH + rows + 1)


def finish(grid, sums, sol, result, span):
    push = sums[9 * ITERS]
    lift = sums[9 * ITERS + 1]
    for r in span:
        i = r - REACH
        u, v = cell(grid, 1, r), cell(grid, 2, r)
        result[0, pl.ds(i * SUB, SUB)] = sol[0, i + 1]
        east = 0.5 * (sol[1, i + 2] - sol[1, i])
        north = 0.5 * (right(sol[2, i + 1]) - left(sol[2, i + 1]))
        result[1, pl.ds(i * SUB, SUB)] = (push * u + lift * v) - (east + coriolis * north)
        east = 0.5 * (sol[2, i + 2] - sol[2, i])
        north = 0.5 * (right(sol[1, i + 1]) - left(sol[1, i + 1]))
        result[2, pl.ds(i * SUB, SUB)] = (push * v - lift * u) + (coriolis * east - north)


def known(rows, r):
    return min(ITERS - 2, r - (REACH + 1), REACH + rows - 2 - r)


def weighted_sums(poly, sums, sol, terms, more, block=6):
    low = REACH - 1
    order = sorted(terms)
    for i in range(0, len(order), block):
        span = order[i : i + block]
        acc = {}
        if more:
            for r in span:
                if len(terms[r]) < ITERS:
                    for g in range(3):
                        acc[g, r] = sol[g, r - low]
        for f in range(3):
            for m in range(ITERS):
                part = [r for r in span if m in terms[r]]
                if not part:
                    continue
                value = [poly[f, m, r] for r in part]
                for g in range(3):
                    c = sums[(g * 3 + f) * ITERS + m]
                    for r, v in zip(part, value):
                        acc[g, r] = acc[g, r] + c * v if (g, r) in acc else c * v
        for (g, r), v in acc.items():
            sol[g, r - low] = v


def strips_of(tiles, side):
    lane = lax.broadcasted_iota(jnp.int32, (SUB, LANES), 1)
    up = [turn(tile, SIDE) for tile in tiles]
    down = [turn(tile, -SIDE) for tile in tiles]
    out = []
    for q in range(len(tiles)):
        out.append(jnp.where(lane < SIDE, up[q - 1] if q else side, up[q]))
        after = down[q + 1] if q + 1 < len(tiles) else side
        out.append(jnp.where(lane < LANES - SIDE, down[q], after))
    return out


def lay(grid, cut, side, at, stride):
    for s, strip in enumerate(strips_of(cut, side)):
        grid[pl.Slice(at * SUB + s, SUB, stride * SUB), :] = strip


def place(side, f):
    return turn(side, SIDE - EDGE - EDGE * f)


def lay_halo(grid, halo, side, main, ext):
    lane = lax.broadcasted_iota(jnp.int32, (SUB, LANES), 1)
    sub = lax.broadcasted_iota(jnp.int32, (SUB, LANES), 0)
    tiles = SUB // 2
    for f in range(4):
        cut = [halo[pl.ds((f * tiles + t) * SUB, SUB)] for t in range(tiles)]
        lay(grid, cut, place(side, f), main * 4 + f, 4)
    line = jnp.where(sub < tiles, side[0:1], side[1:2])
    line = jnp.where(lane < HALF, turn(line, SIDE - 5 * EDGE), turn(line, -SIDE - 5 * EDGE))
    side = line
    block = halo[pl.ds(4 * tiles * SUB, SUB)]
    up, down = turn(block, SIDE), turn(block, -SIDE)
    before = jnp.where(sub % tiles == 0, side, pltpu.roll(up, 1, 0))
    after = jnp.where(sub % tiles == tiles - 1, side, pltpu.roll(down, SUB - 1, 0))
    even = jnp.where(lane < SIDE, before, up)
    odd = jnp.where(lane < LANES - SIDE, down, after)
    for f in (1, 2):
        at = (ext * 4 + f) * SUB
        cut = slice((f - 1) * tiles, f * tiles)
        grid[pl.Slice(at, tiles, 2), :] = even[cut]
        grid[pl.Slice(at + 1, tiles, 2), :] = odd[cut]


def cell(grid, f, r):
    return grid[pl.ds(pl.multiple_of((r * 4 + f) * SUB, SUB), SUB), :]


def left(x):
    return pltpu.roll(x, 1, 1)


def right(x):
    return pltpu.roll(x, LANES - 1, 1)


def prepare(grid, poly, coef, start, count):
    flux_east = [None] * 3
    flux_north = [None] * 3
    depths = [None] * 2
    across = None
    for k in range(count + 2):
        r = start + k
        h = cell(grid, 3, r)
        flux_east = flux_east[1:] + [h * cell(grid, 1, r)]
        flux_north = flux_north[1:] + [h * cell(grid, 2, r)]
        depths = depths[1:] + [h]
        if k >= 1:
            before, across = across, 0.125 * (depths[0] + depths[1])
            coef[0, r - 1] = across
        if k >= 2:
            c = r - 1
            north = 0.125 * (depths[0] + right(depths[0]))
            south = 0.125 * (depths[0] + left(depths[0]))
            coef[1, c] = north
            coef[2, c] = south
            coef[3, c] = 2.0 - ((across + before) + (north + south))
            east_slope = flux_east[2] - flux_east[0]
            north_slope = right(flux_north[1]) - left(flux_north[1])
            poly[1, 0, c] = 0.5 * (east_slope + north_slope)
            east_slope = flux_north[2] - flux_north[0]
            north_slope = right(flux_east[1]) - left(flux_east[1])
            poly[2, 0, c] = 0.5 * (east_slope - north_slope)
            poly[0, 0, c] = cell(grid, 0, c)


def sweep(poly, coef, m, start, count):
    back = [poly[f, m, start - 1] for f in range(3)]
    here = [poly[f, m, start] for f in range(3)]
    below = coef[0, start - 1]
    for k in range(count):
        r = start + k
        above, north, south, diag = coef[0, r], coef[1, r], coef[2, r], coef[3, r]
        ahead = [poly[f, m, r + 1] for f in range(3)]
        for f in range(3):
            value = diag * here[f]
            if m > 0:
                value = value - poly[f, m - 1, r]
            value = value + above * ahead[f]
            value = value + below * back[f]
            value = value + north * right(here[f])
            value = value + south * left(here[f])
            poly[f, m + 1, r] = 0.5 * value if m == 0 else value
        back, here, below = here, ahead, above


def inner_kernel(fields, first, second, grid, poly, coef):
    rows = fields.shape[1]
    for g in range(rows // SUB):
        side = sides_of(first, second, pl.ds(g * SUB, SUB))
        for f in range(4):
            cut = [
                fields[f, pl.ds(g * SUB, SUB), pl.ds(t * LANES, LANES)]
                for t in range(fields.shape[2] // LANES)
            ]
            lay(grid, cut, place(side, f), (REACH + g * SUB) * 4 + f, 4)
    prepare(grid, poly, coef, REACH, rows - 2)
    for m in range(ITERS - 1):
        if rows - 4 - 2 * m > 0:
            sweep(poly, coef, m, REACH + 2 + m, rows - 4 - 2 * m)


def one_side(halo, side, above, height, grid, poly, coef):
    rows = height - 2 * REACH
    below = REACH + rows
    main, ext, start = (1, 0, 0) if above else (below, below + SUB, below - 2)
    grid[pl.ds((ext * 4 + 3) * SUB, SUB), :] = jnp.ones((SUB, LANES), jnp.float32)
    lay_halo(grid, halo, side, main, ext)
    prepare(grid, poly, coef, start, REACH)
    for m in range(ITERS - 1):
        sweep(poly, coef, m, 2 + m if above else below - 2 - m, REACH)


def mid_kernel(near, side, grid_in, poly_in, coef_in, grid, poly, coef):
    _, (_, above) = towards(None, None)
    height = poly.shape[2]
    for way, here in ((True, above), (False, jnp.logical_not(above))):
        pl.when(here)(lambda: one_side(near, side[...], way, height, grid, poly, coef))


def outer_kernel(
    far,
    sums,
    grid_in,
    poly_in,
    coef_in,
    sol_in,
    result_in,
    out,
    grid,
    poly,
    coef,
    sol,
    result,
):
    rows, columns = out.shape[1:]
    lane = lax.broadcasted_iota(jnp.int32, (SUB, LANES), 1)
    (_, above), _ = towards(None, None)

    def far_rows(above):
        side = far[pl.ds(far.shape[0] - SUB, SUB)]
        one_side(far, side, above, poly.shape[2], grid, poly, coef)
        whole = side_rows(rows, above)
        terms = {r: range(max(known(rows, r), -1) + 1, ITERS) for r in whole}
        weighted_sums(poly, sums, sol, terms, True)
        edge = whole.stop if above else whole.start - 1
        finish(grid, sums, sol, result, [r for r in (*whole, edge) if REACH <= r < REACH + rows])

    pl.when(above)(lambda: far_rows(True))
    pl.when(jnp.logical_not(above))(lambda: far_rows(False))

    for k in range(3):
        for g in range(rows // SUB):
            for t in range(columns // LANES):
                one = result[k, pl.Slice(g * SUB * SUB + 2 * t, SUB, SUB), :]
                two = result[k, pl.Slice(g * SUB * SUB + 2 * t + 1, SUB, SUB), :]
                joined = jnp.where(lane < HALF, turn(one, -SIDE), turn(two, SIDE))
                out[k, pl.ds(g * SUB, SUB), pl.ds(t * LANES, LANES)] = joined


def shards(state, depth, pole_real, pole_imag, pole_weight):
    rows, columns = depth.shape
    poles = pole_real.shape[0]
    vmem = pl.BlockSpec(memory_space=pltpu.VMEM)
    small = pltpu.CompilerParams(vmem_limit_bytes=GRANT)

    def f32(*shape):
        return jax.ShapeDtypeStruct(shape, jnp.float32)

    given = [
        pltpu.with_memory_space_constraint(x, pltpu.HBM)
        for x in (state, depth, pole_real, pole_imag, pole_weight)
    ]
    hbm = pl.BlockSpec(memory_space=pltpu.HBM)
    message = pltpu.VMEM((rows, LANES), jnp.float32)
    count = (4 * SUB + 2) * columns // LANES
    fields, first, second, scalars, far, near = pl.pallas_call(
        pack_columns_kernel,
        out_shape=(
            pltpu.VMEM((4, rows, columns), jnp.float32),
            message,
            message,
            pltpu.VMEM((4 * poles, LANES), jnp.float32),
            pltpu.VMEM((count + SUB, LANES), jnp.float32),
            pltpu.VMEM((count, LANES), jnp.float32),
        ),
        in_specs=[hbm] * 5,
        out_specs=(vmem,) * 6,
        scratch_shapes=[
            pltpu.SMEM(pole_real.shape, jnp.float32),
            pltpu.SMEM(pole_imag.shape, jnp.float32),
            pltpu.SMEM(pole_weight.shape, jnp.float32),
            pltpu.SemaphoreType.DMA((5,)),
        ],
        compiler_params=small,
        name="pack_columns",
    )(*given)
    second = swap(second, "pole", 1)
    first = swap(first, "pole", 0)
    far, near_side = pl.pallas_call(
        pack_sides_kernel,
        out_shape=(f32(*far.shape), f32(SUB, LANES)),
        in_specs=[vmem] * 3,
        out_specs=(vmem, vmem),
        input_output_aliases={2: 0},
        compiler_params=small,
        name="pack_sides",
    )(second, first, far)
    far = swap(far, "tile", 1)
    near = swap(near, "tile", 0)
    near_side = swap(near_side, "tile", 0)
    count = lax.axis_size("pole")
    others = jnp.stack([shift(scalars, "pole", step) for step in range(2, count - 1)])
    height = rows + 2 * REACH
    grid = f32(height * 4 * SUB, LANES)
    poly = f32(3, ITERS, height, SUB, LANES)
    coef = f32(4, height, SUB, LANES)
    sol = f32(3, rows + 2, SUB, LANES)
    result = f32(3, rows * SUB, LANES)
    cost = pl.CostEstimate(
        flops=10 * ITERS * rows * SUB * LANES,
        bytes_accessed=4 * SUB * LANES * rows * (4 + 2 * ITERS + 2),
        transcendentals=0,
    )
    inner = pl.pallas_call(
        inner_kernel,
        out_shape=(grid, poly, coef),
        in_specs=[vmem] * 3,
        out_specs=(vmem, vmem, vmem),
        compiler_params=small,
        cost_estimate=cost,
        name="inner",
    )(fields, first, second)
    held = pl.pallas_call(
        mid_kernel,
        out_shape=(grid, poly, coef),
        in_specs=[vmem] * 5,
        out_specs=(vmem,) * 3,
        input_output_aliases={2: 0, 3: 1, 4: 2},
        compiler_params=small,
        cost_estimate=cost,
        name="mid",
    )(near, near_side, *inner)
    sums, *part = pl.pallas_call(
        pole_sums_kernel,
        out_shape=(f32(9 * ITERS + 2, SUB, LANES), sol, result),
        in_specs=[vmem] * 6,
        out_specs=(vmem,) * 3,
        compiler_params=small,
        name="pole_sums",
    )(scalars, first, second, others, *held[:2])
    return pl.pallas_call(
        outer_kernel,
        out_shape=(f32(*state.shape), grid, poly, coef, sol, result),
        in_specs=[vmem] * 7,
        out_specs=(vmem,) * 6,
        input_output_aliases={i: i - 1 for i in range(2, 7)},
        compiler_params=small,
        name="outer",
    )(far, sums, *held, *part)[0]


def solution(mesh):
    return jax.shard_map(
        shards,
        mesh=mesh,
        in_specs=(
            P(None, "tile", "pole"),
            P("tile", "pole"),
            P("pole"),
            P("pole"),
            P(None, "pole"),
        ),
        out_specs=P(None, "tile", "pole"),
        check_vma=False,
    )
```

```python
import jax
import jax.numpy as jnp
from jax import lax
from jax.experimental import pallas as pl
from jax.experimental.pallas import tpu as pltpu
from jax.sharding import PartitionSpec as P

ITERS = 8
REACH = ITERS + 1
SUB = 8
LANES = 128
HALF = LANES // 2
SIDE = 32
EDGE = REACH
EAST = HALF + EDGE
GRANT = 16 * 1024 * 1024

coriolis = 0.7
centre = 8.0
half_width = 8.0


def pairs(count, phase):
    swap = []
    for i in range(phase, count + phase, 2):
        a, b = i % count, (i + 1) % count
        swap += [(a, b), (b, a)]
    return swap


def swap(block, axis, phase):
    return lax.ppermute(block, axis, pairs(lax.axis_size(axis), phase))


def shift(block, axis, step):
    count = lax.axis_size(axis)
    return lax.ppermute(block, axis, [(i, (i + step) % count) for i in range(count)])


def turn(x, lanes):
    return pltpu.roll(x, lanes % LANES, 1) if lanes % LANES else x


def cmul(a, b):
    return (a[0] * b[0] - a[1] * b[1], a[0] * b[1] + a[1] * b[0])


def cinv(a):
    norm = 1.0 / (a[0] * a[0] + a[1] * a[1])
    return (a[0] * norm, -a[1] * norm)


def cscale(a, factor):
    return (a[0] * factor, a[1] * factor)


def pack_columns_kernel(
    state,
    depth,
    real,
    imag,
    weight,
    fields,
    first,
    second,
    scalars,
    far,
    near,
    real_in,
    imag_in,
    weight_in,
    done,
):
    moves = [
        pltpu.make_async_copy(state, fields.at[pl.ds(0, 3)], done.at[0]),
        pltpu.make_async_copy(depth, fields.at[3], done.at[1]),
        pltpu.make_async_copy(real, real_in, done.at[2]),
        pltpu.make_async_copy(imag, imag_in, done.at[3]),
        pltpu.make_async_copy(weight, weight_in, done.at[4]),
    ]
    for move in moves:
        move.start()
    for move in moves:
        move.wait()
    odd = lax.rem(lax.axis_index("pole"), 2) == 1
    rows, columns = fields.shape[1:]
    lane = lax.broadcasted_iota(jnp.int32, (SUB, LANES), 1)
    sub = lax.broadcasted_iota(jnp.int32, (SUB, LANES), 0)
    poles = real.shape[0]
    values = [real_in[i] for i in range(poles)] + [imag_in[i] for i in range(poles)]
    values += [weight_in[0, i] for i in range(poles)] + [weight_in[1, i] for i in range(poles)]
    spread = []
    for g in range(len(values) // SUB):
        block = jnp.full((SUB, LANES), values[g * SUB], jnp.float32)
        for i in range(1, SUB):
            block = jnp.where(sub == i, values[g * SUB + i], block)
        scalars[pl.ds(g * SUB, SUB)] = block
        spread.append(block)
    for g in range(rows // SUB):
        cut = pl.ds(g * SUB, SUB)
        rest = spread[g] if g < len(spread) else jnp.zeros((SUB, LANES), jnp.float32)
        eastward = rest
        westward = rest
        west = [fields[f, cut, 0:LANES] for f in range(4)]
        east = [fields[f, cut, columns - LANES : columns] for f in range(4)]
        west += [west[3] * west[1], west[3] * west[2]]
        east += [east[3] * east[1], east[3] * east[2]]
        for f in range(6):
            low, high = EDGE * f, EDGE * (f + 1)
            take = jnp.logical_and(lane >= low, lane < high)
            eastward = jnp.where(take, turn(east[f], low + EDGE), eastward)
            take = jnp.logical_and(lane >= EAST + low, lane < EAST + high)
            westward = jnp.where(take, turn(west[f], EAST + low), westward)
        first[cut, :] = jnp.where(odd, westward, eastward)
        second[cut, :] = jnp.where(odd, eastward, westward)
    for target, low in towards(far, near):
        pl.when(low)(lambda: pack_rows(target, fields, 0, SUB))
        pl.when(jnp.logical_not(low))(
            lambda: pack_rows(target, fields, rows - SUB, rows - SUB - 1)
        )


def towards(far, near):
    odd = lax.rem(lax.axis_index("tile"), 2) == 1
    return ((far, jnp.logical_not(odd)), (near, odd))


def pack_rows(target, fields, main, ext):
    tiles = fields.shape[2] // LANES
    for f in range(4):
        for t in range(tiles):
            block = fields[f, main : main + SUB, t * LANES : (t + 1) * LANES]
            target[pl.ds((f * tiles + t) * SUB, SUB)] = block
    for f in (1, 2):
        flux = fields[3, ext : ext + 1, :] * fields[f, ext : ext + 1, :]
        for t in range(tiles):
            at = (4 * SUB + f - 1) * tiles + t
            target[at : at + 1] = flux[:, t * LANES : (t + 1) * LANES]


def sides_of(first, second, cut):
    odd = lax.rem(lax.axis_index("pole"), 2) == 1
    lane = lax.broadcasted_iota(jnp.int32, (SUB, LANES), 1)
    from_first = jnp.logical_xor(lane >= HALF, odd)
    return jnp.where(from_first, first[cut, :], second[cut, :])


def pack_sides_kernel(second, first, far_in, far, near_side):
    (_, far_low), (_, near_low) = towards(None, None)
    far[pl.ds(far.shape[0] - SUB, SUB)] = pack_sides(second, first, far_low)
    near_side[...] = pack_sides(second, first, near_low)


def pack_sides(second, first, low):
    rows = first.shape[0]
    sub = lax.broadcasted_iota(jnp.int32, (SUB, LANES), 0)
    lane = lax.broadcasted_iota(jnp.int32, (SUB, LANES), 1)
    side = jnp.where(
        low,
        sides_of(first, second, pl.ds(0, SUB)),
        sides_of(first, second, pl.ds(rows - SUB, SUB)),
    )
    line = jnp.where(
        low,
        sides_of(first, second, pl.ds(SUB, SUB))[0:1],
        sides_of(first, second, pl.ds(rows - 2 * SUB, SUB))[SUB - 1 : SUB],
    )
    line = jnp.broadcast_to(line, (SUB, LANES))
    low, high = 4 * EDGE, 6 * EDGE
    take = jnp.logical_or(
        jnp.logical_and(lane >= low, lane < high),
        jnp.logical_and(lane >= EAST + low, lane < EAST + high),
    )
    side = jnp.where(jnp.logical_and(take, sub == 0), line, side)
    return side


def pole_sums_kernel(scalars, first, second, others, grid, *rest):
    poly, (sums, sol, result) = rest[:ITERS], rest[ITERS:]
    odd = lax.rem(lax.axis_index("pole"), 2) == 1
    count = scalars.shape[0]
    lane = lax.broadcasted_iota(jnp.int32, (SUB, LANES), 1)
    blocks = [[scalars[pl.ds(g, SUB)] for g in range(0, count, SUB)]]
    for i, message in enumerate((first, second)):
        low = jnp.logical_xor(lane < HALF, odd if i == 0 else jnp.logical_not(odd))
        part = []
        for g in range(0, count, SUB):
            x = message[pl.ds(g, SUB), :]
            part.append(jnp.where(low, x, turn(x, HALF)))
        blocks.append(part)
    for i in range(others.shape[0]):
        blocks.append([others[i, pl.ds(g, SUB)] for g in range(0, count, SUB)])
    poles = count // 4
    quantity = []
    for q in range(4):
        cut = []
        for block in blocks:
            whole = jnp.concatenate(block, axis=0)
            cut.append(whole[q * poles : (q + 1) * poles])
        quantity.append(jnp.concatenate(cut, axis=0))
    alpha = (quantity[0], quantity[1])
    beta = (quantity[2], quantity[3])
    square = cmul(alpha, alpha)
    shifted = (square[0] + coriolis * coriolis, square[1])
    sigma = ((shifted[0] + centre) / half_width, shifted[1] / half_width)
    rho = [cinv(sigma)]
    for j in range(1, ITERS):
        rho.append(cinv((2.0 * sigma[0] - rho[-1][0], 2.0 * sigma[1] - rho[-1][1])))
    gain = None
    start = []
    for m in range(ITERS):
        if m == 0:
            start.append(cscale(rho[0], 1.0 / half_width))
        else:
            gain = rho[0] if gain is None else cmul(gain, rho[m - 1])
            start.append(cscale(cmul(rho[m], gain), 2.0 / half_width))
    tail = None
    weight = [None] * ITERS
    for m in reversed(range(ITERS)):
        if tail is None:
            weight[m] = start[m]
            tail = (jnp.ones_like(sigma[0]), jnp.zeros_like(sigma[0]))
        else:
            tail = cmul(cmul(rho[m + 1], rho[m]), tail)
            tail = (tail[0] + 1.0, tail[1])
            weight[m] = cmul(start[m], tail)
    inverse_alpha = cinv(alpha)
    inverse_shift = cinv(shifted)
    by_alpha = cmul(beta, inverse_alpha)
    by_shift = cmul(beta, inverse_shift)
    products = {
        "b": beta,
        "b/a": by_alpha,
        "b/s": by_shift,
        "bs/a": cmul(by_alpha, shifted),
        "ba/s": cmul(by_shift, alpha),
        "b/as": cmul(by_alpha, inverse_shift),
    }

    def total(x):
        s = x[0:SUB]
        for i in range(1, x.shape[0] // SUB):
            s = s + x[i * SUB : (i + 1) * SUB]
        for step in (4, 2, 1):
            s = s + pltpu.roll(s, step, 0)
        return s

    names = [("bs/a", "b", "b/a"), ("b", "ba/s", "b/s"), ("b/a", "b/s", "b/as")]
    factor = (1.0, -1.0, -coriolis)
    found = {}
    for m in range(ITERS):
        for name, w in products.items():
            found[name, m] = total(w[0] * weight[m][0] - w[1] * weight[m][1])
        for g in range(3):
            for f in range(3):
                value = found[names[g][f], m]
                sums[(g * 3 + f) * ITERS + m] = value if f == 0 else factor[f] * value
    sums[9 * ITERS] = total(products["ba/s"][0])
    sums[9 * ITERS + 1] = coriolis * total(products["b/s"][0])

    _, (_, above) = towards(None, None)
    rows = sol.shape[1] - 2
    near = side_rows(rows, above)
    weighted_sums(poly, sums, sol, near, {k: range(ITERS) for k in range(len(near))}, False)
    far = side_rows(rows, jnp.logical_not(above))
    some = {k: range(known(k) + 1) for k in range(len(far)) if known(k) >= 0}
    weighted_sums(poly, sums, sol, far, some, False)
    low = REACH + jnp.where(above, 0, rows // 2 + 1)
    finish(grid, sums, sol, result, low, rows // 2 - 1)


def side_rows(rows, above):
    low, high = REACH - 1, REACH + rows
    return [jnp.where(above, low + k, high - k) for k in range(rows // 2 + 1)]


def known(k):
    return max(min(ITERS - 2, k - 2), -1)


def weighted_sums(poly, sums, sol, rows, terms, more, block=6):
    low = REACH - 1
    order = sorted(terms)
    for i in range(0, len(order), block):
        span = order[i : i + block]
        acc = {}
        if more:
            for k in span:
                if len(terms[k]) < ITERS:
                    for g in range(3):
                        acc[g, k] = sol[g, rows[k] - low]
        for f in range(3):
            for m in range(ITERS):
                part = [k for k in span if m in terms[k]]
                if not part:
                    continue
                value = [poly[m][f, rows[k]] for k in part]
                for g in range(3):
                    c = sums[(g * 3 + f) * ITERS + m]
                    for k, v in zip(part, value):
                        acc[g, k] = acc[g, k] + c * v if (g, k) in acc else c * v
        for (g, k), v in acc.items():
            sol[g, rows[k] - low] = v


def finish(grid, sums, sol, result, low, count):
    push = sums[9 * ITERS]
    lift = sums[9 * ITERS + 1]
    for k in range(count):
        i = low - REACH + k
        u, v = cell(grid, 1, low + k), cell(grid, 2, low + k)
        at = pl.ds(pl.multiple_of(i * SUB, SUB), SUB)
        result[0, at] = sol[0, i + 1]
        east = 0.5 * (sol[1, i + 2] - sol[1, i])
        north = 0.5 * (right(sol[2, i + 1]) - left(sol[2, i + 1]))
        result[1, at] = (push * u + lift * v) - (east + coriolis * north)
        east = 0.5 * (sol[2, i + 2] - sol[2, i])
        north = 0.5 * (right(sol[1, i + 1]) - left(sol[1, i + 1]))
        result[2, at] = (push * v - lift * u) + (coriolis * east - north)


def strips_of(tiles, side):
    lane = lax.broadcasted_iota(jnp.int32, (SUB, LANES), 1)
    up = [turn(tile, SIDE) for tile in tiles]
    down = [turn(tile, -SIDE) for tile in tiles]
    out = []
    for q in range(len(tiles)):
        out.append(jnp.where(lane < SIDE, up[q - 1] if q else side, up[q]))
        after = down[q + 1] if q + 1 < len(tiles) else side
        out.append(jnp.where(lane < LANES - SIDE, down[q], after))
    return out


def lay(grid, cut, side, at, stride):
    for s, strip in enumerate(strips_of(cut, side)):
        grid[pl.Slice(at * SUB + s, SUB, stride * SUB), :] = strip


def place(side, f):
    return turn(side, SIDE - EDGE - EDGE * f)


def lay_halo(grid, halo, side, main, ext):
    lane = lax.broadcasted_iota(jnp.int32, (SUB, LANES), 1)
    sub = lax.broadcasted_iota(jnp.int32, (SUB, LANES), 0)
    tiles = SUB // 2
    for f in range(4):
        cut = [halo[pl.ds((f * tiles + t) * SUB, SUB)] for t in range(tiles)]
        lay(grid, cut, place(side, f), main * 4 + f, 4)
    line = jnp.broadcast_to(side[0:1], (SUB, LANES))
    side = jnp.where(sub < tiles, place(line, 4), place(line, 5))
    block = halo[pl.ds(4 * tiles * SUB, SUB)]
    up, down = turn(block, SIDE), turn(block, -SIDE)
    before = jnp.where(sub % tiles == 0, side, pltpu.roll(up, 1, 0))
    after = jnp.where(sub % tiles == tiles - 1, side, pltpu.roll(down, SUB - 1, 0))
    even = jnp.where(lane < SIDE, before, up)
    odd = jnp.where(lane < LANES - SIDE, down, after)
    for f in (1, 2):
        at = (ext * 4 + f) * SUB
        cut = slice((f - 1) * tiles, f * tiles)
        grid[pl.Slice(at, tiles, 2), :] = even[cut]
        grid[pl.Slice(at + 1, tiles, 2), :] = odd[cut]


def cell(grid, f, r):
    return grid[pl.ds(pl.multiple_of((r * 4 + f) * SUB, SUB), SUB), :]


def left(x):
    return pltpu.roll(x, 1, 1)


def right(x):
    return pltpu.roll(x, LANES - 1, 1)


def prepare(grid, poly, coef, start, count):
    flux_east = [None] * 3
    flux_north = [None] * 3
    depths = [None] * 2
    across = None
    for k in range(count + 2):
        r = start + k
        h = cell(grid, 3, r)
        flux_east = flux_east[1:] + [h * cell(grid, 1, r)]
        flux_north = flux_north[1:] + [h * cell(grid, 2, r)]
        depths = depths[1:] + [h]
        if k >= 1:
            before, across = across, 0.125 * (depths[0] + depths[1])
            coef[0, r - 1] = across
        if k >= 2:
            c = r - 1
            north = 0.125 * (depths[0] + right(depths[0]))
            south = 0.125 * (depths[0] + left(depths[0]))
            coef[1, c] = north
            coef[2, c] = south
            coef[3, c] = 2.0 - ((across + before) + (north + south))
            east_slope = flux_east[2] - flux_east[0]
            north_slope = right(flux_north[1]) - left(flux_north[1])
            poly[0][1, c] = 0.5 * (east_slope + north_slope)
            east_slope = flux_north[2] - flux_north[0]
            north_slope = right(flux_east[1]) - left(flux_east[1])
            poly[0][2, c] = 0.5 * (east_slope - north_slope)
            poly[0][0, c] = cell(grid, 0, c)


def sweep(poly, coef, m, start, count):
    back = [poly[m][f, start - 1] for f in range(3)]
    here = [poly[m][f, start] for f in range(3)]
    below = coef[0, start - 1]
    for k in range(count):
        r = start + k
        above, north, south, diag = coef[0, r], coef[1, r], coef[2, r], coef[3, r]
        ahead = [poly[m][f, r + 1] for f in range(3)]
        for f in range(3):
            value = diag * here[f]
            if m > 0:
                value = value - poly[m - 1][f, r]
            value = value + above * ahead[f]
            value = value + below * back[f]
            value = value + north * right(here[f])
            value = value + south * left(here[f])
            poly[m + 1][f, r] = 0.5 * value if m == 0 else value
        back, here, below = here, ahead, above


def inner_kernel(fields, first, second, grid, coef, *poly):
    rows = fields.shape[1]
    for g in range(rows // SUB):
        side = sides_of(first, second, pl.ds(g * SUB, SUB))
        for f in range(4):
            cut = [
                fields[f, pl.ds(g * SUB, SUB), pl.ds(t * LANES, LANES)]
                for t in range(fields.shape[2] // LANES)
            ]
            lay(grid, cut, place(side, f), (REACH + g * SUB) * 4 + f, 4)
    prepare(grid, poly, coef, REACH, rows - 2)
    for m in range(ITERS - 1):
        if rows - 4 - 2 * m > 0:
            sweep(poly, coef, m, REACH + 2 + m, rows - 4 - 2 * m)


def one_side(halo, side, above, grid, coef, poly):
    height = coef.shape[1]
    below = height - REACH
    main = jnp.where(above, 1, below)
    ext = jnp.where(above, 0, below + SUB)
    start = jnp.where(above, 0, below - 2)
    at = pl.multiple_of((ext * 4 + 3) * SUB, SUB)
    grid[pl.ds(at, SUB), :] = jnp.ones((SUB, LANES), jnp.float32)
    lay_halo(grid, halo, side, main, ext)
    prepare(grid, poly, coef, start, REACH)
    for m in range(ITERS - 1):
        sweep(poly, coef, m, jnp.where(above, 2 + m, below - 2 - m), REACH)


def mid_kernel(near, side, *rest):
    grid, coef, *poly = rest[len(rest) // 2 :]
    _, (_, above) = towards(None, None)
    one_side(near, side[...], above, grid, coef, poly)


def outer_kernel(far, sums, *rest):
    out, grid, coef, sol, result, *poly = rest[len(rest) // 2 :]
    rows, columns = out.shape[1:]
    lane = lax.broadcasted_iota(jnp.int32, (SUB, LANES), 1)
    (_, above), _ = towards(None, None)
    side = far[pl.ds(far.shape[0] - SUB, SUB)]
    one_side(far, side, above, grid, coef, poly)
    whole = side_rows(rows, above)
    terms = {k: range(known(k) + 1, ITERS) for k in range(len(whole))}
    weighted_sums(poly, sums, sol, whole, terms, True)
    low = REACH + jnp.where(above, 0, rows // 2 - 1)
    finish(grid, sums, sol, result, low, rows // 2 + 1)

    for k in range(3):
        for g in range(rows // SUB):
            for t in range(columns // LANES):
                one = result[k, pl.Slice(g * SUB * SUB + 2 * t, SUB, SUB), :]
                two = result[k, pl.Slice(g * SUB * SUB + 2 * t + 1, SUB, SUB), :]
                joined = jnp.where(lane < HALF, turn(one, -SIDE), turn(two, SIDE))
                out[k, pl.ds(g * SUB, SUB), pl.ds(t * LANES, LANES)] = joined


def shards(state, depth, pole_real, pole_imag, pole_weight):
    rows, columns = depth.shape
    poles = pole_real.shape[0]
    vmem = pl.BlockSpec(memory_space=pltpu.VMEM)
    small = pltpu.CompilerParams(vmem_limit_bytes=GRANT)

    def f32(*shape):
        return jax.ShapeDtypeStruct(shape, jnp.float32)

    given = [
        pltpu.with_memory_space_constraint(x, pltpu.HBM)
        for x in (state, depth, pole_real, pole_imag, pole_weight)
    ]
    hbm = pl.BlockSpec(memory_space=pltpu.HBM)
    message = pltpu.VMEM((rows, LANES), jnp.float32)
    count = (4 * SUB + 2) * columns // LANES
    fields, first, second, scalars, far, near = pl.pallas_call(
        pack_columns_kernel,
        out_shape=(
            pltpu.VMEM((4, rows, columns), jnp.float32),
            message,
            message,
            pltpu.VMEM((4 * poles, LANES), jnp.float32),
            pltpu.VMEM((count + SUB, LANES), jnp.float32),
            pltpu.VMEM((count, LANES), jnp.float32),
        ),
        in_specs=[hbm] * 5,
        out_specs=(vmem,) * 6,
        scratch_shapes=[
            pltpu.SMEM(pole_real.shape, jnp.float32),
            pltpu.SMEM(pole_imag.shape, jnp.float32),
            pltpu.SMEM(pole_weight.shape, jnp.float32),
            pltpu.SemaphoreType.DMA((5,)),
        ],
        compiler_params=small,
        name="pack_columns",
    )(*given)
    second = swap(second, "pole", 1)
    first = swap(first, "pole", 0)
    far, near_side = pl.pallas_call(
        pack_sides_kernel,
        out_shape=(f32(*far.shape), f32(SUB, LANES)),
        in_specs=[vmem] * 3,
        out_specs=(vmem, vmem),
        input_output_aliases={2: 0},
        compiler_params=small,
        name="pack_sides",
    )(second, first, far)
    far = swap(far, "tile", 1)
    near = swap(near, "tile", 0)
    near_side = swap(near_side, "tile", 0)
    count = lax.axis_size("pole")
    others = jnp.stack([shift(scalars, "pole", step) for step in range(2, count - 1)])
    height = rows + 2 * REACH
    grid = f32(height * 4 * SUB, LANES)
    poly = [f32(3, height, SUB, LANES)] * ITERS
    coef = f32(4, height, SUB, LANES)
    sol = f32(3, rows + 2, SUB, LANES)
    result = f32(3, rows * SUB, LANES)
    state_of = (grid, coef, *poly)
    cost = pl.CostEstimate(
        flops=10 * ITERS * rows * SUB * LANES,
        bytes_accessed=4 * SUB * LANES * rows * (4 + 2 * ITERS + 2),
        transcendentals=0,
    )
    held = pl.pallas_call(
        inner_kernel,
        out_shape=state_of,
        in_specs=[vmem] * 3,
        out_specs=(vmem,) * len(state_of),
        compiler_params=small,
        cost_estimate=cost,
        name="inner",
    )(fields, first, second)
    held = pl.pallas_call(
        mid_kernel,
        out_shape=state_of,
        in_specs=[vmem] * (2 + len(state_of)),
        out_specs=(vmem,) * len(state_of),
        input_output_aliases={2 + i: i for i in range(len(state_of))},
        compiler_params=small,
        cost_estimate=cost,
        name="mid",
    )(near, near_side, *held)
    grid_held, coef_held, *poly_held = held
    sums, *part = pl.pallas_call(
        pole_sums_kernel,
        out_shape=(f32(9 * ITERS + 2, SUB, LANES), sol, result),
        in_specs=[vmem] * (5 + ITERS),
        out_specs=(vmem,) * 3,
        compiler_params=small,
        name="pole_sums",
    )(scalars, first, second, others, grid_held, *poly_held)
    kept = (grid, coef, sol, result, *poly)
    return pl.pallas_call(
        outer_kernel,
        out_shape=(f32(*state.shape), *kept),
        in_specs=[vmem] * (2 + len(kept)),
        out_specs=(vmem,) * (1 + len(kept)),
        input_output_aliases={2 + i: 1 + i for i in range(len(kept))},
        compiler_params=small,
        name="outer",
    )(far, sums, grid_held, coef_held, *part, *poly_held)[0]


def solution(mesh):
    return jax.shard_map(
        shards,
        mesh=mesh,
        in_specs=(
            P(None, "tile", "pole"),
            P("tile", "pole"),
            P("pole"),
            P("pole"),
            P(None, "pole"),
        ),
        out_specs=P(None, "tile", "pole"),
        check_vma=False,
    )
```

```python
import jax
import jax.numpy as jnp
from jax import lax
from jax.experimental import pallas as pl
from jax.experimental.pallas import tpu as pltpu
from jax.sharding import PartitionSpec as P

ITERS = 8
REACH = ITERS + 1
SUB = 8
LANES = 128
HALF = LANES // 2
SIDE = 32
EDGE = REACH
EAST = HALF + EDGE
GRANT = 16 * 1024 * 1024

coriolis = 0.7
centre = 8.0
half_width = 8.0


def pairs(count, phase):
    swap = []
    for i in range(phase, count + phase, 2):
        a, b = i % count, (i + 1) % count
        swap += [(a, b), (b, a)]
    return swap


def swap(block, axis, phase):
    return lax.ppermute(block, axis, pairs(lax.axis_size(axis), phase))


def shift(block, axis, step):
    count = lax.axis_size(axis)
    return lax.ppermute(block, axis, [(i, (i + step) % count) for i in range(count)])


def turn(x, lanes):
    return pltpu.roll(x, lanes % LANES, 1) if lanes % LANES else x


def cmul(a, b):
    return (a[0] * b[0] - a[1] * b[1], a[0] * b[1] + a[1] * b[0])


def cinv(a):
    norm = 1.0 / (a[0] * a[0] + a[1] * a[1])
    return (a[0] * norm, -a[1] * norm)


def cscale(a, factor):
    return (a[0] * factor, a[1] * factor)


def all_at_once(*pairs_of):
    moves = [pltpu.make_async_copy(*pair) for pair in pairs_of]
    for move in moves:
        move.start()
    for move in moves:
        move.wait()


def pack_columns_kernel(
    state,
    depth,
    real,
    imag,
    weight,
    first,
    second,
    scalars,
    edges,
    real_in,
    imag_in,
    weight_in,
    done,
):
    rows, columns = depth.shape
    west_tile, east_tile = pl.ds(0, LANES), pl.ds(columns - LANES, LANES)
    all_at_once(
        (state.at[:, :, west_tile], edges.at[0, pl.ds(0, 3)], done.at[0]),
        (depth.at[:, west_tile], edges.at[0, 3], done.at[1]),
        (state.at[:, :, east_tile], edges.at[1, pl.ds(0, 3)], done.at[2]),
        (depth.at[:, east_tile], edges.at[1, 3], done.at[3]),
        (real, real_in, done.at[4]),
        (imag, imag_in, done.at[5]),
        (weight, weight_in, done.at[6]),
    )
    odd = lax.rem(lax.axis_index("pole"), 2) == 1
    lane = lax.broadcasted_iota(jnp.int32, (SUB, LANES), 1)
    sub = lax.broadcasted_iota(jnp.int32, (SUB, LANES), 0)
    poles = real.shape[0]
    values = [real_in[i] for i in range(poles)] + [imag_in[i] for i in range(poles)]
    values += [weight_in[0, i] for i in range(poles)] + [weight_in[1, i] for i in range(poles)]
    spread = []
    for g in range(len(values) // SUB):
        block = jnp.full((SUB, LANES), values[g * SUB], jnp.float32)
        for i in range(1, SUB):
            block = jnp.where(sub == i, values[g * SUB + i], block)
        scalars[pl.ds(g * SUB, SUB)] = block
        spread.append(block)
    for g in range(rows // SUB):
        cut = pl.ds(g * SUB, SUB)
        rest = spread[g] if g < len(spread) else jnp.zeros((SUB, LANES), jnp.float32)
        eastward = rest
        westward = rest
        west = [edges[0, f, cut] for f in range(4)]
        east = [edges[1, f, cut] for f in range(4)]
        west += [west[3] * west[1], west[3] * west[2]]
        east += [east[3] * east[1], east[3] * east[2]]
        for f in range(6):
            low, high = EDGE * f, EDGE * (f + 1)
            take = jnp.logical_and(lane >= low, lane < high)
            eastward = jnp.where(take, turn(east[f], low + EDGE), eastward)
            take = jnp.logical_and(lane >= EAST + low, lane < EAST + high)
            westward = jnp.where(take, turn(west[f], EAST + low), westward)
        first[cut, :] = jnp.where(odd, westward, eastward)
        second[cut, :] = jnp.where(odd, eastward, westward)


def load_fields_kernel(state, depth, fields, far, near, done):
    rows = depth.shape[0]
    all_at_once(
        (state, fields.at[pl.ds(0, 3)], done.at[0]),
        (depth, fields.at[3], done.at[1]),
    )
    for target, low in towards(far, near):
        pl.when(low)(lambda: pack_rows(target, fields, 0, SUB))
        pl.when(jnp.logical_not(low))(
            lambda: pack_rows(target, fields, rows - SUB, rows - SUB - 1)
        )


def towards(far, near):
    odd = lax.rem(lax.axis_index("tile"), 2) == 1
    return ((far, jnp.logical_not(odd)), (near, odd))


def pack_rows(target, fields, main, ext):
    tiles = fields.shape[2] // LANES
    for f in range(4):
        for t in range(tiles):
            block = fields[f, main : main + SUB, t * LANES : (t + 1) * LANES]
            target[pl.ds((f * tiles + t) * SUB, SUB)] = block
    for f in (1, 2):
        flux = fields[3, ext : ext + 1, :] * fields[f, ext : ext + 1, :]
        for t in range(tiles):
            at = (4 * SUB + f - 1) * tiles + t
            target[at : at + 1] = flux[:, t * LANES : (t + 1) * LANES]


def sides_of(first, second, cut):
    odd = lax.rem(lax.axis_index("pole"), 2) == 1
    lane = lax.broadcasted_iota(jnp.int32, (SUB, LANES), 1)
    from_first = jnp.logical_xor(lane >= HALF, odd)
    return jnp.where(from_first, first[cut, :], second[cut, :])


def pack_sides_kernel(second, first, far_in, far, near_side):
    (_, far_low), (_, near_low) = towards(None, None)
    far[pl.ds(far.shape[0] - SUB, SUB)] = pack_sides(second, first, far_low)
    near_side[...] = pack_sides(second, first, near_low)


def pack_sides(second, first, low):
    rows = first.shape[0]
    sub = lax.broadcasted_iota(jnp.int32, (SUB, LANES), 0)
    lane = lax.broadcasted_iota(jnp.int32, (SUB, LANES), 1)
    side = jnp.where(
        low,
        sides_of(first, second, pl.ds(0, SUB)),
        sides_of(first, second, pl.ds(rows - SUB, SUB)),
    )
    line = jnp.where(
        low,
        sides_of(first, second, pl.ds(SUB, SUB))[0:1],
        sides_of(first, second, pl.ds(rows - 2 * SUB, SUB))[SUB - 1 : SUB],
    )
    line = jnp.broadcast_to(line, (SUB, LANES))
    low, high = 4 * EDGE, 6 * EDGE
    take = jnp.logical_or(
        jnp.logical_and(lane >= low, lane < high),
        jnp.logical_and(lane >= EAST + low, lane < EAST + high),
    )
    side = jnp.where(jnp.logical_and(take, sub == 0), line, side)
    return side


def pole_sums_kernel(scalars, first, second, others, grid, *rest):
    poly, (sums, sol, result) = rest[:ITERS], rest[ITERS:]
    odd = lax.rem(lax.axis_index("pole"), 2) == 1
    count = scalars.shape[0]
    lane = lax.broadcasted_iota(jnp.int32, (SUB, LANES), 1)
    blocks = [[scalars[pl.ds(g, SUB)] for g in range(0, count, SUB)]]
    for i, message in enumerate((first, second)):
        low = jnp.logical_xor(lane < HALF, odd if i == 0 else jnp.logical_not(odd))
        part = []
        for g in range(0, count, SUB):
            x = message[pl.ds(g, SUB), :]
            part.append(jnp.where(low, x, turn(x, HALF)))
        blocks.append(part)
    for i in range(others.shape[0]):
        blocks.append([others[i, pl.ds(g, SUB)] for g in range(0, count, SUB)])
    poles = count // 4
    quantity = []
    for q in range(4):
        cut = []
        for block in blocks:
            whole = jnp.concatenate(block, axis=0)
            cut.append(whole[q * poles : (q + 1) * poles])
        quantity.append(jnp.concatenate(cut, axis=0))
    alpha = (quantity[0], quantity[1])
    beta = (quantity[2], quantity[3])
    square = cmul(alpha, alpha)
    shifted = (square[0] + coriolis * coriolis, square[1])
    sigma = ((shifted[0] + centre) / half_width, shifted[1] / half_width)
    rho = [cinv(sigma)]
    for j in range(1, ITERS):
        rho.append(cinv((2.0 * sigma[0] - rho[-1][0], 2.0 * sigma[1] - rho[-1][1])))
    gain = None
    start = []
    for m in range(ITERS):
        if m == 0:
            start.append(cscale(rho[0], 1.0 / half_width))
        else:
            gain = rho[0] if gain is None else cmul(gain, rho[m - 1])
            start.append(cscale(cmul(rho[m], gain), 2.0 / half_width))
    tail = None
    weight = [None] * ITERS
    for m in reversed(range(ITERS)):
        if tail is None:
            weight[m] = start[m]
            tail = (jnp.ones_like(sigma[0]), jnp.zeros_like(sigma[0]))
        else:
            tail = cmul(cmul(rho[m + 1], rho[m]), tail)
            tail = (tail[0] + 1.0, tail[1])
            weight[m] = cmul(start[m], tail)
    inverse_alpha = cinv(alpha)
    inverse_shift = cinv(shifted)
    by_alpha = cmul(beta, inverse_alpha)
    by_shift = cmul(beta, inverse_shift)
    products = {
        "b": beta,
        "b/a": by_alpha,
        "b/s": by_shift,
        "bs/a": cmul(by_alpha, shifted),
        "ba/s": cmul(by_shift, alpha),
        "b/as": cmul(by_alpha, inverse_shift),
    }

    def total(x):
        s = x[0:SUB]
        for i in range(1, x.shape[0] // SUB):
            s = s + x[i * SUB : (i + 1) * SUB]
        for step in (4, 2, 1):
            s = s + pltpu.roll(s, step, 0)
        return s

    names = [("bs/a", "b", "b/a"), ("b", "ba/s", "b/s"), ("b/a", "b/s", "b/as")]
    factor = (1.0, -1.0, -coriolis)
    found = {}
    for m in range(ITERS):
        for name, w in products.items():
            found[name, m] = total(w[0] * weight[m][0] - w[1] * weight[m][1])
        for g in range(3):
            for f in range(3):
                value = found[names[g][f], m]
                sums[(g * 3 + f) * ITERS + m] = value if f == 0 else factor[f] * value
    sums[9 * ITERS] = total(products["ba/s"][0])
    sums[9 * ITERS + 1] = coriolis * total(products["b/s"][0])

    _, (_, above) = towards(None, None)
    rows = sol.shape[1] - 2

    def near_rows(above):
        near, far = side_rows(rows, above), side_rows(rows, not above)
        acc = {}
        for m in range(ITERS):
            add(acc, sums, poly, m, near)
        for m in range(ITERS - 1):
            add(acc, sums, poly, m, [r for k, r in enumerate(far) if known(k) >= m])
        for (g, r), v in acc.items():
            sol[g, r - (REACH - 1)] = v
        inside = sorted(near)[1:-1]
        finish(grid, sums, result, acc, [r for r in inside if REACH <= r < REACH + rows])

    pl.when(above)(lambda: near_rows(True))
    pl.when(jnp.logical_not(above))(lambda: near_rows(False))


def side_rows(rows, above):
    low, high = REACH - 1, REACH + rows
    return [low + k if above else high - k for k in range(rows // 2 + 1)]


def known(k):
    return max(min(ITERS - 2, k - 2), -1)


def add(acc, sums, poly, m, rows, values=None):
    for f in range(3):
        if not rows:
            return
        value = {r: poly[m][f, r] if values is None else values[f, r] for r in rows}
        for g in range(3):
            c = sums[(g * 3 + f) * ITERS + m]
            for r in rows:
                acc[g, r] = acc[g, r] + c * value[r] if (g, r) in acc else c * value[r]


def finish(grid, sums, result, acc, span):
    push = sums[9 * ITERS]
    lift = sums[9 * ITERS + 1]
    for r in span:
        u, v = cell(grid, 1, r), cell(grid, 2, r)
        at = pl.ds((r - REACH) * SUB, SUB)
        result[0, at] = acc[0, r]
        east = 0.5 * (acc[1, r + 1] - acc[1, r - 1])
        north = 0.5 * (right(acc[2, r]) - left(acc[2, r]))
        result[1, at] = (push * u + lift * v) - (east + coriolis * north)
        east = 0.5 * (acc[2, r + 1] - acc[2, r - 1])
        north = 0.5 * (right(acc[1, r]) - left(acc[1, r]))
        result[2, at] = (push * v - lift * u) + (coriolis * east - north)


def strips_of(tiles, side):
    lane = lax.broadcasted_iota(jnp.int32, (SUB, LANES), 1)
    up = [turn(tile, SIDE) for tile in tiles]
    down = [turn(tile, -SIDE) for tile in tiles]
    out = []
    for q in range(len(tiles)):
        out.append(jnp.where(lane < SIDE, up[q - 1] if q else side, up[q]))
        after = down[q + 1] if q + 1 < len(tiles) else side
        out.append(jnp.where(lane < LANES - SIDE, down[q], after))
    return out


def lay(grid, cut, side, at, stride):
    for s, strip in enumerate(strips_of(cut, side)):
        grid[pl.Slice(at * SUB + s, SUB, stride * SUB), :] = strip


def place(side, f):
    return turn(side, SIDE - EDGE - EDGE * f)


def lay_halo(grid, halo, side, main, ext):
    lane = lax.broadcasted_iota(jnp.int32, (SUB, LANES), 1)
    sub = lax.broadcasted_iota(jnp.int32, (SUB, LANES), 0)
    tiles = SUB // 2
    for f in range(4):
        cut = [halo[pl.ds((f * tiles + t) * SUB, SUB)] for t in range(tiles)]
        lay(grid, cut, place(side, f), main * 4 + f, 4)
    line = jnp.broadcast_to(side[0:1], (SUB, LANES))
    side = jnp.where(sub < tiles, place(line, 4), place(line, 5))
    block = halo[pl.ds(4 * tiles * SUB, SUB)]
    up, down = turn(block, SIDE), turn(block, -SIDE)
    before = jnp.where(sub % tiles == 0, side, pltpu.roll(up, 1, 0))
    after = jnp.where(sub % tiles == tiles - 1, side, pltpu.roll(down, SUB - 1, 0))
    even = jnp.where(lane < SIDE, before, up)
    odd = jnp.where(lane < LANES - SIDE, down, after)
    for f in (1, 2):
        at = (ext * 4 + f) * SUB
        cut = slice((f - 1) * tiles, f * tiles)
        grid[pl.Slice(at, tiles, 2), :] = even[cut]
        grid[pl.Slice(at + 1, tiles, 2), :] = odd[cut]


def cell(grid, f, r):
    return grid[pl.ds(pl.multiple_of((r * 4 + f) * SUB, SUB), SUB), :]


def left(x):
    return pltpu.roll(x, 1, 1)


def right(x):
    return pltpu.roll(x, LANES - 1, 1)


def prepare(grid, poly, coef, start, count):
    flux_east = [None] * 3
    flux_north = [None] * 3
    depths = [None] * 2
    across = None
    for k in range(count + 2):
        r = start + k
        h = cell(grid, 3, r)
        flux_east = flux_east[1:] + [h * cell(grid, 1, r)]
        flux_north = flux_north[1:] + [h * cell(grid, 2, r)]
        depths = depths[1:] + [h]
        if k >= 1:
            before, across = across, 0.125 * (depths[0] + depths[1])
            coef[0, r - 1] = across
        if k >= 2:
            c = r - 1
            north = 0.125 * (depths[0] + right(depths[0]))
            south = 0.125 * (depths[0] + left(depths[0]))
            coef[1, c] = north
            coef[2, c] = south
            coef[3, c] = 2.0 - ((across + before) + (north + south))
            east_slope = flux_east[2] - flux_east[0]
            north_slope = right(flux_north[1]) - left(flux_north[1])
            poly[0][1, c] = 0.5 * (east_slope + north_slope)
            east_slope = flux_north[2] - flux_north[0]
            north_slope = right(flux_east[1]) - left(flux_east[1])
            poly[0][2, c] = 0.5 * (east_slope - north_slope)
            poly[0][0, c] = cell(grid, 0, c)


def sweep(poly, coef, m, start, count, upwards=False):
    step = -1 if upwards else 1
    order = range(start, start + count)[::step]
    back = [poly[m][f, order[0] - step] for f in range(3)]
    here = [poly[m][f, order[0]] for f in range(3)]
    found = {}
    for r in order:
        north, south, diag = coef[1, r], coef[2, r], coef[3, r]
        above, below = coef[0, r], coef[0, r - 1]
        ahead = [poly[m][f, r + step] for f in range(3)]
        for f in range(3):
            up, down = (back, ahead) if upwards else (ahead, back)
            value = diag * here[f]
            if m > 0:
                value = value - poly[m - 1][f, r]
            value = value + above * up[f]
            value = value + below * down[f]
            value = value + north * right(here[f])
            value = value + south * left(here[f])
            value = 0.5 * value if m == 0 else value
            poly[m + 1][f, r] = value
            found[f, r] = value
        back, here = here, ahead
    return found


def inner_kernel(fields, first, second, grid, coef, *poly):
    rows = fields.shape[1]
    for g in range(rows // SUB):
        side = sides_of(first, second, pl.ds(g * SUB, SUB))
        for f in range(4):
            cut = [
                fields[f, pl.ds(g * SUB, SUB), pl.ds(t * LANES, LANES)]
                for t in range(fields.shape[2] // LANES)
            ]
            lay(grid, cut, place(side, f), (REACH + g * SUB) * 4 + f, 4)
    prepare(grid, poly, coef, REACH, rows - 2)
    for m in range(ITERS - 1):
        if rows - 4 - 2 * m > 0:
            sweep(poly, coef, m, REACH + 2 + m, rows - 4 - 2 * m)


def one_side(halo, side, above, grid, coef, poly, each):
    below = coef.shape[1] - REACH
    main, ext, start = (1, 0, 0) if above else (below, below + SUB, below - 2)
    grid[pl.ds((ext * 4 + 3) * SUB, SUB), :] = jnp.ones((SUB, LANES), jnp.float32)
    lay_halo(grid, halo, side, main, ext)
    prepare(grid, poly, coef, start, REACH)
    each(0, None)
    for m in range(ITERS - 1):
        found = sweep(poly, coef, m, 2 + m if above else below - 2 - m, REACH, above)
        each(m + 1, found)


def mid_kernel(near, side, *rest):
    grid, coef, *poly = rest[len(rest) // 2 :]
    _, (_, above) = towards(None, None)
    for way, here in ((True, above), (False, jnp.logical_not(above))):
        pl.when(here)(
            lambda: one_side(near, side[...], way, grid, coef, poly, lambda m, found: None)
        )


def outer_kernel(far, sums, *rest):
    out, grid, coef, sol, result, *poly = rest[len(rest) // 2 :]
    rows, columns = out.shape[1:]
    lane = lax.broadcasted_iota(jnp.int32, (SUB, LANES), 1)
    (_, above), _ = towards(None, None)

    def far_rows(above):
        side = far[pl.ds(far.shape[0] - SUB, SUB)]
        whole = side_rows(rows, above)
        inside = 1 if above else -1
        edges = [whole[-1] + inside, whole[-1] + 2 * inside]
        acc = {}
        for r in edges + [r for k, r in enumerate(whole) if known(k) >= 0]:
            for g in range(3):
                acc[g, r] = sol[g, r - (REACH - 1)]

        def each(m, found):
            part = [r for k, r in enumerate(whole) if known(k) < m]
            if found is not None:
                held = [r for r in part if (0, r) in found]
                add(acc, sums, poly, m, held, found)
                part = [r for r in part if r not in held]
            add(acc, sums, poly, m, part)

        one_side(far, side, above, grid, coef, poly, each)
        span = [r for r in whole + edges[:1] if REACH <= r < REACH + rows]
        finish(grid, sums, result, acc, span)

    pl.when(above)(lambda: far_rows(True))
    pl.when(jnp.logical_not(above))(lambda: far_rows(False))

    for k in range(3):
        for g in range(rows // SUB):
            for t in range(columns // LANES):
                one = result[k, pl.Slice(g * SUB * SUB + 2 * t, SUB, SUB), :]
                two = result[k, pl.Slice(g * SUB * SUB + 2 * t + 1, SUB, SUB), :]
                joined = jnp.where(lane < HALF, turn(one, -SIDE), turn(two, SIDE))
                out[k, pl.ds(g * SUB, SUB), pl.ds(t * LANES, LANES)] = joined


def shards(state, depth, pole_real, pole_imag, pole_weight):
    rows, columns = depth.shape
    poles = pole_real.shape[0]
    vmem = pl.BlockSpec(memory_space=pltpu.VMEM)
    small = pltpu.CompilerParams(vmem_limit_bytes=GRANT)

    def f32(*shape):
        return jax.ShapeDtypeStruct(shape, jnp.float32)

    given = [
        pltpu.with_memory_space_constraint(x, pltpu.HBM)
        for x in (state, depth, pole_real, pole_imag, pole_weight)
    ]
    hbm = pl.BlockSpec(memory_space=pltpu.HBM)
    message = pltpu.VMEM((rows, LANES), jnp.float32)
    first, second, scalars = pl.pallas_call(
        pack_columns_kernel,
        out_shape=(message, message, pltpu.VMEM((4 * poles, LANES), jnp.float32)),
        in_specs=[hbm] * 5,
        out_specs=(vmem,) * 3,
        scratch_shapes=[
            pltpu.VMEM((2, 4, rows, LANES), jnp.float32),
            pltpu.SMEM(pole_real.shape, jnp.float32),
            pltpu.SMEM(pole_imag.shape, jnp.float32),
            pltpu.SMEM(pole_weight.shape, jnp.float32),
            pltpu.SemaphoreType.DMA((7,)),
        ],
        compiler_params=small,
        name="pack_columns",
    )(*given)
    count = (4 * SUB + 2) * columns // LANES
    fields, far, near = pl.pallas_call(
        load_fields_kernel,
        out_shape=(
            pltpu.VMEM((4, rows, columns), jnp.float32),
            pltpu.VMEM((count + SUB, LANES), jnp.float32),
            pltpu.VMEM((count, LANES), jnp.float32),
        ),
        in_specs=[hbm] * 2,
        out_specs=(vmem,) * 3,
        scratch_shapes=[pltpu.SemaphoreType.DMA((2,))],
        compiler_params=small,
        name="load_fields",
    )(*given[:2])
    second = swap(second, "pole", 1)
    first = swap(first, "pole", 0)
    far, near_side = pl.pallas_call(
        pack_sides_kernel,
        out_shape=(f32(*far.shape), f32(SUB, LANES)),
        in_specs=[vmem] * 3,
        out_specs=(vmem, vmem),
        input_output_aliases={2: 0},
        compiler_params=small,
        name="pack_sides",
    )(second, first, far)
    far = swap(far, "tile", 1)
    near = swap(near, "tile", 0)
    near_side = swap(near_side, "tile", 0)
    count = lax.axis_size("pole")
    others = jnp.stack([shift(scalars, "pole", step) for step in range(2, count - 1)])
    height = rows + 2 * REACH
    grid = f32(height * 4 * SUB, LANES)
    poly = [f32(3, height, SUB, LANES)] * ITERS
    coef = f32(4, height, SUB, LANES)
    sol = f32(3, rows + 2, SUB, LANES)
    result = f32(3, rows * SUB, LANES)
    state_of = (grid, coef, *poly)
    cost = pl.CostEstimate(
        flops=10 * ITERS * rows * SUB * LANES,
        bytes_accessed=4 * SUB * LANES * rows * (4 + 2 * ITERS + 2),
        transcendentals=0,
    )
    held = pl.pallas_call(
        inner_kernel,
        out_shape=state_of,
        in_specs=[vmem] * 3,
        out_specs=(vmem,) * len(state_of),
        compiler_params=small,
        cost_estimate=cost,
        name="inner",
    )(fields, first, second)
    held = pl.pallas_call(
        mid_kernel,
        out_shape=state_of,
        in_specs=[vmem] * (2 + len(state_of)),
        out_specs=(vmem,) * len(state_of),
        input_output_aliases={2 + i: i for i in range(len(state_of))},
        compiler_params=small,
        cost_estimate=cost,
        name="mid",
    )(near, near_side, *held)
    grid_held, coef_held, *poly_held = held
    sums, *part = pl.pallas_call(
        pole_sums_kernel,
        out_shape=(f32(9 * ITERS + 2, SUB, LANES), sol, result),
        in_specs=[vmem] * (5 + ITERS),
        out_specs=(vmem,) * 3,
        compiler_params=small,
        name="pole_sums",
    )(scalars, first, second, others, grid_held, *poly_held)
    kept = (grid, coef, sol, result, *poly)
    return pl.pallas_call(
        outer_kernel,
        out_shape=(f32(*state.shape), *kept),
        in_specs=[vmem] * (2 + len(kept)),
        out_specs=(vmem,) * (1 + len(kept)),
        input_output_aliases={2 + i: 1 + i for i in range(len(kept))},
        compiler_params=small,
        name="outer",
    )(far, sums, grid_held, coef_held, *part, *poly_held)[0]


def solution(mesh):
    return jax.shard_map(
        shards,
        mesh=mesh,
        in_specs=(
            P(None, "tile", "pole"),
            P("tile", "pole"),
            P("pole"),
            P("pole"),
            P(None, "pole"),
        ),
        out_specs=P(None, "tile", "pole"),
        check_vma=False,
    )
```

```python
import jax
import jax.numpy as jnp
from jax import lax
from jax.experimental import pallas as pl
from jax.experimental.pallas import tpu as pltpu
from jax.sharding import PartitionSpec as P

ITERS = 8
REACH = ITERS + 1
SUB = 8
LANES = 128
HALF = LANES // 2
SIDE = 32
EDGE = REACH
EAST = HALF + EDGE
GRANT = 16 * 1024 * 1024

coriolis = 0.7
centre = 8.0
half_width = 8.0


def pairs(count, phase):
    swap = []
    for i in range(phase, count + phase, 2):
        a, b = i % count, (i + 1) % count
        swap += [(a, b), (b, a)]
    return swap


def swap(block, axis, phase):
    return lax.ppermute(block, axis, pairs(lax.axis_size(axis), phase))


def shift(block, axis, step):
    count = lax.axis_size(axis)
    return lax.ppermute(block, axis, [(i, (i + step) % count) for i in range(count)])


def turn(x, lanes):
    return pltpu.roll(x, lanes % LANES, 1) if lanes % LANES else x


def cmul(a, b):
    return (a[0] * b[0] - a[1] * b[1], a[0] * b[1] + a[1] * b[0])


def cinv(a):
    norm = 1.0 / (a[0] * a[0] + a[1] * a[1])
    return (a[0] * norm, -a[1] * norm)


def cscale(a, factor):
    return (a[0] * factor, a[1] * factor)


def all_at_once(*pairs_of):
    moves = [pltpu.make_async_copy(*pair) for pair in pairs_of]
    for move in moves:
        move.start()
    for move in moves:
        move.wait()


def pack_columns_kernel(
    state,
    depth,
    real,
    imag,
    weight,
    fields,
    first,
    second,
    scalars,
    far_early,
    far,
    near_early,
    near,
    real_in,
    imag_in,
    weight_in,
    done,
):
    all_at_once(
        (state, fields.at[pl.ds(0, 3)], done.at[0]),
        (depth, fields.at[3], done.at[1]),
        (real, real_in, done.at[2]),
        (imag, imag_in, done.at[3]),
        (weight, weight_in, done.at[4]),
    )
    odd = lax.rem(lax.axis_index("pole"), 2) == 1
    rows, columns = fields.shape[1:]
    lane = lax.broadcasted_iota(jnp.int32, (SUB, LANES), 1)
    sub = lax.broadcasted_iota(jnp.int32, (SUB, LANES), 0)
    poles = real.shape[0]
    values = [real_in[i] for i in range(poles)] + [imag_in[i] for i in range(poles)]
    values += [weight_in[0, i] for i in range(poles)] + [weight_in[1, i] for i in range(poles)]
    spread = []
    for g in range(len(values) // SUB):
        block = jnp.full((SUB, LANES), values[g * SUB], jnp.float32)
        for i in range(1, SUB):
            block = jnp.where(sub == i, values[g * SUB + i], block)
        scalars[pl.ds(g * SUB, SUB)] = block
        spread.append(block)
    for g in range(rows // SUB):
        cut = pl.ds(g * SUB, SUB)
        rest = spread[g] if g < len(spread) else jnp.zeros((SUB, LANES), jnp.float32)
        eastward = rest
        westward = rest
        west = [fields[f, cut, 0:LANES] for f in range(4)]
        east = [fields[f, cut, columns - LANES : columns] for f in range(4)]
        west += [west[3] * west[1], west[3] * west[2]]
        east += [east[3] * east[1], east[3] * east[2]]
        for f in range(6):
            low, high = EDGE * f, EDGE * (f + 1)
            take = jnp.logical_and(lane >= low, lane < high)
            eastward = jnp.where(take, turn(east[f], low + EDGE), eastward)
            take = jnp.logical_and(lane >= EAST + low, lane < EAST + high)
            westward = jnp.where(take, turn(west[f], EAST + low), westward)
        first[cut, :] = jnp.where(odd, westward, eastward)
        second[cut, :] = jnp.where(odd, eastward, westward)
    for (parts, low) in towards((far_early, far), (near_early, near)):
        at = 0
        for part in parts:
            pl.when(low)(lambda: pack_rows(part, at, fields, 0, SUB))
            pl.when(jnp.logical_not(low))(
                lambda: pack_rows(part, at, fields, rows - SUB, rows - SUB - 1)
            )
            at += part.shape[0] // SUB


def towards(far, near):
    odd = lax.rem(lax.axis_index("tile"), 2) == 1
    return ((far, jnp.logical_not(odd)), (near, odd))


def pack_rows(target, at, fields, main, ext):
    tiles = fields.shape[2] // LANES
    for i in range(target.shape[0] // SUB):
        f, t = divmod(at + i, tiles)
        if f < 4:
            block = fields[f, main : main + SUB, t * LANES : (t + 1) * LANES]
            target[pl.ds(i * SUB, SUB)] = block
        elif t == 0:
            for f in (1, 2):
                flux = fields[3, ext : ext + 1, :] * fields[f, ext : ext + 1, :]
                for t in range(tiles):
                    row = i * SUB + (f - 1) * tiles + t
                    target[row : row + 1] = flux[:, t * LANES : (t + 1) * LANES]


def block_of(parts, at):
    early, late = parts
    count = early.shape[0] // SUB
    if at < count:
        return early[pl.ds(at * SUB, SUB)]
    return late[pl.ds((at - count) * SUB, SUB)]


def sides_of(first, second, cut):
    odd = lax.rem(lax.axis_index("pole"), 2) == 1
    lane = lax.broadcasted_iota(jnp.int32, (SUB, LANES), 1)
    from_first = jnp.logical_xor(lane >= HALF, odd)
    return jnp.where(from_first, first[cut, :], second[cut, :])


def pack_sides_kernel(second, first, far_in, near_in, far, near):
    for target, low in towards(far, near):
        target[pl.ds(target.shape[0] - SUB, SUB)] = pack_sides(second, first, low)


def pack_sides(second, first, low):
    rows = first.shape[0]
    sub = lax.broadcasted_iota(jnp.int32, (SUB, LANES), 0)
    lane = lax.broadcasted_iota(jnp.int32, (SUB, LANES), 1)
    side = jnp.where(
        low,
        sides_of(first, second, pl.ds(0, SUB)),
        sides_of(first, second, pl.ds(rows - SUB, SUB)),
    )
    line = jnp.where(
        low,
        sides_of(first, second, pl.ds(SUB, SUB))[0:1],
        sides_of(first, second, pl.ds(rows - 2 * SUB, SUB))[SUB - 1 : SUB],
    )
    line = jnp.broadcast_to(line, (SUB, LANES))
    low, high = 4 * EDGE, 6 * EDGE
    take = jnp.logical_or(
        jnp.logical_and(lane >= low, lane < high),
        jnp.logical_and(lane >= EAST + low, lane < EAST + high),
    )
    side = jnp.where(jnp.logical_and(take, sub == 0), line, side)
    return side


def pole_sums_kernel(scalars, first, second, others, grid, *rest):
    poly, (sums, sol, result) = rest[:ITERS], rest[ITERS:]
    odd = lax.rem(lax.axis_index("pole"), 2) == 1
    count = scalars.shape[0]
    lane = lax.broadcasted_iota(jnp.int32, (SUB, LANES), 1)
    blocks = [[scalars[pl.ds(g, SUB)] for g in range(0, count, SUB)]]
    for i, message in enumerate((first, second)):
        low = jnp.logical_xor(lane < HALF, odd if i == 0 else jnp.logical_not(odd))
        part = []
        for g in range(0, count, SUB):
            x = message[pl.ds(g, SUB), :]
            part.append(jnp.where(low, x, turn(x, HALF)))
        blocks.append(part)
    for i in range(others.shape[0]):
        blocks.append([others[i, pl.ds(g, SUB)] for g in range(0, count, SUB)])
    poles = count // 4
    quantity = []
    for q in range(4):
        cut = []
        for block in blocks:
            whole = jnp.concatenate(block, axis=0)
            cut.append(whole[q * poles : (q + 1) * poles])
        quantity.append(jnp.concatenate(cut, axis=0))
    alpha = (quantity[0], quantity[1])
    beta = (quantity[2], quantity[3])
    square = cmul(alpha, alpha)
    shifted = (square[0] + coriolis * coriolis, square[1])
    sigma = ((shifted[0] + centre) / half_width, shifted[1] / half_width)
    rho = [cinv(sigma)]
    for j in range(1, ITERS):
        rho.append(cinv((2.0 * sigma[0] - rho[-1][0], 2.0 * sigma[1] - rho[-1][1])))
    gain = None
    start = []
    for m in range(ITERS):
        if m == 0:
            start.append(cscale(rho[0], 1.0 / half_width))
        else:
            gain = rho[0] if gain is None else cmul(gain, rho[m - 1])
            start.append(cscale(cmul(rho[m], gain), 2.0 / half_width))
    tail = None
    weight = [None] * ITERS
    for m in reversed(range(ITERS)):
        if tail is None:
            weight[m] = start[m]
            tail = (jnp.ones_like(sigma[0]), jnp.zeros_like(sigma[0]))
        else:
            tail = cmul(cmul(rho[m + 1], rho[m]), tail)
            tail = (tail[0] + 1.0, tail[1])
            weight[m] = cmul(start[m], tail)
    inverse_alpha = cinv(alpha)
    inverse_shift = cinv(shifted)
    by_alpha = cmul(beta, inverse_alpha)
    by_shift = cmul(beta, inverse_shift)
    products = {
        "b": beta,
        "b/a": by_alpha,
        "b/s": by_shift,
        "bs/a": cmul(by_alpha, shifted),
        "ba/s": cmul(by_shift, alpha),
        "b/as": cmul(by_alpha, inverse_shift),
    }

    def total(x):
        s = x[0:SUB]
        for i in range(1, x.shape[0] // SUB):
            s = s + x[i * SUB : (i + 1) * SUB]
        for step in (4, 2, 1):
            s = s + pltpu.roll(s, step, 0)
        return s

    names = [("bs/a", "b", "b/a"), ("b", "ba/s", "b/s"), ("b/a", "b/s", "b/as")]
    factor = (1.0, -1.0, -coriolis)
    found = {}
    for m in range(ITERS):
        for name, w in products.items():
            found[name, m] = total(w[0] * weight[m][0] - w[1] * weight[m][1])
        for g in range(3):
            for f in range(3):
                value = found[names[g][f], m]
                sums[(g * 3 + f) * ITERS + m] = value if f == 0 else factor[f] * value
    sums[9 * ITERS] = total(products["ba/s"][0])
    sums[9 * ITERS + 1] = coriolis * total(products["b/s"][0])

    _, (_, above) = towards(None, None)
    rows = sol.shape[1] - 2

    def near_rows(above):
        near, far = side_rows(rows, above), side_rows(rows, not above)
        acc = {}
        for m in range(ITERS):
            add(acc, sums, poly, m, near)
        for m in range(ITERS - 1):
            add(acc, sums, poly, m, [r for k, r in enumerate(far) if known(k) >= m])
        for (g, r), v in acc.items():
            sol[g, r - (REACH - 1)] = v
        inside = sorted(near)[1:-1]
        finish(grid, sums, result, acc, [r for r in inside if REACH <= r < REACH + rows])

    pl.when(above)(lambda: near_rows(True))
    pl.when(jnp.logical_not(above))(lambda: near_rows(False))


def side_rows(rows, above):
    low, high = REACH - 1, REACH + rows
    return [low + k if above else high - k for k in range(rows // 2 + 1)]


def known(k):
    return max(min(ITERS - 2, k - 2), -1)


def add(acc, sums, poly, m, rows, values=None):
    for f in range(3):
        if not rows:
            return
        value = {r: poly[m][f, r] if values is None else values[f, r] for r in rows}
        for g in range(3):
            c = sums[(g * 3 + f) * ITERS + m]
            for r in rows:
                acc[g, r] = acc[g, r] + c * value[r] if (g, r) in acc else c * value[r]


def finish(grid, sums, result, acc, span):
    push = sums[9 * ITERS]
    lift = sums[9 * ITERS + 1]
    for r in span:
        u, v = cell(grid, 1, r), cell(grid, 2, r)
        at = pl.ds((r - REACH) * SUB, SUB)
        result[0, at] = acc[0, r]
        east = 0.5 * (acc[1, r + 1] - acc[1, r - 1])
        north = 0.5 * (right(acc[2, r]) - left(acc[2, r]))
        result[1, at] = (push * u + lift * v) - (east + coriolis * north)
        east = 0.5 * (acc[2, r + 1] - acc[2, r - 1])
        north = 0.5 * (right(acc[1, r]) - left(acc[1, r]))
        result[2, at] = (push * v - lift * u) + (coriolis * east - north)


def strips_of(tiles, side):
    lane = lax.broadcasted_iota(jnp.int32, (SUB, LANES), 1)
    up = [turn(tile, SIDE) for tile in tiles]
    down = [turn(tile, -SIDE) for tile in tiles]
    out = []
    for q in range(len(tiles)):
        out.append(jnp.where(lane < SIDE, up[q - 1] if q else side, up[q]))
        after = down[q + 1] if q + 1 < len(tiles) else side
        out.append(jnp.where(lane < LANES - SIDE, down[q], after))
    return out


def lay(grid, cut, side, at, stride):
    for s, strip in enumerate(strips_of(cut, side)):
        grid[pl.Slice(at * SUB + s, SUB, stride * SUB), :] = strip


def place(side, f):
    return turn(side, SIDE - EDGE - EDGE * f)


def lay_halo(grid, halo, side, main, ext):
    lane = lax.broadcasted_iota(jnp.int32, (SUB, LANES), 1)
    sub = lax.broadcasted_iota(jnp.int32, (SUB, LANES), 0)
    tiles = SUB // 2
    for f in range(4):
        cut = [block_of(halo, f * tiles + t) for t in range(tiles)]
        lay(grid, cut, place(side, f), main * 4 + f, 4)
    line = jnp.broadcast_to(side[0:1], (SUB, LANES))
    side = jnp.where(sub < tiles, place(line, 4), place(line, 5))
    block = block_of(halo, 4 * tiles)
    up, down = turn(block, SIDE), turn(block, -SIDE)
    before = jnp.where(sub % tiles == 0, side, pltpu.roll(up, 1, 0))
    after = jnp.where(sub % tiles == tiles - 1, side, pltpu.roll(down, SUB - 1, 0))
    even = jnp.where(lane < SIDE, before, up)
    odd = jnp.where(lane < LANES - SIDE, down, after)
    for f in (1, 2):
        at = (ext * 4 + f) * SUB
        cut = slice((f - 1) * tiles, f * tiles)
        grid[pl.Slice(at, tiles, 2), :] = even[cut]
        grid[pl.Slice(at + 1, tiles, 2), :] = odd[cut]


def cell(grid, f, r):
    return grid[pl.ds(pl.multiple_of((r * 4 + f) * SUB, SUB), SUB), :]


def left(x):
    return pltpu.roll(x, 1, 1)


def right(x):
    return pltpu.roll(x, LANES - 1, 1)


def prepare(grid, poly, coef, start, count):
    flux_east = [None] * 3
    flux_north = [None] * 3
    depths = [None] * 2
    across = None
    for k in range(count + 2):
        r = start + k
        h = cell(grid, 3, r)
        flux_east = flux_east[1:] + [h * cell(grid, 1, r)]
        flux_north = flux_north[1:] + [h * cell(grid, 2, r)]
        depths = depths[1:] + [h]
        if k >= 1:
            before, across = across, 0.125 * (depths[0] + depths[1])
            coef[0, r - 1] = across
        if k >= 2:
            c = r - 1
            north = 0.125 * (depths[0] + right(depths[0]))
            south = 0.125 * (depths[0] + left(depths[0]))
            coef[1, c] = north
            coef[2, c] = south
            coef[3, c] = 2.0 - ((across + before) + (north + south))
            east_slope = flux_east[2] - flux_east[0]
            north_slope = right(flux_north[1]) - left(flux_north[1])
            poly[0][1, c] = 0.5 * (east_slope + north_slope)
            east_slope = flux_north[2] - flux_north[0]
            north_slope = right(flux_east[1]) - left(flux_east[1])
            poly[0][2, c] = 0.5 * (east_slope - north_slope)
            poly[0][0, c] = cell(grid, 0, c)


def sweep(poly, coef, m, start, count, upwards=False):
    step = -1 if upwards else 1
    order = range(start, start + count)[::step]
    back = [poly[m][f, order[0] - step] for f in range(3)]
    here = [poly[m][f, order[0]] for f in range(3)]
    found = {}
    for r in order:
        north, south, diag = coef[1, r], coef[2, r], coef[3, r]
        above, below = coef[0, r], coef[0, r - 1]
        ahead = [poly[m][f, r + step] for f in range(3)]
        for f in range(3):
            up, down = (back, ahead) if upwards else (ahead, back)
            value = diag * here[f]
            if m > 0:
                value = value - poly[m - 1][f, r]
            value = value + above * up[f]
            value = value + below * down[f]
            value = value + north * right(here[f])
            value = value + south * left(here[f])
            value = 0.5 * value if m == 0 else value
            poly[m + 1][f, r] = value
            found[f, r] = value
        back, here = here, ahead
    return found


def inner_kernel(fields, first, second, grid, coef, *poly):
    rows = fields.shape[1]
    for g in range(rows // SUB):
        side = sides_of(first, second, pl.ds(g * SUB, SUB))
        for f in range(4):
            cut = [
                fields[f, pl.ds(g * SUB, SUB), pl.ds(t * LANES, LANES)]
                for t in range(fields.shape[2] // LANES)
            ]
            lay(grid, cut, place(side, f), (REACH + g * SUB) * 4 + f, 4)
    prepare(grid, poly, coef, REACH, rows - 2)
    for m in range(ITERS - 1):
        if rows - 4 - 2 * m > 0:
            sweep(poly, coef, m, REACH + 2 + m, rows - 4 - 2 * m)


def one_side(halo, side, above, grid, coef, poly, each):
    below = coef.shape[1] - REACH
    main, ext, start = (1, 0, 0) if above else (below, below + SUB, below - 2)
    grid[pl.ds((ext * 4 + 3) * SUB, SUB), :] = jnp.ones((SUB, LANES), jnp.float32)
    lay_halo(grid, halo, side, main, ext)
    prepare(grid, poly, coef, start, REACH)
    each(0, None)
    for m in range(ITERS - 1):
        found = sweep(poly, coef, m, 2 + m if above else below - 2 - m, REACH, above)
        each(m + 1, found)


def mid_kernel(near_early, near, *rest):
    grid, coef, *poly = rest[len(rest) // 2 :]
    _, (_, above) = towards(None, None)
    side = near[pl.ds(near.shape[0] - SUB, SUB)]
    for way, here in ((True, above), (False, jnp.logical_not(above))):
        pl.when(here)(
            lambda: one_side((near_early, near), side, way, grid, coef, poly, lambda m, found: None)
        )


def outer_kernel(far_early, far, sums, *rest):
    out, grid, coef, sol, result, *poly = rest[len(rest) // 2 :]
    rows, columns = out.shape[1:]
    lane = lax.broadcasted_iota(jnp.int32, (SUB, LANES), 1)
    (_, above), _ = towards(None, None)

    def far_rows(above):
        side = far[pl.ds(far.shape[0] - SUB, SUB)]
        whole = side_rows(rows, above)
        inside = 1 if above else -1
        edges = [whole[-1] + inside, whole[-1] + 2 * inside]
        acc = {}
        for r in edges + [r for k, r in enumerate(whole) if known(k) >= 0]:
            for g in range(3):
                acc[g, r] = sol[g, r - (REACH - 1)]

        def each(m, found):
            part = [r for k, r in enumerate(whole) if known(k) < m]
            if found is not None:
                held = [r for r in part if (0, r) in found]
                add(acc, sums, poly, m, held, found)
                part = [r for r in part if r not in held]
            add(acc, sums, poly, m, part)

        one_side((far_early, far), side, above, grid, coef, poly, each)
        span = [r for r in whole + edges[:1] if REACH <= r < REACH + rows]
        finish(grid, sums, result, acc, span)

    pl.when(above)(lambda: far_rows(True))
    pl.when(jnp.logical_not(above))(lambda: far_rows(False))

    for k in range(3):
        for g in range(rows // SUB):
            for t in range(columns // LANES):
                one = result[k, pl.Slice(g * SUB * SUB + 2 * t, SUB, SUB), :]
                two = result[k, pl.Slice(g * SUB * SUB + 2 * t + 1, SUB, SUB), :]
                joined = jnp.where(lane < HALF, turn(one, -SIDE), turn(two, SIDE))
                out[k, pl.ds(g * SUB, SUB), pl.ds(t * LANES, LANES)] = joined


def shards(state, depth, pole_real, pole_imag, pole_weight):
    rows, columns = depth.shape
    poles = pole_real.shape[0]
    vmem = pl.BlockSpec(memory_space=pltpu.VMEM)
    small = pltpu.CompilerParams(vmem_limit_bytes=GRANT)

    def f32(*shape):
        return jax.ShapeDtypeStruct(shape, jnp.float32)

    given = [
        pltpu.with_memory_space_constraint(x, pltpu.HBM)
        for x in (state, depth, pole_real, pole_imag, pole_weight)
    ]
    hbm = pl.BlockSpec(memory_space=pltpu.HBM)
    message = pltpu.VMEM((rows, LANES), jnp.float32)
    blocks = 4 * columns // LANES + 2
    parts = (blocks // 2, blocks - blocks // 2, blocks // 2 + 1, blocks - blocks // 2 - 1)
    fields, first, second, scalars, far_early, far, near_early, near = pl.pallas_call(
        pack_columns_kernel,
        out_shape=(
            pltpu.VMEM((4, rows, columns), jnp.float32),
            message,
            message,
            pltpu.VMEM((4 * poles, LANES), jnp.float32),
            *(pltpu.VMEM((part * SUB, LANES), jnp.float32) for part in parts),
        ),
        in_specs=[hbm] * 5,
        out_specs=(vmem,) * 8,
        scratch_shapes=[
            pltpu.SMEM(pole_real.shape, jnp.float32),
            pltpu.SMEM(pole_imag.shape, jnp.float32),
            pltpu.SMEM(pole_weight.shape, jnp.float32),
            pltpu.SemaphoreType.DMA((5,)),
        ],
        compiler_params=small,
        name="pack_columns",
    )(*given)
    second = swap(second, "pole", 1)
    first = swap(first, "pole", 0)
    far, near = pl.pallas_call(
        pack_sides_kernel,
        out_shape=(f32(*far.shape), f32(*near.shape)),
        in_specs=[vmem] * 4,
        out_specs=(vmem, vmem),
        input_output_aliases={2: 0, 3: 1},
        compiler_params=small,
        name="pack_sides",
    )(second, first, far, near)
    far_early = swap(far_early, "tile", 1)
    far = swap(far, "tile", 1)
    near_early = swap(near_early, "tile", 0)
    near = swap(near, "tile", 0)
    count = lax.axis_size("pole")
    others = jnp.stack([shift(scalars, "pole", step) for step in range(2, count - 1)])
    height = rows + 2 * REACH
    grid = f32(height * 4 * SUB, LANES)
    poly = [f32(3, height, SUB, LANES)] * ITERS
    coef = f32(4, height, SUB, LANES)
    sol = f32(3, rows + 2, SUB, LANES)
    result = f32(3, rows * SUB, LANES)
    state_of = (grid, coef, *poly)
    cost = pl.CostEstimate(
        flops=10 * ITERS * rows * SUB * LANES,
        bytes_accessed=4 * SUB * LANES * rows * (4 + 2 * ITERS + 2),
        transcendentals=0,
    )
    held = pl.pallas_call(
        inner_kernel,
        out_shape=state_of,
        in_specs=[vmem] * 3,
        out_specs=(vmem,) * len(state_of),
        compiler_params=small,
        cost_estimate=cost,
        name="inner",
    )(fields, first, second)
    held = pl.pallas_call(
        mid_kernel,
        out_shape=state_of,
        in_specs=[vmem] * (2 + len(state_of)),
        out_specs=(vmem,) * len(state_of),
        input_output_aliases={2 + i: i for i in range(len(state_of))},
        compiler_params=small,
        cost_estimate=cost,
        name="mid",
    )(near_early, near, *held)
    grid_held, coef_held, *poly_held = held
    sums, *part = pl.pallas_call(
        pole_sums_kernel,
        out_shape=(f32(9 * ITERS + 2, SUB, LANES), sol, result),
        in_specs=[vmem] * (5 + ITERS),
        out_specs=(vmem,) * 3,
        compiler_params=small,
        name="pole_sums",
    )(scalars, first, second, others, grid_held, *poly_held)
    kept = (grid, coef, sol, result, *poly)
    return pl.pallas_call(
        outer_kernel,
        out_shape=(f32(*state.shape), *kept),
        in_specs=[vmem] * (3 + len(kept)),
        out_specs=(vmem,) * (1 + len(kept)),
        input_output_aliases={3 + i: 1 + i for i in range(len(kept))},
        compiler_params=small,
        name="outer",
    )(far_early, far, sums, grid_held, coef_held, *part, *poly_held)[0]


def solution(mesh):
    return jax.shard_map(
        shards,
        mesh=mesh,
        in_specs=(
            P(None, "tile", "pole"),
            P("tile", "pole"),
            P("pole"),
            P("pole"),
            P(None, "pole"),
        ),
        out_specs=P(None, "tile", "pole"),
        check_vma=False,
    )
```

```python
import functools

import jax
import jax.numpy as jnp
from jax import lax
from jax.experimental import pallas as pl
from jax.experimental.pallas import tpu as pltpu
from jax.sharding import PartitionSpec as P

ITERS = 8
REACH = ITERS + 1
SUB = 8
LANES = 128
HALF = LANES // 2
SIDE = 32
EDGE = REACH
EAST = HALF + EDGE
GRANT = 16 * 1024 * 1024

coriolis = 0.7
centre = 8.0
half_width = 8.0


def pairs(count, phase):
    swap = []
    for i in range(phase, count + phase, 2):
        a, b = i % count, (i + 1) % count
        swap += [(a, b), (b, a)]
    return swap


def swap(block, axis, phase):
    return lax.ppermute(block, axis, pairs(lax.axis_size(axis), phase))


def shift(block, axis, step):
    count = lax.axis_size(axis)
    return lax.ppermute(block, axis, [(i, (i + step) % count) for i in range(count)])


def turn(x, lanes):
    return pltpu.roll(x, lanes % LANES, 1) if lanes % LANES else x


def cmul(a, b):
    return (a[0] * b[0] - a[1] * b[1], a[0] * b[1] + a[1] * b[0])


def cinv(a):
    norm = 1.0 / (a[0] * a[0] + a[1] * a[1])
    return (a[0] * norm, -a[1] * norm)


def cscale(a, factor):
    return (a[0] * factor, a[1] * factor)


def all_at_once(*pairs_of):
    moves = [pltpu.make_async_copy(*pair) for pair in pairs_of]
    for move in moves:
        move.start()
    for move in moves:
        move.wait()


def pack_columns_kernel(
    state,
    depth,
    real,
    imag,
    weight,
    fields,
    first,
    second,
    scalars,
    far_early,
    far,
    near_early,
    near,
    real_in,
    imag_in,
    weight_in,
    done,
):
    all_at_once(
        (state, fields.at[pl.ds(0, 3)], done.at[0]),
        (depth, fields.at[3], done.at[1]),
        (real, real_in, done.at[2]),
        (imag, imag_in, done.at[3]),
        (weight, weight_in, done.at[4]),
    )
    odd = lax.rem(lax.axis_index("pole"), 2) == 1
    rows, columns = fields.shape[1:]
    lane = lax.broadcasted_iota(jnp.int32, (SUB, LANES), 1)
    sub = lax.broadcasted_iota(jnp.int32, (SUB, LANES), 0)
    poles = real.shape[0]
    values = [real_in[i] for i in range(poles)] + [imag_in[i] for i in range(poles)]
    values += [weight_in[0, i] for i in range(poles)] + [weight_in[1, i] for i in range(poles)]
    spread = []
    for g in range(len(values) // SUB):
        block = jnp.full((SUB, LANES), values[g * SUB], jnp.float32)
        for i in range(1, SUB):
            block = jnp.where(sub == i, values[g * SUB + i], block)
        scalars[pl.ds(g * SUB, SUB)] = block
        spread.append(block)
    for g in range(len(spread), scalars.shape[0] // SUB):
        scalars[pl.ds(g * SUB, SUB)] = jnp.zeros((SUB, LANES), jnp.float32)
    for g in range(rows // SUB):
        cut = pl.ds(g * SUB, SUB)
        rest = spread[g] if g < len(spread) else jnp.zeros((SUB, LANES), jnp.float32)
        eastward = rest
        westward = rest
        west = [fields[f, cut, 0:LANES] for f in range(4)]
        east = [fields[f, cut, columns - LANES : columns] for f in range(4)]
        west += [west[3] * west[1], west[3] * west[2]]
        east += [east[3] * east[1], east[3] * east[2]]
        for f in range(6):
            low, high = EDGE * f, EDGE * (f + 1)
            take = jnp.logical_and(lane >= low, lane < high)
            eastward = jnp.where(take, turn(east[f], low + EDGE), eastward)
            take = jnp.logical_and(lane >= EAST + low, lane < EAST + high)
            westward = jnp.where(take, turn(west[f], EAST + low), westward)
        first[cut, :] = jnp.where(odd, westward, eastward)
        second[cut, :] = jnp.where(odd, eastward, westward)
    for (parts, low) in towards((far_early, far), (near_early, near)):
        at = 0
        for part in parts:
            pl.when(low)(lambda: pack_rows(part, at, fields, 0, SUB))
            pl.when(jnp.logical_not(low))(
                lambda: pack_rows(part, at, fields, rows - SUB, rows - SUB - 1)
            )
            at += part.shape[0] // SUB


def towards(far, near):
    odd = lax.rem(lax.axis_index("tile"), 2) == 1
    return ((far, jnp.logical_not(odd)), (near, odd))


def pack_rows(target, at, fields, main, ext):
    tiles = fields.shape[2] // LANES
    for i in range(target.shape[0] // SUB):
        f, t = divmod(at + i, tiles)
        if f < 4:
            block = fields[f, main : main + SUB, t * LANES : (t + 1) * LANES]
            target[pl.ds(i * SUB, SUB)] = block
        elif t == 0:
            for f in (1, 2):
                flux = fields[3, ext : ext + 1, :] * fields[f, ext : ext + 1, :]
                for t in range(tiles):
                    row = i * SUB + (f - 1) * tiles + t
                    target[row : row + 1] = flux[:, t * LANES : (t + 1) * LANES]


def block_of(parts, at):
    early, late = parts
    count = early.shape[0] // SUB
    if at < count:
        return early[pl.ds(at * SUB, SUB)]
    return late[pl.ds((at - count) * SUB, SUB)]


def sides_of(first, second, cut):
    odd = lax.rem(lax.axis_index("pole"), 2) == 1
    lane = lax.broadcasted_iota(jnp.int32, (SUB, LANES), 1)
    from_first = jnp.logical_xor(lane >= HALF, odd)
    return jnp.where(from_first, first[cut, :], second[cut, :])


def pack_sides_kernel(second, first, far_in, near_in, far, near):
    for target, low in towards(far, near):
        target[pl.ds(target.shape[0] - SUB, SUB)] = pack_sides(second, first, low)


def pack_sides(second, first, low):
    rows = first.shape[0]
    sub = lax.broadcasted_iota(jnp.int32, (SUB, LANES), 0)
    lane = lax.broadcasted_iota(jnp.int32, (SUB, LANES), 1)
    side = jnp.where(
        low,
        sides_of(first, second, pl.ds(0, SUB)),
        sides_of(first, second, pl.ds(rows - SUB, SUB)),
    )
    line = jnp.where(
        low,
        sides_of(first, second, pl.ds(SUB, SUB))[0:1],
        sides_of(first, second, pl.ds(rows - 2 * SUB, SUB))[SUB - 1 : SUB],
    )
    line = jnp.broadcast_to(line, (SUB, LANES))
    low, high = 4 * EDGE, 6 * EDGE
    take = jnp.logical_or(
        jnp.logical_and(lane >= low, lane < high),
        jnp.logical_and(lane >= EAST + low, lane < EAST + high),
    )
    side = jnp.where(jnp.logical_and(take, sub == 0), line, side)
    return side


def pole_sums_kernel(count, scalars, first, second, others, grid, *rest):
    poly, (sums, sol, result) = rest[:ITERS], rest[ITERS:]
    odd = lax.rem(lax.axis_index("pole"), 2) == 1
    lane = lax.broadcasted_iota(jnp.int32, (SUB, LANES), 1)
    blocks = [[scalars[pl.ds(g, SUB)] for g in range(0, count, SUB)]]
    for i, message in enumerate((first, second)):
        low = jnp.logical_xor(lane < HALF, odd if i == 0 else jnp.logical_not(odd))
        part = []
        for g in range(0, count, SUB):
            x = message[pl.ds(g, SUB), :]
            part.append(jnp.where(low, x, turn(x, HALF)))
        blocks.append(part)
    for i in range(others.shape[0]):
        blocks.append([others[i, pl.ds(g, SUB)] for g in range(0, count, SUB)])
    poles = count // 4
    quantity = []
    for q in range(4):
        cut = []
        for block in blocks:
            whole = jnp.concatenate(block, axis=0)
            cut.append(whole[q * poles : (q + 1) * poles])
        quantity.append(jnp.concatenate(cut, axis=0))
    alpha = (quantity[0], quantity[1])
    beta = (quantity[2], quantity[3])
    square = cmul(alpha, alpha)
    shifted = (square[0] + coriolis * coriolis, square[1])
    sigma = ((shifted[0] + centre) / half_width, shifted[1] / half_width)
    rho = [cinv(sigma)]
    for j in range(1, ITERS):
        rho.append(cinv((2.0 * sigma[0] - rho[-1][0], 2.0 * sigma[1] - rho[-1][1])))
    gain = None
    start = []
    for m in range(ITERS):
        if m == 0:
            start.append(cscale(rho[0], 1.0 / half_width))
        else:
            gain = rho[0] if gain is None else cmul(gain, rho[m - 1])
            start.append(cscale(cmul(rho[m], gain), 2.0 / half_width))
    tail = None
    weight = [None] * ITERS
    for m in reversed(range(ITERS)):
        if tail is None:
            weight[m] = start[m]
            tail = (jnp.ones_like(sigma[0]), jnp.zeros_like(sigma[0]))
        else:
            tail = cmul(cmul(rho[m + 1], rho[m]), tail)
            tail = (tail[0] + 1.0, tail[1])
            weight[m] = cmul(start[m], tail)
    inverse_alpha = cinv(alpha)
    inverse_shift = cinv(shifted)
    by_alpha = cmul(beta, inverse_alpha)
    by_shift = cmul(beta, inverse_shift)
    products = {
        "b": beta,
        "b/a": by_alpha,
        "b/s": by_shift,
        "bs/a": cmul(by_alpha, shifted),
        "ba/s": cmul(by_shift, alpha),
        "b/as": cmul(by_alpha, inverse_shift),
    }

    def total(x):
        s = x[0:SUB]
        for i in range(1, x.shape[0] // SUB):
            s = s + x[i * SUB : (i + 1) * SUB]
        for step in (4, 2, 1):
            s = s + pltpu.roll(s, step, 0)
        return s

    names = [("bs/a", "b", "b/a"), ("b", "ba/s", "b/s"), ("b/a", "b/s", "b/as")]
    factor = (1.0, -1.0, -coriolis)
    found = {}
    for m in range(ITERS):
        for name, w in products.items():
            found[name, m] = total(w[0] * weight[m][0] - w[1] * weight[m][1])
        for g in range(3):
            for f in range(3):
                value = found[names[g][f], m]
                sums[(g * 3 + f) * ITERS + m] = value if f == 0 else factor[f] * value
    sums[9 * ITERS] = total(products["ba/s"][0])
    sums[9 * ITERS + 1] = coriolis * total(products["b/s"][0])

    _, (_, above) = towards(None, None)
    rows = sol.shape[1] - 2

    def near_rows(above):
        near, far = side_rows(rows, above), side_rows(rows, not above)
        acc = {}
        for m in range(ITERS):
            add(acc, sums, poly, m, near)
        for m in range(ITERS - 1):
            add(acc, sums, poly, m, [r for k, r in enumerate(far) if known(k) >= m])
        for (g, r), v in acc.items():
            sol[g, r - (REACH - 1)] = v
        inside = sorted(near)[1:-1]
        finish(grid, sums, result, acc, [r for r in inside if REACH <= r < REACH + rows])

    pl.when(above)(lambda: near_rows(True))
    pl.when(jnp.logical_not(above))(lambda: near_rows(False))


def side_rows(rows, above):
    low, high = REACH - 1, REACH + rows
    return [low + k if above else high - k for k in range(rows // 2 + 1)]


def known(k):
    return max(min(ITERS - 2, k - 2), -1)


def add(acc, sums, poly, m, rows, values=None):
    for f in range(3):
        if not rows:
            return
        value = {r: poly[m][f, r] if values is None else values[f, r] for r in rows}
        for g in range(3):
            c = sums[(g * 3 + f) * ITERS + m]
            for r in rows:
                acc[g, r] = acc[g, r] + c * value[r] if (g, r) in acc else c * value[r]


def finish(grid, sums, result, acc, span):
    push = sums[9 * ITERS]
    lift = sums[9 * ITERS + 1]
    for r in span:
        u, v = cell(grid, 1, r), cell(grid, 2, r)
        at = pl.ds((r - REACH) * SUB, SUB)
        result[0, at] = acc[0, r]
        east = 0.5 * (acc[1, r + 1] - acc[1, r - 1])
        north = 0.5 * (right(acc[2, r]) - left(acc[2, r]))
        result[1, at] = (push * u + lift * v) - (east + coriolis * north)
        east = 0.5 * (acc[2, r + 1] - acc[2, r - 1])
        north = 0.5 * (right(acc[1, r]) - left(acc[1, r]))
        result[2, at] = (push * v - lift * u) + (coriolis * east - north)


def strips_of(tiles, side):
    lane = lax.broadcasted_iota(jnp.int32, (SUB, LANES), 1)
    up = [turn(tile, SIDE) for tile in tiles]
    down = [turn(tile, -SIDE) for tile in tiles]
    out = []
    for q in range(len(tiles)):
        out.append(jnp.where(lane < SIDE, up[q - 1] if q else side, up[q]))
        after = down[q + 1] if q + 1 < len(tiles) else side
        out.append(jnp.where(lane < LANES - SIDE, down[q], after))
    return out


def lay(grid, cut, side, at, stride):
    for s, strip in enumerate(strips_of(cut, side)):
        grid[pl.Slice(at * SUB + s, SUB, stride * SUB), :] = strip


def place(side, f):
    return turn(side, SIDE - EDGE - EDGE * f)


def lay_halo(grid, halo, side, main, ext):
    lane = lax.broadcasted_iota(jnp.int32, (SUB, LANES), 1)
    sub = lax.broadcasted_iota(jnp.int32, (SUB, LANES), 0)
    tiles = SUB // 2
    for f in range(4):
        cut = [block_of(halo, f * tiles + t) for t in range(tiles)]
        lay(grid, cut, place(side, f), main * 4 + f, 4)
    line = jnp.broadcast_to(side[0:1], (SUB, LANES))
    side = jnp.where(sub < tiles, place(line, 4), place(line, 5))
    block = block_of(halo, 4 * tiles)
    up, down = turn(block, SIDE), turn(block, -SIDE)
    before = jnp.where(sub % tiles == 0, side, pltpu.roll(up, 1, 0))
    after = jnp.where(sub % tiles == tiles - 1, side, pltpu.roll(down, SUB - 1, 0))
    even = jnp.where(lane < SIDE, before, up)
    odd = jnp.where(lane < LANES - SIDE, down, after)
    for f in (1, 2):
        at = (ext * 4 + f) * SUB
        cut = slice((f - 1) * tiles, f * tiles)
        grid[pl.Slice(at, tiles, 2), :] = even[cut]
        grid[pl.Slice(at + 1, tiles, 2), :] = odd[cut]


def cell(grid, f, r):
    return grid[pl.ds(pl.multiple_of((r * 4 + f) * SUB, SUB), SUB), :]


def left(x):
    return pltpu.roll(x, 1, 1)


def right(x):
    return pltpu.roll(x, LANES - 1, 1)


def prepare(grid, poly, coef, start, count):
    flux_east = [None] * 3
    flux_north = [None] * 3
    depths = [None] * 2
    across = None
    for k in range(count + 2):
        r = start + k
        h = cell(grid, 3, r)
        flux_east = flux_east[1:] + [h * cell(grid, 1, r)]
        flux_north = flux_north[1:] + [h * cell(grid, 2, r)]
        depths = depths[1:] + [h]
        if k >= 1:
            before, across = across, 0.125 * (depths[0] + depths[1])
            coef[0, r - 1] = across
        if k >= 2:
            c = r - 1
            north = 0.125 * (depths[0] + right(depths[0]))
            south = 0.125 * (depths[0] + left(depths[0]))
            coef[1, c] = north
            coef[2, c] = south
            coef[3, c] = 2.0 - ((across + before) + (north + south))
            east_slope = flux_east[2] - flux_east[0]
            north_slope = right(flux_north[1]) - left(flux_north[1])
            poly[0][1, c] = 0.5 * (east_slope + north_slope)
            east_slope = flux_north[2] - flux_north[0]
            north_slope = right(flux_east[1]) - left(flux_east[1])
            poly[0][2, c] = 0.5 * (east_slope - north_slope)
            poly[0][0, c] = cell(grid, 0, c)


def sweep(poly, coef, m, start, count, upwards=False):
    step = -1 if upwards else 1
    order = range(start, start + count)[::step]
    back = [poly[m][f, order[0] - step] for f in range(3)]
    here = [poly[m][f, order[0]] for f in range(3)]
    found = {}
    for r in order:
        north, south, diag = coef[1, r], coef[2, r], coef[3, r]
        above, below = coef[0, r], coef[0, r - 1]
        ahead = [poly[m][f, r + step] for f in range(3)]
        for f in range(3):
            up, down = (back, ahead) if upwards else (ahead, back)
            value = diag * here[f]
            if m > 0:
                value = value - poly[m - 1][f, r]
            value = value + above * up[f]
            value = value + below * down[f]
            value = value + north * right(here[f])
            value = value + south * left(here[f])
            value = 0.5 * value if m == 0 else value
            poly[m + 1][f, r] = value
            found[f, r] = value
        back, here = here, ahead
    return found


def inner_kernel(fields, first, second, grid, coef, *poly):
    rows = fields.shape[1]
    for g in range(rows // SUB):
        side = sides_of(first, second, pl.ds(g * SUB, SUB))
        for f in range(4):
            cut = [
                fields[f, pl.ds(g * SUB, SUB), pl.ds(t * LANES, LANES)]
                for t in range(fields.shape[2] // LANES)
            ]
            lay(grid, cut, place(side, f), (REACH + g * SUB) * 4 + f, 4)
    prepare(grid, poly, coef, REACH, rows - 2)
    for m in range(ITERS - 1):
        if rows - 4 - 2 * m > 0:
            sweep(poly, coef, m, REACH + 2 + m, rows - 4 - 2 * m)


def one_side(halo, side, above, grid, coef, poly, each):
    below = coef.shape[1] - REACH
    main, ext, start = (1, 0, 0) if above else (below, below + SUB, below - 2)
    grid[pl.ds((ext * 4 + 3) * SUB, SUB), :] = jnp.ones((SUB, LANES), jnp.float32)
    lay_halo(grid, halo, side, main, ext)
    prepare(grid, poly, coef, start, REACH)
    each(0, None)
    for m in range(ITERS - 1):
        found = sweep(poly, coef, m, 2 + m if above else below - 2 - m, REACH, above)
        each(m + 1, found)


def mid_kernel(near_early, near, *rest):
    grid, coef, *poly = rest[len(rest) // 2 :]
    _, (_, above) = towards(None, None)
    side = near[pl.ds(near.shape[0] - SUB, SUB)]
    for way, here in ((True, above), (False, jnp.logical_not(above))):
        pl.when(here)(
            lambda: one_side((near_early, near), side, way, grid, coef, poly, lambda m, found: None)
        )


def outer_kernel(far_early, far, sums, *rest):
    out, grid, coef, sol, result, *poly = rest[len(rest) // 2 :]
    rows, columns = out.shape[1:]
    lane = lax.broadcasted_iota(jnp.int32, (SUB, LANES), 1)
    (_, above), _ = towards(None, None)

    def far_rows(above):
        side = far[pl.ds(far.shape[0] - SUB, SUB)]
        whole = side_rows(rows, above)
        inside = 1 if above else -1
        edges = [whole[-1] + inside, whole[-1] + 2 * inside]
        acc = {}
        for r in edges + [r for k, r in enumerate(whole) if known(k) >= 0]:
            for g in range(3):
                acc[g, r] = sol[g, r - (REACH - 1)]

        def each(m, found):
            part = [r for k, r in enumerate(whole) if known(k) < m]
            if found is not None:
                held = [r for r in part if (0, r) in found]
                add(acc, sums, poly, m, held, found)
                part = [r for r in part if r not in held]
            add(acc, sums, poly, m, part)

        one_side((far_early, far), side, above, grid, coef, poly, each)
        span = [r for r in whole + edges[:1] if REACH <= r < REACH + rows]
        finish(grid, sums, result, acc, span)

    pl.when(above)(lambda: far_rows(True))
    pl.when(jnp.logical_not(above))(lambda: far_rows(False))

    for k in range(3):
        for g in range(rows // SUB):
            for t in range(columns // LANES):
                one = result[k, pl.Slice(g * SUB * SUB + 2 * t, SUB, SUB), :]
                two = result[k, pl.Slice(g * SUB * SUB + 2 * t + 1, SUB, SUB), :]
                joined = jnp.where(lane < HALF, turn(one, -SIDE), turn(two, SIDE))
                out[k, pl.ds(g * SUB, SUB), pl.ds(t * LANES, LANES)] = joined


def shards(state, depth, pole_real, pole_imag, pole_weight):
    rows, columns = depth.shape
    poles = pole_real.shape[0]
    vmem = pl.BlockSpec(memory_space=pltpu.VMEM)
    small = pltpu.CompilerParams(vmem_limit_bytes=GRANT)

    def f32(*shape):
        return jax.ShapeDtypeStruct(shape, jnp.float32)

    given = [
        pltpu.with_memory_space_constraint(x, pltpu.HBM)
        for x in (state, depth, pole_real, pole_imag, pole_weight)
    ]
    hbm = pl.BlockSpec(memory_space=pltpu.HBM)
    message = pltpu.VMEM((rows, LANES), jnp.float32)
    blocks = 4 * columns // LANES + 2
    parts = (blocks // 2, blocks - blocks // 2, blocks // 2 + 1, blocks - blocks // 2 - 1)
    wide = max(4 * poles, (blocks // 2 + 0) * SUB)
    fields, first, second, scalars, far_early, far, near_early, near = pl.pallas_call(
        pack_columns_kernel,
        out_shape=(
            pltpu.VMEM((4, rows, columns), jnp.float32),
            message,
            message,
            pltpu.VMEM((wide, LANES), jnp.float32),
            *(pltpu.VMEM((part * SUB, LANES), jnp.float32) for part in parts),
        ),
        in_specs=[hbm] * 5,
        out_specs=(vmem,) * 8,
        scratch_shapes=[
            pltpu.SMEM(pole_real.shape, jnp.float32),
            pltpu.SMEM(pole_imag.shape, jnp.float32),
            pltpu.SMEM(pole_weight.shape, jnp.float32),
            pltpu.SemaphoreType.DMA((5,)),
        ],
        compiler_params=small,
        name="pack_columns",
    )(*given)
    second = swap(second, "pole", 1)
    first = swap(first, "pole", 0)
    far, near = pl.pallas_call(
        pack_sides_kernel,
        out_shape=(f32(*far.shape), f32(*near.shape)),
        in_specs=[vmem] * 4,
        out_specs=(vmem, vmem),
        input_output_aliases={2: 0, 3: 1},
        compiler_params=small,
        name="pack_sides",
    )(second, first, far, near)
    far_early = swap(far_early, "tile", 1)
    far = swap(far, "tile", 1)
    near_early = swap(near_early, "tile", 0)
    near = swap(near, "tile", 0)
    count = lax.axis_size("pole")
    others = jnp.stack([shift(scalars, "pole", step) for step in range(2, count - 1)])
    height = rows + 2 * REACH
    grid = f32(height * 4 * SUB, LANES)
    poly = [f32(3, height, SUB, LANES)] * ITERS
    coef = f32(4, height, SUB, LANES)
    sol = f32(3, rows + 2, SUB, LANES)
    result = f32(3, rows * SUB, LANES)
    state_of = (grid, coef, *poly)
    cost = pl.CostEstimate(
        flops=10 * ITERS * rows * SUB * LANES,
        bytes_accessed=4 * SUB * LANES * rows * (4 + 2 * ITERS + 2),
        transcendentals=0,
    )
    held = pl.pallas_call(
        inner_kernel,
        out_shape=state_of,
        in_specs=[vmem] * 3,
        out_specs=(vmem,) * len(state_of),
        compiler_params=small,
        cost_estimate=cost,
        name="inner",
    )(fields, first, second)
    held = pl.pallas_call(
        mid_kernel,
        out_shape=state_of,
        in_specs=[vmem] * (2 + len(state_of)),
        out_specs=(vmem,) * len(state_of),
        input_output_aliases={2 + i: i for i in range(len(state_of))},
        compiler_params=small,
        cost_estimate=cost,
        name="mid",
    )(near_early, near, *held)
    grid_held, coef_held, *poly_held = held
    sums, *part = pl.pallas_call(
        functools.partial(pole_sums_kernel, 4 * poles),
        out_shape=(f32(9 * ITERS + 2, SUB, LANES), sol, result),
        in_specs=[vmem] * (5 + ITERS),
        out_specs=(vmem,) * 3,
        compiler_params=small,
        name="pole_sums",
    )(scalars, first, second, others, grid_held, *poly_held)
    kept = (grid, coef, sol, result, *poly)
    return pl.pallas_call(
        outer_kernel,
        out_shape=(f32(*state.shape), *kept),
        in_specs=[vmem] * (3 + len(kept)),
        out_specs=(vmem,) * (1 + len(kept)),
        input_output_aliases={3 + i: 1 + i for i in range(len(kept))},
        compiler_params=small,
        name="outer",
    )(far_early, far, sums, grid_held, coef_held, *part, *poly_held)[0]


def solution(mesh):
    return jax.shard_map(
        shards,
        mesh=mesh,
        in_specs=(
            P(None, "tile", "pole"),
            P("tile", "pole"),
            P("pole"),
            P("pole"),
            P(None, "pole"),
        ),
        out_specs=P(None, "tile", "pole"),
        check_vma=False,
    )
```

```python
import functools

import jax
import jax.numpy as jnp
from jax import lax
from jax.experimental import pallas as pl
from jax.experimental.pallas import tpu as pltpu
from jax.sharding import PartitionSpec as P

ITERS = 8
REACH = ITERS + 1
SUB = 8
LANES = 128
HALF = LANES // 2
SIDE = 32
EDGE = REACH
EAST = HALF + EDGE
GRANT = 16 * 1024 * 1024

coriolis = 0.7
centre = 8.0
half_width = 8.0


def pairs(count, phase):
    swap = []
    for i in range(phase, count + phase, 2):
        a, b = i % count, (i + 1) % count
        swap += [(a, b), (b, a)]
    return swap


def swap(block, axis, phase):
    return lax.ppermute(block, axis, pairs(lax.axis_size(axis), phase))


def shift(block, axis, step):
    count = lax.axis_size(axis)
    return lax.ppermute(block, axis, [(i, (i + step) % count) for i in range(count)])


def turn(x, lanes):
    return pltpu.roll(x, lanes % LANES, 1) if lanes % LANES else x


def cmul(a, b):
    return (a[0] * b[0] - a[1] * b[1], a[0] * b[1] + a[1] * b[0])


def cinv(a):
    norm = 1.0 / (a[0] * a[0] + a[1] * a[1])
    return (a[0] * norm, -a[1] * norm)


def cscale(a, factor):
    return (a[0] * factor, a[1] * factor)


def all_at_once(*pairs_of):
    moves = [pltpu.make_async_copy(*pair) for pair in pairs_of]
    for move in moves:
        move.start()
    for move in moves:
        move.wait()


def pack_columns_kernel(
    state,
    depth,
    real,
    imag,
    weight,
    fields,
    first,
    second,
    scalars,
    far_early,
    far,
    near_early,
    near,
    real_in,
    imag_in,
    weight_in,
    done,
):
    all_at_once(
        (state, fields.at[pl.ds(0, 3)], done.at[0]),
        (depth, fields.at[3], done.at[1]),
        (real, real_in, done.at[2]),
        (imag, imag_in, done.at[3]),
        (weight, weight_in, done.at[4]),
    )
    odd = lax.rem(lax.axis_index("pole"), 2) == 1
    rows, columns = fields.shape[1:]
    lane = lax.broadcasted_iota(jnp.int32, (SUB, LANES), 1)
    sub = lax.broadcasted_iota(jnp.int32, (SUB, LANES), 0)
    poles = real.shape[0]
    values = [real_in[i] for i in range(poles)] + [imag_in[i] for i in range(poles)]
    values += [weight_in[0, i] for i in range(poles)] + [weight_in[1, i] for i in range(poles)]
    spread = []
    for g in range(len(values) // SUB):
        block = jnp.full((SUB, LANES), values[g * SUB], jnp.float32)
        for i in range(1, SUB):
            block = jnp.where(sub == i, values[g * SUB + i], block)
        scalars[pl.ds(g * SUB, SUB)] = block
        spread.append(block)
    for g in range(len(spread), scalars.shape[0] // SUB):
        scalars[pl.ds(g * SUB, SUB)] = jnp.zeros((SUB, LANES), jnp.float32)
    for g in range(rows // SUB):
        cut = pl.ds(g * SUB, SUB)
        rest = spread[g] if g < len(spread) else jnp.zeros((SUB, LANES), jnp.float32)
        eastward = rest
        westward = rest
        west = [fields[f, cut, 0:LANES] for f in range(4)]
        east = [fields[f, cut, columns - LANES : columns] for f in range(4)]
        west += [west[3] * west[1], west[3] * west[2]]
        east += [east[3] * east[1], east[3] * east[2]]
        for f in range(6):
            low, high = EDGE * f, EDGE * (f + 1)
            take = jnp.logical_and(lane >= low, lane < high)
            eastward = jnp.where(take, turn(east[f], low + EDGE), eastward)
            take = jnp.logical_and(lane >= EAST + low, lane < EAST + high)
            westward = jnp.where(take, turn(west[f], EAST + low), westward)
        first[cut, :] = jnp.where(odd, westward, eastward)
        second[cut, :] = jnp.where(odd, eastward, westward)
    for (parts, low) in towards((far_early, far), (near_early, near)):
        at = 0
        for part in parts:
            pl.when(low)(lambda: pack_rows(part, at, fields, 0, SUB))
            pl.when(jnp.logical_not(low))(
                lambda: pack_rows(part, at, fields, rows - SUB, rows - SUB - 1)
            )
            at += part.shape[0] // SUB


def towards(far, near):
    odd = lax.rem(lax.axis_index("tile"), 2) == 1
    return ((far, jnp.logical_not(odd)), (near, odd))


def pack_rows(target, at, fields, main, ext):
    tiles = fields.shape[2] // LANES
    for i in range(target.shape[0] // SUB):
        f, t = divmod(at + i, tiles)
        if f < 4:
            block = fields[f, main : main + SUB, t * LANES : (t + 1) * LANES]
            target[pl.ds(i * SUB, SUB)] = block
        elif t == 0:
            for f in (1, 2):
                flux = fields[3, ext : ext + 1, :] * fields[f, ext : ext + 1, :]
                for t in range(tiles):
                    row = i * SUB + (f - 1) * tiles + t
                    target[row : row + 1] = flux[:, t * LANES : (t + 1) * LANES]


def block_of(parts, at):
    early, late = parts
    count = early.shape[0] // SUB
    if at < count:
        return early[pl.ds(at * SUB, SUB)]
    return late[pl.ds((at - count) * SUB, SUB)]


def sides_of(first, second, cut):
    odd = lax.rem(lax.axis_index("pole"), 2) == 1
    lane = lax.broadcasted_iota(jnp.int32, (SUB, LANES), 1)
    from_first = jnp.logical_xor(lane >= HALF, odd)
    return jnp.where(from_first, first[cut, :], second[cut, :])


def pack_sides_kernel(second, first, far_in, near_in, far, near):
    for target, low in towards(far, near):
        target[pl.ds(target.shape[0] - SUB, SUB)] = pack_sides(second, first, low)


def pack_sides(second, first, low):
    rows = first.shape[0]
    sub = lax.broadcasted_iota(jnp.int32, (SUB, LANES), 0)
    lane = lax.broadcasted_iota(jnp.int32, (SUB, LANES), 1)
    side = jnp.where(
        low,
        sides_of(first, second, pl.ds(0, SUB)),
        sides_of(first, second, pl.ds(rows - SUB, SUB)),
    )
    line = jnp.where(
        low,
        sides_of(first, second, pl.ds(SUB, SUB))[0:1],
        sides_of(first, second, pl.ds(rows - 2 * SUB, SUB))[SUB - 1 : SUB],
    )
    line = jnp.broadcast_to(line, (SUB, LANES))
    low, high = 4 * EDGE, 6 * EDGE
    take = jnp.logical_or(
        jnp.logical_and(lane >= low, lane < high),
        jnp.logical_and(lane >= EAST + low, lane < EAST + high),
    )
    side = jnp.where(jnp.logical_and(take, sub == 0), line, side)
    return side


def pole_sums_kernel(count, scalars, first, second, others, grid, *rest):
    poly, (sums, sol, result) = rest[:ITERS], rest[ITERS:]
    odd = lax.rem(lax.axis_index("pole"), 2) == 1
    lane = lax.broadcasted_iota(jnp.int32, (SUB, LANES), 1)
    blocks = [[scalars[pl.ds(g, SUB)] for g in range(0, count, SUB)]]
    for i, message in enumerate((first, second)):
        low = jnp.logical_xor(lane < HALF, odd if i == 0 else jnp.logical_not(odd))
        part = []
        for g in range(0, count, SUB):
            x = message[pl.ds(g, SUB), :]
            part.append(jnp.where(low, x, turn(x, HALF)))
        blocks.append(part)
    for i in range(others.shape[0]):
        blocks.append([others[i, pl.ds(g, SUB)] for g in range(0, count, SUB)])
    poles = count // 4
    quantity = []
    for q in range(4):
        cut = []
        for block in blocks:
            whole = jnp.concatenate(block, axis=0)
            cut.append(whole[q * poles : (q + 1) * poles])
        quantity.append(jnp.concatenate(cut, axis=0))
    alpha = (quantity[0], quantity[1])
    beta = (quantity[2], quantity[3])
    square = cmul(alpha, alpha)
    shifted = (square[0] + coriolis * coriolis, square[1])
    sigma = ((shifted[0] + centre) / half_width, shifted[1] / half_width)
    rho = [cinv(sigma)]
    for j in range(1, ITERS):
        rho.append(cinv((2.0 * sigma[0] - rho[-1][0], 2.0 * sigma[1] - rho[-1][1])))
    gain = None
    start = []
    for m in range(ITERS):
        if m == 0:
            start.append(cscale(rho[0], 1.0 / half_width))
        else:
            gain = rho[0] if gain is None else cmul(gain, rho[m - 1])
            start.append(cscale(cmul(rho[m], gain), 2.0 / half_width))
    tail = None
    weight = [None] * ITERS
    for m in reversed(range(ITERS)):
        if tail is None:
            weight[m] = start[m]
            tail = (jnp.ones_like(sigma[0]), jnp.zeros_like(sigma[0]))
        else:
            tail = cmul(cmul(rho[m + 1], rho[m]), tail)
            tail = (tail[0] + 1.0, tail[1])
            weight[m] = cmul(start[m], tail)
    inverse_alpha = cinv(alpha)
    inverse_shift = cinv(shifted)
    by_alpha = cmul(beta, inverse_alpha)
    by_shift = cmul(beta, inverse_shift)
    products = {
        "b": beta,
        "b/a": by_alpha,
        "b/s": by_shift,
        "bs/a": cmul(by_alpha, shifted),
        "ba/s": cmul(by_shift, alpha),
        "b/as": cmul(by_alpha, inverse_shift),
    }

    def total(x):
        s = x[0:SUB]
        for i in range(1, x.shape[0] // SUB):
            s = s + x[i * SUB : (i + 1) * SUB]
        for step in (4, 2, 1):
            s = s + pltpu.roll(s, step, 0)
        return s

    names = [("bs/a", "b", "b/a"), ("b", "ba/s", "b/s"), ("b/a", "b/s", "b/as")]
    factor = (1.0, -1.0, -coriolis)
    found = {}
    for m in range(ITERS):
        for name, w in products.items():
            found[name, m] = total(w[0] * weight[m][0] - w[1] * weight[m][1])
        for g in range(3):
            for f in range(3):
                value = found[names[g][f], m]
                sums[(g * 3 + f) * ITERS + m] = value if f == 0 else factor[f] * value
    sums[9 * ITERS] = total(products["ba/s"][0])
    sums[9 * ITERS + 1] = coriolis * total(products["b/s"][0])

    _, (_, above) = towards(None, None)
    rows = sol.shape[1] - 2

    def near_rows(above):
        near, far = side_rows(rows, above), side_rows(rows, not above)
        acc = {}
        for m in range(ITERS):
            add(acc, sums, poly, m, near)
        for m in range(ITERS - 1):
            add(acc, sums, poly, m, [r for k, r in enumerate(far) if known(k) >= m])
        for (g, r), v in acc.items():
            sol[g, r - (REACH - 1)] = v
        inside = sorted(near)[1:-1]
        finish(grid, sums, result, acc, [r for r in inside if REACH <= r < REACH + rows])

    pl.when(above)(lambda: near_rows(True))
    pl.when(jnp.logical_not(above))(lambda: near_rows(False))


def side_rows(rows, above):
    low, high = REACH - 1, REACH + rows
    return [low + k if above else high - k for k in range(rows // 2 + 1)]


def known(k):
    return max(min(ITERS - 2, k - 2), -1)


def add(acc, sums, poly, m, rows, values=None):
    for f in range(3):
        if not rows:
            return
        value = {r: poly[m][f, r] if values is None else values[f, r] for r in rows}
        for g in range(3):
            c = sums[(g * 3 + f) * ITERS + m]
            for r in rows:
                acc[g, r] = acc[g, r] + c * value[r] if (g, r) in acc else c * value[r]


def finish(grid, sums, result, acc, span):
    push = sums[9 * ITERS]
    lift = sums[9 * ITERS + 1]
    for r in span:
        u, v = cell(grid, 1, r), cell(grid, 2, r)
        at = pl.ds((r - REACH) * SUB, SUB)
        result[0, at] = acc[0, r]
        east = 0.5 * (acc[1, r + 1] - acc[1, r - 1])
        north = 0.5 * (right(acc[2, r]) - left(acc[2, r]))
        result[1, at] = (push * u + lift * v) - (east + coriolis * north)
        east = 0.5 * (acc[2, r + 1] - acc[2, r - 1])
        north = 0.5 * (right(acc[1, r]) - left(acc[1, r]))
        result[2, at] = (push * v - lift * u) + (coriolis * east - north)


def strips_of(tiles, side):
    lane = lax.broadcasted_iota(jnp.int32, (SUB, LANES), 1)
    up = [turn(tile, SIDE) for tile in tiles]
    down = [turn(tile, -SIDE) for tile in tiles]
    out = []
    for q in range(len(tiles)):
        out.append(jnp.where(lane < SIDE, up[q - 1] if q else side, up[q]))
        after = down[q + 1] if q + 1 < len(tiles) else side
        out.append(jnp.where(lane < LANES - SIDE, down[q], after))
    return out


def lay(grid, cut, side, at, stride):
    for s, strip in enumerate(strips_of(cut, side)):
        grid[pl.Slice(at * SUB + s, SUB, stride * SUB), :] = strip


def place(side, f):
    return turn(side, SIDE - EDGE - EDGE * f)


def lay_halo(grid, halo, side, main, ext):
    lane = lax.broadcasted_iota(jnp.int32, (SUB, LANES), 1)
    sub = lax.broadcasted_iota(jnp.int32, (SUB, LANES), 0)
    tiles = SUB // 2
    for f in range(4):
        cut = [block_of(halo, f * tiles + t) for t in range(tiles)]
        lay(grid, cut, place(side, f), main * 4 + f, 4)
    line = jnp.broadcast_to(side[0:1], (SUB, LANES))
    side = jnp.where(sub < tiles, place(line, 4), place(line, 5))
    block = block_of(halo, 4 * tiles)
    up, down = turn(block, SIDE), turn(block, -SIDE)
    before = jnp.where(sub % tiles == 0, side, pltpu.roll(up, 1, 0))
    after = jnp.where(sub % tiles == tiles - 1, side, pltpu.roll(down, SUB - 1, 0))
    even = jnp.where(lane < SIDE, before, up)
    odd = jnp.where(lane < LANES - SIDE, down, after)
    for f in (1, 2):
        at = (ext * 4 + f) * SUB
        cut = slice((f - 1) * tiles, f * tiles)
        grid[pl.Slice(at, tiles, 2), :] = even[cut]
        grid[pl.Slice(at + 1, tiles, 2), :] = odd[cut]


def cell(grid, f, r):
    return grid[pl.ds(pl.multiple_of((r * 4 + f) * SUB, SUB), SUB), :]


def left(x):
    return pltpu.roll(x, 1, 1)


def right(x):
    return pltpu.roll(x, LANES - 1, 1)


def prepare(grid, poly, coef, start, count):
    flux_east = [None] * 3
    flux_north = [None] * 3
    depths = [None] * 2
    across = None
    for k in range(count + 2):
        r = start + k
        h = cell(grid, 3, r)
        flux_east = flux_east[1:] + [h * cell(grid, 1, r)]
        flux_north = flux_north[1:] + [h * cell(grid, 2, r)]
        depths = depths[1:] + [h]
        if k >= 1:
            before, across = across, 0.125 * (depths[0] + depths[1])
            coef[0, r - 1] = across
        if k >= 2:
            c = r - 1
            north = 0.125 * (depths[0] + right(depths[0]))
            south = 0.125 * (depths[0] + left(depths[0]))
            coef[1, c] = north
            coef[2, c] = south
            coef[3, c] = 2.0 - ((across + before) + (north + south))
            east_slope = flux_east[2] - flux_east[0]
            north_slope = right(flux_north[1]) - left(flux_north[1])
            poly[0][1, c] = 0.5 * (east_slope + north_slope)
            east_slope = flux_north[2] - flux_north[0]
            north_slope = right(flux_east[1]) - left(flux_east[1])
            poly[0][2, c] = 0.5 * (east_slope - north_slope)
            poly[0][0, c] = cell(grid, 0, c)


def sweep(poly, coef, m, start, count, upwards=False):
    step = -1 if upwards else 1
    order = range(start, start + count)[::step]
    back = [poly[m][f, order[0] - step] for f in range(3)]
    here = [poly[m][f, order[0]] for f in range(3)]
    found = {}
    for r in order:
        north, south, diag = coef[1, r], coef[2, r], coef[3, r]
        above, below = coef[0, r], coef[0, r - 1]
        ahead = [poly[m][f, r + step] for f in range(3)]
        for f in range(3):
            up, down = (back, ahead) if upwards else (ahead, back)
            value = diag * here[f]
            if m > 0:
                value = value - poly[m - 1][f, r]
            value = value + above * up[f]
            value = value + below * down[f]
            value = value + north * right(here[f])
            value = value + south * left(here[f])
            value = 0.5 * value if m == 0 else value
            poly[m + 1][f, r] = value
            found[f, r] = value
        back, here = here, ahead
    return found


def inner_kernel(fields, first, second, grid, coef, *poly):
    rows = fields.shape[1]
    for g in range(rows // SUB):
        side = sides_of(first, second, pl.ds(g * SUB, SUB))
        for f in range(4):
            cut = [
                fields[f, pl.ds(g * SUB, SUB), pl.ds(t * LANES, LANES)]
                for t in range(fields.shape[2] // LANES)
            ]
            lay(grid, cut, place(side, f), (REACH + g * SUB) * 4 + f, 4)
    prepare(grid, poly, coef, REACH, rows - 2)
    for m in range(ITERS - 1):
        if rows - 4 - 2 * m > 0:
            sweep(poly, coef, m, REACH + 2 + m, rows - 4 - 2 * m)


def one_side(halo, side, above, grid, coef, poly, each):
    below = coef.shape[1] - REACH
    main, ext, start = (1, 0, 0) if above else (below, below + SUB, below - 2)
    grid[pl.ds((ext * 4 + 3) * SUB, SUB), :] = jnp.ones((SUB, LANES), jnp.float32)
    lay_halo(grid, halo, side, main, ext)
    prepare(grid, poly, coef, start, REACH)
    each(0, None)
    for m in range(ITERS - 1):
        found = sweep(poly, coef, m, 2 + m if above else below - 2 - m, REACH, above)
        each(m + 1, found)


def mid_kernel(near_early, near, *rest):
    grid, coef, *poly = rest[len(rest) // 2 :]
    _, (_, above) = towards(None, None)
    side = near[pl.ds(near.shape[0] - SUB, SUB)]
    for way, here in ((True, above), (False, jnp.logical_not(above))):
        pl.when(here)(
            lambda: one_side((near_early, near), side, way, grid, coef, poly, lambda m, found: None)
        )


def outer_kernel(far_early, far, sums, *rest):
    out, grid, coef, sol, result, *poly = rest[len(rest) // 2 :]
    rows, columns = out.shape[1:]
    lane = lax.broadcasted_iota(jnp.int32, (SUB, LANES), 1)
    (_, above), _ = towards(None, None)

    def far_rows(above):
        side = far[pl.ds(far.shape[0] - SUB, SUB)]
        whole = side_rows(rows, above)
        inside = 1 if above else -1
        edges = [whole[-1] + inside, whole[-1] + 2 * inside]
        acc = {}
        for r in edges + [r for k, r in enumerate(whole) if known(k) >= 0]:
            for g in range(3):
                acc[g, r] = sol[g, r - (REACH - 1)]

        def each(m, found):
            part = [r for k, r in enumerate(whole) if known(k) < m]
            if found is not None:
                held = [r for r in part if (0, r) in found]
                add(acc, sums, poly, m, held, found)
                part = [r for r in part if r not in held]
            add(acc, sums, poly, m, part)

        one_side((far_early, far), side, above, grid, coef, poly, each)
        span = [r for r in whole + edges[:1] if REACH <= r < REACH + rows]
        finish(grid, sums, result, acc, span)

    pl.when(above)(lambda: far_rows(True))
    pl.when(jnp.logical_not(above))(lambda: far_rows(False))

    for k in range(3):
        for g in range(rows // SUB):
            for t in range(columns // LANES):
                one = result[k, pl.Slice(g * SUB * SUB + 2 * t, SUB, SUB), :]
                two = result[k, pl.Slice(g * SUB * SUB + 2 * t + 1, SUB, SUB), :]
                joined = jnp.where(lane < HALF, turn(one, -SIDE), turn(two, SIDE))
                out[k, pl.ds(g * SUB, SUB), pl.ds(t * LANES, LANES)] = joined


def shards(state, depth, pole_real, pole_imag, pole_weight):
    rows, columns = depth.shape
    poles = pole_real.shape[0]
    vmem = pl.BlockSpec(memory_space=pltpu.VMEM)
    small = pltpu.CompilerParams(vmem_limit_bytes=GRANT)

    def f32(*shape):
        return jax.ShapeDtypeStruct(shape, jnp.float32)

    given = [
        pltpu.with_memory_space_constraint(x, pltpu.HBM)
        for x in (state, depth, pole_real, pole_imag, pole_weight)
    ]
    hbm = pl.BlockSpec(memory_space=pltpu.HBM)
    message = pltpu.VMEM((rows, LANES), jnp.float32)
    blocks = 4 * columns // LANES + 2
    half = blocks // 2 * SUB
    parts = (half + SUB + 4, half, half + SUB, half - SUB)
    wide = max(4 * poles, half)
    fields, first, second, scalars, far_early, far, near_early, near = pl.pallas_call(
        pack_columns_kernel,
        out_shape=(
            pltpu.VMEM((4, rows, columns), jnp.float32),
            message,
            message,
            pltpu.VMEM((wide, LANES), jnp.float32),
            *(pltpu.VMEM((part, LANES), jnp.float32) for part in parts),
        ),
        in_specs=[hbm] * 5,
        out_specs=(vmem,) * 8,
        scratch_shapes=[
            pltpu.SMEM(pole_real.shape, jnp.float32),
            pltpu.SMEM(pole_imag.shape, jnp.float32),
            pltpu.SMEM(pole_weight.shape, jnp.float32),
            pltpu.SemaphoreType.DMA((5,)),
        ],
        compiler_params=small,
        name="pack_columns",
    )(*given)
    second = swap(second, "pole", 1)
    first = swap(first, "pole", 0)
    far, near = pl.pallas_call(
        pack_sides_kernel,
        out_shape=(f32(*far.shape), f32(*near.shape)),
        in_specs=[vmem] * 4,
        out_specs=(vmem, vmem),
        input_output_aliases={2: 0, 3: 1},
        compiler_params=small,
        name="pack_sides",
    )(second, first, far, near)
    far_early = swap(far_early, "tile", 1)
    far = swap(far, "tile", 1)
    near_early = swap(near_early, "tile", 0)
    near = swap(near, "tile", 0)
    count = lax.axis_size("pole")
    others = jnp.stack([shift(scalars, "pole", step) for step in range(2, count - 1)])
    height = rows + 2 * REACH
    grid = f32(height * 4 * SUB, LANES)
    poly = [f32(3, height, SUB, LANES)] * ITERS
    coef = f32(4, height, SUB, LANES)
    sol = f32(3, rows + 2, SUB, LANES)
    result = f32(3, rows * SUB, LANES)
    state_of = (grid, coef, *poly)
    cost = pl.CostEstimate(
        flops=10 * ITERS * rows * SUB * LANES,
        bytes_accessed=4 * SUB * LANES * rows * (4 + 2 * ITERS + 2),
        transcendentals=0,
    )
    held = pl.pallas_call(
        inner_kernel,
        out_shape=state_of,
        in_specs=[vmem] * 3,
        out_specs=(vmem,) * len(state_of),
        compiler_params=small,
        cost_estimate=cost,
        name="inner",
    )(fields, first, second)
    held = pl.pallas_call(
        mid_kernel,
        out_shape=state_of,
        in_specs=[vmem] * (2 + len(state_of)),
        out_specs=(vmem,) * len(state_of),
        input_output_aliases={2 + i: i for i in range(len(state_of))},
        compiler_params=small,
        cost_estimate=cost,
        name="mid",
    )(near_early, near, *held)
    grid_held, coef_held, *poly_held = held
    sums, *part = pl.pallas_call(
        functools.partial(pole_sums_kernel, 4 * poles),
        out_shape=(f32(9 * ITERS + 2, SUB, LANES), sol, result),
        in_specs=[vmem] * (5 + ITERS),
        out_specs=(vmem,) * 3,
        compiler_params=small,
        name="pole_sums",
    )(scalars, first, second, others, grid_held, *poly_held)
    kept = (grid, coef, sol, result, *poly)
    return pl.pallas_call(
        outer_kernel,
        out_shape=(f32(*state.shape), *kept),
        in_specs=[vmem] * (3 + len(kept)),
        out_specs=(vmem,) * (1 + len(kept)),
        input_output_aliases={3 + i: 1 + i for i in range(len(kept))},
        compiler_params=small,
        name="outer",
    )(far_early, far, sums, grid_held, coef_held, *part, *poly_held)[0]


def solution(mesh):
    return jax.shard_map(
        shards,
        mesh=mesh,
        in_specs=(
            P(None, "tile", "pole"),
            P("tile", "pole"),
            P("pole"),
            P("pole"),
            P(None, "pole"),
        ),
        out_specs=P(None, "tile", "pole"),
        check_vma=False,
    )
```

```python
import functools

import jax
import jax.numpy as jnp
from jax import lax
from jax.experimental import pallas as pl
from jax.experimental.pallas import tpu as pltpu
from jax.sharding import PartitionSpec as P

ITERS = 8
REACH = ITERS + 1
SUB = 8
LANES = 128
HALF = LANES // 2
SIDE = 32
EDGE = REACH
EAST = HALF + EDGE
GRANT = 16 * 1024 * 1024

coriolis = 0.7
centre = 8.0
half_width = 8.0


def pairs(count, phase):
    swap = []
    for i in range(phase, count + phase, 2):
        a, b = i % count, (i + 1) % count
        swap += [(a, b), (b, a)]
    return swap


def swap(block, axis, phase):
    return lax.ppermute(block, axis, pairs(lax.axis_size(axis), phase))


def shift(block, axis, step):
    count = lax.axis_size(axis)
    return lax.ppermute(block, axis, [(i, (i + step) % count) for i in range(count)])


def turn(x, lanes):
    return pltpu.roll(x, lanes % LANES, 1) if lanes % LANES else x


def cmul(a, b):
    return (a[0] * b[0] - a[1] * b[1], a[0] * b[1] + a[1] * b[0])


def cinv(a):
    norm = 1.0 / (a[0] * a[0] + a[1] * a[1])
    return (a[0] * norm, -a[1] * norm)


def cscale(a, factor):
    return (a[0] * factor, a[1] * factor)


def all_at_once(*pairs_of):
    moves = [pltpu.make_async_copy(*pair) for pair in pairs_of]
    for move in moves:
        move.start()
    for move in moves:
        move.wait()


def pack_columns_kernel(
    state,
    depth,
    real,
    imag,
    weight,
    fields,
    first,
    second,
    scalars,
    far_early,
    far,
    near_early,
    near,
    real_in,
    imag_in,
    weight_in,
    done,
):
    all_at_once(
        (state, fields.at[pl.ds(0, 3)], done.at[0]),
        (depth, fields.at[3], done.at[1]),
        (real, real_in, done.at[2]),
        (imag, imag_in, done.at[3]),
        (weight, weight_in, done.at[4]),
    )
    odd = lax.rem(lax.axis_index("pole"), 2) == 1
    rows, columns = fields.shape[1:]
    lane = lax.broadcasted_iota(jnp.int32, (SUB, LANES), 1)
    sub = lax.broadcasted_iota(jnp.int32, (SUB, LANES), 0)
    poles = real.shape[0]
    values = [real_in[i] for i in range(poles)] + [imag_in[i] for i in range(poles)]
    values += [weight_in[0, i] for i in range(poles)] + [weight_in[1, i] for i in range(poles)]
    spread = []
    for g in range(len(values) // SUB):
        block = jnp.full((SUB, LANES), values[g * SUB], jnp.float32)
        for i in range(1, SUB):
            block = jnp.where(sub == i, values[g * SUB + i], block)
        scalars[pl.ds(g * SUB, SUB)] = block
        spread.append(block)
    for g in range(len(spread), scalars.shape[0] // SUB):
        scalars[pl.ds(g * SUB, SUB)] = jnp.zeros((SUB, LANES), jnp.float32)
    for g in range(rows // SUB):
        cut = pl.ds(g * SUB, SUB)
        rest = spread[g] if g < len(spread) else jnp.zeros((SUB, LANES), jnp.float32)
        eastward = rest
        westward = rest
        west = [fields[f, cut, 0:LANES] for f in range(4)]
        east = [fields[f, cut, columns - LANES : columns] for f in range(4)]
        west += [west[3] * west[1], west[3] * west[2]]
        east += [east[3] * east[1], east[3] * east[2]]
        for f in range(6):
            low, high = EDGE * f, EDGE * (f + 1)
            take = jnp.logical_and(lane >= low, lane < high)
            eastward = jnp.where(take, turn(east[f], low + EDGE), eastward)
            take = jnp.logical_and(lane >= EAST + low, lane < EAST + high)
            westward = jnp.where(take, turn(west[f], EAST + low), westward)
        first[cut, :] = jnp.where(odd, westward, eastward)
        second[cut, :] = jnp.where(odd, eastward, westward)
    for (parts, low) in towards((far_early, far), (near_early, near)):
        at = 0
        for part in parts:
            pl.when(low)(lambda: pack_rows(part, at, fields, 0, SUB))
            pl.when(jnp.logical_not(low))(
                lambda: pack_rows(part, at, fields, rows - SUB, rows - SUB - 1)
            )
            at += part.shape[0] // SUB


def towards(far, near):
    odd = lax.rem(lax.axis_index("tile"), 2) == 1
    return ((far, jnp.logical_not(odd)), (near, odd))


def pack_rows(target, at, fields, main, ext):
    tiles = fields.shape[2] // LANES
    for i in range(target.shape[0] // SUB):
        f, t = divmod(at + i, tiles)
        if f < 4:
            block = fields[f, main : main + SUB, t * LANES : (t + 1) * LANES]
            target[pl.ds(i * SUB, SUB)] = block
        elif t == 0:
            for f in (1, 2):
                flux = fields[3, ext : ext + 1, :] * fields[f, ext : ext + 1, :]
                for t in range(tiles):
                    row = i * SUB + (f - 1) * tiles + t
                    target[row : row + 1] = flux[:, t * LANES : (t + 1) * LANES]


def block_of(parts, at):
    early, late = parts
    count = early.shape[0] // SUB
    if at < count:
        return early[pl.ds(at * SUB, SUB)]
    return late[pl.ds((at - count) * SUB, SUB)]


def sides_of(first, second, cut):
    odd = lax.rem(lax.axis_index("pole"), 2) == 1
    lane = lax.broadcasted_iota(jnp.int32, (SUB, LANES), 1)
    from_first = jnp.logical_xor(lane >= HALF, odd)
    return jnp.where(from_first, first[cut, :], second[cut, :])


def pack_sides_kernel(second, first, far_in, near_in, far, near):
    for target, low in towards(far, near):
        target[pl.ds(target.shape[0] - SUB, SUB)] = pack_sides(second, first, low)


def pack_sides(second, first, low):
    rows = first.shape[0]
    sub = lax.broadcasted_iota(jnp.int32, (SUB, LANES), 0)
    lane = lax.broadcasted_iota(jnp.int32, (SUB, LANES), 1)
    side = jnp.where(
        low,
        sides_of(first, second, pl.ds(0, SUB)),
        sides_of(first, second, pl.ds(rows - SUB, SUB)),
    )
    line = jnp.where(
        low,
        sides_of(first, second, pl.ds(SUB, SUB))[0:1],
        sides_of(first, second, pl.ds(rows - 2 * SUB, SUB))[SUB - 1 : SUB],
    )
    line = jnp.broadcast_to(line, (SUB, LANES))
    low, high = 4 * EDGE, 6 * EDGE
    take = jnp.logical_or(
        jnp.logical_and(lane >= low, lane < high),
        jnp.logical_and(lane >= EAST + low, lane < EAST + high),
    )
    side = jnp.where(jnp.logical_and(take, sub == 0), line, side)
    return side


def pole_sums_kernel(count, scalars, first, second, others, grid, *rest):
    poly, (sums, sol, result) = rest[:ITERS], rest[ITERS:]
    odd = lax.rem(lax.axis_index("pole"), 2) == 1
    lane = lax.broadcasted_iota(jnp.int32, (SUB, LANES), 1)
    blocks = [[scalars[pl.ds(g, SUB)] for g in range(0, count, SUB)]]
    for i, message in enumerate((first, second)):
        low = jnp.logical_xor(lane < HALF, odd if i == 0 else jnp.logical_not(odd))
        part = []
        for g in range(0, count, SUB):
            x = message[pl.ds(g, SUB), :]
            part.append(jnp.where(low, x, turn(x, HALF)))
        blocks.append(part)
    for i in range(others.shape[0]):
        blocks.append([others[i, pl.ds(g, SUB)] for g in range(0, count, SUB)])
    poles = count // 4
    quantity = []
    for q in range(4):
        cut = []
        for block in blocks:
            whole = jnp.concatenate(block, axis=0)
            cut.append(whole[q * poles : (q + 1) * poles])
        quantity.append(jnp.concatenate(cut, axis=0))
    alpha = (quantity[0], quantity[1])
    beta = (quantity[2], quantity[3])
    square = cmul(alpha, alpha)
    shifted = (square[0] + coriolis * coriolis, square[1])
    sigma = ((shifted[0] + centre) / half_width, shifted[1] / half_width)
    rho = [cinv(sigma)]
    for j in range(1, ITERS):
        rho.append(cinv((2.0 * sigma[0] - rho[-1][0], 2.0 * sigma[1] - rho[-1][1])))
    gain = None
    start = []
    for m in range(ITERS):
        if m == 0:
            start.append(cscale(rho[0], 1.0 / half_width))
        else:
            gain = rho[0] if gain is None else cmul(gain, rho[m - 1])
            start.append(cscale(cmul(rho[m], gain), 2.0 / half_width))
    tail = None
    weight = [None] * ITERS
    for m in reversed(range(ITERS)):
        if tail is None:
            weight[m] = start[m]
            tail = (jnp.ones_like(sigma[0]), jnp.zeros_like(sigma[0]))
        else:
            tail = cmul(cmul(rho[m + 1], rho[m]), tail)
            tail = (tail[0] + 1.0, tail[1])
            weight[m] = cmul(start[m], tail)
    inverse_alpha = cinv(alpha)
    inverse_shift = cinv(shifted)
    by_alpha = cmul(beta, inverse_alpha)
    by_shift = cmul(beta, inverse_shift)
    products = {
        "b": beta,
        "b/a": by_alpha,
        "b/s": by_shift,
        "bs/a": cmul(by_alpha, shifted),
        "ba/s": cmul(by_shift, alpha),
        "b/as": cmul(by_alpha, inverse_shift),
    }

    def total(x):
        s = x[0:SUB]
        for i in range(1, x.shape[0] // SUB):
            s = s + x[i * SUB : (i + 1) * SUB]
        for step in (4, 2, 1):
            s = s + pltpu.roll(s, step, 0)
        return s

    names = [("bs/a", "b", "b/a"), ("b", "ba/s", "b/s"), ("b/a", "b/s", "b/as")]
    factor = (1.0, -1.0, -coriolis)
    found = {}
    for m in range(ITERS):
        for name, w in products.items():
            found[name, m] = total(w[0] * weight[m][0] - w[1] * weight[m][1])
        for g in range(3):
            for f in range(3):
                value = found[names[g][f], m]
                sums[(g * 3 + f) * ITERS + m] = value if f == 0 else factor[f] * value
    sums[9 * ITERS] = total(products["ba/s"][0])
    sums[9 * ITERS + 1] = coriolis * total(products["b/s"][0])

    _, (_, above) = towards(None, None)
    rows = sol.shape[1] - 2

    def near_rows(above):
        near, far = side_rows(rows, above), side_rows(rows, not above)
        acc = {}
        for m in range(ITERS):
            add(acc, sums, poly, m, near)
        for m in range(ITERS - 1):
            add(acc, sums, poly, m, [r for k, r in enumerate(far) if known(k) >= m])
        for (g, r), v in acc.items():
            sol[g, r - (REACH - 1)] = v
        inside = sorted(near)[1:-1]
        finish(grid, sums, result, acc, [r for r in inside if REACH <= r < REACH + rows])

    pl.when(above)(lambda: near_rows(True))
    pl.when(jnp.logical_not(above))(lambda: near_rows(False))


def side_rows(rows, above):
    low, high = REACH - 1, REACH + rows
    return [low + k if above else high - k for k in range(rows // 2 + 1)]


def known(k):
    return max(min(ITERS - 2, k - 2), -1)


def add(acc, sums, poly, m, rows, values=None):
    for f in range(3):
        if not rows:
            return
        value = {r: poly[m][f, r] if values is None else values[f, r] for r in rows}
        for g in range(3):
            c = sums[(g * 3 + f) * ITERS + m]
            for r in rows:
                acc[g, r] = acc[g, r] + c * value[r] if (g, r) in acc else c * value[r]


def finish(grid, sums, result, acc, span):
    push = sums[9 * ITERS]
    lift = sums[9 * ITERS + 1]
    for r in span:
        u, v = cell(grid, 1, r), cell(grid, 2, r)
        at = pl.ds((r - REACH) * SUB, SUB)
        result[0, at] = acc[0, r]
        east = 0.5 * (acc[1, r + 1] - acc[1, r - 1])
        north = 0.5 * (right(acc[2, r]) - left(acc[2, r]))
        result[1, at] = (push * u + lift * v) - (east + coriolis * north)
        east = 0.5 * (acc[2, r + 1] - acc[2, r - 1])
        north = 0.5 * (right(acc[1, r]) - left(acc[1, r]))
        result[2, at] = (push * v - lift * u) + (coriolis * east - north)


def strips_of(tiles, side):
    lane = lax.broadcasted_iota(jnp.int32, (SUB, LANES), 1)
    up = [turn(tile, SIDE) for tile in tiles]
    down = [turn(tile, -SIDE) for tile in tiles]
    out = []
    for q in range(len(tiles)):
        out.append(jnp.where(lane < SIDE, up[q - 1] if q else side, up[q]))
        after = down[q + 1] if q + 1 < len(tiles) else side
        out.append(jnp.where(lane < LANES - SIDE, down[q], after))
    return out


def lay(grid, cut, side, at, stride):
    for s, strip in enumerate(strips_of(cut, side)):
        grid[pl.Slice(at * SUB + s, SUB, stride * SUB), :] = strip


def place(side, f):
    return turn(side, SIDE - EDGE - EDGE * f)


def lay_halo(grid, halo, side, main, ext):
    lane = lax.broadcasted_iota(jnp.int32, (SUB, LANES), 1)
    sub = lax.broadcasted_iota(jnp.int32, (SUB, LANES), 0)
    tiles = SUB // 2
    for f in range(4):
        cut = [block_of(halo, f * tiles + t) for t in range(tiles)]
        lay(grid, cut, place(side, f), main * 4 + f, 4)
    line = jnp.broadcast_to(side[0:1], (SUB, LANES))
    side = jnp.where(sub < tiles, place(line, 4), place(line, 5))
    block = block_of(halo, 4 * tiles)
    up, down = turn(block, SIDE), turn(block, -SIDE)
    before = jnp.where(sub % tiles == 0, side, pltpu.roll(up, 1, 0))
    after = jnp.where(sub % tiles == tiles - 1, side, pltpu.roll(down, SUB - 1, 0))
    even = jnp.where(lane < SIDE, before, up)
    odd = jnp.where(lane < LANES - SIDE, down, after)
    for f in (1, 2):
        at = (ext * 4 + f) * SUB
        cut = slice((f - 1) * tiles, f * tiles)
        grid[pl.Slice(at, tiles, 2), :] = even[cut]
        grid[pl.Slice(at + 1, tiles, 2), :] = odd[cut]


def cell(grid, f, r):
    return grid[pl.ds(pl.multiple_of((r * 4 + f) * SUB, SUB), SUB), :]


def left(x):
    return pltpu.roll(x, 1, 1)


def right(x):
    return pltpu.roll(x, LANES - 1, 1)


def prepare(grid, poly, coef, start, count):
    flux_east = [None] * 3
    flux_north = [None] * 3
    depths = [None] * 2
    across = None
    for k in range(count + 2):
        r = start + k
        h = cell(grid, 3, r)
        flux_east = flux_east[1:] + [h * cell(grid, 1, r)]
        flux_north = flux_north[1:] + [h * cell(grid, 2, r)]
        depths = depths[1:] + [h]
        if k >= 1:
            before, across = across, 0.125 * (depths[0] + depths[1])
            coef[0, r - 1] = across
        if k >= 2:
            c = r - 1
            north = 0.125 * (depths[0] + right(depths[0]))
            south = 0.125 * (depths[0] + left(depths[0]))
            coef[1, c] = north
            coef[2, c] = south
            coef[3, c] = 2.0 - ((across + before) + (north + south))
            east_slope = flux_east[2] - flux_east[0]
            north_slope = right(flux_north[1]) - left(flux_north[1])
            poly[0][1, c] = 0.5 * (east_slope + north_slope)
            east_slope = flux_north[2] - flux_north[0]
            north_slope = right(flux_east[1]) - left(flux_east[1])
            poly[0][2, c] = 0.5 * (east_slope - north_slope)
            poly[0][0, c] = cell(grid, 0, c)


def sweep(poly, coef, m, start, count, upwards=False):
    step = -1 if upwards else 1
    order = range(start, start + count)[::step]
    back = [poly[m][f, order[0] - step] for f in range(3)]
    here = [poly[m][f, order[0]] for f in range(3)]
    found = {}
    for r in order:
        north, south, diag = coef[1, r], coef[2, r], coef[3, r]
        above, below = coef[0, r], coef[0, r - 1]
        ahead = [poly[m][f, r + step] for f in range(3)]
        for f in range(3):
            up, down = (back, ahead) if upwards else (ahead, back)
            value = diag * here[f]
            if m > 0:
                value = value - poly[m - 1][f, r]
            value = value + above * up[f]
            value = value + below * down[f]
            value = value + north * right(here[f])
            value = value + south * left(here[f])
            value = 0.5 * value if m == 0 else value
            poly[m + 1][f, r] = value
            found[f, r] = value
        back, here = here, ahead
    return found


def inner_kernel(fields, first, second, grid, coef, *poly):
    rows = fields.shape[1]
    for g in range(rows // SUB):
        side = sides_of(first, second, pl.ds(g * SUB, SUB))
        for f in range(4):
            cut = [
                fields[f, pl.ds(g * SUB, SUB), pl.ds(t * LANES, LANES)]
                for t in range(fields.shape[2] // LANES)
            ]
            lay(grid, cut, place(side, f), (REACH + g * SUB) * 4 + f, 4)
    prepare(grid, poly, coef, REACH, rows - 2)
    for m in range(ITERS - 1):
        if rows - 4 - 2 * m > 0:
            sweep(poly, coef, m, REACH + 2 + m, rows - 4 - 2 * m)


def one_side(halo, side, above, grid, coef, poly, each):
    below = coef.shape[1] - REACH
    main, ext, start = (1, 0, 0) if above else (below, below + SUB, below - 2)
    grid[pl.ds((ext * 4 + 3) * SUB, SUB), :] = jnp.ones((SUB, LANES), jnp.float32)
    lay_halo(grid, halo, side, main, ext)
    prepare(grid, poly, coef, start, REACH)
    each(0, None)
    for m in range(ITERS - 1):
        found = sweep(poly, coef, m, 2 + m if above else below - 2 - m, REACH, above)
        each(m + 1, found)


def mid_kernel(near_early, near, *rest):
    grid, coef, *poly = rest[len(rest) // 2 :]
    _, (_, above) = towards(None, None)
    side = near[pl.ds(near.shape[0] - SUB, SUB)]
    for way, here in ((True, above), (False, jnp.logical_not(above))):
        pl.when(here)(
            lambda: one_side((near_early, near), side, way, grid, coef, poly, lambda m, found: None)
        )


def outer_kernel(far_early, far, sums, *rest):
    *rest, lines, done = rest
    out, grid, coef, sol, result, *poly = rest[len(rest) // 2 :]
    rows, columns = out.shape[1:]
    lane = lax.broadcasted_iota(jnp.int32, (SUB, LANES), 1)
    (_, above), _ = towards(None, None)

    def far_rows(above):
        side = far[pl.ds(far.shape[0] - SUB, SUB)]
        whole = side_rows(rows, above)
        inside = 1 if above else -1
        edges = [whole[-1] + inside, whole[-1] + 2 * inside]
        acc = {}
        for r in edges + [r for k, r in enumerate(whole) if known(k) >= 0]:
            for g in range(3):
                acc[g, r] = sol[g, r - (REACH - 1)]

        def each(m, found):
            part = [r for k, r in enumerate(whole) if known(k) < m]
            if found is not None:
                held = [r for r in part if (0, r) in found]
                add(acc, sums, poly, m, held, found)
                part = [r for r in part if r not in held]
            add(acc, sums, poly, m, part)

        one_side((far_early, far), side, above, grid, coef, poly, each)
        span = [r for r in whole + edges[:1] if REACH <= r < REACH + rows]
        finish(grid, sums, result, acc, span)

    pl.when(above)(lambda: far_rows(True))
    pl.when(jnp.logical_not(above))(lambda: far_rows(False))

    moves = []
    for k in range(3):
        for g in range(rows // SUB):
            cut = pl.ds(g * SUB, SUB)
            for t in range(columns // LANES):
                one = result[k, pl.Slice(g * SUB * SUB + 2 * t, SUB, SUB), :]
                two = result[k, pl.Slice(g * SUB * SUB + 2 * t + 1, SUB, SUB), :]
                joined = jnp.where(lane < HALF, turn(one, -SIDE), turn(two, SIDE))
                lines[k, cut, pl.ds(t * LANES, LANES)] = joined
            move = pltpu.make_async_copy(lines.at[k, cut], out.at[k, cut], done.at[k, g])
            move.start()
            moves.append(move)
    for move in moves:
        move.wait()


def shards(state, depth, pole_real, pole_imag, pole_weight):
    rows, columns = depth.shape
    poles = pole_real.shape[0]
    vmem = pl.BlockSpec(memory_space=pltpu.VMEM)
    small = pltpu.CompilerParams(vmem_limit_bytes=GRANT)

    def f32(*shape):
        return jax.ShapeDtypeStruct(shape, jnp.float32)

    given = [
        pltpu.with_memory_space_constraint(x, pltpu.HBM)
        for x in (state, depth, pole_real, pole_imag, pole_weight)
    ]
    hbm = pl.BlockSpec(memory_space=pltpu.HBM)
    message = pltpu.VMEM((rows, LANES), jnp.float32)
    blocks = 4 * columns // LANES + 2
    half = blocks // 2 * SUB
    parts = (half + SUB + 4, half, half + SUB, half - SUB)
    wide = max(4 * poles, half)
    fields, first, second, scalars, far_early, far, near_early, near = pl.pallas_call(
        pack_columns_kernel,
        out_shape=(
            pltpu.VMEM((4, rows, columns), jnp.float32),
            message,
            message,
            pltpu.VMEM((wide, LANES), jnp.float32),
            *(pltpu.VMEM((part, LANES), jnp.float32) for part in parts),
        ),
        in_specs=[hbm] * 5,
        out_specs=(vmem,) * 8,
        scratch_shapes=[
            pltpu.SMEM(pole_real.shape, jnp.float32),
            pltpu.SMEM(pole_imag.shape, jnp.float32),
            pltpu.SMEM(pole_weight.shape, jnp.float32),
            pltpu.SemaphoreType.DMA((5,)),
        ],
        compiler_params=small,
        name="pack_columns",
    )(*given)
    second = swap(second, "pole", 1)
    first = swap(first, "pole", 0)
    far, near = pl.pallas_call(
        pack_sides_kernel,
        out_shape=(f32(*far.shape), f32(*near.shape)),
        in_specs=[vmem] * 4,
        out_specs=(vmem, vmem),
        input_output_aliases={2: 0, 3: 1},
        compiler_params=small,
        name="pack_sides",
    )(second, first, far, near)
    far_early = swap(far_early, "tile", 1)
    far = swap(far, "tile", 1)
    near_early = swap(near_early, "tile", 0)
    near = swap(near, "tile", 0)
    count = lax.axis_size("pole")
    others = jnp.stack([shift(scalars, "pole", step) for step in range(2, count - 1)])
    height = rows + 2 * REACH
    grid = f32(height * 4 * SUB, LANES)
    poly = [f32(3, height, SUB, LANES)] * ITERS
    coef = f32(4, height, SUB, LANES)
    sol = f32(3, rows + 2, SUB, LANES)
    result = f32(3, rows * SUB, LANES)
    state_of = (grid, coef, *poly)
    cost = pl.CostEstimate(
        flops=10 * ITERS * rows * SUB * LANES,
        bytes_accessed=4 * SUB * LANES * rows * (4 + 2 * ITERS + 2),
        transcendentals=0,
    )
    held = pl.pallas_call(
        inner_kernel,
        out_shape=state_of,
        in_specs=[vmem] * 3,
        out_specs=(vmem,) * len(state_of),
        compiler_params=small,
        cost_estimate=cost,
        name="inner",
    )(fields, first, second)
    held = pl.pallas_call(
        mid_kernel,
        out_shape=state_of,
        in_specs=[vmem] * (2 + len(state_of)),
        out_specs=(vmem,) * len(state_of),
        input_output_aliases={2 + i: i for i in range(len(state_of))},
        compiler_params=small,
        cost_estimate=cost,
        name="mid",
    )(near_early, near, *held)
    grid_held, coef_held, *poly_held = held
    sums, *part = pl.pallas_call(
        functools.partial(pole_sums_kernel, 4 * poles),
        out_shape=(f32(9 * ITERS + 2, SUB, LANES), sol, result),
        in_specs=[vmem] * (5 + ITERS),
        out_specs=(vmem,) * 3,
        compiler_params=small,
        name="pole_sums",
    )(scalars, first, second, others, grid_held, *poly_held)
    kept = (grid, coef, sol, result, *poly)
    return pl.pallas_call(
        outer_kernel,
        out_shape=(f32(*state.shape), *kept),
        in_specs=[vmem] * (3 + len(kept)),
        out_specs=(hbm, *(vmem,) * len(kept)),
        scratch_shapes=[
            pltpu.VMEM(state.shape, jnp.float32),
            pltpu.SemaphoreType.DMA((3, rows // SUB)),
        ],
        input_output_aliases={3 + i: 1 + i for i in range(len(kept))},
        compiler_params=small,
        name="outer",
    )(far_early, far, sums, grid_held, coef_held, *part, *poly_held)[0]


def solution(mesh):
    return jax.shard_map(
        shards,
        mesh=mesh,
        in_specs=(
            P(None, "tile", "pole"),
            P("tile", "pole"),
            P("pole"),
            P("pole"),
            P(None, "pole"),
        ),
        out_specs=P(None, "tile", "pole"),
        check_vma=False,
    )
```

```python
import functools

import jax
import jax.numpy as jnp
from jax import lax
from jax.experimental import pallas as pl
from jax.experimental.pallas import tpu as pltpu
from jax.sharding import PartitionSpec as P

ITERS = 8
REACH = ITERS + 1
SUB = 8
LANES = 128
HALF = LANES // 2
SIDE = 32
EDGE = REACH
EAST = HALF + EDGE
GRANT = 16 * 1024 * 1024

coriolis = 0.7
centre = 8.0
half_width = 8.0


def pairs(count, phase):
    swap = []
    for i in range(phase, count + phase, 2):
        a, b = i % count, (i + 1) % count
        swap += [(a, b), (b, a)]
    return swap


def swap(block, axis, phase):
    return lax.ppermute(block, axis, pairs(lax.axis_size(axis), phase))


def shift(block, axis, step):
    count = lax.axis_size(axis)
    return lax.ppermute(block, axis, [(i, (i + step) % count) for i in range(count)])


def turn(x, lanes):
    return pltpu.roll(x, lanes % LANES, 1) if lanes % LANES else x


def cmul(a, b):
    return (a[0] * b[0] - a[1] * b[1], a[0] * b[1] + a[1] * b[0])


def cinv(a):
    norm = 1.0 / (a[0] * a[0] + a[1] * a[1])
    return (a[0] * norm, -a[1] * norm)


def cscale(a, factor):
    return (a[0] * factor, a[1] * factor)


def pack_columns_kernel(
    state, depth, real, imag, weight, fields, first, second, real_in, imag_in, weight_in, done
):
    moves = [
        pltpu.make_async_copy(depth, fields.at[3], done.at[0]),
        pltpu.make_async_copy(state, fields.at[pl.ds(0, 3)], done.at[1]),
        pltpu.make_async_copy(real, real_in, done.at[2]),
        pltpu.make_async_copy(imag, imag_in, done.at[3]),
        pltpu.make_async_copy(weight, weight_in, done.at[4]),
    ]
    for move in moves:
        move.start()
    for move in moves:
        move.wait()
    odd = lax.rem(lax.axis_index("pole"), 2) == 1
    rows, columns = fields.shape[1:]
    lane = lax.broadcasted_iota(jnp.int32, (SUB, LANES), 1)
    sub = lax.broadcasted_iota(jnp.int32, (SUB, LANES), 0)
    poles = real.shape[0]
    values = [real_in[i] for i in range(poles)] + [imag_in[i] for i in range(poles)]
    values += [weight_in[0, i] for i in range(poles)] + [weight_in[1, i] for i in range(poles)]
    for g in range(rows // SUB):
        cut = pl.ds(g * SUB, SUB)
        west = [fields[f, cut, 0:LANES] for f in range(4)]
        east = [fields[f, cut, columns - LANES : columns] for f in range(4)]
        west += [west[3] * west[1], west[3] * west[2]]
        east += [east[3] * east[1], east[3] * east[2]]
        rest = jnp.zeros((SUB, LANES), jnp.float32)
        for i, value in enumerate(values[g * SUB : (g + 1) * SUB]):
            rest = jnp.where(sub == i, value, rest)
        eastward = rest
        westward = rest
        for f in range(6):
            low, high = EDGE * f, EDGE * (f + 1)
            take = jnp.logical_and(lane >= low, lane < high)
            eastward = jnp.where(take, turn(east[f], low + EDGE), eastward)
            take = jnp.logical_and(lane >= EAST + low, lane < EAST + high)
            westward = jnp.where(take, turn(west[f], EAST + low), westward)
        first[cut, :] = jnp.where(odd, westward, eastward)
        second[cut, :] = jnp.where(odd, eastward, westward)


def pack_rows_kernel(count, fields, second, first, far_early, far, near_early, near, scalars):
    rows = fields.shape[1]
    for parts, low in towards((far_early, far), (near_early, near)):
        at = 0
        for part in parts:
            pl.when(low)(lambda: pack_rows(part, at, fields, 0, SUB))
            pl.when(jnp.logical_not(low))(
                lambda: pack_rows(part, at, fields, rows - SUB, rows - SUB - 1)
            )
            at += part.shape[0] // SUB
    odd = lax.rem(lax.axis_index("pole"), 2) == 1
    lane = lax.broadcasted_iota(jnp.int32, (SUB, LANES), 1)
    from_first = jnp.logical_xor(lane >= HALF, odd)
    for g in range(0, scalars.shape[0], SUB):
        if g < count:
            block = jnp.where(from_first, first[pl.ds(g, SUB)], second[pl.ds(g, SUB)])
        else:
            block = jnp.zeros((SUB, LANES), jnp.float32)
        scalars[pl.ds(g, SUB)] = block


def towards(far, near):
    odd = lax.rem(lax.axis_index("tile"), 2) == 1
    return ((far, jnp.logical_not(odd)), (near, odd))


def pack_rows(target, at, fields, main, ext):
    tiles = fields.shape[2] // LANES
    for i in range(target.shape[0] // SUB):
        f, t = divmod(at + i, tiles)
        if f < 4:
            block = fields[f, main : main + SUB, t * LANES : (t + 1) * LANES]
            target[pl.ds(i * SUB, SUB)] = block
        elif t == 0:
            for f in (1, 2):
                flux = fields[3, ext : ext + 1, :] * fields[f, ext : ext + 1, :]
                for t in range(tiles):
                    row = i * SUB + (f - 1) * tiles + t
                    target[row : row + 1] = flux[:, t * LANES : (t + 1) * LANES]


def block_of(parts, at):
    early, late = parts
    count = early.shape[0] // SUB
    if at < count:
        return early[pl.ds(at * SUB, SUB)]
    return late[pl.ds((at - count) * SUB, SUB)]


def sides_of(first, second, cut):
    odd = lax.rem(lax.axis_index("pole"), 2) == 1
    lane = lax.broadcasted_iota(jnp.int32, (SUB, LANES), 1)
    from_first = jnp.logical_xor(lane >= HALF, odd)
    return jnp.where(from_first, first[cut, :], second[cut, :])


def pack_sides_kernel(second, first, far_in, near_in, far, near):
    for target, low in towards(far, near):
        target[pl.ds(target.shape[0] - SUB, SUB)] = pack_sides(second, first, low)


def pack_sides(second, first, low):
    rows = first.shape[0]
    sub = lax.broadcasted_iota(jnp.int32, (SUB, LANES), 0)
    lane = lax.broadcasted_iota(jnp.int32, (SUB, LANES), 1)
    side = jnp.where(
        low,
        sides_of(first, second, pl.ds(0, SUB)),
        sides_of(first, second, pl.ds(rows - SUB, SUB)),
    )
    line = jnp.where(
        low,
        sides_of(first, second, pl.ds(SUB, SUB))[0:1],
        sides_of(first, second, pl.ds(rows - 2 * SUB, SUB))[SUB - 1 : SUB],
    )
    line = jnp.broadcast_to(line, (SUB, LANES))
    low, high = 4 * EDGE, 6 * EDGE
    take = jnp.logical_or(
        jnp.logical_and(lane >= low, lane < high),
        jnp.logical_and(lane >= EAST + low, lane < EAST + high),
    )
    side = jnp.where(jnp.logical_and(take, sub == 0), line, side)
    return side


def pole_sums_kernel(count, scalars, first, second, others, grid, *rest):
    poly, (sums, sol, result) = rest[:ITERS], rest[ITERS:]
    odd = lax.rem(lax.axis_index("pole"), 2) == 1
    lane = lax.broadcasted_iota(jnp.int32, (SUB, LANES), 1)
    blocks = [[scalars[pl.ds(g, SUB)] for g in range(0, count, SUB)]]
    for i, message in enumerate((first, second)):
        low = jnp.logical_xor(lane < HALF, odd if i == 0 else jnp.logical_not(odd))
        part = []
        for g in range(0, count, SUB):
            x = message[pl.ds(g, SUB), :]
            part.append(jnp.where(low, x, turn(x, HALF)))
        blocks.append(part)
    for i in range(others.shape[0]):
        blocks.append([others[i, pl.ds(g, SUB)] for g in range(0, count, SUB)])
    poles = count // 4
    quantity = []
    for q in range(4):
        cut = []
        for block in blocks:
            whole = jnp.concatenate(block, axis=0)
            cut.append(whole[q * poles : (q + 1) * poles])
        quantity.append(jnp.concatenate(cut, axis=0))
    alpha = (quantity[0], quantity[1])
    beta = (quantity[2], quantity[3])
    square = cmul(alpha, alpha)
    shifted = (square[0] + coriolis * coriolis, square[1])
    sigma = ((shifted[0] + centre) / half_width, shifted[1] / half_width)
    rho = [cinv(sigma)]
    for j in range(1, ITERS):
        rho.append(cinv((2.0 * sigma[0] - rho[-1][0], 2.0 * sigma[1] - rho[-1][1])))
    gain = None
    start = []
    for m in range(ITERS):
        if m == 0:
            start.append(cscale(rho[0], 1.0 / half_width))
        else:
            gain = rho[0] if gain is None else cmul(gain, rho[m - 1])
            start.append(cscale(cmul(rho[m], gain), 2.0 / half_width))
    tail = None
    weight = [None] * ITERS
    for m in reversed(range(ITERS)):
        if tail is None:
            weight[m] = start[m]
            tail = (jnp.ones_like(sigma[0]), jnp.zeros_like(sigma[0]))
        else:
            tail = cmul(cmul(rho[m + 1], rho[m]), tail)
            tail = (tail[0] + 1.0, tail[1])
            weight[m] = cmul(start[m], tail)
    inverse_alpha = cinv(alpha)
    inverse_shift = cinv(shifted)
    by_alpha = cmul(beta, inverse_alpha)
    by_shift = cmul(beta, inverse_shift)
    products = {
        "b": beta,
        "b/a": by_alpha,
        "b/s": by_shift,
        "bs/a": cmul(by_alpha, shifted),
        "ba/s": cmul(by_shift, alpha),
        "b/as": cmul(by_alpha, inverse_shift),
    }

    def total(x):
        s = x[0:SUB]
        for i in range(1, x.shape[0] // SUB):
            s = s + x[i * SUB : (i + 1) * SUB]
        for step in (4, 2, 1):
            s = s + pltpu.roll(s, step, 0)
        return s

    names = [("bs/a", "b", "b/a"), ("b", "ba/s", "b/s"), ("b/a", "b/s", "b/as")]
    factor = (1.0, -1.0, -coriolis)
    found = {}
    for m in range(ITERS):
        for name, w in products.items():
            found[name, m] = total(w[0] * weight[m][0] - w[1] * weight[m][1])
        for g in range(3):
            for f in range(3):
                value = found[names[g][f], m]
                sums[(g * 3 + f) * ITERS + m] = value if f == 0 else factor[f] * value
    sums[9 * ITERS] = total(products["ba/s"][0])
    sums[9 * ITERS + 1] = coriolis * total(products["b/s"][0])

    _, (_, above) = towards(None, None)
    rows = sol.shape[1] - 2

    def near_rows(above):
        near, far = side_rows(rows, above), side_rows(rows, not above)
        acc = {}
        for m in range(ITERS):
            add(acc, sums, poly, m, near)
        for m in range(ITERS - 1):
            add(acc, sums, poly, m, [r for k, r in enumerate(far) if known(k) >= m])
        for (g, r), v in acc.items():
            sol[g, r - (REACH - 1)] = v
        inside = sorted(near)[1:-1]
        finish(grid, sums, result, acc, [r for r in inside if REACH <= r < REACH + rows])

    pl.when(above)(lambda: near_rows(True))
    pl.when(jnp.logical_not(above))(lambda: near_rows(False))


def side_rows(rows, above):
    low, high = REACH - 1, REACH + rows
    return [low + k if above else high - k for k in range(rows // 2 + 1)]


def known(k):
    return max(min(ITERS - 2, k - 2), -1)


def add(acc, sums, poly, m, rows, values=None):
    for f in range(3):
        if not rows:
            return
        value = {r: poly[m][f, r] if values is None else values[f, r] for r in rows}
        for g in range(3):
            c = sums[(g * 3 + f) * ITERS + m]
            for r in rows:
                acc[g, r] = acc[g, r] + c * value[r] if (g, r) in acc else c * value[r]


def finish(grid, sums, result, acc, span):
    push = sums[9 * ITERS]
    lift = sums[9 * ITERS + 1]
    for r in span:
        u, v = cell(grid, 1, r), cell(grid, 2, r)
        at = pl.ds((r - REACH) * SUB, SUB)
        result[0, at] = acc[0, r]
        east = 0.5 * (acc[1, r + 1] - acc[1, r - 1])
        north = 0.5 * (right(acc[2, r]) - left(acc[2, r]))
        result[1, at] = (push * u + lift * v) - (east + coriolis * north)
        east = 0.5 * (acc[2, r + 1] - acc[2, r - 1])
        north = 0.5 * (right(acc[1, r]) - left(acc[1, r]))
        result[2, at] = (push * v - lift * u) + (coriolis * east - north)


def strips_of(tiles, side):
    lane = lax.broadcasted_iota(jnp.int32, (SUB, LANES), 1)
    up = [turn(tile, SIDE) for tile in tiles]
    down = [turn(tile, -SIDE) for tile in tiles]
    out = []
    for q in range(len(tiles)):
        out.append(jnp.where(lane < SIDE, up[q - 1] if q else side, up[q]))
        after = down[q + 1] if q + 1 < len(tiles) else side
        out.append(jnp.where(lane < LANES - SIDE, down[q], after))
    return out


def lay(grid, cut, side, at, stride):
    for s, strip in enumerate(strips_of(cut, side)):
        grid[pl.Slice(at * SUB + s, SUB, stride * SUB), :] = strip


def place(side, f):
    return turn(side, SIDE - EDGE - EDGE * f)


def lay_halo(grid, halo, side, main, ext):
    lane = lax.broadcasted_iota(jnp.int32, (SUB, LANES), 1)
    sub = lax.broadcasted_iota(jnp.int32, (SUB, LANES), 0)
    tiles = SUB // 2
    for f in range(4):
        cut = [block_of(halo, f * tiles + t) for t in range(tiles)]
        lay(grid, cut, place(side, f), main * 4 + f, 4)
    line = jnp.broadcast_to(side[0:1], (SUB, LANES))
    side = jnp.where(sub < tiles, place(line, 4), place(line, 5))
    block = block_of(halo, 4 * tiles)
    up, down = turn(block, SIDE), turn(block, -SIDE)
    before = jnp.where(sub % tiles == 0, side, pltpu.roll(up, 1, 0))
    after = jnp.where(sub % tiles == tiles - 1, side, pltpu.roll(down, SUB - 1, 0))
    even = jnp.where(lane < SIDE, before, up)
    odd = jnp.where(lane < LANES - SIDE, down, after)
    for f in (1, 2):
        at = (ext * 4 + f) * SUB
        cut = slice((f - 1) * tiles, f * tiles)
        grid[pl.Slice(at, tiles, 2), :] = even[cut]
        grid[pl.Slice(at + 1, tiles, 2), :] = odd[cut]


def cell(grid, f, r):
    return grid[pl.ds(pl.multiple_of((r * 4 + f) * SUB, SUB), SUB), :]


def left(x):
    return pltpu.roll(x, 1, 1)


def right(x):
    return pltpu.roll(x, LANES - 1, 1)


def prepare(grid, poly, coef, start, count):
    flux_east = [None] * 3
    flux_north = [None] * 3
    depths = [None] * 2
    across = None
    for k in range(count + 2):
        r = start + k
        h = cell(grid, 3, r)
        flux_east = flux_east[1:] + [h * cell(grid, 1, r)]
        flux_north = flux_north[1:] + [h * cell(grid, 2, r)]
        depths = depths[1:] + [h]
        if k >= 1:
            before, across = across, 0.125 * (depths[0] + depths[1])
            coef[0, r - 1] = across
        if k >= 2:
            c = r - 1
            north = 0.125 * (depths[0] + right(depths[0]))
            south = 0.125 * (depths[0] + left(depths[0]))
            coef[1, c] = north
            coef[2, c] = south
            coef[3, c] = 2.0 - ((across + before) + (north + south))
            east_slope = flux_east[2] - flux_east[0]
            north_slope = right(flux_north[1]) - left(flux_north[1])
            poly[0][1, c] = 0.5 * (east_slope + north_slope)
            east_slope = flux_north[2] - flux_north[0]
            north_slope = right(flux_east[1]) - left(flux_east[1])
            poly[0][2, c] = 0.5 * (east_slope - north_slope)
            poly[0][0, c] = cell(grid, 0, c)


def sweep(poly, coef, m, start, count, upwards=False):
    step = -1 if upwards else 1
    order = range(start, start + count)[::step]
    back = [poly[m][f, order[0] - step] for f in range(3)]
    here = [poly[m][f, order[0]] for f in range(3)]
    found = {}
    for r in order:
        north, south, diag = coef[1, r], coef[2, r], coef[3, r]
        above, below = coef[0, r], coef[0, r - 1]
        ahead = [poly[m][f, r + step] for f in range(3)]
        for f in range(3):
            up, down = (back, ahead) if upwards else (ahead, back)
            value = diag * here[f]
            if m > 0:
                value = value - poly[m - 1][f, r]
            value = value + above * up[f]
            value = value + below * down[f]
            value = value + north * right(here[f])
            value = value + south * left(here[f])
            value = 0.5 * value if m == 0 else value
            poly[m + 1][f, r] = value
            found[f, r] = value
        back, here = here, ahead
    return found


def inner_kernel(fields, first, second, grid, coef, *poly):
    rows = fields.shape[1]
    for g in range(rows // SUB):
        side = sides_of(first, second, pl.ds(g * SUB, SUB))
        for f in range(4):
            cut = [
                fields[f, pl.ds(g * SUB, SUB), pl.ds(t * LANES, LANES)]
                for t in range(fields.shape[2] // LANES)
            ]
            lay(grid, cut, place(side, f), (REACH + g * SUB) * 4 + f, 4)
    prepare(grid, poly, coef, REACH, rows - 2)
    for m in range(ITERS - 1):
        if rows - 4 - 2 * m > 0:
            sweep(poly, coef, m, REACH + 2 + m, rows - 4 - 2 * m)


def one_side(halo, side, above, grid, coef, poly, each):
    below = coef.shape[1] - REACH
    main, ext, start = (1, 0, 0) if above else (below, below + SUB, below - 2)
    grid[pl.ds((ext * 4 + 3) * SUB, SUB), :] = jnp.ones((SUB, LANES), jnp.float32)
    lay_halo(grid, halo, side, main, ext)
    prepare(grid, poly, coef, start, REACH)
    each(0, None)
    for m in range(ITERS - 1):
        found = sweep(poly, coef, m, 2 + m if above else below - 2 - m, REACH, above)
        each(m + 1, found)


def mid_kernel(near_early, near, *rest):
    grid, coef, *poly = rest[len(rest) // 2 :]
    _, (_, above) = towards(None, None)
    side = near[pl.ds(near.shape[0] - SUB, SUB)]
    for way, here in ((True, above), (False, jnp.logical_not(above))):
        pl.when(here)(
            lambda: one_side((near_early, near), side, way, grid, coef, poly, lambda m, found: None)
        )


def outer_kernel(far_early, far, sums, *rest):
    *rest, lines, done = rest
    out, grid, coef, sol, result, *poly = rest[len(rest) // 2 :]
    rows, columns = out.shape[1:]
    lane = lax.broadcasted_iota(jnp.int32, (SUB, LANES), 1)
    (_, above), _ = towards(None, None)

    def far_rows(above):
        side = far[pl.ds(far.shape[0] - SUB, SUB)]
        whole = side_rows(rows, above)
        inside = 1 if above else -1
        edges = [whole[-1] + inside, whole[-1] + 2 * inside]
        acc = {}
        for r in edges + [r for k, r in enumerate(whole) if known(k) >= 0]:
            for g in range(3):
                acc[g, r] = sol[g, r - (REACH - 1)]

        def each(m, found):
            part = [r for k, r in enumerate(whole) if known(k) < m]
            if found is not None:
                held = [r for r in part if (0, r) in found]
                add(acc, sums, poly, m, held, found)
                part = [r for r in part if r not in held]
            add(acc, sums, poly, m, part)

        one_side((far_early, far), side, above, grid, coef, poly, each)
        span = [r for r in whole + edges[:1] if REACH <= r < REACH + rows]
        finish(grid, sums, result, acc, span)

    pl.when(above)(lambda: far_rows(True))
    pl.when(jnp.logical_not(above))(lambda: far_rows(False))

    moves = []
    for k in range(3):
        for g in range(rows // SUB):
            cut = pl.ds(g * SUB, SUB)
            for t in range(columns // LANES):
                one = result[k, pl.Slice(g * SUB * SUB + 2 * t, SUB, SUB), :]
                two = result[k, pl.Slice(g * SUB * SUB + 2 * t + 1, SUB, SUB), :]
                joined = jnp.where(lane < HALF, turn(one, -SIDE), turn(two, SIDE))
                lines[k, cut, pl.ds(t * LANES, LANES)] = joined
            move = pltpu.make_async_copy(lines.at[k, cut], out.at[k, cut], done.at[k, g])
            move.start()
            moves.append(move)
    for move in moves:
        move.wait()


def shards(state, depth, pole_real, pole_imag, pole_weight):
    rows, columns = depth.shape
    poles = pole_real.shape[0]
    vmem = pl.BlockSpec(memory_space=pltpu.VMEM)
    small = pltpu.CompilerParams(vmem_limit_bytes=GRANT)

    def f32(*shape):
        return jax.ShapeDtypeStruct(shape, jnp.float32)

    given = [
        pltpu.with_memory_space_constraint(x, pltpu.HBM)
        for x in (state, depth, pole_real, pole_imag, pole_weight)
    ]
    hbm = pl.BlockSpec(memory_space=pltpu.HBM)
    message = pltpu.VMEM((rows, LANES), jnp.float32)
    fields, first, second = pl.pallas_call(
        pack_columns_kernel,
        out_shape=(pltpu.VMEM((4, rows, columns), jnp.float32), message, message),
        in_specs=[hbm] * 5,
        out_specs=(vmem,) * 3,
        scratch_shapes=[
            pltpu.SMEM(pole_real.shape, jnp.float32),
            pltpu.SMEM(pole_imag.shape, jnp.float32),
            pltpu.SMEM(pole_weight.shape, jnp.float32),
            pltpu.SemaphoreType.DMA((5,)),
        ],
        compiler_params=small,
        name="pack_columns",
    )(*given)
    blocks = 4 * columns // LANES + 2
    half = blocks // 2 * SUB
    parts = (half + SUB + 4, half, half + SUB, half - SUB, max(4 * poles, half))
    far_early, far, near_early, near, scalars = pl.pallas_call(
        functools.partial(pack_rows_kernel, 4 * poles),
        out_shape=tuple(f32(part, LANES) for part in parts),
        in_specs=[vmem] * 3,
        out_specs=(vmem,) * 5,
        compiler_params=small,
        name="pack_rows",
    )(fields, second, first)
    second = swap(second, "pole", 1)
    first = swap(first, "pole", 0)
    far, near = pl.pallas_call(
        pack_sides_kernel,
        out_shape=(f32(*far.shape), f32(*near.shape)),
        in_specs=[vmem] * 4,
        out_specs=(vmem, vmem),
        input_output_aliases={2: 0, 3: 1},
        compiler_params=small,
        name="pack_sides",
    )(second, first, far, near)
    far_early = swap(far_early, "tile", 1)
    far = swap(far, "tile", 1)
    near_early = swap(near_early, "tile", 0)
    near = swap(near, "tile", 0)
    count = lax.axis_size("pole")
    others = jnp.stack([shift(scalars, "pole", step) for step in range(2, count - 1)])
    height = rows + 2 * REACH
    grid = f32(height * 4 * SUB, LANES)
    poly = [f32(3, height, SUB, LANES)] * ITERS
    coef = f32(4, height, SUB, LANES)
    sol = f32(3, rows + 2, SUB, LANES)
    result = f32(3, rows * SUB, LANES)
    state_of = (grid, coef, *poly)
    cost = pl.CostEstimate(
        flops=10 * ITERS * rows * SUB * LANES,
        bytes_accessed=4 * SUB * LANES * rows * (4 + 2 * ITERS + 2),
        transcendentals=0,
    )
    held = pl.pallas_call(
        inner_kernel,
        out_shape=state_of,
        in_specs=[vmem] * 3,
        out_specs=(vmem,) * len(state_of),
        compiler_params=small,
        cost_estimate=cost,
        name="inner",
    )(fields, first, second)
    held = pl.pallas_call(
        mid_kernel,
        out_shape=state_of,
        in_specs=[vmem] * (2 + len(state_of)),
        out_specs=(vmem,) * len(state_of),
        input_output_aliases={2 + i: i for i in range(len(state_of))},
        compiler_params=small,
        cost_estimate=cost,
        name="mid",
    )(near_early, near, *held)
    grid_held, coef_held, *poly_held = held
    sums, *part = pl.pallas_call(
        functools.partial(pole_sums_kernel, 4 * poles),
        out_shape=(f32(9 * ITERS + 2, SUB, LANES), sol, result),
        in_specs=[vmem] * (5 + ITERS),
        out_specs=(vmem,) * 3,
        compiler_params=small,
        name="pole_sums",
    )(scalars, first, second, others, grid_held, *poly_held)
    kept = (grid, coef, sol, result, *poly)
    return pl.pallas_call(
        outer_kernel,
        out_shape=(f32(*state.shape), *kept),
        in_specs=[vmem] * (3 + len(kept)),
        out_specs=(hbm, *(vmem,) * len(kept)),
        scratch_shapes=[
            pltpu.VMEM(state.shape, jnp.float32),
            pltpu.SemaphoreType.DMA((3, rows // SUB)),
        ],
        input_output_aliases={3 + i: 1 + i for i in range(len(kept))},
        compiler_params=small,
        name="outer",
    )(far_early, far, sums, grid_held, coef_held, *part, *poly_held)[0]


def solution(mesh):
    return jax.shard_map(
        shards,
        mesh=mesh,
        in_specs=(
            P(None, "tile", "pole"),
            P("tile", "pole"),
            P("pole"),
            P("pole"),
            P(None, "pole"),
        ),
        out_specs=P(None, "tile", "pole"),
        check_vma=False,
    )
```

```python
import functools

import jax
import jax.numpy as jnp
from jax import lax
from jax.experimental import pallas as pl
from jax.experimental.pallas import tpu as pltpu
from jax.sharding import PartitionSpec as P

ITERS = 8
REACH = ITERS + 1
SUB = 8
LANES = 128
HALF = LANES // 2
SIDE = 32
EDGE = REACH
EAST = HALF + EDGE
GRANT = 16 * 1024 * 1024

coriolis = 0.7
centre = 8.0
half_width = 8.0


def pairs(count, phase):
    swap = []
    for i in range(phase, count + phase, 2):
        a, b = i % count, (i + 1) % count
        swap += [(a, b), (b, a)]
    return swap


def swap(block, axis, phase):
    return lax.ppermute(block, axis, pairs(lax.axis_size(axis), phase))


def shift(block, axis, step):
    count = lax.axis_size(axis)
    return lax.ppermute(block, axis, [(i, (i + step) % count) for i in range(count)])


def turn(x, lanes):
    return pltpu.roll(x, lanes % LANES, 1) if lanes % LANES else x


def cmul(a, b):
    return (a[0] * b[0] - a[1] * b[1], a[0] * b[1] + a[1] * b[0])


def cinv(a):
    norm = 1.0 / (a[0] * a[0] + a[1] * a[1])
    return (a[0] * norm, -a[1] * norm)


def cscale(a, factor):
    return (a[0] * factor, a[1] * factor)


def pack_columns_kernel(
    state, depth, real, imag, weight, fields, first, second, real_in, imag_in, weight_in, done
):
    moves = [
        pltpu.make_async_copy(depth, fields.at[3], done.at[0]),
        pltpu.make_async_copy(state, fields.at[pl.ds(0, 3)], done.at[1]),
        pltpu.make_async_copy(real, real_in, done.at[2]),
        pltpu.make_async_copy(imag, imag_in, done.at[3]),
        pltpu.make_async_copy(weight, weight_in, done.at[4]),
    ]
    for move in moves:
        move.start()
    for move in moves:
        move.wait()
    odd = lax.rem(lax.axis_index("pole"), 2) == 1
    rows, columns = fields.shape[1:]
    lane = lax.broadcasted_iota(jnp.int32, (SUB, LANES), 1)
    sub = lax.broadcasted_iota(jnp.int32, (SUB, LANES), 0)
    poles = real.shape[0]
    values = [real_in[i] for i in range(poles)] + [imag_in[i] for i in range(poles)]
    values += [weight_in[0, i] for i in range(poles)] + [weight_in[1, i] for i in range(poles)]
    for g in range(rows // SUB):
        cut = pl.ds(g * SUB, SUB)
        west = [fields[f, cut, 0:LANES] for f in range(4)]
        east = [fields[f, cut, columns - LANES : columns] for f in range(4)]
        west += [west[3] * west[1], west[3] * west[2]]
        east += [east[3] * east[1], east[3] * east[2]]
        rest = jnp.zeros((SUB, LANES), jnp.float32)
        for i, value in enumerate(values[g * SUB : (g + 1) * SUB]):
            rest = jnp.where(sub == i, value, rest)
        eastward = rest
        westward = rest
        for f in range(6):
            low, high = EDGE * f, EDGE * (f + 1)
            take = jnp.logical_and(lane >= low, lane < high)
            eastward = jnp.where(take, turn(east[f], low + EDGE), eastward)
            take = jnp.logical_and(lane >= EAST + low, lane < EAST + high)
            westward = jnp.where(take, turn(west[f], EAST + low), westward)
        first[cut, :] = jnp.where(odd, westward, eastward)
        second[cut, :] = jnp.where(odd, eastward, westward)


def pack_rows_kernel(count, fields, second, first, far_early, far, near_early, near, scalars):
    rows = fields.shape[1]
    for parts, low in towards((far_early, far), (near_early, near)):
        at = 0
        for part in parts:
            pl.when(low)(lambda: pack_rows(part, at, fields, 0, SUB))
            pl.when(jnp.logical_not(low))(
                lambda: pack_rows(part, at, fields, rows - SUB, rows - SUB - 1)
            )
            at += part.shape[0] // SUB
    odd = lax.rem(lax.axis_index("pole"), 2) == 1
    lane = lax.broadcasted_iota(jnp.int32, (SUB, LANES), 1)
    from_first = jnp.logical_xor(lane >= HALF, odd)
    for g in range(0, scalars.shape[0], SUB):
        if g < count:
            block = jnp.where(from_first, first[pl.ds(g, SUB)], second[pl.ds(g, SUB)])
        else:
            block = jnp.zeros((SUB, LANES), jnp.float32)
        scalars[pl.ds(g, SUB)] = block


def towards(far, near):
    odd = lax.rem(lax.axis_index("tile"), 2) == 1
    return ((far, jnp.logical_not(odd)), (near, odd))


def pack_rows(target, at, fields, main, ext):
    tiles = fields.shape[2] // LANES
    for i in range(target.shape[0] // SUB):
        f, t = divmod(at + i, tiles)
        if f < 4:
            block = fields[f, main : main + SUB, t * LANES : (t + 1) * LANES]
            target[pl.ds(i * SUB, SUB)] = block
        elif t == 0:
            for f in (1, 2):
                flux = fields[3, ext : ext + 1, :] * fields[f, ext : ext + 1, :]
                for t in range(tiles):
                    row = i * SUB + (f - 1) * tiles + t
                    target[row : row + 1] = flux[:, t * LANES : (t + 1) * LANES]


def block_of(parts, at):
    early, late = parts
    count = early.shape[0] // SUB
    if at < count:
        return early[pl.ds(at * SUB, SUB)]
    return late[pl.ds((at - count) * SUB, SUB)]


def sides_of(first, second, cut):
    odd = lax.rem(lax.axis_index("pole"), 2) == 1
    lane = lax.broadcasted_iota(jnp.int32, (SUB, LANES), 1)
    from_first = jnp.logical_xor(lane >= HALF, odd)
    return jnp.where(from_first, first[cut, :], second[cut, :])


def pack_sides_kernel(second, first, far_in, near_in, far, near):
    for target, low in towards(far, near):
        target[pl.ds(target.shape[0] - SUB, SUB)] = pack_sides(second, first, low)


def pack_sides(second, first, low):
    rows = first.shape[0]
    sub = lax.broadcasted_iota(jnp.int32, (SUB, LANES), 0)
    lane = lax.broadcasted_iota(jnp.int32, (SUB, LANES), 1)
    side = jnp.where(
        low,
        sides_of(first, second, pl.ds(0, SUB)),
        sides_of(first, second, pl.ds(rows - SUB, SUB)),
    )
    line = jnp.where(
        low,
        sides_of(first, second, pl.ds(SUB, SUB))[0:1],
        sides_of(first, second, pl.ds(rows - 2 * SUB, SUB))[SUB - 1 : SUB],
    )
    line = jnp.broadcast_to(line, (SUB, LANES))
    low, high = 4 * EDGE, 6 * EDGE
    take = jnp.logical_or(
        jnp.logical_and(lane >= low, lane < high),
        jnp.logical_and(lane >= EAST + low, lane < EAST + high),
    )
    side = jnp.where(jnp.logical_and(take, sub == 0), line, side)
    return side


def pole_sums_kernel(count, scalars, first, second, others, grid, *rest):
    poly, (sums, sol, result) = rest[:ITERS], rest[ITERS:]
    odd = lax.rem(lax.axis_index("pole"), 2) == 1
    lane = lax.broadcasted_iota(jnp.int32, (SUB, LANES), 1)
    blocks = [[scalars[pl.ds(g, SUB)] for g in range(0, count, SUB)]]
    for i, message in enumerate((first, second)):
        low = jnp.logical_xor(lane < HALF, odd if i == 0 else jnp.logical_not(odd))
        part = []
        for g in range(0, count, SUB):
            x = message[pl.ds(g, SUB), :]
            part.append(jnp.where(low, x, turn(x, HALF)))
        blocks.append(part)
    for i in range(others.shape[0]):
        blocks.append([others[i, pl.ds(g, SUB)] for g in range(0, count, SUB)])
    poles = count // 4
    quantity = []
    for q in range(4):
        cut = []
        for block in blocks:
            whole = jnp.concatenate(block, axis=0)
            cut.append(whole[q * poles : (q + 1) * poles])
        quantity.append(jnp.concatenate(cut, axis=0))
    alpha = (quantity[0], quantity[1])
    beta = (quantity[2], quantity[3])
    square = cmul(alpha, alpha)
    shifted = (square[0] + coriolis * coriolis, square[1])
    sigma = ((shifted[0] + centre) / half_width, shifted[1] / half_width)
    rho = [cinv(sigma)]
    for j in range(1, ITERS):
        rho.append(cinv((2.0 * sigma[0] - rho[-1][0], 2.0 * sigma[1] - rho[-1][1])))
    gain = None
    start = []
    for m in range(ITERS):
        if m == 0:
            start.append(cscale(rho[0], 1.0 / half_width))
        else:
            gain = rho[0] if gain is None else cmul(gain, rho[m - 1])
            start.append(cscale(cmul(rho[m], gain), 2.0 / half_width))
    tail = None
    weight = [None] * ITERS
    for m in reversed(range(ITERS)):
        if tail is None:
            weight[m] = start[m]
            tail = (jnp.ones_like(sigma[0]), jnp.zeros_like(sigma[0]))
        else:
            tail = cmul(cmul(rho[m + 1], rho[m]), tail)
            tail = (tail[0] + 1.0, tail[1])
            weight[m] = cmul(start[m], tail)
    inverse_alpha = cinv(alpha)
    inverse_shift = cinv(shifted)
    by_alpha = cmul(beta, inverse_alpha)
    by_shift = cmul(beta, inverse_shift)
    products = {
        "b": beta,
        "b/a": by_alpha,
        "b/s": by_shift,
        "bs/a": cmul(by_alpha, shifted),
        "ba/s": cmul(by_shift, alpha),
        "b/as": cmul(by_alpha, inverse_shift),
    }

    def total(x):
        s = x[0:SUB]
        for i in range(1, x.shape[0] // SUB):
            s = s + x[i * SUB : (i + 1) * SUB]
        for step in (4, 2, 1):
            s = s + pltpu.roll(s, step, 0)
        return s

    names = [("bs/a", "b", "b/a"), ("b", "ba/s", "b/s"), ("b/a", "b/s", "b/as")]
    factor = (1.0, -1.0, -coriolis)
    found = {}
    for m in range(ITERS):
        for name, w in products.items():
            found[name, m] = total(w[0] * weight[m][0] - w[1] * weight[m][1])
        for g in range(3):
            for f in range(3):
                value = found[names[g][f], m]
                sums[(g * 3 + f) * ITERS + m] = value if f == 0 else factor[f] * value
    sums[9 * ITERS] = total(products["ba/s"][0])
    sums[9 * ITERS + 1] = coriolis * total(products["b/s"][0])

    _, (_, above) = towards(None, None)
    rows = sol.shape[1] - 2

    def near_rows(above):
        near, far = side_rows(rows, above), side_rows(rows, not above)
        acc = {}
        for m in range(ITERS):
            add(acc, sums, poly, m, near)
        for m in range(ITERS - 1):
            add(acc, sums, poly, m, [r for k, r in enumerate(far) if known(k) >= m])
        for (g, r), v in acc.items():
            sol[g, r - (REACH - 1)] = v
        inside = sorted(near)[1:-1]
        finish(grid, sums, result, acc, [r for r in inside if REACH <= r < REACH + rows])

    pl.when(above)(lambda: near_rows(True))
    pl.when(jnp.logical_not(above))(lambda: near_rows(False))


def side_rows(rows, above):
    low, high = REACH - 1, REACH + rows
    return [low + k if above else high - k for k in range(rows // 2 + 1)]


def known(k):
    return max(min(ITERS - 2, k - 2), -1)


def add(acc, sums, poly, m, rows, values=None):
    for f in range(3):
        if not rows:
            return
        value = {r: poly[m][f, r] if values is None else values[f, r] for r in rows}
        for g in range(3):
            c = sums[(g * 3 + f) * ITERS + m]
            for r in rows:
                acc[g, r] = acc[g, r] + c * value[r] if (g, r) in acc else c * value[r]


def finish(grid, sums, result, acc, span):
    push = sums[9 * ITERS]
    lift = sums[9 * ITERS + 1]
    for r in span:
        u, v = cell(grid, 1, r), cell(grid, 2, r)
        at = pl.ds((r - REACH) * SUB, SUB)
        result[0, at] = acc[0, r]
        east = 0.5 * (acc[1, r + 1] - acc[1, r - 1])
        north = 0.5 * (right(acc[2, r]) - left(acc[2, r]))
        result[1, at] = (push * u + lift * v) - (east + coriolis * north)
        east = 0.5 * (acc[2, r + 1] - acc[2, r - 1])
        north = 0.5 * (right(acc[1, r]) - left(acc[1, r]))
        result[2, at] = (push * v - lift * u) + (coriolis * east - north)


def strips_of(tiles, side):
    lane = lax.broadcasted_iota(jnp.int32, (SUB, LANES), 1)
    up = [turn(tile, SIDE) for tile in tiles]
    down = [turn(tile, -SIDE) for tile in tiles]
    out = []
    for q in range(len(tiles)):
        out.append(jnp.where(lane < SIDE, up[q - 1] if q else side, up[q]))
        after = down[q + 1] if q + 1 < len(tiles) else side
        out.append(jnp.where(lane < LANES - SIDE, down[q], after))
    return out


def lay(grid, cut, side, at, stride):
    for s, strip in enumerate(strips_of(cut, side)):
        grid[pl.Slice(at * SUB + s, SUB, stride * SUB), :] = strip


def place(side, f):
    return turn(side, SIDE - EDGE - EDGE * f)


def lay_halo(grid, halo, side, main, ext):
    lane = lax.broadcasted_iota(jnp.int32, (SUB, LANES), 1)
    sub = lax.broadcasted_iota(jnp.int32, (SUB, LANES), 0)
    tiles = SUB // 2
    for f in range(4):
        cut = [block_of(halo, f * tiles + t) for t in range(tiles)]
        lay(grid, cut, place(side, f), main * 4 + f, 4)
    line = jnp.broadcast_to(side[0:1], (SUB, LANES))
    side = jnp.where(sub < tiles, place(line, 4), place(line, 5))
    block = block_of(halo, 4 * tiles)
    up, down = turn(block, SIDE), turn(block, -SIDE)
    before = jnp.where(sub % tiles == 0, side, pltpu.roll(up, 1, 0))
    after = jnp.where(sub % tiles == tiles - 1, side, pltpu.roll(down, SUB - 1, 0))
    even = jnp.where(lane < SIDE, before, up)
    odd = jnp.where(lane < LANES - SIDE, down, after)
    for f in (1, 2):
        at = (ext * 4 + f) * SUB
        cut = slice((f - 1) * tiles, f * tiles)
        grid[pl.Slice(at, tiles, 2), :] = even[cut]
        grid[pl.Slice(at + 1, tiles, 2), :] = odd[cut]


def cell(grid, f, r):
    return grid[pl.ds(pl.multiple_of((r * 4 + f) * SUB, SUB), SUB), :]


def left(x):
    return pltpu.roll(x, 1, 1)


def right(x):
    return pltpu.roll(x, LANES - 1, 1)


def prepare(grid, poly, coef, start, count):
    flux_east = [None] * 3
    flux_north = [None] * 3
    depths = [None] * 2
    across = None
    found = {}
    for k in range(count + 2):
        r = start + k
        h = cell(grid, 3, r)
        flux_east = flux_east[1:] + [h * cell(grid, 1, r)]
        flux_north = flux_north[1:] + [h * cell(grid, 2, r)]
        depths = depths[1:] + [h]
        if k >= 1:
            before, across = across, 0.125 * (depths[0] + depths[1])
            coef[0, r - 1] = across
        if k >= 2:
            c = r - 1
            north = 0.125 * (depths[0] + right(depths[0]))
            south = 0.125 * (depths[0] + left(depths[0]))
            coef[1, c] = north
            coef[2, c] = south
            coef[3, c] = 2.0 - ((across + before) + (north + south))
            east_slope = flux_east[2] - flux_east[0]
            north_slope = right(flux_north[1]) - left(flux_north[1])
            poly[0][1, c] = found[1, c] = 0.5 * (east_slope + north_slope)
            east_slope = flux_north[2] - flux_north[0]
            north_slope = right(flux_east[1]) - left(flux_east[1])
            poly[0][2, c] = found[2, c] = 0.5 * (east_slope - north_slope)
            poly[0][0, c] = found[0, c] = cell(grid, 0, c)
    return found


def sweep(poly, coef, m, start, count, last, upwards=False):
    def take(f, r):
        return last[f, r] if (f, r) in last else poly[m][f, r]

    step = -1 if upwards else 1
    order = range(start, start + count)[::step]
    back = [take(f, order[0] - step) for f in range(3)]
    here = [take(f, order[0]) for f in range(3)]
    found = {}
    for r in order:
        north, south, diag = coef[1, r], coef[2, r], coef[3, r]
        above, below = coef[0, r], coef[0, r - 1]
        ahead = [take(f, r + step) for f in range(3)]
        for f in range(3):
            up, down = (back, ahead) if upwards else (ahead, back)
            value = diag * here[f]
            if m > 0:
                value = value - poly[m - 1][f, r]
            value = value + above * up[f]
            value = value + below * down[f]
            value = value + north * right(here[f])
            value = value + south * left(here[f])
            value = 0.5 * value if m == 0 else value
            poly[m + 1][f, r] = value
            found[f, r] = value
        back, here = here, ahead
    return found


def inner_kernel(fields, first, second, grid, coef, *poly):
    rows = fields.shape[1]
    for g in range(rows // SUB):
        side = sides_of(first, second, pl.ds(g * SUB, SUB))
        for f in range(4):
            cut = [
                fields[f, pl.ds(g * SUB, SUB), pl.ds(t * LANES, LANES)]
                for t in range(fields.shape[2] // LANES)
            ]
            lay(grid, cut, place(side, f), (REACH + g * SUB) * 4 + f, 4)
    found = prepare(grid, poly, coef, REACH, rows - 2)
    for m in range(ITERS - 1):
        if rows - 4 - 2 * m > 0:
            found = sweep(poly, coef, m, REACH + 2 + m, rows - 4 - 2 * m, found)


def one_side(halo, side, above, grid, coef, poly, each):
    below = coef.shape[1] - REACH
    main, ext, start = (1, 0, 0) if above else (below, below + SUB, below - 2)
    grid[pl.ds((ext * 4 + 3) * SUB, SUB), :] = jnp.ones((SUB, LANES), jnp.float32)
    lay_halo(grid, halo, side, main, ext)
    found = prepare(grid, poly, coef, start, REACH)
    each(0, found)
    for m in range(ITERS - 1):
        low = 2 + m if above else below - 2 - m
        found = sweep(poly, coef, m, low, REACH, found, above)
        each(m + 1, found)


def mid_kernel(near_early, near, *rest):
    grid, coef, *poly = rest[len(rest) // 2 :]
    _, (_, above) = towards(None, None)
    side = near[pl.ds(near.shape[0] - SUB, SUB)]
    for way, here in ((True, above), (False, jnp.logical_not(above))):
        pl.when(here)(
            lambda: one_side((near_early, near), side, way, grid, coef, poly, lambda m, found: None)
        )


def outer_kernel(far_early, far, sums, *rest):
    *rest, lines, done = rest
    out, grid, coef, sol, result, *poly = rest[len(rest) // 2 :]
    rows, columns = out.shape[1:]
    lane = lax.broadcasted_iota(jnp.int32, (SUB, LANES), 1)
    (_, above), _ = towards(None, None)

    def far_rows(above):
        side = far[pl.ds(far.shape[0] - SUB, SUB)]
        whole = side_rows(rows, above)
        inside = 1 if above else -1
        edges = [whole[-1] + inside, whole[-1] + 2 * inside]
        acc = {}
        for r in edges + [r for k, r in enumerate(whole) if known(k) >= 0]:
            for g in range(3):
                acc[g, r] = sol[g, r - (REACH - 1)]

        def each(m, found):
            part = [r for k, r in enumerate(whole) if known(k) < m]
            held = [r for r in part if (0, r) in found]
            add(acc, sums, poly, m, held, found)
            add(acc, sums, poly, m, [r for r in part if r not in held])

        one_side((far_early, far), side, above, grid, coef, poly, each)
        span = [r for r in whole + edges[:1] if REACH <= r < REACH + rows]
        finish(grid, sums, result, acc, span)

    pl.when(above)(lambda: far_rows(True))
    pl.when(jnp.logical_not(above))(lambda: far_rows(False))

    moves = []
    for k in range(3):
        for g in range(rows // SUB):
            cut = pl.ds(g * SUB, SUB)
            for t in range(columns // LANES):
                one = result[k, pl.Slice(g * SUB * SUB + 2 * t, SUB, SUB), :]
                two = result[k, pl.Slice(g * SUB * SUB + 2 * t + 1, SUB, SUB), :]
                joined = jnp.where(lane < HALF, turn(one, -SIDE), turn(two, SIDE))
                lines[k, cut, pl.ds(t * LANES, LANES)] = joined
            move = pltpu.make_async_copy(lines.at[k, cut], out.at[k, cut], done.at[k, g])
            move.start()
            moves.append(move)
    for move in moves:
        move.wait()


def shards(state, depth, pole_real, pole_imag, pole_weight):
    rows, columns = depth.shape
    poles = pole_real.shape[0]
    vmem = pl.BlockSpec(memory_space=pltpu.VMEM)
    small = pltpu.CompilerParams(vmem_limit_bytes=GRANT)

    def f32(*shape):
        return jax.ShapeDtypeStruct(shape, jnp.float32)

    given = [
        pltpu.with_memory_space_constraint(x, pltpu.HBM)
        for x in (state, depth, pole_real, pole_imag, pole_weight)
    ]
    hbm = pl.BlockSpec(memory_space=pltpu.HBM)
    message = pltpu.VMEM((rows, LANES), jnp.float32)
    fields, first, second = pl.pallas_call(
        pack_columns_kernel,
        out_shape=(pltpu.VMEM((4, rows, columns), jnp.float32), message, message),
        in_specs=[hbm] * 5,
        out_specs=(vmem,) * 3,
        scratch_shapes=[
            pltpu.SMEM(pole_real.shape, jnp.float32),
            pltpu.SMEM(pole_imag.shape, jnp.float32),
            pltpu.SMEM(pole_weight.shape, jnp.float32),
            pltpu.SemaphoreType.DMA((5,)),
        ],
        compiler_params=small,
        name="pack_columns",
    )(*given)
    blocks = 4 * columns // LANES + 2
    half = blocks // 2 * SUB
    parts = (half + SUB + 4, half, half + SUB, half - SUB, max(4 * poles, half))
    far_early, far, near_early, near, scalars = pl.pallas_call(
        functools.partial(pack_rows_kernel, 4 * poles),
        out_shape=tuple(f32(part, LANES) for part in parts),
        in_specs=[vmem] * 3,
        out_specs=(vmem,) * 5,
        compiler_params=small,
        name="pack_rows",
    )(fields, second, first)
    second = swap(second, "pole", 1)
    first = swap(first, "pole", 0)
    far, near = pl.pallas_call(
        pack_sides_kernel,
        out_shape=(f32(*far.shape), f32(*near.shape)),
        in_specs=[vmem] * 4,
        out_specs=(vmem, vmem),
        input_output_aliases={2: 0, 3: 1},
        compiler_params=small,
        name="pack_sides",
    )(second, first, far, near)
    far_early = swap(far_early, "tile", 1)
    far = swap(far, "tile", 1)
    near_early = swap(near_early, "tile", 0)
    near = swap(near, "tile", 0)
    count = lax.axis_size("pole")
    others = jnp.stack([shift(scalars, "pole", step) for step in range(2, count - 1)])
    height = rows + 2 * REACH
    grid = f32(height * 4 * SUB, LANES)
    poly = [f32(3, height, SUB, LANES)] * ITERS
    coef = f32(4, height, SUB, LANES)
    sol = f32(3, rows + 2, SUB, LANES)
    result = f32(3, rows * SUB, LANES)
    state_of = (grid, coef, *poly)
    cost = pl.CostEstimate(
        flops=10 * ITERS * rows * SUB * LANES,
        bytes_accessed=4 * SUB * LANES * rows * (4 + 2 * ITERS + 2),
        transcendentals=0,
    )
    held = pl.pallas_call(
        inner_kernel,
        out_shape=state_of,
        in_specs=[vmem] * 3,
        out_specs=(vmem,) * len(state_of),
        compiler_params=small,
        cost_estimate=cost,
        name="inner",
    )(fields, first, second)
    held = pl.pallas_call(
        mid_kernel,
        out_shape=state_of,
        in_specs=[vmem] * (2 + len(state_of)),
        out_specs=(vmem,) * len(state_of),
        input_output_aliases={2 + i: i for i in range(len(state_of))},
        compiler_params=small,
        cost_estimate=cost,
        name="mid",
    )(near_early, near, *held)
    grid_held, coef_held, *poly_held = held
    sums, *part = pl.pallas_call(
        functools.partial(pole_sums_kernel, 4 * poles),
        out_shape=(f32(9 * ITERS + 2, SUB, LANES), sol, result),
        in_specs=[vmem] * (5 + ITERS),
        out_specs=(vmem,) * 3,
        compiler_params=small,
        name="pole_sums",
    )(scalars, first, second, others, grid_held, *poly_held)
    kept = (grid, coef, sol, result, *poly)
    return pl.pallas_call(
        outer_kernel,
        out_shape=(f32(*state.shape), *kept),
        in_specs=[vmem] * (3 + len(kept)),
        out_specs=(hbm, *(vmem,) * len(kept)),
        scratch_shapes=[
            pltpu.VMEM(state.shape, jnp.float32),
            pltpu.SemaphoreType.DMA((3, rows // SUB)),
        ],
        input_output_aliases={3 + i: 1 + i for i in range(len(kept))},
        compiler_params=small,
        name="outer",
    )(far_early, far, sums, grid_held, coef_held, *part, *poly_held)[0]


def solution(mesh):
    return jax.shard_map(
        shards,
        mesh=mesh,
        in_specs=(
            P(None, "tile", "pole"),
            P("tile", "pole"),
            P("pole"),
            P("pole"),
            P(None, "pole"),
        ),
        out_specs=P(None, "tile", "pole"),
        check_vma=False,
    )
```

```python
import functools

import jax
import jax.numpy as jnp
from jax import lax
from jax.experimental import pallas as pl
from jax.experimental.pallas import tpu as pltpu
from jax.sharding import PartitionSpec as P

ITERS = 8
REACH = ITERS + 1
SUB = 8
LANES = 128
HALF = LANES // 2
SIDE = 32
EDGE = REACH
EAST = HALF + EDGE
GRANT = 16 * 1024 * 1024

coriolis = 0.7
centre = 8.0
half_width = 8.0


def pairs(count, phase):
    swap = []
    for i in range(phase, count + phase, 2):
        a, b = i % count, (i + 1) % count
        swap += [(a, b), (b, a)]
    return swap


def swap(block, axis, phase):
    return lax.ppermute(block, axis, pairs(lax.axis_size(axis), phase))


def shift(block, axis, step):
    count = lax.axis_size(axis)
    return lax.ppermute(block, axis, [(i, (i + step) % count) for i in range(count)])


def turn(x, lanes):
    return pltpu.roll(x, lanes % LANES, 1) if lanes % LANES else x


def cmul(a, b):
    return (a[0] * b[0] - a[1] * b[1], a[0] * b[1] + a[1] * b[0])


def cinv(a):
    norm = 1.0 / (a[0] * a[0] + a[1] * a[1])
    return (a[0] * norm, -a[1] * norm)


def cscale(a, factor):
    return (a[0] * factor, a[1] * factor)


def pack_columns_kernel(
    state, depth, real, imag, weight, fields, first, second, real_in, imag_in, weight_in, done
):
    moves = [
        pltpu.make_async_copy(depth, fields.at[3], done.at[0]),
        pltpu.make_async_copy(state, fields.at[pl.ds(0, 3)], done.at[1]),
        pltpu.make_async_copy(real, real_in, done.at[2]),
        pltpu.make_async_copy(imag, imag_in, done.at[3]),
        pltpu.make_async_copy(weight, weight_in, done.at[4]),
    ]
    for move in moves:
        move.start()
    for move in moves:
        move.wait()
    odd = lax.rem(lax.axis_index("pole"), 2) == 1
    rows, columns = fields.shape[1:]
    lane = lax.broadcasted_iota(jnp.int32, (SUB, LANES), 1)
    poles = real.shape[1]
    quantity = jnp.concatenate([real_in[...], imag_in[...], weight_in[...]], axis=0)
    diagonal = lax.broadcasted_iota(jnp.int32, (poles, poles), 0)
    diagonal = diagonal == lax.broadcasted_iota(jnp.int32, (poles, poles), 1)
    spread = []
    for q in range(4):
        line = jnp.where(diagonal, quantity[q : q + 1], 0.0)
        spread.append(jnp.broadcast_to(jnp.sum(line, 1, keepdims=True), (poles, LANES)))
    spread = jnp.concatenate(spread, axis=0)
    for g in range(rows // SUB):
        cut = pl.ds(g * SUB, SUB)
        west = [fields[f, cut, 0:LANES] for f in range(4)]
        east = [fields[f, cut, columns - LANES : columns] for f in range(4)]
        west += [west[3] * west[1], west[3] * west[2]]
        east += [east[3] * east[1], east[3] * east[2]]
        rest = spread[g * SUB : (g + 1) * SUB]
        if rest.shape[0] < SUB:
            rest = jnp.zeros((SUB, LANES), jnp.float32)
        eastward = rest
        westward = rest
        for f in range(6):
            low, high = EDGE * f, EDGE * (f + 1)
            take = jnp.logical_and(lane >= low, lane < high)
            eastward = jnp.where(take, turn(east[f], low + EDGE), eastward)
            take = jnp.logical_and(lane >= EAST + low, lane < EAST + high)
            westward = jnp.where(take, turn(west[f], EAST + low), westward)
        first[cut, :] = jnp.where(odd, westward, eastward)
        second[cut, :] = jnp.where(odd, eastward, westward)


def pack_rows_kernel(count, fields, second, first, far_early, far, near_early, near, scalars):
    rows = fields.shape[1]
    for parts, low in towards((far_early, far), (near_early, near)):
        at = 0
        for part in parts:
            pl.when(low)(lambda: pack_rows(part, at, fields, 0, SUB))
            pl.when(jnp.logical_not(low))(
                lambda: pack_rows(part, at, fields, rows - SUB, rows - SUB - 1)
            )
            at += part.shape[0] // SUB
    odd = lax.rem(lax.axis_index("pole"), 2) == 1
    lane = lax.broadcasted_iota(jnp.int32, (SUB, LANES), 1)
    from_first = jnp.logical_xor(lane >= HALF, odd)
    for g in range(0, scalars.shape[0], SUB):
        if g < count:
            block = jnp.where(from_first, first[pl.ds(g, SUB)], second[pl.ds(g, SUB)])
        else:
            block = jnp.zeros((SUB, LANES), jnp.float32)
        scalars[pl.ds(g, SUB)] = block


def towards(far, near):
    odd = lax.rem(lax.axis_index("tile"), 2) == 1
    return ((far, jnp.logical_not(odd)), (near, odd))


def pack_rows(target, at, fields, main, ext):
    tiles = fields.shape[2] // LANES
    for i in range(target.shape[0] // SUB):
        f, t = divmod(at + i, tiles)
        if f < 4:
            block = fields[f, main : main + SUB, t * LANES : (t + 1) * LANES]
            target[pl.ds(i * SUB, SUB)] = block
        elif t == 0:
            for f in (1, 2):
                flux = fields[3, ext : ext + 1, :] * fields[f, ext : ext + 1, :]
                for t in range(tiles):
                    row = i * SUB + (f - 1) * tiles + t
                    target[row : row + 1] = flux[:, t * LANES : (t + 1) * LANES]


def block_of(parts, at):
    early, late = parts
    count = early.shape[0] // SUB
    if at < count:
        return early[pl.ds(at * SUB, SUB)]
    return late[pl.ds((at - count) * SUB, SUB)]


def sides_of(first, second, cut):
    odd = lax.rem(lax.axis_index("pole"), 2) == 1
    lane = lax.broadcasted_iota(jnp.int32, (SUB, LANES), 1)
    from_first = jnp.logical_xor(lane >= HALF, odd)
    return jnp.where(from_first, first[cut, :], second[cut, :])


def pack_sides_kernel(second, first, far_in, near_in, far, near):
    for target, low in towards(far, near):
        target[pl.ds(target.shape[0] - SUB, SUB)] = pack_sides(second, first, low)


def pack_sides(second, first, low):
    rows = first.shape[0]
    sub = lax.broadcasted_iota(jnp.int32, (SUB, LANES), 0)
    lane = lax.broadcasted_iota(jnp.int32, (SUB, LANES), 1)
    side = jnp.where(
        low,
        sides_of(first, second, pl.ds(0, SUB)),
        sides_of(first, second, pl.ds(rows - SUB, SUB)),
    )
    line = jnp.where(
        low,
        sides_of(first, second, pl.ds(SUB, SUB))[0:1],
        sides_of(first, second, pl.ds(rows - 2 * SUB, SUB))[SUB - 1 : SUB],
    )
    line = jnp.broadcast_to(line, (SUB, LANES))
    low, high = 4 * EDGE, 6 * EDGE
    take = jnp.logical_or(
        jnp.logical_and(lane >= low, lane < high),
        jnp.logical_and(lane >= EAST + low, lane < EAST + high),
    )
    side = jnp.where(jnp.logical_and(take, sub == 0), line, side)
    return side


def pole_sums_kernel(count, scalars, first, second, others, grid, *rest):
    poly, (sums, sol, result) = rest[:ITERS], rest[ITERS:]
    odd = lax.rem(lax.axis_index("pole"), 2) == 1
    lane = lax.broadcasted_iota(jnp.int32, (SUB, LANES), 1)
    blocks = [[scalars[pl.ds(g, SUB)] for g in range(0, count, SUB)]]
    for i, message in enumerate((first, second)):
        low = jnp.logical_xor(lane < HALF, odd if i == 0 else jnp.logical_not(odd))
        part = []
        for g in range(0, count, SUB):
            x = message[pl.ds(g, SUB), :]
            part.append(jnp.where(low, x, turn(x, HALF)))
        blocks.append(part)
    for i in range(others.shape[0]):
        blocks.append([others[i, pl.ds(g, SUB)] for g in range(0, count, SUB)])
    poles = count // 4
    quantity = []
    for q in range(4):
        cut = []
        for block in blocks:
            whole = jnp.concatenate(block, axis=0)
            cut.append(whole[q * poles : (q + 1) * poles])
        quantity.append(jnp.concatenate(cut, axis=0))
    alpha = (quantity[0], quantity[1])
    beta = (quantity[2], quantity[3])
    square = cmul(alpha, alpha)
    shifted = (square[0] + coriolis * coriolis, square[1])
    sigma = ((shifted[0] + centre) / half_width, shifted[1] / half_width)
    rho = [cinv(sigma)]
    for j in range(1, ITERS):
        rho.append(cinv((2.0 * sigma[0] - rho[-1][0], 2.0 * sigma[1] - rho[-1][1])))
    gain = None
    start = []
    for m in range(ITERS):
        if m == 0:
            start.append(cscale(rho[0], 1.0 / half_width))
        else:
            gain = rho[0] if gain is None else cmul(gain, rho[m - 1])
            start.append(cscale(cmul(rho[m], gain), 2.0 / half_width))
    tail = None
    weight = [None] * ITERS
    for m in reversed(range(ITERS)):
        if tail is None:
            weight[m] = start[m]
            tail = (jnp.ones_like(sigma[0]), jnp.zeros_like(sigma[0]))
        else:
            tail = cmul(cmul(rho[m + 1], rho[m]), tail)
            tail = (tail[0] + 1.0, tail[1])
            weight[m] = cmul(start[m], tail)
    inverse_alpha = cinv(alpha)
    inverse_shift = cinv(shifted)
    by_alpha = cmul(beta, inverse_alpha)
    by_shift = cmul(beta, inverse_shift)
    products = {
        "b": beta,
        "b/a": by_alpha,
        "b/s": by_shift,
        "bs/a": cmul(by_alpha, shifted),
        "ba/s": cmul(by_shift, alpha),
        "b/as": cmul(by_alpha, inverse_shift),
    }

    def total(x):
        s = x[0:SUB]
        for i in range(1, x.shape[0] // SUB):
            s = s + x[i * SUB : (i + 1) * SUB]
        for step in (4, 2, 1):
            s = s + pltpu.roll(s, step, 0)
        return s

    names = [("bs/a", "b", "b/a"), ("b", "ba/s", "b/s"), ("b/a", "b/s", "b/as")]
    factor = (1.0, -1.0, -coriolis)
    found = {}
    for m in range(ITERS):
        for name, w in products.items():
            found[name, m] = total(w[0] * weight[m][0] - w[1] * weight[m][1])
        for g in range(3):
            for f in range(3):
                value = found[names[g][f], m]
                sums[(g * 3 + f) * ITERS + m] = value if f == 0 else factor[f] * value
    sums[9 * ITERS] = total(products["ba/s"][0])
    sums[9 * ITERS + 1] = coriolis * total(products["b/s"][0])

    _, (_, above) = towards(None, None)
    rows = sol.shape[1] - 2

    def near_rows(above):
        near, far = side_rows(rows, above), side_rows(rows, not above)
        acc = {}
        for m in range(ITERS):
            add(acc, sums, poly, m, near)
        for m in range(ITERS - 1):
            add(acc, sums, poly, m, [r for k, r in enumerate(far) if known(k) >= m])
        for (g, r), v in acc.items():
            sol[g, r - (REACH - 1)] = v
        inside = sorted(near)[1:-1]
        finish(grid, sums, result, acc, [r for r in inside if REACH <= r < REACH + rows])

    pl.when(above)(lambda: near_rows(True))
    pl.when(jnp.logical_not(above))(lambda: near_rows(False))


def side_rows(rows, above):
    low, high = REACH - 1, REACH + rows
    return [low + k if above else high - k for k in range(rows // 2 + 1)]


def known(k):
    return max(min(ITERS - 2, k - 2), -1)


def add(acc, sums, poly, m, rows, values=None):
    for f in range(3):
        if not rows:
            return
        value = {r: poly[m][f, r] if values is None else values[f, r] for r in rows}
        for g in range(3):
            c = sums[(g * 3 + f) * ITERS + m]
            for r in rows:
                acc[g, r] = acc[g, r] + c * value[r] if (g, r) in acc else c * value[r]


def finish(grid, sums, result, acc, span):
    push = sums[9 * ITERS]
    lift = sums[9 * ITERS + 1]
    for r in span:
        u, v = cell(grid, 1, r), cell(grid, 2, r)
        at = pl.ds((r - REACH) * SUB, SUB)
        result[0, at] = acc[0, r]
        east = 0.5 * (acc[1, r + 1] - acc[1, r - 1])
        north = 0.5 * (right(acc[2, r]) - left(acc[2, r]))
        result[1, at] = (push * u + lift * v) - (east + coriolis * north)
        east = 0.5 * (acc[2, r + 1] - acc[2, r - 1])
        north = 0.5 * (right(acc[1, r]) - left(acc[1, r]))
        result[2, at] = (push * v - lift * u) + (coriolis * east - north)


def strips_of(tiles, side):
    lane = lax.broadcasted_iota(jnp.int32, (SUB, LANES), 1)
    up = [turn(tile, SIDE) for tile in tiles]
    down = [turn(tile, -SIDE) for tile in tiles]
    out = []
    for q in range(len(tiles)):
        out.append(jnp.where(lane < SIDE, up[q - 1] if q else side, up[q]))
        after = down[q + 1] if q + 1 < len(tiles) else side
        out.append(jnp.where(lane < LANES - SIDE, down[q], after))
    return out


def lay(grid, cut, side, at, stride):
    for s, strip in enumerate(strips_of(cut, side)):
        grid[pl.Slice(at * SUB + s, SUB, stride * SUB), :] = strip


def place(side, f):
    return turn(side, SIDE - EDGE - EDGE * f)


def lay_halo(grid, halo, side, main, ext):
    lane = lax.broadcasted_iota(jnp.int32, (SUB, LANES), 1)
    sub = lax.broadcasted_iota(jnp.int32, (SUB, LANES), 0)
    tiles = SUB // 2
    for f in range(4):
        cut = [block_of(halo, f * tiles + t) for t in range(tiles)]
        lay(grid, cut, place(side, f), main * 4 + f, 4)
    line = jnp.broadcast_to(side[0:1], (SUB, LANES))
    side = jnp.where(sub < tiles, place(line, 4), place(line, 5))
    block = block_of(halo, 4 * tiles)
    up, down = turn(block, SIDE), turn(block, -SIDE)
    before = jnp.where(sub % tiles == 0, side, pltpu.roll(up, 1, 0))
    after = jnp.where(sub % tiles == tiles - 1, side, pltpu.roll(down, SUB - 1, 0))
    even = jnp.where(lane < SIDE, before, up)
    odd = jnp.where(lane < LANES - SIDE, down, after)
    for f in (1, 2):
        at = (ext * 4 + f) * SUB
        cut = slice((f - 1) * tiles, f * tiles)
        grid[pl.Slice(at, tiles, 2), :] = even[cut]
        grid[pl.Slice(at + 1, tiles, 2), :] = odd[cut]


def cell(grid, f, r):
    return grid[pl.ds(pl.multiple_of((r * 4 + f) * SUB, SUB), SUB), :]


def left(x):
    return pltpu.roll(x, 1, 1)


def right(x):
    return pltpu.roll(x, LANES - 1, 1)


def prepare(grid, poly, coef, start, count):
    flux_east = [None] * 3
    flux_north = [None] * 3
    depths = [None] * 2
    across = None
    found = {}
    for k in range(count + 2):
        r = start + k
        h = cell(grid, 3, r)
        flux_east = flux_east[1:] + [h * cell(grid, 1, r)]
        flux_north = flux_north[1:] + [h * cell(grid, 2, r)]
        depths = depths[1:] + [h]
        if k >= 1:
            before, across = across, 0.125 * (depths[0] + depths[1])
            coef[0, r - 1] = across
        if k >= 2:
            c = r - 1
            north = 0.125 * (depths[0] + right(depths[0]))
            south = 0.125 * (depths[0] + left(depths[0]))
            coef[1, c] = north
            coef[2, c] = south
            coef[3, c] = 2.0 - ((across + before) + (north + south))
            east_slope = flux_east[2] - flux_east[0]
            north_slope = right(flux_north[1]) - left(flux_north[1])
            poly[0][1, c] = found[1, c] = 0.5 * (east_slope + north_slope)
            east_slope = flux_north[2] - flux_north[0]
            north_slope = right(flux_east[1]) - left(flux_east[1])
            poly[0][2, c] = found[2, c] = 0.5 * (east_slope - north_slope)
            poly[0][0, c] = found[0, c] = cell(grid, 0, c)
    return found


def sweep(poly, coef, m, start, count, last, upwards=False):
    def take(f, r):
        return last[f, r] if (f, r) in last else poly[m][f, r]

    step = -1 if upwards else 1
    order = range(start, start + count)[::step]
    back = [take(f, order[0] - step) for f in range(3)]
    here = [take(f, order[0]) for f in range(3)]
    found = {}
    for r in order:
        north, south, diag = coef[1, r], coef[2, r], coef[3, r]
        above, below = coef[0, r], coef[0, r - 1]
        ahead = [take(f, r + step) for f in range(3)]
        for f in range(3):
            up, down = (back, ahead) if upwards else (ahead, back)
            value = diag * here[f]
            if m > 0:
                value = value - poly[m - 1][f, r]
            value = value + above * up[f]
            value = value + below * down[f]
            value = value + north * right(here[f])
            value = value + south * left(here[f])
            value = 0.5 * value if m == 0 else value
            poly[m + 1][f, r] = value
            found[f, r] = value
        back, here = here, ahead
    return found


def inner_kernel(fields, first, second, grid, coef, *poly):
    rows = fields.shape[1]
    for g in range(rows // SUB):
        side = sides_of(first, second, pl.ds(g * SUB, SUB))
        for f in range(4):
            cut = [
                fields[f, pl.ds(g * SUB, SUB), pl.ds(t * LANES, LANES)]
                for t in range(fields.shape[2] // LANES)
            ]
            lay(grid, cut, place(side, f), (REACH + g * SUB) * 4 + f, 4)
    found = prepare(grid, poly, coef, REACH, rows - 2)
    for m in range(ITERS - 1):
        if rows - 4 - 2 * m > 0:
            found = sweep(poly, coef, m, REACH + 2 + m, rows - 4 - 2 * m, found)


def one_side(halo, side, above, grid, coef, poly, each):
    below = coef.shape[1] - REACH
    main, ext, start = (1, 0, 0) if above else (below, below + SUB, below - 2)
    grid[pl.ds((ext * 4 + 3) * SUB, SUB), :] = jnp.ones((SUB, LANES), jnp.float32)
    lay_halo(grid, halo, side, main, ext)
    found = prepare(grid, poly, coef, start, REACH)
    each(0, found)
    for m in range(ITERS - 1):
        low = 2 + m if above else below - 2 - m
        found = sweep(poly, coef, m, low, REACH, found, above)
        each(m + 1, found)


def mid_kernel(near_early, near, *rest):
    grid, coef, *poly = rest[len(rest) // 2 :]
    _, (_, above) = towards(None, None)
    side = near[pl.ds(near.shape[0] - SUB, SUB)]
    for way, here in ((True, above), (False, jnp.logical_not(above))):
        pl.when(here)(
            lambda: one_side((near_early, near), side, way, grid, coef, poly, lambda m, found: None)
        )


def outer_kernel(far_early, far, sums, *rest):
    *rest, lines, done = rest
    out, grid, coef, sol, result, *poly = rest[len(rest) // 2 :]
    rows, columns = out.shape[1:]
    lane = lax.broadcasted_iota(jnp.int32, (SUB, LANES), 1)
    (_, above), _ = towards(None, None)

    def far_rows(above):
        side = far[pl.ds(far.shape[0] - SUB, SUB)]
        whole = side_rows(rows, above)
        inside = 1 if above else -1
        edges = [whole[-1] + inside, whole[-1] + 2 * inside]
        acc = {}
        for r in edges + [r for k, r in enumerate(whole) if known(k) >= 0]:
            for g in range(3):
                acc[g, r] = sol[g, r - (REACH - 1)]

        def each(m, found):
            part = [r for k, r in enumerate(whole) if known(k) < m]
            held = [r for r in part if (0, r) in found]
            add(acc, sums, poly, m, held, found)
            add(acc, sums, poly, m, [r for r in part if r not in held])

        one_side((far_early, far), side, above, grid, coef, poly, each)
        span = [r for r in whole + edges[:1] if REACH <= r < REACH + rows]
        finish(grid, sums, result, acc, span)

    pl.when(above)(lambda: far_rows(True))
    pl.when(jnp.logical_not(above))(lambda: far_rows(False))

    moves = []
    for k in range(3):
        for g in range(rows // SUB):
            cut = pl.ds(g * SUB, SUB)
            for t in range(columns // LANES):
                one = result[k, pl.Slice(g * SUB * SUB + 2 * t, SUB, SUB), :]
                two = result[k, pl.Slice(g * SUB * SUB + 2 * t + 1, SUB, SUB), :]
                joined = jnp.where(lane < HALF, turn(one, -SIDE), turn(two, SIDE))
                lines[k, cut, pl.ds(t * LANES, LANES)] = joined
            move = pltpu.make_async_copy(lines.at[k, cut], out.at[k, cut], done.at[k, g])
            move.start()
            moves.append(move)
    for move in moves:
        move.wait()


def shards(state, depth, pole_real, pole_imag, pole_weight):
    rows, columns = depth.shape
    poles = pole_real.shape[0]
    vmem = pl.BlockSpec(memory_space=pltpu.VMEM)
    small = pltpu.CompilerParams(vmem_limit_bytes=GRANT)

    def f32(*shape):
        return jax.ShapeDtypeStruct(shape, jnp.float32)

    given = [
        pltpu.with_memory_space_constraint(x, pltpu.HBM)
        for x in (state, depth, pole_real[None], pole_imag[None], pole_weight)
    ]
    hbm = pl.BlockSpec(memory_space=pltpu.HBM)
    message = pltpu.VMEM((rows, LANES), jnp.float32)
    fields, first, second = pl.pallas_call(
        pack_columns_kernel,
        out_shape=(pltpu.VMEM((4, rows, columns), jnp.float32), message, message),
        in_specs=[hbm] * 5,
        out_specs=(vmem,) * 3,
        scratch_shapes=[
            pltpu.VMEM((1, poles), jnp.float32),
            pltpu.VMEM((1, poles), jnp.float32),
            pltpu.VMEM((2, poles), jnp.float32),
            pltpu.SemaphoreType.DMA((5,)),
        ],
        compiler_params=small,
        name="pack_columns",
    )(*given)
    blocks = 4 * columns // LANES + 2
    half = blocks // 2 * SUB
    parts = (half + SUB + 4, half, half + SUB, half - SUB, max(4 * poles, half))
    far_early, far, near_early, near, scalars = pl.pallas_call(
        functools.partial(pack_rows_kernel, 4 * poles),
        out_shape=tuple(f32(part, LANES) for part in parts),
        in_specs=[vmem] * 3,
        out_specs=(vmem,) * 5,
        compiler_params=small,
        name="pack_rows",
    )(fields, second, first)
    second = swap(second, "pole", 1)
    first = swap(first, "pole", 0)
    far, near = pl.pallas_call(
        pack_sides_kernel,
        out_shape=(f32(*far.shape), f32(*near.shape)),
        in_specs=[vmem] * 4,
        out_specs=(vmem, vmem),
        input_output_aliases={2: 0, 3: 1},
        compiler_params=small,
        name="pack_sides",
    )(second, first, far, near)
    far_early = swap(far_early, "tile", 1)
    far = swap(far, "tile", 1)
    near_early = swap(near_early, "tile", 0)
    near = swap(near, "tile", 0)
    count = lax.axis_size("pole")
    others = jnp.stack([shift(scalars, "pole", step) for step in range(2, count - 1)])
    height = rows + 2 * REACH
    grid = f32(height * 4 * SUB, LANES)
    poly = [f32(3, height, SUB, LANES)] * ITERS
    coef = f32(4, height, SUB, LANES)
    sol = f32(3, rows + 2, SUB, LANES)
    result = f32(3, rows * SUB, LANES)
    state_of = (grid, coef, *poly)
    cost = pl.CostEstimate(
        flops=10 * ITERS * rows * SUB * LANES,
        bytes_accessed=4 * SUB * LANES * rows * (4 + 2 * ITERS + 2),
        transcendentals=0,
    )
    held = pl.pallas_call(
        inner_kernel,
        out_shape=state_of,
        in_specs=[vmem] * 3,
        out_specs=(vmem,) * len(state_of),
        compiler_params=small,
        cost_estimate=cost,
        name="inner",
    )(fields, first, second)
    held = pl.pallas_call(
        mid_kernel,
        out_shape=state_of,
        in_specs=[vmem] * (2 + len(state_of)),
        out_specs=(vmem,) * len(state_of),
        input_output_aliases={2 + i: i for i in range(len(state_of))},
        compiler_params=small,
        cost_estimate=cost,
        name="mid",
    )(near_early, near, *held)
    grid_held, coef_held, *poly_held = held
    sums, *part = pl.pallas_call(
        functools.partial(pole_sums_kernel, 4 * poles),
        out_shape=(f32(9 * ITERS + 2, SUB, LANES), sol, result),
        in_specs=[vmem] * (5 + ITERS),
        out_specs=(vmem,) * 3,
        compiler_params=small,
        name="pole_sums",
    )(scalars, first, second, others, grid_held, *poly_held)
    kept = (grid, coef, sol, result, *poly)
    return pl.pallas_call(
        outer_kernel,
        out_shape=(f32(*state.shape), *kept),
        in_specs=[vmem] * (3 + len(kept)),
        out_specs=(hbm, *(vmem,) * len(kept)),
        scratch_shapes=[
            pltpu.VMEM(state.shape, jnp.float32),
            pltpu.SemaphoreType.DMA((3, rows // SUB)),
        ],
        input_output_aliases={3 + i: 1 + i for i in range(len(kept))},
        compiler_params=small,
        name="outer",
    )(far_early, far, sums, grid_held, coef_held, *part, *poly_held)[0]


def solution(mesh):
    return jax.shard_map(
        shards,
        mesh=mesh,
        in_specs=(
            P(None, "tile", "pole"),
            P("tile", "pole"),
            P("pole"),
            P("pole"),
            P(None, "pole"),
        ),
        out_specs=P(None, "tile", "pole"),
        check_vma=False,
    )
```

```python
import functools

import jax
import jax.numpy as jnp
from jax import lax
from jax.experimental import pallas as pl
from jax.experimental.pallas import tpu as pltpu
from jax.sharding import PartitionSpec as P

ITERS = 8
REACH = ITERS + 1
SUB = 8
LANES = 128
HALF = LANES // 2
SIDE = 32
EDGE = REACH
EAST = HALF + EDGE
GRANT = 16 * 1024 * 1024

coriolis = 0.7
centre = 8.0
half_width = 8.0


def pairs(count, phase):
    swap = []
    for i in range(phase, count + phase, 2):
        a, b = i % count, (i + 1) % count
        swap += [(a, b), (b, a)]
    return swap


def swap(block, axis, phase):
    return lax.ppermute(block, axis, pairs(lax.axis_size(axis), phase))


def shift(block, axis, step):
    count = lax.axis_size(axis)
    return lax.ppermute(block, axis, [(i, (i + step) % count) for i in range(count)])


def turn(x, lanes):
    return pltpu.roll(x, lanes % LANES, 1) if lanes % LANES else x


def cmul(a, b):
    return (a[0] * b[0] - a[1] * b[1], a[0] * b[1] + a[1] * b[0])


def cinv(a):
    norm = 1.0 / (a[0] * a[0] + a[1] * a[1])
    return (a[0] * norm, -a[1] * norm)


def cscale(a, factor):
    return (a[0] * factor, a[1] * factor)


def pack_columns_kernel(
    state, depth, real, imag, weight, fields, first, second, real_in, imag_in, weight_in, done
):
    rows, columns = depth.shape
    halves = [pl.ds(0, rows // 2), pl.ds(rows // 2, rows // 2)]
    moves = []
    for f in range(4):
        source = depth if f == 3 else state.at[f]
        for cut in halves:
            move = (source.at[cut], fields.at[f, cut])
            moves.append(pltpu.make_async_copy(*move, done.at[len(moves)]))
    for move in ((real, real_in), (imag, imag_in), (weight, weight_in)):
        moves.append(pltpu.make_async_copy(*move, done.at[len(moves)]))
    for move in moves:
        move.start()
    for move in moves:
        move.wait()
    odd = lax.rem(lax.axis_index("pole"), 2) == 1
    lane = lax.broadcasted_iota(jnp.int32, (SUB, LANES), 1)
    sub = lax.broadcasted_iota(jnp.int32, (SUB, LANES), 0)
    poles = real.shape[0]
    values = [real_in[i] for i in range(poles)] + [imag_in[i] for i in range(poles)]
    values += [weight_in[0, i] for i in range(poles)] + [weight_in[1, i] for i in range(poles)]
    for g in range(rows // SUB):
        cut = pl.ds(g * SUB, SUB)
        west = [fields[f, cut, 0:LANES] for f in range(4)]
        east = [fields[f, cut, columns - LANES : columns] for f in range(4)]
        west += [west[3] * west[1], west[3] * west[2]]
        east += [east[3] * east[1], east[3] * east[2]]
        rest = jnp.zeros((SUB, LANES), jnp.float32)
        for i, value in enumerate(values[g * SUB : (g + 1) * SUB]):
            rest = jnp.where(sub == i, value, rest)
        eastward = rest
        westward = rest
        for f in range(6):
            low, high = EDGE * f, EDGE * (f + 1)
            take = jnp.logical_and(lane >= low, lane < high)
            eastward = jnp.where(take, turn(east[f], low + EDGE), eastward)
            take = jnp.logical_and(lane >= EAST + low, lane < EAST + high)
            westward = jnp.where(take, turn(west[f], EAST + low), westward)
        first[cut, :] = jnp.where(odd, westward, eastward)
        second[cut, :] = jnp.where(odd, eastward, westward)


def pack_rows_kernel(count, fields, second, first, far_early, far, near_early, near, scalars):
    rows = fields.shape[1]
    for parts, low in towards((far_early, far), (near_early, near)):
        at = 0
        for part in parts:
            pl.when(low)(lambda: pack_rows(part, at, fields, 0, SUB))
            pl.when(jnp.logical_not(low))(
                lambda: pack_rows(part, at, fields, rows - SUB, rows - SUB - 1)
            )
            at += part.shape[0] // SUB
    odd = lax.rem(lax.axis_index("pole"), 2) == 1
    lane = lax.broadcasted_iota(jnp.int32, (SUB, LANES), 1)
    from_first = jnp.logical_xor(lane >= HALF, odd)
    for g in range(0, scalars.shape[0], SUB):
        if g < count:
            block = jnp.where(from_first, first[pl.ds(g, SUB)], second[pl.ds(g, SUB)])
        else:
            block = jnp.zeros((SUB, LANES), jnp.float32)
        scalars[pl.ds(g, SUB)] = block


def towards(far, near):
    odd = lax.rem(lax.axis_index("tile"), 2) == 1
    return ((far, jnp.logical_not(odd)), (near, odd))


def pack_rows(target, at, fields, main, ext):
    tiles = fields.shape[2] // LANES
    for i in range(target.shape[0] // SUB):
        f, t = divmod(at + i, tiles)
        if f < 4:
            block = fields[f, main : main + SUB, t * LANES : (t + 1) * LANES]
            target[pl.ds(i * SUB, SUB)] = block
        elif t == 0:
            for f in (1, 2):
                flux = fields[3, ext : ext + 1, :] * fields[f, ext : ext + 1, :]
                for t in range(tiles):
                    row = i * SUB + (f - 1) * tiles + t
                    target[row : row + 1] = flux[:, t * LANES : (t + 1) * LANES]


def block_of(parts, at):
    early, late = parts
    count = early.shape[0] // SUB
    if at < count:
        return early[pl.ds(at * SUB, SUB)]
    return late[pl.ds((at - count) * SUB, SUB)]


def sides_of(first, second, cut):
    odd = lax.rem(lax.axis_index("pole"), 2) == 1
    lane = lax.broadcasted_iota(jnp.int32, (SUB, LANES), 1)
    from_first = jnp.logical_xor(lane >= HALF, odd)
    return jnp.where(from_first, first[cut, :], second[cut, :])


def pack_sides_kernel(second, first, far_in, near_in, far, near):
    for target, low in towards(far, near):
        target[pl.ds(target.shape[0] - SUB, SUB)] = pack_sides(second, first, low)


def pack_sides(second, first, low):
    rows = first.shape[0]
    sub = lax.broadcasted_iota(jnp.int32, (SUB, LANES), 0)
    lane = lax.broadcasted_iota(jnp.int32, (SUB, LANES), 1)
    side = jnp.where(
        low,
        sides_of(first, second, pl.ds(0, SUB)),
        sides_of(first, second, pl.ds(rows - SUB, SUB)),
    )
    line = jnp.where(
        low,
        sides_of(first, second, pl.ds(SUB, SUB))[0:1],
        sides_of(first, second, pl.ds(rows - 2 * SUB, SUB))[SUB - 1 : SUB],
    )
    line = jnp.broadcast_to(line, (SUB, LANES))
    low, high = 4 * EDGE, 6 * EDGE
    take = jnp.logical_or(
        jnp.logical_and(lane >= low, lane < high),
        jnp.logical_and(lane >= EAST + low, lane < EAST + high),
    )
    side = jnp.where(jnp.logical_and(take, sub == 0), line, side)
    return side


def pole_sums_kernel(count, scalars, first, second, others, grid, *rest):
    poly, (sums, sol, result) = rest[:ITERS], rest[ITERS:]
    odd = lax.rem(lax.axis_index("pole"), 2) == 1
    lane = lax.broadcasted_iota(jnp.int32, (SUB, LANES), 1)
    blocks = [[scalars[pl.ds(g, SUB)] for g in range(0, count, SUB)]]
    for i, message in enumerate((first, second)):
        low = jnp.logical_xor(lane < HALF, odd if i == 0 else jnp.logical_not(odd))
        part = []
        for g in range(0, count, SUB):
            x = message[pl.ds(g, SUB), :]
            part.append(jnp.where(low, x, turn(x, HALF)))
        blocks.append(part)
    for i in range(others.shape[0]):
        blocks.append([others[i, pl.ds(g, SUB)] for g in range(0, count, SUB)])
    poles = count // 4
    quantity = []
    for q in range(4):
        cut = []
        for block in blocks:
            whole = jnp.concatenate(block, axis=0)
            cut.append(whole[q * poles : (q + 1) * poles])
        quantity.append(jnp.concatenate(cut, axis=0))
    alpha = (quantity[0], quantity[1])
    beta = (quantity[2], quantity[3])
    square = cmul(alpha, alpha)
    shifted = (square[0] + coriolis * coriolis, square[1])
    sigma = ((shifted[0] + centre) / half_width, shifted[1] / half_width)
    rho = [cinv(sigma)]
    for j in range(1, ITERS):
        rho.append(cinv((2.0 * sigma[0] - rho[-1][0], 2.0 * sigma[1] - rho[-1][1])))
    gain = None
    start = []
    for m in range(ITERS):
        if m == 0:
            start.append(cscale(rho[0], 1.0 / half_width))
        else:
            gain = rho[0] if gain is None else cmul(gain, rho[m - 1])
            start.append(cscale(cmul(rho[m], gain), 2.0 / half_width))
    tail = None
    weight = [None] * ITERS
    for m in reversed(range(ITERS)):
        if tail is None:
            weight[m] = start[m]
            tail = (jnp.ones_like(sigma[0]), jnp.zeros_like(sigma[0]))
        else:
            tail = cmul(cmul(rho[m + 1], rho[m]), tail)
            tail = (tail[0] + 1.0, tail[1])
            weight[m] = cmul(start[m], tail)
    inverse_alpha = cinv(alpha)
    inverse_shift = cinv(shifted)
    by_alpha = cmul(beta, inverse_alpha)
    by_shift = cmul(beta, inverse_shift)
    products = {
        "b": beta,
        "b/a": by_alpha,
        "b/s": by_shift,
        "bs/a": cmul(by_alpha, shifted),
        "ba/s": cmul(by_shift, alpha),
        "b/as": cmul(by_alpha, inverse_shift),
    }

    def total(x):
        s = x[0:SUB]
        for i in range(1, x.shape[0] // SUB):
            s = s + x[i * SUB : (i + 1) * SUB]
        for step in (4, 2, 1):
            s = s + pltpu.roll(s, step, 0)
        return s

    names = [("bs/a", "b", "b/a"), ("b", "ba/s", "b/s"), ("b/a", "b/s", "b/as")]
    factor = (1.0, -1.0, -coriolis)
    found = {}
    for m in range(ITERS):
        for name, w in products.items():
            found[name, m] = total(w[0] * weight[m][0] - w[1] * weight[m][1])
        for g in range(3):
            for f in range(3):
                value = found[names[g][f], m]
                sums[(g * 3 + f) * ITERS + m] = value if f == 0 else factor[f] * value
    sums[9 * ITERS] = total(products["ba/s"][0])
    sums[9 * ITERS + 1] = coriolis * total(products["b/s"][0])

    _, (_, above) = towards(None, None)
    rows = sol.shape[1] - 2

    def near_rows(above):
        near, far = side_rows(rows, above), side_rows(rows, not above)
        acc = {}
        for m in range(ITERS):
            add(acc, sums, poly, m, near)
        for m in range(ITERS - 1):
            add(acc, sums, poly, m, [r for k, r in enumerate(far) if known(k) >= m])
        for (g, r), v in acc.items():
            sol[g, r - (REACH - 1)] = v
        inside = sorted(near)[1:-1]
        finish(grid, sums, result, acc, [r for r in inside if REACH <= r < REACH + rows])

    pl.when(above)(lambda: near_rows(True))
    pl.when(jnp.logical_not(above))(lambda: near_rows(False))


def side_rows(rows, above):
    low, high = REACH - 1, REACH + rows
    return [low + k if above else high - k for k in range(rows // 2 + 1)]


def known(k):
    return max(min(ITERS - 2, k - 2), -1)


def add(acc, sums, poly, m, rows, values=None):
    for f in range(3):
        if not rows:
            return
        value = {r: poly[m][f, r] if values is None else values[f, r] for r in rows}
        for g in range(3):
            c = sums[(g * 3 + f) * ITERS + m]
            for r in rows:
                acc[g, r] = acc[g, r] + c * value[r] if (g, r) in acc else c * value[r]


def finish(grid, sums, result, acc, span):
    push = sums[9 * ITERS]
    lift = sums[9 * ITERS + 1]
    for r in span:
        u, v = cell(grid, 1, r), cell(grid, 2, r)
        at = pl.ds((r - REACH) * SUB, SUB)
        result[0, at] = acc[0, r]
        east = 0.5 * (acc[1, r + 1] - acc[1, r - 1])
        north = 0.5 * (right(acc[2, r]) - left(acc[2, r]))
        result[1, at] = (push * u + lift * v) - (east + coriolis * north)
        east = 0.5 * (acc[2, r + 1] - acc[2, r - 1])
        north = 0.5 * (right(acc[1, r]) - left(acc[1, r]))
        result[2, at] = (push * v - lift * u) + (coriolis * east - north)


def strips_of(tiles, side):
    lane = lax.broadcasted_iota(jnp.int32, (SUB, LANES), 1)
    up = [turn(tile, SIDE) for tile in tiles]
    down = [turn(tile, -SIDE) for tile in tiles]
    out = []
    for q in range(len(tiles)):
        out.append(jnp.where(lane < SIDE, up[q - 1] if q else side, up[q]))
        after = down[q + 1] if q + 1 < len(tiles) else side
        out.append(jnp.where(lane < LANES - SIDE, down[q], after))
    return out


def lay(grid, cut, side, at, stride):
    for s, strip in enumerate(strips_of(cut, side)):
        grid[pl.Slice(at * SUB + s, SUB, stride * SUB), :] = strip


def place(side, f):
    return turn(side, SIDE - EDGE - EDGE * f)


def lay_halo(grid, halo, side, main, ext):
    lane = lax.broadcasted_iota(jnp.int32, (SUB, LANES), 1)
    sub = lax.broadcasted_iota(jnp.int32, (SUB, LANES), 0)
    tiles = SUB // 2
    for f in range(4):
        cut = [block_of(halo, f * tiles + t) for t in range(tiles)]
        lay(grid, cut, place(side, f), main * 4 + f, 4)
    line = jnp.broadcast_to(side[0:1], (SUB, LANES))
    side = jnp.where(sub < tiles, place(line, 4), place(line, 5))
    block = block_of(halo, 4 * tiles)
    up, down = turn(block, SIDE), turn(block, -SIDE)
    before = jnp.where(sub % tiles == 0, side, pltpu.roll(up, 1, 0))
    after = jnp.where(sub % tiles == tiles - 1, side, pltpu.roll(down, SUB - 1, 0))
    even = jnp.where(lane < SIDE, before, up)
    odd = jnp.where(lane < LANES - SIDE, down, after)
    for f in (1, 2):
        at = (ext * 4 + f) * SUB
        cut = slice((f - 1) * tiles, f * tiles)
        grid[pl.Slice(at, tiles, 2), :] = even[cut]
        grid[pl.Slice(at + 1, tiles, 2), :] = odd[cut]


def cell(grid, f, r):
    return grid[pl.ds(pl.multiple_of((r * 4 + f) * SUB, SUB), SUB), :]


def left(x):
    return pltpu.roll(x, 1, 1)


def right(x):
    return pltpu.roll(x, LANES - 1, 1)


def prepare(grid, poly, coef, start, count):
    flux_east = [None] * 3
    flux_north = [None] * 3
    depths = [None] * 2
    across = None
    found = {}
    for k in range(count + 2):
        r = start + k
        h = cell(grid, 3, r)
        flux_east = flux_east[1:] + [h * cell(grid, 1, r)]
        flux_north = flux_north[1:] + [h * cell(grid, 2, r)]
        depths = depths[1:] + [h]
        if k >= 1:
            before, across = across, 0.125 * (depths[0] + depths[1])
            coef[0, r - 1] = across
        if k >= 2:
            c = r - 1
            north = 0.125 * (depths[0] + right(depths[0]))
            south = 0.125 * (depths[0] + left(depths[0]))
            coef[1, c] = north
            coef[2, c] = south
            coef[3, c] = 2.0 - ((across + before) + (north + south))
            east_slope = flux_east[2] - flux_east[0]
            north_slope = right(flux_north[1]) - left(flux_north[1])
            poly[0][1, c] = found[1, c] = 0.5 * (east_slope + north_slope)
            east_slope = flux_north[2] - flux_north[0]
            north_slope = right(flux_east[1]) - left(flux_east[1])
            poly[0][2, c] = found[2, c] = 0.5 * (east_slope - north_slope)
            poly[0][0, c] = found[0, c] = cell(grid, 0, c)
    return found


def sweep(poly, coef, m, start, count, last, upwards=False):
    def take(f, r):
        return last[f, r] if (f, r) in last else poly[m][f, r]

    step = -1 if upwards else 1
    order = range(start, start + count)[::step]
    back = [take(f, order[0] - step) for f in range(3)]
    here = [take(f, order[0]) for f in range(3)]
    found = {}
    for r in order:
        north, south, diag = coef[1, r], coef[2, r], coef[3, r]
        above, below = coef[0, r], coef[0, r - 1]
        ahead = [take(f, r + step) for f in range(3)]
        for f in range(3):
            up, down = (back, ahead) if upwards else (ahead, back)
            value = diag * here[f]
            if m > 0:
                value = value - poly[m - 1][f, r]
            value = value + above * up[f]
            value = value + below * down[f]
            value = value + north * right(here[f])
            value = value + south * left(here[f])
            value = 0.5 * value if m == 0 else value
            poly[m + 1][f, r] = value
            found[f, r] = value
        back, here = here, ahead
    return found


def inner_kernel(fields, first, second, grid, coef, *poly):
    rows = fields.shape[1]
    for g in range(rows // SUB):
        side = sides_of(first, second, pl.ds(g * SUB, SUB))
        for f in range(4):
            cut = [
                fields[f, pl.ds(g * SUB, SUB), pl.ds(t * LANES, LANES)]
                for t in range(fields.shape[2] // LANES)
            ]
            lay(grid, cut, place(side, f), (REACH + g * SUB) * 4 + f, 4)
    found = prepare(grid, poly, coef, REACH, rows - 2)
    for m in range(ITERS - 1):
        if rows - 4 - 2 * m > 0:
            found = sweep(poly, coef, m, REACH + 2 + m, rows - 4 - 2 * m, found)


def one_side(halo, side, above, grid, coef, poly, each):
    below = coef.shape[1] - REACH
    main, ext, start = (1, 0, 0) if above else (below, below + SUB, below - 2)
    grid[pl.ds((ext * 4 + 3) * SUB, SUB), :] = jnp.ones((SUB, LANES), jnp.float32)
    lay_halo(grid, halo, side, main, ext)
    found = prepare(grid, poly, coef, start, REACH)
    each(0, found)
    for m in range(ITERS - 1):
        low = 2 + m if above else below - 2 - m
        found = sweep(poly, coef, m, low, REACH, found, above)
        each(m + 1, found)


def mid_kernel(near_early, near, *rest):
    grid, coef, *poly = rest[len(rest) // 2 :]
    _, (_, above) = towards(None, None)
    side = near[pl.ds(near.shape[0] - SUB, SUB)]
    for way, here in ((True, above), (False, jnp.logical_not(above))):
        pl.when(here)(
            lambda: one_side((near_early, near), side, way, grid, coef, poly, lambda m, found: None)
        )


def outer_kernel(far_early, far, sums, *rest):
    *rest, lines, done = rest
    out, grid, coef, sol, result, *poly = rest[len(rest) // 2 :]
    rows, columns = out.shape[1:]
    lane = lax.broadcasted_iota(jnp.int32, (SUB, LANES), 1)
    (_, above), _ = towards(None, None)

    def far_rows(above):
        side = far[pl.ds(far.shape[0] - SUB, SUB)]
        whole = side_rows(rows, above)
        inside = 1 if above else -1
        edges = [whole[-1] + inside, whole[-1] + 2 * inside]
        acc = {}
        for r in edges + [r for k, r in enumerate(whole) if known(k) >= 0]:
            for g in range(3):
                acc[g, r] = sol[g, r - (REACH - 1)]

        def each(m, found):
            part = [r for k, r in enumerate(whole) if known(k) < m]
            held = [r for r in part if (0, r) in found]
            add(acc, sums, poly, m, held, found)
            add(acc, sums, poly, m, [r for r in part if r not in held])

        one_side((far_early, far), side, above, grid, coef, poly, each)
        span = [r for r in whole + edges[:1] if REACH <= r < REACH + rows]
        finish(grid, sums, result, acc, span)

    pl.when(above)(lambda: far_rows(True))
    pl.when(jnp.logical_not(above))(lambda: far_rows(False))

    moves = []
    for k in range(3):
        for g in range(rows // SUB):
            cut = pl.ds(g * SUB, SUB)
            for t in range(columns // LANES):
                one = result[k, pl.Slice(g * SUB * SUB + 2 * t, SUB, SUB), :]
                two = result[k, pl.Slice(g * SUB * SUB + 2 * t + 1, SUB, SUB), :]
                joined = jnp.where(lane < HALF, turn(one, -SIDE), turn(two, SIDE))
                lines[k, cut, pl.ds(t * LANES, LANES)] = joined
            move = pltpu.make_async_copy(lines.at[k, cut], out.at[k, cut], done.at[k, g])
            move.start()
            moves.append(move)
    for move in moves:
        move.wait()


def shards(state, depth, pole_real, pole_imag, pole_weight):
    rows, columns = depth.shape
    poles = pole_real.shape[0]
    vmem = pl.BlockSpec(memory_space=pltpu.VMEM)
    small = pltpu.CompilerParams(vmem_limit_bytes=GRANT)

    def f32(*shape):
        return jax.ShapeDtypeStruct(shape, jnp.float32)

    given = [
        pltpu.with_memory_space_constraint(x, pltpu.HBM)
        for x in (state, depth, pole_real, pole_imag, pole_weight)
    ]
    hbm = pl.BlockSpec(memory_space=pltpu.HBM)
    message = pltpu.VMEM((rows, LANES), jnp.float32)
    fields, first, second = pl.pallas_call(
        pack_columns_kernel,
        out_shape=(pltpu.VMEM((4, rows, columns), jnp.float32), message, message),
        in_specs=[hbm] * 5,
        out_specs=(vmem,) * 3,
        scratch_shapes=[
            pltpu.SMEM(pole_real.shape, jnp.float32),
            pltpu.SMEM(pole_imag.shape, jnp.float32),
            pltpu.SMEM(pole_weight.shape, jnp.float32),
            pltpu.SemaphoreType.DMA((11,)),
        ],
        compiler_params=small,
        name="pack_columns",
    )(*given)
    blocks = 4 * columns // LANES + 2
    half = blocks // 2 * SUB
    parts = (half + SUB + 4, half, half + SUB, half - SUB, max(4 * poles, half))
    far_early, far, near_early, near, scalars = pl.pallas_call(
        functools.partial(pack_rows_kernel, 4 * poles),
        out_shape=tuple(f32(part, LANES) for part in parts),
        in_specs=[vmem] * 3,
        out_specs=(vmem,) * 5,
        compiler_params=small,
        name="pack_rows",
    )(fields, second, first)
    second = swap(second, "pole", 1)
    first = swap(first, "pole", 0)
    far, near = pl.pallas_call(
        pack_sides_kernel,
        out_shape=(f32(*far.shape), f32(*near.shape)),
        in_specs=[vmem] * 4,
        out_specs=(vmem, vmem),
        input_output_aliases={2: 0, 3: 1},
        compiler_params=small,
        name="pack_sides",
    )(second, first, far, near)
    far_early = swap(far_early, "tile", 1)
    far = swap(far, "tile", 1)
    near_early = swap(near_early, "tile", 0)
    near = swap(near, "tile", 0)
    count = lax.axis_size("pole")
    others = jnp.stack([shift(scalars, "pole", step) for step in range(2, count - 1)])
    height = rows + 2 * REACH
    grid = f32(height * 4 * SUB, LANES)
    poly = [f32(3, height, SUB, LANES)] * ITERS
    coef = f32(4, height, SUB, LANES)
    sol = f32(3, rows + 2, SUB, LANES)
    result = f32(3, (rows + 1) * SUB, LANES)
    state_of = (grid, coef, *poly)
    cost = pl.CostEstimate(
        flops=10 * ITERS * rows * SUB * LANES,
        bytes_accessed=4 * SUB * LANES * rows * (4 + 2 * ITERS + 2),
        transcendentals=0,
    )
    held = pl.pallas_call(
        inner_kernel,
        out_shape=state_of,
        in_specs=[vmem] * 3,
        out_specs=(vmem,) * len(state_of),
        compiler_params=small,
        cost_estimate=cost,
        name="inner",
    )(fields, first, second)
    held = pl.pallas_call(
        mid_kernel,
        out_shape=state_of,
        in_specs=[vmem] * (2 + len(state_of)),
        out_specs=(vmem,) * len(state_of),
        input_output_aliases={2 + i: i for i in range(len(state_of))},
        compiler_params=small,
        cost_estimate=cost,
        name="mid",
    )(near_early, near, *held)
    grid_held, coef_held, *poly_held = held
    sums, *part = pl.pallas_call(
        functools.partial(pole_sums_kernel, 4 * poles),
        out_shape=(f32(9 * ITERS + 2, SUB, LANES), sol, result),
        in_specs=[vmem] * (5 + ITERS),
        out_specs=(vmem,) * 3,
        compiler_params=small,
        name="pole_sums",
    )(scalars, first, second, others, grid_held, *poly_held)
    kept = (grid, coef, sol, result, *poly)
    return pl.pallas_call(
        outer_kernel,
        out_shape=(f32(*state.shape), *kept),
        in_specs=[vmem] * (3 + len(kept)),
        out_specs=(hbm, *(vmem,) * len(kept)),
        scratch_shapes=[
            pltpu.VMEM(state.shape, jnp.float32),
            pltpu.SemaphoreType.DMA((3, rows // SUB)),
        ],
        input_output_aliases={3 + i: 1 + i for i in range(len(kept))},
        compiler_params=small,
        name="outer",
    )(far_early, far, sums, grid_held, coef_held, *part, *poly_held)[0]


def solution(mesh):
    return jax.shard_map(
        shards,
        mesh=mesh,
        in_specs=(
            P(None, "tile", "pole"),
            P("tile", "pole"),
            P("pole"),
            P("pole"),
            P(None, "pole"),
        ),
        out_specs=P(None, "tile", "pole"),
        check_vma=False,
    )
```

```python
import functools

import jax
import jax.numpy as jnp
from jax import lax
from jax.experimental import pallas as pl
from jax.experimental.pallas import tpu as pltpu
from jax.sharding import PartitionSpec as P

ITERS = 8
REACH = ITERS + 1
SUB = 8
LANES = 128
HALF = LANES // 2
SIDE = 32
EDGE = REACH
EAST = HALF + EDGE
GRANT = 16 * 1024 * 1024

coriolis = 0.7
centre = 8.0
half_width = 8.0


def pairs(count, phase):
    swap = []
    for i in range(phase, count + phase, 2):
        a, b = i % count, (i + 1) % count
        swap += [(a, b), (b, a)]
    return swap


def swap(block, axis, phase):
    return lax.ppermute(block, axis, pairs(lax.axis_size(axis), phase))


def shift(block, axis, step):
    count = lax.axis_size(axis)
    return lax.ppermute(block, axis, [(i, (i + step) % count) for i in range(count)])


def turn(x, lanes):
    return pltpu.roll(x, lanes % LANES, 1) if lanes % LANES else x


def cmul(a, b):
    return (a[0] * b[0] - a[1] * b[1], a[0] * b[1] + a[1] * b[0])


def cinv(a):
    norm = 1.0 / (a[0] * a[0] + a[1] * a[1])
    return (a[0] * norm, -a[1] * norm)


def cscale(a, factor):
    return (a[0] * factor, a[1] * factor)


def pack_columns_kernel(
    state, depth, real, imag, weight, fields, first, second, real_in, imag_in, weight_in, done
):
    moves = [
        pltpu.make_async_copy(depth, fields.at[3], done.at[0]),
        pltpu.make_async_copy(state, fields.at[pl.ds(0, 3)], done.at[1]),
        pltpu.make_async_copy(real, real_in, done.at[2]),
        pltpu.make_async_copy(imag, imag_in, done.at[3]),
        pltpu.make_async_copy(weight, weight_in, done.at[4]),
    ]
    for move in moves:
        move.start()
    for move in moves:
        move.wait()
    odd = lax.rem(lax.axis_index("pole"), 2) == 1
    rows, columns = fields.shape[1:]
    lane = lax.broadcasted_iota(jnp.int32, (SUB, LANES), 1)
    sub = lax.broadcasted_iota(jnp.int32, (SUB, LANES), 0)
    poles = real.shape[0]
    values = [real_in[i] for i in range(poles)] + [imag_in[i] for i in range(poles)]
    values += [weight_in[0, i] for i in range(poles)] + [weight_in[1, i] for i in range(poles)]
    for g in range(rows // SUB):
        cut = pl.ds(g * SUB, SUB)
        west = [fields[f, cut, 0:LANES] for f in range(4)]
        east = [fields[f, cut, columns - LANES : columns] for f in range(4)]
        west += [west[3] * west[1], west[3] * west[2]]
        east += [east[3] * east[1], east[3] * east[2]]
        rest = jnp.zeros((SUB, LANES), jnp.float32)
        for i, value in enumerate(values[g * SUB : (g + 1) * SUB]):
            rest = jnp.where(sub == i, value, rest)
        eastward = rest
        westward = rest
        for f in range(6):
            low, high = EDGE * f, EDGE * (f + 1)
            take = jnp.logical_and(lane >= low, lane < high)
            eastward = jnp.where(take, turn(east[f], low + EDGE), eastward)
            take = jnp.logical_and(lane >= EAST + low, lane < EAST + high)
            westward = jnp.where(take, turn(west[f], EAST + low), westward)
        first[cut, :] = jnp.where(odd, westward, eastward)
        second[cut, :] = jnp.where(odd, eastward, westward)


def pack_rows_kernel(count, fields, second, first, far_early, far, near_early, near, scalars):
    rows = fields.shape[1]
    for parts, low in towards((far_early, far), (near_early, near)):
        at = 0
        for part in parts:
            pl.when(low)(lambda: pack_rows(part, at, fields, 0, SUB))
            pl.when(jnp.logical_not(low))(
                lambda: pack_rows(part, at, fields, rows - SUB, rows - SUB - 1)
            )
            at += part.shape[0] // SUB
    odd = lax.rem(lax.axis_index("pole"), 2) == 1
    lane = lax.broadcasted_iota(jnp.int32, (SUB, LANES), 1)
    from_first = jnp.logical_xor(lane >= HALF, odd)
    for g in range(0, scalars.shape[0], SUB):
        if g < count:
            block = jnp.where(from_first, first[pl.ds(g, SUB)], second[pl.ds(g, SUB)])
        else:
            block = jnp.zeros((SUB, LANES), jnp.float32)
        scalars[pl.ds(g, SUB)] = block


def towards(far, near):
    odd = lax.rem(lax.axis_index("tile"), 2) == 1
    return ((far, jnp.logical_not(odd)), (near, odd))


def pack_rows(target, at, fields, main, ext):
    tiles = fields.shape[2] // LANES
    for i in range(target.shape[0] // SUB):
        f, t = divmod(at + i, tiles)
        if f < 4:
            block = fields[f, main : main + SUB, t * LANES : (t + 1) * LANES]
            target[pl.ds(i * SUB, SUB)] = block
        elif t == 0:
            for f in (1, 2):
                flux = fields[3, ext : ext + 1, :] * fields[f, ext : ext + 1, :]
                for t in range(tiles):
                    row = i * SUB + (f - 1) * tiles + t
                    target[row : row + 1] = flux[:, t * LANES : (t + 1) * LANES]


def block_of(parts, at):
    early, late = parts
    count = early.shape[0] // SUB
    if at < count:
        return early[pl.ds(at * SUB, SUB)]
    return late[pl.ds((at - count) * SUB, SUB)]


def sides_of(first, second, cut):
    odd = lax.rem(lax.axis_index("pole"), 2) == 1
    lane = lax.broadcasted_iota(jnp.int32, (SUB, LANES), 1)
    from_first = jnp.logical_xor(lane >= HALF, odd)
    return jnp.where(from_first, first[cut, :], second[cut, :])


def pack_sides_kernel(second, first, far_in, near_in, far, near):
    for target, low in towards(far, near):
        target[pl.ds(target.shape[0] - SUB, SUB)] = pack_sides(second, first, low)


def pack_sides(second, first, low):
    rows = first.shape[0]
    sub = lax.broadcasted_iota(jnp.int32, (SUB, LANES), 0)
    lane = lax.broadcasted_iota(jnp.int32, (SUB, LANES), 1)
    side = jnp.where(
        low,
        sides_of(first, second, pl.ds(0, SUB)),
        sides_of(first, second, pl.ds(rows - SUB, SUB)),
    )
    line = jnp.where(
        low,
        sides_of(first, second, pl.ds(SUB, SUB))[0:1],
        sides_of(first, second, pl.ds(rows - 2 * SUB, SUB))[SUB - 1 : SUB],
    )
    line = jnp.broadcast_to(line, (SUB, LANES))
    low, high = 4 * EDGE, 6 * EDGE
    take = jnp.logical_or(
        jnp.logical_and(lane >= low, lane < high),
        jnp.logical_and(lane >= EAST + low, lane < EAST + high),
    )
    side = jnp.where(jnp.logical_and(take, sub == 0), line, side)
    return side


def pole_sums_kernel(count, scalars, first, second, others, grid, *rest):
    poly, (sums, sol, result) = rest[:ITERS], rest[ITERS:]
    odd = lax.rem(lax.axis_index("pole"), 2) == 1
    lane = lax.broadcasted_iota(jnp.int32, (SUB, LANES), 1)
    blocks = [[scalars[pl.ds(g, SUB)] for g in range(0, count, SUB)]]
    for i, message in enumerate((first, second)):
        low = jnp.logical_xor(lane < HALF, odd if i == 0 else jnp.logical_not(odd))
        part = []
        for g in range(0, count, SUB):
            x = message[pl.ds(g, SUB), :]
            part.append(jnp.where(low, x, turn(x, HALF)))
        blocks.append(part)
    for i in range(others.shape[0]):
        blocks.append([others[i, pl.ds(g, SUB)] for g in range(0, count, SUB)])
    poles = count // 4
    quantity = []
    for q in range(4):
        cut = []
        for block in blocks:
            whole = jnp.concatenate(block, axis=0)
            cut.append(whole[q * poles : (q + 1) * poles])
        quantity.append(jnp.concatenate(cut, axis=0))
    alpha = (quantity[0], quantity[1])
    beta = (quantity[2], quantity[3])
    square = cmul(alpha, alpha)
    shifted = (square[0] + coriolis * coriolis, square[1])
    sigma = ((shifted[0] + centre) / half_width, shifted[1] / half_width)
    rho = [cinv(sigma)]
    for j in range(1, ITERS):
        rho.append(cinv((2.0 * sigma[0] - rho[-1][0], 2.0 * sigma[1] - rho[-1][1])))
    gain = None
    start = []
    for m in range(ITERS):
        if m == 0:
            start.append(cscale(rho[0], 1.0 / half_width))
        else:
            gain = rho[0] if gain is None else cmul(gain, rho[m - 1])
            start.append(cscale(cmul(rho[m], gain), 2.0 / half_width))
    tail = None
    weight = [None] * ITERS
    for m in reversed(range(ITERS)):
        if tail is None:
            weight[m] = start[m]
            tail = (jnp.ones_like(sigma[0]), jnp.zeros_like(sigma[0]))
        else:
            tail = cmul(cmul(rho[m + 1], rho[m]), tail)
            tail = (tail[0] + 1.0, tail[1])
            weight[m] = cmul(start[m], tail)
    inverse_alpha = cinv(alpha)
    inverse_shift = cinv(shifted)
    by_alpha = cmul(beta, inverse_alpha)
    by_shift = cmul(beta, inverse_shift)
    products = {
        "b": beta,
        "b/a": by_alpha,
        "b/s": by_shift,
        "bs/a": cmul(by_alpha, shifted),
        "ba/s": cmul(by_shift, alpha),
        "b/as": cmul(by_alpha, inverse_shift),
    }

    def total(x):
        s = x[0:SUB]
        for i in range(1, x.shape[0] // SUB):
            s = s + x[i * SUB : (i + 1) * SUB]
        for step in (4, 2, 1):
            s = s + pltpu.roll(s, step, 0)
        return s

    names = [("bs/a", "b", "b/a"), ("b", "ba/s", "b/s"), ("b/a", "b/s", "b/as")]
    factor = (1.0, -1.0, -coriolis)
    found = {}
    for m in range(ITERS):
        for name, w in products.items():
            found[name, m] = total(w[0] * weight[m][0] - w[1] * weight[m][1])
        for g in range(3):
            for f in range(3):
                value = found[names[g][f], m]
                sums[(g * 3 + f) * ITERS + m] = value if f == 0 else factor[f] * value
    sums[9 * ITERS] = total(products["ba/s"][0])
    sums[9 * ITERS + 1] = coriolis * total(products["b/s"][0])

    _, (_, above) = towards(None, None)
    rows = sol.shape[1] - 2

    def near_rows(above):
        near, far = side_rows(rows, above), side_rows(rows, not above)
        acc = {}
        for m in range(ITERS):
            add(acc, sums, poly, m, near)
        for m in range(ITERS - 1):
            add(acc, sums, poly, m, [r for k, r in enumerate(far) if known(k) >= m])
        for (g, r), v in acc.items():
            sol[g, r - (REACH - 1)] = v
        inside = sorted(near)[1:-1]
        finish(grid, sums, result, acc, [r for r in inside if REACH <= r < REACH + rows])

    pl.when(above)(lambda: near_rows(True))
    pl.when(jnp.logical_not(above))(lambda: near_rows(False))


def side_rows(rows, above):
    low, high = REACH - 1, REACH + rows
    return [low + k if above else high - k for k in range(rows // 2 + 1)]


def known(k):
    return max(min(ITERS - 2, k - 2), -1)


def add(acc, sums, poly, m, rows, values=None):
    for f in range(3):
        if not rows:
            return
        value = {r: poly[m][f, r] if values is None else values[f, r] for r in rows}
        for g in range(3):
            c = sums[(g * 3 + f) * ITERS + m]
            for r in rows:
                acc[g, r] = acc[g, r] + c * value[r] if (g, r) in acc else c * value[r]


def finish(grid, sums, result, acc, span):
    push = sums[9 * ITERS]
    lift = sums[9 * ITERS + 1]
    for r in span:
        u, v = cell(grid, 1, r), cell(grid, 2, r)
        at = pl.ds((r - REACH) * SUB, SUB)
        result[0, at] = acc[0, r]
        east = 0.5 * (acc[1, r + 1] - acc[1, r - 1])
        north = 0.5 * (right(acc[2, r]) - left(acc[2, r]))
        result[1, at] = (push * u + lift * v) - (east + coriolis * north)
        east = 0.5 * (acc[2, r + 1] - acc[2, r - 1])
        north = 0.5 * (right(acc[1, r]) - left(acc[1, r]))
        result[2, at] = (push * v - lift * u) + (coriolis * east - north)


def strips_of(tiles, side):
    lane = lax.broadcasted_iota(jnp.int32, (SUB, LANES), 1)
    up = [turn(tile, SIDE) for tile in tiles]
    down = [turn(tile, -SIDE) for tile in tiles]
    out = []
    for q in range(len(tiles)):
        out.append(jnp.where(lane < SIDE, up[q - 1] if q else side, up[q]))
        after = down[q + 1] if q + 1 < len(tiles) else side
        out.append(jnp.where(lane < LANES - SIDE, down[q], after))
    return out


def lay(grid, cut, side, at, stride):
    for s, strip in enumerate(strips_of(cut, side)):
        grid[pl.Slice(at * SUB + s, SUB, stride * SUB), :] = strip


def place(side, f):
    return turn(side, SIDE - EDGE - EDGE * f)


def lay_halo(grid, halo, side, main, ext):
    lane = lax.broadcasted_iota(jnp.int32, (SUB, LANES), 1)
    sub = lax.broadcasted_iota(jnp.int32, (SUB, LANES), 0)
    tiles = SUB // 2
    for f in range(4):
        cut = [block_of(halo, f * tiles + t) for t in range(tiles)]
        lay(grid, cut, place(side, f), main * 4 + f, 4)
    line = jnp.broadcast_to(side[0:1], (SUB, LANES))
    side = jnp.where(sub < tiles, place(line, 4), place(line, 5))
    block = block_of(halo, 4 * tiles)
    up, down = turn(block, SIDE), turn(block, -SIDE)
    before = jnp.where(sub % tiles == 0, side, pltpu.roll(up, 1, 0))
    after = jnp.where(sub % tiles == tiles - 1, side, pltpu.roll(down, SUB - 1, 0))
    even = jnp.where(lane < SIDE, before, up)
    odd = jnp.where(lane < LANES - SIDE, down, after)
    for f in (1, 2):
        at = (ext * 4 + f) * SUB
        cut = slice((f - 1) * tiles, f * tiles)
        grid[pl.Slice(at, tiles, 2), :] = even[cut]
        grid[pl.Slice(at + 1, tiles, 2), :] = odd[cut]


def cell(grid, f, r):
    return grid[pl.ds(pl.multiple_of((r * 4 + f) * SUB, SUB), SUB), :]


def left(x):
    return pltpu.roll(x, 1, 1)


def right(x):
    return pltpu.roll(x, LANES - 1, 1)


def prepare(grid, poly, coef, start, count):
    flux_east = [None] * 3
    flux_north = [None] * 3
    depths = [None] * 2
    across = None
    found = {}
    for k in range(count + 2):
        r = start + k
        h = cell(grid, 3, r)
        flux_east = flux_east[1:] + [h * cell(grid, 1, r)]
        flux_north = flux_north[1:] + [h * cell(grid, 2, r)]
        depths = depths[1:] + [h]
        if k >= 1:
            before, across = across, 0.125 * (depths[0] + depths[1])
            coef[0, r - 1] = across
        if k >= 2:
            c = r - 1
            north = 0.125 * (depths[0] + right(depths[0]))
            south = 0.125 * (depths[0] + left(depths[0]))
            coef[1, c] = north
            coef[2, c] = south
            coef[3, c] = 2.0 - ((across + before) + (north + south))
            east_slope = flux_east[2] - flux_east[0]
            north_slope = right(flux_north[1]) - left(flux_north[1])
            poly[0][1, c] = found[1, c] = 0.5 * (east_slope + north_slope)
            east_slope = flux_north[2] - flux_north[0]
            north_slope = right(flux_east[1]) - left(flux_east[1])
            poly[0][2, c] = found[2, c] = 0.5 * (east_slope - north_slope)
            poly[0][0, c] = found[0, c] = cell(grid, 0, c)
    return found


def sweep(poly, coef, m, start, count, last, upwards=False, earlier=None):
    def take(f, r):
        return last[f, r] if (f, r) in last else poly[m][f, r]

    step = -1 if upwards else 1
    order = range(start, start + count)[::step]
    back = [take(f, order[0] - step) for f in range(3)]
    here = [take(f, order[0]) for f in range(3)]
    found = {}
    for r in order:
        north, south, diag = coef[1, r], coef[2, r], coef[3, r]
        above, below = coef[0, r], coef[0, r - 1]
        ahead = [take(f, r + step) for f in range(3)]
        for f in range(3):
            up, down = (back, ahead) if upwards else (ahead, back)
            value = diag * here[f]
            if m > 0:
                held = earlier is not None and (f, r) in earlier
                value = value - (earlier[f, r] if held else poly[m - 1][f, r])
            value = value + above * up[f]
            value = value + below * down[f]
            value = value + north * right(here[f])
            value = value + south * left(here[f])
            value = 0.5 * value if m == 0 else value
            if earlier is None:
                poly[m + 1][f, r] = value
            found[f, r] = value
        back, here = here, ahead
    return found


def inner_kernel(fields, first, second, grid, coef, *poly):
    rows = fields.shape[1]
    for g in range(rows // SUB):
        side = sides_of(first, second, pl.ds(g * SUB, SUB))
        for f in range(4):
            cut = [
                fields[f, pl.ds(g * SUB, SUB), pl.ds(t * LANES, LANES)]
                for t in range(fields.shape[2] // LANES)
            ]
            lay(grid, cut, place(side, f), (REACH + g * SUB) * 4 + f, 4)
    found = prepare(grid, poly, coef, REACH, rows - 2)
    for m in range(ITERS - 1):
        if rows - 4 - 2 * m > 0:
            found = sweep(poly, coef, m, REACH + 2 + m, rows - 4 - 2 * m, found)


def one_side(halo, side, above, grid, coef, poly, each=None):
    below = coef.shape[1] - REACH
    main, ext, start = (1, 0, 0) if above else (below, below + SUB, below - 2)
    grid[pl.ds((ext * 4 + 3) * SUB, SUB), :] = jnp.ones((SUB, LANES), jnp.float32)
    lay_halo(grid, halo, side, main, ext)
    found = prepare(grid, poly, coef, start, REACH)
    earlier = None if each is None else {}
    for m in range(ITERS - 1):
        if each is not None:
            each(m, found)
        low = 2 + m if above else below - 2 - m
        following = sweep(poly, coef, m, low, REACH, found, above, earlier)
        earlier, found = (None if each is None else found), following
    if each is not None:
        each(ITERS - 1, found)


def mid_kernel(near_early, near, *rest):
    grid, coef, *poly = rest[len(rest) // 2 :]
    _, (_, above) = towards(None, None)
    side = near[pl.ds(near.shape[0] - SUB, SUB)]
    for way, here in ((True, above), (False, jnp.logical_not(above))):
        pl.when(here)(
            lambda: one_side((near_early, near), side, way, grid, coef, poly)
        )


def outer_kernel(far_early, far, sums, *rest):
    *rest, lines, done = rest
    out, grid, coef, sol, result, *poly = rest[len(rest) // 2 :]
    rows, columns = out.shape[1:]
    lane = lax.broadcasted_iota(jnp.int32, (SUB, LANES), 1)
    (_, above), _ = towards(None, None)

    def far_rows(above):
        side = far[pl.ds(far.shape[0] - SUB, SUB)]
        whole = side_rows(rows, above)
        inside = 1 if above else -1
        edges = [whole[-1] + inside, whole[-1] + 2 * inside]
        acc = {}
        for r in edges + [r for k, r in enumerate(whole) if known(k) >= 0]:
            for g in range(3):
                acc[g, r] = sol[g, r - (REACH - 1)]

        def each(m, found):
            part = [r for k, r in enumerate(whole) if known(k) < m]
            held = [r for r in part if (0, r) in found]
            add(acc, sums, poly, m, held, found)
            add(acc, sums, poly, m, [r for r in part if r not in held])

        one_side((far_early, far), side, above, grid, coef, poly, each)
        span = [r for r in whole + edges[:1] if REACH <= r < REACH + rows]
        finish(grid, sums, result, acc, span)

    pl.when(above)(lambda: far_rows(True))
    pl.when(jnp.logical_not(above))(lambda: far_rows(False))

    moves = []
    for k in range(3):
        for g in range(rows // SUB):
            cut = pl.ds(g * SUB, SUB)
            for t in range(columns // LANES):
                one = result[k, pl.Slice(g * SUB * SUB + 2 * t, SUB, SUB), :]
                two = result[k, pl.Slice(g * SUB * SUB + 2 * t + 1, SUB, SUB), :]
                joined = jnp.where(lane < HALF, turn(one, -SIDE), turn(two, SIDE))
                lines[k, cut, pl.ds(t * LANES, LANES)] = joined
            move = pltpu.make_async_copy(lines.at[k, cut], out.at[k, cut], done.at[k, g])
            move.start()
            moves.append(move)
    for move in moves:
        move.wait()


def shards(state, depth, pole_real, pole_imag, pole_weight):
    rows, columns = depth.shape
    poles = pole_real.shape[0]
    vmem = pl.BlockSpec(memory_space=pltpu.VMEM)
    small = pltpu.CompilerParams(vmem_limit_bytes=GRANT)

    def f32(*shape):
        return jax.ShapeDtypeStruct(shape, jnp.float32)

    given = [
        pltpu.with_memory_space_constraint(x, pltpu.HBM)
        for x in (state, depth, pole_real, pole_imag, pole_weight)
    ]
    hbm = pl.BlockSpec(memory_space=pltpu.HBM)
    message = pltpu.VMEM((rows, LANES), jnp.float32)
    fields, first, second = pl.pallas_call(
        pack_columns_kernel,
        out_shape=(pltpu.VMEM((4, rows, columns), jnp.float32), message, message),
        in_specs=[hbm] * 5,
        out_specs=(vmem,) * 3,
        scratch_shapes=[
            pltpu.SMEM(pole_real.shape, jnp.float32),
            pltpu.SMEM(pole_imag.shape, jnp.float32),
            pltpu.SMEM(pole_weight.shape, jnp.float32),
            pltpu.SemaphoreType.DMA((5,)),
        ],
        compiler_params=small,
        name="pack_columns",
    )(*given)
    blocks = 4 * columns // LANES + 2
    half = blocks // 2 * SUB
    parts = (half + SUB + 4, half, half + SUB, half - SUB, max(4 * poles, half))
    far_early, far, near_early, near, scalars = pl.pallas_call(
        functools.partial(pack_rows_kernel, 4 * poles),
        out_shape=tuple(f32(part, LANES) for part in parts),
        in_specs=[vmem] * 3,
        out_specs=(vmem,) * 5,
        compiler_params=small,
        name="pack_rows",
    )(fields, second, first)
    second = swap(second, "pole", 1)
    first = swap(first, "pole", 0)
    far, near = pl.pallas_call(
        pack_sides_kernel,
        out_shape=(f32(*far.shape), f32(*near.shape)),
        in_specs=[vmem] * 4,
        out_specs=(vmem, vmem),
        input_output_aliases={2: 0, 3: 1},
        compiler_params=small,
        name="pack_sides",
    )(second, first, far, near)
    far_early = swap(far_early, "tile", 1)
    far = swap(far, "tile", 1)
    near_early = swap(near_early, "tile", 0)
    near = swap(near, "tile", 0)
    count = lax.axis_size("pole")
    others = jnp.stack([shift(scalars, "pole", step) for step in range(2, count - 1)])
    height = rows + 2 * REACH
    grid = f32(height * 4 * SUB, LANES)
    poly = [f32(3, height, SUB, LANES)] * ITERS
    coef = f32(4, height, SUB, LANES)
    sol = f32(3, rows + 2, SUB, LANES)
    result = f32(3, (rows + 1) * SUB, LANES)
    state_of = (grid, coef, *poly)
    cost = pl.CostEstimate(
        flops=10 * ITERS * rows * SUB * LANES,
        bytes_accessed=4 * SUB * LANES * rows * (4 + 2 * ITERS + 2),
        transcendentals=0,
    )
    held = pl.pallas_call(
        inner_kernel,
        out_shape=state_of,
        in_specs=[vmem] * 3,
        out_specs=(vmem,) * len(state_of),
        compiler_params=small,
        cost_estimate=cost,
        name="inner",
    )(fields, first, second)
    held = pl.pallas_call(
        mid_kernel,
        out_shape=state_of,
        in_specs=[vmem] * (2 + len(state_of)),
        out_specs=(vmem,) * len(state_of),
        input_output_aliases={2 + i: i for i in range(len(state_of))},
        compiler_params=small,
        cost_estimate=cost,
        name="mid",
    )(near_early, near, *held)
    grid_held, coef_held, *poly_held = held
    sums, *part = pl.pallas_call(
        functools.partial(pole_sums_kernel, 4 * poles),
        out_shape=(f32(9 * ITERS + 2, SUB, LANES), sol, result),
        in_specs=[vmem] * (5 + ITERS),
        out_specs=(vmem,) * 3,
        compiler_params=small,
        name="pole_sums",
    )(scalars, first, second, others, grid_held, *poly_held)
    kept = (grid, coef, sol, result, *poly)
    return pl.pallas_call(
        outer_kernel,
        out_shape=(f32(*state.shape), *kept),
        in_specs=[vmem] * (3 + len(kept)),
        out_specs=(hbm, *(vmem,) * len(kept)),
        scratch_shapes=[
            pltpu.VMEM(state.shape, jnp.float32),
            pltpu.SemaphoreType.DMA((3, rows // SUB)),
        ],
        input_output_aliases={3 + i: 1 + i for i in range(len(kept))},
        compiler_params=small,
        name="outer",
    )(far_early, far, sums, grid_held, coef_held, *part, *poly_held)[0]


def solution(mesh):
    return jax.shard_map(
        shards,
        mesh=mesh,
        in_specs=(
            P(None, "tile", "pole"),
            P("tile", "pole"),
            P("pole"),
            P("pole"),
            P(None, "pole"),
        ),
        out_specs=P(None, "tile", "pole"),
        check_vma=False,
    )
```

```python
import functools

import jax
import jax.numpy as jnp
from jax import lax
from jax.experimental import pallas as pl
from jax.experimental.pallas import tpu as pltpu
from jax.sharding import PartitionSpec as P

ITERS = 8
REACH = ITERS + 1
SUB = 8
LANES = 128
HALF = LANES // 2
SIDE = 32
EDGE = REACH
EAST = HALF + EDGE
GRANT = 16 * 1024 * 1024

coriolis = 0.7
centre = 8.0
half_width = 8.0


def pairs(count, phase):
    swap = []
    for i in range(phase, count + phase, 2):
        a, b = i % count, (i + 1) % count
        swap += [(a, b), (b, a)]
    return swap


def swap(block, axis, phase):
    return lax.ppermute(block, axis, pairs(lax.axis_size(axis), phase))


def shift(block, axis, step):
    count = lax.axis_size(axis)
    return lax.ppermute(block, axis, [(i, (i + step) % count) for i in range(count)])


def turn(x, lanes):
    return pltpu.roll(x, lanes % LANES, 1) if lanes % LANES else x


def cmul(a, b):
    return (a[0] * b[0] - a[1] * b[1], a[0] * b[1] + a[1] * b[0])


def cinv(a):
    norm = 1.0 / (a[0] * a[0] + a[1] * a[1])
    return (a[0] * norm, -a[1] * norm)


def cscale(a, factor):
    return (a[0] * factor, a[1] * factor)


def pack_columns_kernel(
    state, depth, real, imag, weight, fields, first, second, real_in, imag_in, weight_in, done
):
    moves = [
        pltpu.make_async_copy(depth, fields.at[3], done.at[0]),
        pltpu.make_async_copy(state, fields.at[pl.ds(0, 3)], done.at[1]),
        pltpu.make_async_copy(real, real_in, done.at[2]),
        pltpu.make_async_copy(imag, imag_in, done.at[3]),
        pltpu.make_async_copy(weight, weight_in, done.at[4]),
    ]
    for move in moves:
        move.start()
    for move in moves:
        move.wait()
    odd = lax.rem(lax.axis_index("pole"), 2) == 1
    rows, columns = fields.shape[1:]
    lane = lax.broadcasted_iota(jnp.int32, (SUB, LANES), 1)
    sub = lax.broadcasted_iota(jnp.int32, (SUB, LANES), 0)
    poles = real.shape[0]
    values = [real_in[i] for i in range(poles)] + [imag_in[i] for i in range(poles)]
    values += [weight_in[0, i] for i in range(poles)] + [weight_in[1, i] for i in range(poles)]
    for g in range(rows // SUB):
        cut = pl.ds(g * SUB, SUB)
        west = [fields[f, cut, 0:LANES] for f in range(4)]
        east = [fields[f, cut, columns - LANES : columns] for f in range(4)]
        west += [west[3] * west[1], west[3] * west[2]]
        east += [east[3] * east[1], east[3] * east[2]]
        rest = jnp.zeros((SUB, LANES), jnp.float32)
        for i, value in enumerate(values[g * SUB : (g + 1) * SUB]):
            rest = jnp.where(sub == i, value, rest)
        eastward = rest
        westward = rest
        for f in range(6):
            low, high = EDGE * f, EDGE * (f + 1)
            take = jnp.logical_and(lane >= low, lane < high)
            eastward = jnp.where(take, turn(east[f], low + EDGE), eastward)
            take = jnp.logical_and(lane >= EAST + low, lane < EAST + high)
            westward = jnp.where(take, turn(west[f], EAST + low), westward)
        first[cut, :] = jnp.where(odd, westward, eastward)
        second[cut, :] = jnp.where(odd, eastward, westward)


def pack_rows_kernel(count, fields, second, first, far_early, far, near_early, near, scalars):
    rows = fields.shape[1]
    for parts, low in towards((far_early, far), (near_early, near)):
        at = 0
        for part in parts:
            pl.when(low)(lambda: pack_rows(part, at, fields, 0, SUB))
            pl.when(jnp.logical_not(low))(
                lambda: pack_rows(part, at, fields, rows - SUB, rows - SUB - 1)
            )
            at += part.shape[0] // SUB
    odd = lax.rem(lax.axis_index("pole"), 2) == 1
    lane = lax.broadcasted_iota(jnp.int32, (SUB, LANES), 1)
    from_first = jnp.logical_xor(lane >= HALF, odd)
    for g in range(0, scalars.shape[0], SUB):
        if g < count:
            block = jnp.where(from_first, first[pl.ds(g, SUB)], second[pl.ds(g, SUB)])
        else:
            block = jnp.zeros((SUB, LANES), jnp.float32)
        scalars[pl.ds(g, SUB)] = block


def towards(far, near):
    odd = lax.rem(lax.axis_index("tile"), 2) == 1
    return ((far, jnp.logical_not(odd)), (near, odd))


def pack_rows(target, at, fields, main, ext):
    tiles = fields.shape[2] // LANES
    for i in range(target.shape[0] // SUB):
        f, t = divmod(at + i, tiles)
        if f < 4:
            block = fields[f, main : main + SUB, t * LANES : (t + 1) * LANES]
            target[pl.ds(i * SUB, SUB)] = block
        elif t == 0:
            for f in (1, 2):
                flux = fields[3, ext : ext + 1, :] * fields[f, ext : ext + 1, :]
                for t in range(tiles):
                    row = i * SUB + (f - 1) * tiles + t
                    target[row : row + 1] = flux[:, t * LANES : (t + 1) * LANES]


def block_of(parts, at):
    early, late = parts
    count = early.shape[0] // SUB
    if at < count:
        return early[pl.ds(at * SUB, SUB)]
    return late[pl.ds((at - count) * SUB, SUB)]


def sides_of(first, second, cut):
    odd = lax.rem(lax.axis_index("pole"), 2) == 1
    lane = lax.broadcasted_iota(jnp.int32, (SUB, LANES), 1)
    from_first = jnp.logical_xor(lane >= HALF, odd)
    return jnp.where(from_first, first[cut, :], second[cut, :])


def pack_sides_kernel(second, first, far_in, near_in, far, near):
    for target, low in towards(far, near):
        target[pl.ds(target.shape[0] - SUB, SUB)] = pack_sides(second, first, low)


def pack_sides(second, first, low):
    rows = first.shape[0]
    sub = lax.broadcasted_iota(jnp.int32, (SUB, LANES), 0)
    lane = lax.broadcasted_iota(jnp.int32, (SUB, LANES), 1)
    side = jnp.where(
        low,
        sides_of(first, second, pl.ds(0, SUB)),
        sides_of(first, second, pl.ds(rows - SUB, SUB)),
    )
    line = jnp.where(
        low,
        sides_of(first, second, pl.ds(SUB, SUB))[0:1],
        sides_of(first, second, pl.ds(rows - 2 * SUB, SUB))[SUB - 1 : SUB],
    )
    line = jnp.broadcast_to(line, (SUB, LANES))
    low, high = 4 * EDGE, 6 * EDGE
    take = jnp.logical_or(
        jnp.logical_and(lane >= low, lane < high),
        jnp.logical_and(lane >= EAST + low, lane < EAST + high),
    )
    side = jnp.where(jnp.logical_and(take, sub == 0), line, side)
    return side


def pole_sums_kernel(count, scalars, first, second, others, grid, *rest):
    poly, (sums, sol, result) = rest[:ITERS], rest[ITERS:]
    odd = lax.rem(lax.axis_index("pole"), 2) == 1
    lane = lax.broadcasted_iota(jnp.int32, (SUB, LANES), 1)
    blocks = [[scalars[pl.ds(g, SUB)] for g in range(0, count, SUB)]]
    for i, message in enumerate((first, second)):
        low = jnp.logical_xor(lane < HALF, odd if i == 0 else jnp.logical_not(odd))
        part = []
        for g in range(0, count, SUB):
            x = message[pl.ds(g, SUB), :]
            part.append(jnp.where(low, x, turn(x, HALF)))
        blocks.append(part)
    for i in range(others.shape[0]):
        blocks.append([others[i, pl.ds(g, SUB)] for g in range(0, count, SUB)])
    poles = count // 4
    quantity = []
    for q in range(4):
        cut = []
        for block in blocks:
            whole = jnp.concatenate(block, axis=0)
            cut.append(whole[q * poles : (q + 1) * poles])
        quantity.append(jnp.concatenate(cut, axis=0))
    alpha = (quantity[0], quantity[1])
    beta = (quantity[2], quantity[3])
    square = cmul(alpha, alpha)
    shifted = (square[0] + coriolis * coriolis, square[1])
    sigma = ((shifted[0] + centre) / half_width, shifted[1] / half_width)
    rho = [cinv(sigma)]
    for j in range(1, ITERS):
        rho.append(cinv((2.0 * sigma[0] - rho[-1][0], 2.0 * sigma[1] - rho[-1][1])))
    gain = None
    start = []
    for m in range(ITERS):
        if m == 0:
            start.append(cscale(rho[0], 1.0 / half_width))
        else:
            gain = rho[0] if gain is None else cmul(gain, rho[m - 1])
            start.append(cscale(cmul(rho[m], gain), 2.0 / half_width))
    tail = None
    weight = [None] * ITERS
    for m in reversed(range(ITERS)):
        if tail is None:
            weight[m] = start[m]
            tail = (jnp.ones_like(sigma[0]), jnp.zeros_like(sigma[0]))
        else:
            tail = cmul(cmul(rho[m + 1], rho[m]), tail)
            tail = (tail[0] + 1.0, tail[1])
            weight[m] = cmul(start[m], tail)
    inverse_alpha = cinv(alpha)
    inverse_shift = cinv(shifted)
    by_alpha = cmul(beta, inverse_alpha)
    by_shift = cmul(beta, inverse_shift)
    products = {
        "b": beta,
        "b/a": by_alpha,
        "b/s": by_shift,
        "bs/a": cmul(by_alpha, shifted),
        "ba/s": cmul(by_shift, alpha),
        "b/as": cmul(by_alpha, inverse_shift),
    }

    def total(x):
        s = x[0:SUB]
        for i in range(1, x.shape[0] // SUB):
            s = s + x[i * SUB : (i + 1) * SUB]
        for step in (4, 2, 1):
            s = s + pltpu.roll(s, step, 0)
        return s

    names = [("bs/a", "b", "b/a"), ("b", "ba/s", "b/s"), ("b/a", "b/s", "b/as")]
    factor = (1.0, -1.0, -coriolis)
    found = {}
    for m in range(ITERS):
        for name, w in products.items():
            found[name, m] = total(w[0] * weight[m][0] - w[1] * weight[m][1])
        for g in range(3):
            for f in range(3):
                value = found[names[g][f], m]
                sums[(g * 3 + f) * ITERS + m] = value if f == 0 else factor[f] * value
    sums[9 * ITERS] = total(products["ba/s"][0])
    sums[9 * ITERS + 1] = coriolis * total(products["b/s"][0])

    _, (_, above) = towards(None, None)
    rows = sol.shape[1] - 2

    def near_rows(above):
        near, far = side_rows(rows, above), side_rows(rows, not above)
        acc = {}
        for m in range(ITERS):
            add(acc, sums, poly, m, near)
        for m in range(ITERS - 1):
            add(acc, sums, poly, m, [r for k, r in enumerate(far) if known(k) >= m])
        for (g, r), v in acc.items():
            sol[g, r - (REACH - 1)] = v
        inside = sorted(near)[1:-1]
        finish(grid, sums, result, acc, [r for r in inside if REACH <= r < REACH + rows])

    pl.when(above)(lambda: near_rows(True))
    pl.when(jnp.logical_not(above))(lambda: near_rows(False))


def side_rows(rows, above):
    low, high = REACH - 1, REACH + rows
    return [low + k if above else high - k for k in range(rows // 2 + 1)]


def known(k):
    return max(min(ITERS - 2, k - 2), -1)


def add(acc, sums, poly, m, rows, values=None):
    for f in range(3):
        if not rows:
            return
        value = {r: poly[m][f, r] if values is None else values[f, r] for r in rows}
        for g in range(3):
            c = sums[(g * 3 + f) * ITERS + m]
            for r in rows:
                acc[g, r] = acc[g, r] + c * value[r] if (g, r) in acc else c * value[r]


def finish(grid, sums, result, acc, span):
    push = sums[9 * ITERS]
    lift = sums[9 * ITERS + 1]
    for r in span:
        u, v = cell(grid, 1, r), cell(grid, 2, r)
        at = pl.ds((r - REACH) * SUB, SUB)
        result[0, at] = acc[0, r]
        east = 0.5 * (acc[1, r + 1] - acc[1, r - 1])
        north = 0.5 * (right(acc[2, r]) - left(acc[2, r]))
        result[1, at] = (push * u + lift * v) - (east + coriolis * north)
        east = 0.5 * (acc[2, r + 1] - acc[2, r - 1])
        north = 0.5 * (right(acc[1, r]) - left(acc[1, r]))
        result[2, at] = (push * v - lift * u) + (coriolis * east - north)


def strips_of(tiles, side):
    lane = lax.broadcasted_iota(jnp.int32, (SUB, LANES), 1)
    up = [turn(tile, SIDE) for tile in tiles]
    down = [turn(tile, -SIDE) for tile in tiles]
    out = []
    for q in range(len(tiles)):
        out.append(jnp.where(lane < SIDE, up[q - 1] if q else side, up[q]))
        after = down[q + 1] if q + 1 < len(tiles) else side
        out.append(jnp.where(lane < LANES - SIDE, down[q], after))
    return out


def lay(grid, cut, side, at, stride):
    for s, strip in enumerate(strips_of(cut, side)):
        grid[pl.Slice(at * SUB + s, SUB, stride * SUB), :] = strip


def place(side, f):
    return turn(side, SIDE - EDGE - EDGE * f)


def lay_halo(grid, halo, side, main, ext):
    lane = lax.broadcasted_iota(jnp.int32, (SUB, LANES), 1)
    sub = lax.broadcasted_iota(jnp.int32, (SUB, LANES), 0)
    tiles = SUB // 2
    for f in range(4):
        cut = [block_of(halo, f * tiles + t) for t in range(tiles)]
        lay(grid, cut, place(side, f), main * 4 + f, 4)
    line = jnp.broadcast_to(side[0:1], (SUB, LANES))
    side = jnp.where(sub < tiles, place(line, 4), place(line, 5))
    block = block_of(halo, 4 * tiles)
    up, down = turn(block, SIDE), turn(block, -SIDE)
    before = jnp.where(sub % tiles == 0, side, pltpu.roll(up, 1, 0))
    after = jnp.where(sub % tiles == tiles - 1, side, pltpu.roll(down, SUB - 1, 0))
    even = jnp.where(lane < SIDE, before, up)
    odd = jnp.where(lane < LANES - SIDE, down, after)
    for f in (1, 2):
        at = (ext * 4 + f) * SUB
        cut = slice((f - 1) * tiles, f * tiles)
        grid[pl.Slice(at, tiles, 2), :] = even[cut]
        grid[pl.Slice(at + 1, tiles, 2), :] = odd[cut]


def cell(grid, f, r):
    return grid[pl.ds(pl.multiple_of((r * 4 + f) * SUB, SUB), SUB), :]


def left(x):
    return pltpu.roll(x, 1, 1)


def right(x):
    return pltpu.roll(x, LANES - 1, 1)


def prepare(grid, poly, coef, start, count):
    flux_east = [None] * 3
    flux_north = [None] * 3
    depths = [None] * 2
    across = None
    found = {}
    for k in range(count + 2):
        r = start + k
        h = cell(grid, 3, r)
        flux_east = flux_east[1:] + [h * cell(grid, 1, r)]
        flux_north = flux_north[1:] + [h * cell(grid, 2, r)]
        depths = depths[1:] + [h]
        if k >= 1:
            before, across = across, 0.125 * (depths[0] + depths[1])
            coef[0, r - 1] = across
        if k >= 2:
            c = r - 1
            north = 0.125 * (depths[0] + right(depths[0]))
            south = 0.125 * (depths[0] + left(depths[0]))
            coef[1, c] = north
            coef[2, c] = south
            coef[3, c] = 2.0 - ((across + before) + (north + south))
            east_slope = flux_east[2] - flux_east[0]
            north_slope = right(flux_north[1]) - left(flux_north[1])
            poly[0][1, c] = found[1, c] = 0.5 * (east_slope + north_slope)
            east_slope = flux_north[2] - flux_north[0]
            north_slope = right(flux_east[1]) - left(flux_east[1])
            poly[0][2, c] = found[2, c] = 0.5 * (east_slope - north_slope)
            poly[0][0, c] = found[0, c] = cell(grid, 0, c)
    return found


def sweep(poly, coef, m, start, count, last, upwards=False):
    def take(f, r):
        return last[f, r] if (f, r) in last else poly[m][f, r]

    step = -1 if upwards else 1
    order = range(start, start + count)[::step]
    back = [take(f, order[0] - step) for f in range(3)]
    here = [take(f, order[0]) for f in range(3)]
    found = {}
    for r in order:
        north, south, diag = coef[1, r], coef[2, r], coef[3, r]
        above, below = coef[0, r], coef[0, r - 1]
        ahead = [take(f, r + step) for f in range(3)]
        for f in range(3):
            up, down = (back, ahead) if upwards else (ahead, back)
            value = diag * here[f]
            if m > 0:
                value = value - poly[m - 1][f, r]
            value = value + above * up[f]
            value = value + below * down[f]
            value = value + north * right(here[f])
            value = value + south * left(here[f])
            value = 0.5 * value if m == 0 else value
            poly[m + 1][f, r] = value
            found[f, r] = value
        back, here = here, ahead
    return found


def inner_kernel(fields, first, second, grid, coef, *poly):
    rows = fields.shape[1]
    for g in range(rows // SUB):
        side = sides_of(first, second, pl.ds(g * SUB, SUB))
        for f in range(4):
            cut = [
                fields[f, pl.ds(g * SUB, SUB), pl.ds(t * LANES, LANES)]
                for t in range(fields.shape[2] // LANES)
            ]
            lay(grid, cut, place(side, f), (REACH + g * SUB) * 4 + f, 4)
    found = prepare(grid, poly, coef, REACH, rows - 2)
    for m in range(ITERS - 1):
        if rows - 4 - 2 * m > 0:
            found = sweep(poly, coef, m, REACH + 2 + m, rows - 4 - 2 * m, found)


def one_side(halo, side, above, grid, coef, poly, each):
    below = coef.shape[1] - REACH
    main, ext, start = (1, 0, 0) if above else (below, below + SUB, below - 2)
    grid[pl.ds((ext * 4 + 3) * SUB, SUB), :] = jnp.ones((SUB, LANES), jnp.float32)
    lay_halo(grid, halo, side, main, ext)
    found = prepare(grid, poly, coef, start, REACH)
    each(0, found)
    for m in range(ITERS - 1):
        low = 2 + m if above else below - 2 - m
        found = sweep(poly, coef, m, low, REACH, found, above)
        each(m + 1, found)


def mid_kernel(near_early, near, *rest):
    grid, coef, *poly = rest[len(rest) // 2 :]
    _, (_, above) = towards(None, None)
    side = near[pl.ds(near.shape[0] - SUB, SUB)]
    for way, here in ((True, above), (False, jnp.logical_not(above))):
        pl.when(here)(
            lambda: one_side((near_early, near), side, way, grid, coef, poly, lambda m, found: None)
        )


def outer_kernel(far_early, far, sums, *rest):
    *rest, lines, done = rest
    out, grid, coef, sol, result, *poly = rest[len(rest) // 2 :]
    rows, columns = out.shape[1:]
    lane = lax.broadcasted_iota(jnp.int32, (SUB, LANES), 1)
    (_, above), _ = towards(None, None)

    def far_rows(above):
        side = far[pl.ds(far.shape[0] - SUB, SUB)]
        whole = side_rows(rows, above)
        inside = 1 if above else -1
        edges = [whole[-1] + inside, whole[-1] + 2 * inside]
        acc = {}
        for r in edges + [r for k, r in enumerate(whole) if known(k) >= 0]:
            for g in range(3):
                acc[g, r] = sol[g, r - (REACH - 1)]

        def each(m, found):
            part = [r for k, r in enumerate(whole) if known(k) < m]
            held = [r for r in part if (0, r) in found]
            add(acc, sums, poly, m, held, found)
            add(acc, sums, poly, m, [r for r in part if r not in held])

        one_side((far_early, far), side, above, grid, coef, poly, each)
        span = [r for r in whole + edges[:1] if REACH <= r < REACH + rows]
        finish(grid, sums, result, acc, span)

    pl.when(above)(lambda: far_rows(True))
    pl.when(jnp.logical_not(above))(lambda: far_rows(False))

    moves = []
    for k in range(3):
        for g in range(rows // SUB):
            cut = pl.ds(g * SUB, SUB)
            for t in range(columns // LANES):
                one = result[k, pl.Slice(g * SUB * SUB + 2 * t, SUB, SUB), :]
                two = result[k, pl.Slice(g * SUB * SUB + 2 * t + 1, SUB, SUB), :]
                joined = jnp.where(lane < HALF, turn(one, -SIDE), turn(two, SIDE))
                lines[k, cut, pl.ds(t * LANES, LANES)] = joined
            move = pltpu.make_async_copy(lines.at[k, cut], out.at[k, cut], done.at[k, g])
            move.start()
            moves.append(move)
    for move in moves:
        move.wait()


def shards(state, depth, pole_real, pole_imag, pole_weight):
    rows, columns = depth.shape
    poles = pole_real.shape[0]
    vmem = pl.BlockSpec(memory_space=pltpu.VMEM)
    small = pltpu.CompilerParams(vmem_limit_bytes=GRANT)

    def f32(*shape):
        return jax.ShapeDtypeStruct(shape, jnp.float32)

    given = [
        pltpu.with_memory_space_constraint(x, pltpu.HBM)
        for x in (state, depth, pole_real, pole_imag, pole_weight)
    ]
    hbm = pl.BlockSpec(memory_space=pltpu.HBM)
    message = pltpu.VMEM((rows, LANES), jnp.float32)
    fields, first, second = pl.pallas_call(
        pack_columns_kernel,
        out_shape=(pltpu.VMEM((4, rows, columns), jnp.float32), message, message),
        in_specs=[hbm] * 5,
        out_specs=(vmem,) * 3,
        scratch_shapes=[
            pltpu.SMEM(pole_real.shape, jnp.float32),
            pltpu.SMEM(pole_imag.shape, jnp.float32),
            pltpu.SMEM(pole_weight.shape, jnp.float32),
            pltpu.SemaphoreType.DMA((5,)),
        ],
        compiler_params=small,
        name="pack_columns",
    )(*given)
    blocks = 4 * columns // LANES + 2
    half = blocks // 2 * SUB
    parts = (half + SUB + 4, half, half + SUB, half - SUB, max(4 * poles, half))
    far_early, far, near_early, near, scalars = pl.pallas_call(
        functools.partial(pack_rows_kernel, 4 * poles),
        out_shape=tuple(f32(part, LANES) for part in parts),
        in_specs=[vmem] * 3,
        out_specs=(vmem,) * 5,
        compiler_params=small,
        name="pack_rows",
    )(fields, second, first)
    second = swap(second, "pole", 1)
    first = swap(first, "pole", 0)
    far, near = pl.pallas_call(
        pack_sides_kernel,
        out_shape=(f32(*far.shape), f32(*near.shape)),
        in_specs=[vmem] * 4,
        out_specs=(vmem, vmem),
        input_output_aliases={2: 0, 3: 1},
        compiler_params=small,
        name="pack_sides",
    )(second, first, far, near)
    far_early = swap(far_early, "tile", 1)
    far = swap(far, "tile", 1)
    near_early = swap(near_early, "tile", 0)
    near = swap(near, "tile", 0)
    count = lax.axis_size("pole")
    others = jnp.stack([shift(scalars, "pole", step) for step in range(2, count - 1)])
    height = rows + 2 * REACH
    grid = f32(height * 4 * SUB, LANES)
    poly = [f32(3, height, SUB, LANES)] * ITERS
    coef = f32(4, height, SUB, LANES)
    sol = f32(3, rows + 2, SUB, LANES)
    result = f32(3, (rows + 1) * SUB, LANES)
    state_of = (grid, coef, *poly)
    cost = pl.CostEstimate(
        flops=10 * ITERS * rows * SUB * LANES,
        bytes_accessed=4 * SUB * LANES * rows * (4 + 2 * ITERS + 2),
        transcendentals=0,
    )
    held = pl.pallas_call(
        inner_kernel,
        out_shape=state_of,
        in_specs=[vmem] * 3,
        out_specs=(vmem,) * len(state_of),
        compiler_params=small,
        cost_estimate=cost,
        name="inner",
    )(fields, first, second)
    held = pl.pallas_call(
        mid_kernel,
        out_shape=state_of,
        in_specs=[vmem] * (2 + len(state_of)),
        out_specs=(vmem,) * len(state_of),
        input_output_aliases={2 + i: i for i in range(len(state_of))},
        compiler_params=small,
        cost_estimate=cost,
        name="mid",
    )(near_early, near, *held)
    grid_held, coef_held, *poly_held = held
    sums, *part = pl.pallas_call(
        functools.partial(pole_sums_kernel, 4 * poles),
        out_shape=(f32(9 * ITERS + 2, SUB, LANES), sol, result),
        in_specs=[vmem] * (5 + ITERS),
        out_specs=(vmem,) * 3,
        compiler_params=small,
        name="pole_sums",
    )(scalars, first, second, others, grid_held, *poly_held)
    kept = (grid, coef, sol, result, *poly)
    return pl.pallas_call(
        outer_kernel,
        out_shape=(f32(*state.shape), *kept),
        in_specs=[vmem] * (3 + len(kept)),
        out_specs=(hbm, *(vmem,) * len(kept)),
        scratch_shapes=[
            pltpu.VMEM(state.shape, jnp.float32),
            pltpu.SemaphoreType.DMA((3, rows // SUB)),
        ],
        input_output_aliases={3 + i: 1 + i for i in range(len(kept))},
        compiler_params=small,
        name="outer",
    )(far_early, far, sums, grid_held, coef_held, *part, *poly_held)[0]


def solution(mesh):
    return jax.shard_map(
        shards,
        mesh=mesh,
        in_specs=(
            P(None, "tile", "pole"),
            P("tile", "pole"),
            P("pole"),
            P("pole"),
            P(None, "pole"),
        ),
        out_specs=P(None, "tile", "pole"),
        check_vma=False,
    )
```

```python
import functools

import jax
import jax.numpy as jnp
from jax import lax
from jax.experimental import pallas as pl
from jax.experimental.pallas import tpu as pltpu
from jax.sharding import PartitionSpec as P

ITERS = 8
REACH = ITERS + 1
SUB = 8
LANES = 128
HALF = LANES // 2
SIDE = 32
EDGE = REACH
EAST = HALF + EDGE
GRANT = 16 * 1024 * 1024

coriolis = 0.7
centre = 8.0
half_width = 8.0


def pairs(count, phase):
    swap = []
    for i in range(phase, count + phase, 2):
        a, b = i % count, (i + 1) % count
        swap += [(a, b), (b, a)]
    return swap


def swap(block, axis, phase):
    return lax.ppermute(block, axis, pairs(lax.axis_size(axis), phase))


def shift(block, axis, step):
    count = lax.axis_size(axis)
    return lax.ppermute(block, axis, [(i, (i + step) % count) for i in range(count)])


def turn(x, lanes):
    return pltpu.roll(x, lanes % LANES, 1) if lanes % LANES else x


def cmul(a, b):
    return (a[0] * b[0] - a[1] * b[1], a[0] * b[1] + a[1] * b[0])


def cinv(a):
    norm = 1.0 / (a[0] * a[0] + a[1] * a[1])
    return (a[0] * norm, -a[1] * norm)


def cscale(a, factor):
    return (a[0] * factor, a[1] * factor)


def pack_columns_kernel(
    state, depth, real, imag, weight, fields, first, second, real_in, imag_in, weight_in, done
):
    moves = [
        pltpu.make_async_copy(depth, fields.at[3], done.at[0]),
        pltpu.make_async_copy(state, fields.at[pl.ds(0, 3)], done.at[1]),
        pltpu.make_async_copy(real, real_in, done.at[2]),
        pltpu.make_async_copy(imag, imag_in, done.at[3]),
        pltpu.make_async_copy(weight, weight_in, done.at[4]),
    ]
    for move in moves:
        move.start()
    for move in moves:
        move.wait()
    odd = lax.rem(lax.axis_index("pole"), 2) == 1
    rows, columns = fields.shape[1:]
    lane = lax.broadcasted_iota(jnp.int32, (SUB, LANES), 1)
    sub = lax.broadcasted_iota(jnp.int32, (SUB, LANES), 0)
    poles = real.shape[0]
    values = [real_in[i] for i in range(poles)] + [imag_in[i] for i in range(poles)]
    values += [weight_in[0, i] for i in range(poles)] + [weight_in[1, i] for i in range(poles)]
    for g in range(rows // SUB):
        cut = pl.ds(g * SUB, SUB)
        west = [fields[f, cut, 0:LANES] for f in range(4)]
        east = [fields[f, cut, columns - LANES : columns] for f in range(4)]
        west += [west[3] * west[1], west[3] * west[2]]
        east += [east[3] * east[1], east[3] * east[2]]
        rest = jnp.zeros((SUB, LANES), jnp.float32)
        for i, value in enumerate(values[g * SUB : (g + 1) * SUB]):
            rest = jnp.where(sub == i, value, rest)
        eastward = rest
        westward = rest
        for f in range(6):
            low, high = EDGE * f, EDGE * (f + 1)
            take = jnp.logical_and(lane >= low, lane < high)
            eastward = jnp.where(take, turn(east[f], low + EDGE), eastward)
            take = jnp.logical_and(lane >= EAST + low, lane < EAST + high)
            westward = jnp.where(take, turn(west[f], EAST + low), westward)
        first[cut, :] = jnp.where(odd, westward, eastward)
        second[cut, :] = jnp.where(odd, eastward, westward)


def pack_rows_kernel(count, fields, second, first, far_early, far, near_early, near, scalars):
    rows = fields.shape[1]
    for parts, low in towards((far_early, far), (near_early, near)):
        at = 0
        for part in parts:
            pl.when(low)(lambda: pack_rows(part, at, fields, 0, SUB))
            pl.when(jnp.logical_not(low))(
                lambda: pack_rows(part, at, fields, rows - SUB, rows - SUB - 1)
            )
            at += part.shape[0] // SUB
    odd = lax.rem(lax.axis_index("pole"), 2) == 1
    lane = lax.broadcasted_iota(jnp.int32, (SUB, LANES), 1)
    from_first = jnp.logical_xor(lane >= HALF, odd)
    for g in range(0, scalars.shape[0], SUB):
        if g < count:
            block = jnp.where(from_first, first[pl.ds(g, SUB)], second[pl.ds(g, SUB)])
        else:
            block = jnp.zeros((SUB, LANES), jnp.float32)
        scalars[pl.ds(g, SUB)] = block


def towards(far, near):
    odd = lax.rem(lax.axis_index("tile"), 2) == 1
    return ((far, jnp.logical_not(odd)), (near, odd))


def pack_rows(target, at, fields, main, ext):
    tiles = fields.shape[2] // LANES
    for i in range(target.shape[0] // SUB):
        f, t = divmod(at + i, tiles)
        if f < 4:
            block = fields[f, main : main + SUB, t * LANES : (t + 1) * LANES]
            target[pl.ds(i * SUB, SUB)] = block
        elif t == 0:
            for f in (1, 2):
                flux = fields[3, ext : ext + 1, :] * fields[f, ext : ext + 1, :]
                for t in range(tiles):
                    row = i * SUB + (f - 1) * tiles + t
                    target[row : row + 1] = flux[:, t * LANES : (t + 1) * LANES]


def block_of(parts, at):
    early, late = parts
    count = early.shape[0] // SUB
    if at < count:
        return early[pl.ds(at * SUB, SUB)]
    return late[pl.ds((at - count) * SUB, SUB)]


def sides_of(first, second, cut):
    odd = lax.rem(lax.axis_index("pole"), 2) == 1
    lane = lax.broadcasted_iota(jnp.int32, (SUB, LANES), 1)
    from_first = jnp.logical_xor(lane >= HALF, odd)
    return jnp.where(from_first, first[cut, :], second[cut, :])


def pack_sides_kernel(second, first, far_in, near_in, far, near):
    for target, low in towards(far, near):
        target[pl.ds(target.shape[0] - SUB, SUB)] = pack_sides(second, first, low)


def pack_sides(second, first, low):
    rows = first.shape[0]
    sub = lax.broadcasted_iota(jnp.int32, (SUB, LANES), 0)
    lane = lax.broadcasted_iota(jnp.int32, (SUB, LANES), 1)
    side = jnp.where(
        low,
        sides_of(first, second, pl.ds(0, SUB)),
        sides_of(first, second, pl.ds(rows - SUB, SUB)),
    )
    line = jnp.where(
        low,
        sides_of(first, second, pl.ds(SUB, SUB))[0:1],
        sides_of(first, second, pl.ds(rows - 2 * SUB, SUB))[SUB - 1 : SUB],
    )
    line = jnp.broadcast_to(line, (SUB, LANES))
    low, high = 4 * EDGE, 6 * EDGE
    take = jnp.logical_or(
        jnp.logical_and(lane >= low, lane < high),
        jnp.logical_and(lane >= EAST + low, lane < EAST + high),
    )
    side = jnp.where(jnp.logical_and(take, sub == 0), line, side)
    return side


def pole_sums_kernel(count, scalars, first, second, others, grid, *rest):
    poly, (sums, sol, result) = rest[:ITERS], rest[ITERS:]
    odd = lax.rem(lax.axis_index("pole"), 2) == 1
    lane = lax.broadcasted_iota(jnp.int32, (SUB, LANES), 1)
    blocks = [[scalars[pl.ds(g, SUB)] for g in range(0, count, SUB)]]
    for i, message in enumerate((first, second)):
        low = jnp.logical_xor(lane < HALF, odd if i == 0 else jnp.logical_not(odd))
        part = []
        for g in range(0, count, SUB):
            x = message[pl.ds(g, SUB), :]
            part.append(jnp.where(low, x, turn(x, HALF)))
        blocks.append(part)
    for i in range(others.shape[0]):
        blocks.append([others[i, pl.ds(g, SUB)] for g in range(0, count, SUB)])
    poles = count // 4
    quantity = []
    for q in range(4):
        cut = []
        for block in blocks:
            whole = jnp.concatenate(block, axis=0)
            cut.append(whole[q * poles : (q + 1) * poles])
        quantity.append(jnp.concatenate(cut, axis=0))
    alpha = (quantity[0], quantity[1])
    beta = (quantity[2], quantity[3])
    square = cmul(alpha, alpha)
    shifted = (square[0] + coriolis * coriolis, square[1])
    sigma = ((shifted[0] + centre) / half_width, shifted[1] / half_width)
    rho = [cinv(sigma)]
    for j in range(1, ITERS):
        rho.append(cinv((2.0 * sigma[0] - rho[-1][0], 2.0 * sigma[1] - rho[-1][1])))
    gain = None
    start = []
    for m in range(ITERS):
        if m == 0:
            start.append(cscale(rho[0], 1.0 / half_width))
        else:
            gain = rho[0] if gain is None else cmul(gain, rho[m - 1])
            start.append(cscale(cmul(rho[m], gain), 2.0 / half_width))
    tail = None
    weight = [None] * ITERS
    for m in reversed(range(ITERS)):
        if tail is None:
            weight[m] = start[m]
            tail = (jnp.ones_like(sigma[0]), jnp.zeros_like(sigma[0]))
        else:
            tail = cmul(cmul(rho[m + 1], rho[m]), tail)
            tail = (tail[0] + 1.0, tail[1])
            weight[m] = cmul(start[m], tail)
    inverse_alpha = cinv(alpha)
    inverse_shift = cinv(shifted)
    by_alpha = cmul(beta, inverse_alpha)
    by_shift = cmul(beta, inverse_shift)
    products = {
        "b": beta,
        "b/a": by_alpha,
        "b/s": by_shift,
        "bs/a": cmul(by_alpha, shifted),
        "ba/s": cmul(by_shift, alpha),
        "b/as": cmul(by_alpha, inverse_shift),
    }

    def total(x):
        s = x[0:SUB]
        for i in range(1, x.shape[0] // SUB):
            s = s + x[i * SUB : (i + 1) * SUB]
        for step in (4, 2, 1):
            s = s + pltpu.roll(s, step, 0)
        return s

    names = [("bs/a", "b", "b/a"), ("b", "ba/s", "b/s"), ("b/a", "b/s", "b/as")]
    factor = (1.0, -1.0, -coriolis)
    found = {}
    for m in range(ITERS):
        for name, w in products.items():
            found[name, m] = total(w[0] * weight[m][0] - w[1] * weight[m][1])
        for g in range(3):
            for f in range(3):
                value = found[names[g][f], m]
                sums[(g * 3 + f) * ITERS + m] = value if f == 0 else factor[f] * value
    sums[9 * ITERS] = total(products["ba/s"][0])
    sums[9 * ITERS + 1] = coriolis * total(products["b/s"][0])

    _, (_, above) = towards(None, None)
    rows = sol.shape[1] - 2

    def near_rows(above):
        near, far = side_rows(rows, above), side_rows(rows, not above)
        acc = {}
        for m in range(ITERS):
            add(acc, sums, poly, m, near)
        for m in range(ITERS - 1):
            add(acc, sums, poly, m, [r for k, r in enumerate(far) if known(k) >= m])
        for (g, r), v in acc.items():
            sol[g, r - (REACH - 1)] = v
        inside = sorted(near)[1:-1]
        finish(grid, sums, result, acc, [r for r in inside if REACH <= r < REACH + rows])

    pl.when(above)(lambda: near_rows(True))
    pl.when(jnp.logical_not(above))(lambda: near_rows(False))


def side_rows(rows, above):
    low, high = REACH - 1, REACH + rows
    return [low + k if above else high - k for k in range(rows // 2 + 1)]


def known(k):
    return max(min(ITERS - 2, k - 2), -1)


def add(acc, sums, poly, m, rows, values=None):
    for f in range(3):
        if not rows:
            return
        value = {r: poly[m][f, r] if values is None else values[f, r] for r in rows}
        for g in range(3):
            c = sums[(g * 3 + f) * ITERS + m]
            for r in rows:
                acc[g, r] = acc[g, r] + c * value[r] if (g, r) in acc else c * value[r]


def finish(grid, sums, result, acc, span):
    push = sums[9 * ITERS]
    lift = sums[9 * ITERS + 1]
    for r in span:
        u, v = cell(grid, 1, r), cell(grid, 2, r)
        at = pl.ds((r - REACH) * SUB, SUB)
        result[0, at] = acc[0, r]
        east = 0.5 * (acc[1, r + 1] - acc[1, r - 1])
        north = 0.5 * (right(acc[2, r]) - left(acc[2, r]))
        result[1, at] = (push * u + lift * v) - (east + coriolis * north)
        east = 0.5 * (acc[2, r + 1] - acc[2, r - 1])
        north = 0.5 * (right(acc[1, r]) - left(acc[1, r]))
        result[2, at] = (push * v - lift * u) + (coriolis * east - north)


def strips_of(tiles, side):
    lane = lax.broadcasted_iota(jnp.int32, (SUB, LANES), 1)
    up = [turn(tile, SIDE) for tile in tiles]
    down = [turn(tile, -SIDE) for tile in tiles]
    out = []
    for q in range(len(tiles)):
        out.append(jnp.where(lane < SIDE, up[q - 1] if q else side, up[q]))
        after = down[q + 1] if q + 1 < len(tiles) else side
        out.append(jnp.where(lane < LANES - SIDE, down[q], after))
    return out


def lay(grid, cut, side, at, stride):
    for s, strip in enumerate(strips_of(cut, side)):
        grid[pl.Slice(at * SUB + s, SUB, stride * SUB), :] = strip


def place(side, f):
    return turn(side, SIDE - EDGE - EDGE * f)


def lay_halo(grid, halo, side, main, ext):
    lane = lax.broadcasted_iota(jnp.int32, (SUB, LANES), 1)
    sub = lax.broadcasted_iota(jnp.int32, (SUB, LANES), 0)
    tiles = SUB // 2
    for f in range(4):
        cut = [block_of(halo, f * tiles + t) for t in range(tiles)]
        lay(grid, cut, place(side, f), main * 4 + f, 4)
    line = jnp.broadcast_to(side[0:1], (SUB, LANES))
    side = jnp.where(sub < tiles, place(line, 4), place(line, 5))
    block = block_of(halo, 4 * tiles)
    up, down = turn(block, SIDE), turn(block, -SIDE)
    before = jnp.where(sub % tiles == 0, side, pltpu.roll(up, 1, 0))
    after = jnp.where(sub % tiles == tiles - 1, side, pltpu.roll(down, SUB - 1, 0))
    even = jnp.where(lane < SIDE, before, up)
    odd = jnp.where(lane < LANES - SIDE, down, after)
    for f in (1, 2):
        at = (ext * 4 + f) * SUB
        cut = slice((f - 1) * tiles, f * tiles)
        grid[pl.Slice(at, tiles, 2), :] = even[cut]
        grid[pl.Slice(at + 1, tiles, 2), :] = odd[cut]


def cell(grid, f, r):
    return grid[pl.ds(pl.multiple_of((r * 4 + f) * SUB, SUB), SUB), :]


def left(x):
    return pltpu.roll(x, 1, 1)


def right(x):
    return pltpu.roll(x, LANES - 1, 1)


def prepare(grid, poly, coef, start, count):
    flux_east = [None] * 3
    flux_north = [None] * 3
    depths = [None] * 2
    across = None
    found = {}
    for k in range(count + 2):
        r = start + k
        h = cell(grid, 3, r)
        flux_east = flux_east[1:] + [h * cell(grid, 1, r)]
        flux_north = flux_north[1:] + [h * cell(grid, 2, r)]
        depths = depths[1:] + [h]
        if k >= 1:
            before, across = across, 0.125 * (depths[0] + depths[1])
            coef[0, r - 1] = across
        if k >= 2:
            c = r - 1
            north = 0.125 * (depths[0] + right(depths[0]))
            south = 0.125 * (depths[0] + left(depths[0]))
            coef[1, c] = north
            coef[2, c] = south
            coef[3, c] = 2.0 - ((across + before) + (north + south))
            east_slope = flux_east[2] - flux_east[0]
            north_slope = right(flux_north[1]) - left(flux_north[1])
            poly[0][1, c] = found[1, c] = 0.5 * (east_slope + north_slope)
            east_slope = flux_north[2] - flux_north[0]
            north_slope = right(flux_east[1]) - left(flux_east[1])
            poly[0][2, c] = found[2, c] = 0.5 * (east_slope - north_slope)
            poly[0][0, c] = found[0, c] = cell(grid, 0, c)
    return found


def sweep(poly, coef, m, start, count, last, upwards=False):
    def take(f, r):
        return last[f, r] if (f, r) in last else poly[m][f, r]

    step = -1 if upwards else 1
    order = range(start, start + count)[::step]
    back = [take(f, order[0] - step) for f in range(3)]
    here = [take(f, order[0]) for f in range(3)]
    found = {}
    for r in order:
        north, south, diag = coef[1, r], coef[2, r], coef[3, r]
        above, below = coef[0, r], coef[0, r - 1]
        ahead = [take(f, r + step) for f in range(3)]
        for f in range(3):
            up, down = (back, ahead) if upwards else (ahead, back)
            value = diag * here[f]
            if m > 0:
                value = value - poly[m - 1][f, r]
            value = value + above * up[f]
            value = value + below * down[f]
            value = value + north * right(here[f])
            value = value + south * left(here[f])
            value = 0.5 * value if m == 0 else value
            poly[m + 1][f, r] = value
            found[f, r] = value
        back, here = here, ahead
    return found


def inner_kernel(fields, first, second, grid, coef, *poly):
    rows = fields.shape[1]
    for g in range(rows // SUB):
        side = sides_of(first, second, pl.ds(g * SUB, SUB))
        for f in range(4):
            cut = [
                fields[f, pl.ds(g * SUB, SUB), pl.ds(t * LANES, LANES)]
                for t in range(fields.shape[2] // LANES)
            ]
            lay(grid, cut, place(side, f), (REACH + g * SUB) * 4 + f, 4)
    found = prepare(grid, poly, coef, REACH, rows - 2)
    for m in range(ITERS - 1):
        if rows - 4 - 2 * m > 0:
            found = sweep(poly, coef, m, REACH + 2 + m, rows - 4 - 2 * m, found)


def one_side(halo, side, above, grid, coef, poly, each):
    below = coef.shape[1] - REACH
    main, ext, start = (1, 0, 0) if above else (below, below + SUB, below - 2)
    grid[pl.ds((ext * 4 + 3) * SUB, SUB), :] = jnp.ones((SUB, LANES), jnp.float32)
    lay_halo(grid, halo, side, main, ext)
    found = prepare(grid, poly, coef, start, REACH)
    each(0, found)
    for m in range(ITERS - 1):
        low = 2 + m if above else below - 2 - m
        found = sweep(poly, coef, m, low, REACH, found, above)
        each(m + 1, found)


def mid_kernel(near_early, near, *rest):
    grid, coef, *poly = rest[len(rest) // 2 :]
    _, (_, above) = towards(None, None)
    side = near[pl.ds(near.shape[0] - SUB, SUB)]
    for way, here in ((True, above), (False, jnp.logical_not(above))):
        pl.when(here)(
            lambda: one_side((near_early, near), side, way, grid, coef, poly, lambda m, found: None)
        )


def outer_kernel(far_early, far, sums, *rest):
    *rest, lines, done = rest
    out, grid, coef, sol, result, *poly = rest[len(rest) // 2 :]
    rows, columns = out.shape[1:]
    lane = lax.broadcasted_iota(jnp.int32, (SUB, LANES), 1)
    (_, above), _ = towards(None, None)

    def far_rows(above):
        side = far[pl.ds(far.shape[0] - SUB, SUB)]
        whole = side_rows(rows, above)
        inside = 1 if above else -1
        edges = [whole[-1] + inside, whole[-1] + 2 * inside]
        acc = {}
        for r in edges + [r for k, r in enumerate(whole) if known(k) >= 0]:
            for g in range(3):
                acc[g, r] = sol[g, r - (REACH - 1)]

        def each(m, found):
            part = [r for k, r in enumerate(whole) if known(k) < m]
            held = [r for r in part if (0, r) in found]
            add(acc, sums, poly, m, held, found)
            add(acc, sums, poly, m, [r for r in part if r not in held])

        one_side((far_early, far), side, above, grid, coef, poly, each)
        span = [r for r in whole + edges[:1] if REACH <= r < REACH + rows]
        finish(grid, sums, result, acc, span)

    pl.when(jnp.logical_not(above))(lambda: far_rows(False))
    pl.when(above)(lambda: far_rows(True))

    moves = []
    for k in range(3):
        for g in range(rows // SUB):
            cut = pl.ds(g * SUB, SUB)
            for t in range(columns // LANES):
                one = result[k, pl.Slice(g * SUB * SUB + 2 * t, SUB, SUB), :]
                two = result[k, pl.Slice(g * SUB * SUB + 2 * t + 1, SUB, SUB), :]
                joined = jnp.where(lane < HALF, turn(one, -SIDE), turn(two, SIDE))
                lines[k, cut, pl.ds(t * LANES, LANES)] = joined
            move = pltpu.make_async_copy(lines.at[k, cut], out.at[k, cut], done.at[k, g])
            move.start()
            moves.append(move)
    for move in moves:
        move.wait()


def shards(state, depth, pole_real, pole_imag, pole_weight):
    rows, columns = depth.shape
    poles = pole_real.shape[0]
    vmem = pl.BlockSpec(memory_space=pltpu.VMEM)
    small = pltpu.CompilerParams(vmem_limit_bytes=GRANT)

    def f32(*shape):
        return jax.ShapeDtypeStruct(shape, jnp.float32)

    given = [
        pltpu.with_memory_space_constraint(x, pltpu.HBM)
        for x in (state, depth, pole_real, pole_imag, pole_weight)
    ]
    hbm = pl.BlockSpec(memory_space=pltpu.HBM)
    message = pltpu.VMEM((rows, LANES), jnp.float32)
    fields, first, second = pl.pallas_call(
        pack_columns_kernel,
        out_shape=(pltpu.VMEM((4, rows, columns), jnp.float32), message, message),
        in_specs=[hbm] * 5,
        out_specs=(vmem,) * 3,
        scratch_shapes=[
            pltpu.SMEM(pole_real.shape, jnp.float32),
            pltpu.SMEM(pole_imag.shape, jnp.float32),
            pltpu.SMEM(pole_weight.shape, jnp.float32),
            pltpu.SemaphoreType.DMA((5,)),
        ],
        compiler_params=small,
        name="pack_columns",
    )(*given)
    blocks = 4 * columns // LANES + 2
    half = blocks // 2 * SUB
    parts = (half + SUB + 4, half, half + SUB, half - SUB, max(4 * poles, half))
    far_early, far, near_early, near, scalars = pl.pallas_call(
        functools.partial(pack_rows_kernel, 4 * poles),
        out_shape=tuple(f32(part, LANES) for part in parts),
        in_specs=[vmem] * 3,
        out_specs=(vmem,) * 5,
        compiler_params=small,
        name="pack_rows",
    )(fields, second, first)
    second = swap(second, "pole", 1)
    first = swap(first, "pole", 0)
    far, near = pl.pallas_call(
        pack_sides_kernel,
        out_shape=(f32(*far.shape), f32(*near.shape)),
        in_specs=[vmem] * 4,
        out_specs=(vmem, vmem),
        input_output_aliases={2: 0, 3: 1},
        compiler_params=small,
        name="pack_sides",
    )(second, first, far, near)
    far_early = swap(far_early, "tile", 1)
    far = swap(far, "tile", 1)
    near_early = swap(near_early, "tile", 0)
    near = swap(near, "tile", 0)
    count = lax.axis_size("pole")
    others = jnp.stack([shift(scalars, "pole", step) for step in range(2, count - 1)])
    height = rows + 2 * REACH
    grid = f32(height * 4 * SUB, LANES)
    poly = [f32(3, height, SUB, LANES)] * ITERS
    coef = f32(4, height, SUB, LANES)
    sol = f32(3, rows + 2, SUB, LANES)
    result = f32(3, (rows + 1) * SUB, LANES)
    state_of = (grid, coef, *poly)
    cost = pl.CostEstimate(
        flops=10 * ITERS * rows * SUB * LANES,
        bytes_accessed=4 * SUB * LANES * rows * (4 + 2 * ITERS + 2),
        transcendentals=0,
    )
    held = pl.pallas_call(
        inner_kernel,
        out_shape=state_of,
        in_specs=[vmem] * 3,
        out_specs=(vmem,) * len(state_of),
        compiler_params=small,
        cost_estimate=cost,
        name="inner",
    )(fields, first, second)
    held = pl.pallas_call(
        mid_kernel,
        out_shape=state_of,
        in_specs=[vmem] * (2 + len(state_of)),
        out_specs=(vmem,) * len(state_of),
        input_output_aliases={2 + i: i for i in range(len(state_of))},
        compiler_params=small,
        cost_estimate=cost,
        name="mid",
    )(near_early, near, *held)
    grid_held, coef_held, *poly_held = held
    sums, *part = pl.pallas_call(
        functools.partial(pole_sums_kernel, 4 * poles),
        out_shape=(f32(9 * ITERS + 2, SUB, LANES), sol, result),
        in_specs=[vmem] * (5 + ITERS),
        out_specs=(vmem,) * 3,
        compiler_params=small,
        name="pole_sums",
    )(scalars, first, second, others, grid_held, *poly_held)
    kept = (grid, coef, sol, result, *poly)
    return pl.pallas_call(
        outer_kernel,
        out_shape=(f32(*state.shape), *kept),
        in_specs=[vmem] * (3 + len(kept)),
        out_specs=(hbm, *(vmem,) * len(kept)),
        scratch_shapes=[
            pltpu.VMEM(state.shape, jnp.float32),
            pltpu.SemaphoreType.DMA((3, rows // SUB)),
        ],
        input_output_aliases={3 + i: 1 + i for i in range(len(kept))},
        compiler_params=small,
        name="outer",
    )(far_early, far, sums, grid_held, coef_held, *part, *poly_held)[0]


def solution(mesh):
    return jax.shard_map(
        shards,
        mesh=mesh,
        in_specs=(
            P(None, "tile", "pole"),
            P("tile", "pole"),
            P("pole"),
            P("pole"),
            P(None, "pole"),
        ),
        out_specs=P(None, "tile", "pole"),
        check_vma=False,
    )
```
